32 devices in a mesh: dp: 2 (over x), wide: 16 (over z, y, core).
Axes of the slice: x: 2, y: 2, z: 4, core: 2. Of those that a mesh axis runs over, the one named last changes fastest.
Arguments:
- features: bfloat16 [2, 128, 64, 2048], P('dp', 'wide'), may hold values from -28 to 28
- scale_sizes: int32 [2, 4], P('dp'), may hold values from 12 to 32, as said below
- cotangent: bfloat16 [2, 256, 8192], P('dp', 'wide'), may hold values from -6 to 6
- branch_weight: float32 [29, 256, 2048], P(None, 'wide'), may hold values from -0.088388348 to 0.088388348
- branch_first: float32 [29, 256, 2048], P(None, 'wide'), may hold values from -12 to 12
- branch_second: float32 [29, 256, 2048], P(None, 'wide'), may hold values from 0.5 to 2
- head_weight: float32 [256, 1280], P('wide'), may hold values from -0.15625 to 0.15625
- head_first: float32 [256, 1280], P('wide'), may hold values from -24 to 24
- head_second: float32 [256, 1280], P('wide'), may hold values from 2 to 8
- norm_params: float32 [2, 6, 256], P(None, None, 'wide'), may hold values from -1 to 2
- norm_first: float32 [2, 6, 256], P(None, None, 'wide'), may hold values from -24 to 24
- norm_second: float32 [2, 6, 256], P(None, None, 'wide'), may hold values from 1 to 4
- running_stats: float32 [2, 6, 256], P(None, None, 'wide'), may hold values from 0.02 to 0.2
Outputs:
- head_output: bfloat16 [2, 256, 8192], P('dp', 'wide')
- input_grad: bfloat16 [2, 128, 64, 2048], P('dp', 'wide')
- branch_grads: float32 [29, 256, 2048], P(None, 'wide')
- branch_means: float32 [29, 256, 2048], P(None, 'wide')
- branch_squares: float32 [29, 256, 2048], P(None, 'wide')
- branch_updated: float32 [29, 256, 2048], P(None, 'wide')
- head_grads: float32 [256, 1280], P('wide')
- head_means: float32 [256, 1280], P('wide')
- head_squares: float32 [256, 1280], P('wide')
- head_updated: float32 [256, 1280], P('wide')
- norm_grads: float32 [2, 6, 256], P(None, None, 'wide')
- norm_means: float32 [2, 6, 256], P(None, None, 'wide')
- norm_squares: float32 [2, 6, 256], P(None, None, 'wide')
- norm_updated: float32 [2, 6, 256], P(None, None, 'wide')
- running_next: float32 [2, 6, 256], P(None, None, 'wide')
The draws below stay inside these ranges and needn't reach their ends.
Inputs may be any that keep to these rules, and one draw needn't show every extreme that they name: `scale_sizes`: image i of index g of dp has valid rows 0 to s - 1 and valid columns 0 to 2 s - 1 of its slot, s the entry.
All inputs are finite; a program needn't handle non-finite values.
Results may differ from the reference program's by a relative error of at most 0.02.
Values may be sent and summed in bfloat16 or wider, within the bound.
No kernel may reach another device: no remote copies, remote signals or barrier semaphores. Data moves between devices by JAX's collectives and lax.ppermute only.
A program may use at most 320 MiB of HBM per device.

```python
import math
import jax
import jax.numpy as jnp
from jax import lax

CIN = 2048
CH = 256
SLOT_H = 32
STEP = 10
ROWS = 128
WC = 64
PIXELS = 16384
N_DP = 2


def draw_features(key, part):
    key = jax.random.fold_in(key, 7)
    noise_key, centre_key = jax.random.split(key, 2)
    image_count = ROWS // SLOT_H
    noise = jnp.clip(jax.random.normal(noise_key, (N_DP, ROWS, WC, CIN), jnp.float32), -4.0, 4.0)
    centres = 0.5 * jnp.clip(jax.random.normal(centre_key, (N_DP, image_count, 1, 1, CIN), jnp.float32), -4.0, 4.0)
    centres = jnp.broadcast_to(centres, (N_DP, image_count, SLOT_H, WC, CIN)).reshape(N_DP, ROWS, WC, CIN)
    return (noise + centres).astype(jnp.bfloat16)


def draw_scale_sizes(key, part):
    key = jax.random.fold_in(key, 3)
    spread_key, pick_key = jax.random.split(key)
    image_count = ROWS // SLOT_H
    smallest = SLOT_H * 3 // 8
    group_ids = jnp.arange(N_DP, dtype=jnp.int32)[:, None]
    spans = (SLOT_H - smallest) * (group_ids + 1) // N_DP + 1
    raw_values = jax.random.randint(spread_key, (N_DP, image_count), 0, 1 << 20, dtype=jnp.int32)
    heights = smallest + raw_values % spans
    picked = jax.random.randint(pick_key, (), 0, image_count, dtype=jnp.int32)
    image_ids = jnp.arange(image_count, dtype=jnp.int32)[None, :]
    largest = jnp.logical_and(group_ids == N_DP - 1, image_ids == picked)
    return jnp.where(largest, SLOT_H, heights).astype(jnp.int32)


def draw_branch_weight(key, part):
    key = jax.random.fold_in(key, 5)
    values = jnp.clip(jax.random.normal(key, (29, CH, CIN), jnp.float32), -4.0, 4.0)
    tap_ids = jnp.arange(29)
    scales = jnp.where(jnp.logical_or(tap_ids == 0, tap_ids == 28), CIN ** (-0.5), (9 * CIN) ** (-0.5))
    return values * scales[:, None, None]


def draw_norm_params(key, part):
    key = jax.random.fold_in(key, 9)
    gain_key, shift_key = jax.random.split(key)
    gains = jax.random.uniform(gain_key, (1, 6, CH), jnp.float32, 0.5, 2.0)
    shifts = jnp.clip(0.4 * jax.random.normal(shift_key, (1, 6, CH), jnp.float32), -1.0, 1.0)
    return jnp.concatenate([gains, shifts], axis=0)


def steps_of(own_key, dims, cuts, low, high):
    factor_of, own = 1.0, jax.random.fold_in(own_key, 6)
    for axis_at, parts in cuts:
        steps = jnp.exp(jax.random.uniform(jax.random.fold_in(own, axis_at), (parts,), jnp.float32, low / len(cuts), high / len(cuts)))
        factor_of = factor_of * jnp.repeat(steps, dims[axis_at] // parts).reshape([-1 if axis == axis_at else 1 for axis in range(len(dims))])
    return factor_of


def normal_values(rng, dims, width, reach, cuts=(), kind=jnp.bfloat16):
    drawn = jax.random.normal(rng, dims, jnp.float32) * width
    if len(cuts) > 0:
        drawn = steps_of(rng, dims, cuts, -0.22, 0.18) * drawn
    return jnp.clip(drawn, min=-reach, max=reach).astype(kind)


def setup_inputs(seed: int = 0) -> dict:
    keys = jax.random.split(jax.random.key(seed), 14)
    return {
        "features": draw_features(jax.random.fold_in(keys[13], 71), 0),
        "scale_sizes": draw_scale_sizes(jax.random.fold_in(keys[13], 71), 0),
        "cotangent": normal_values(keys[2], (N_DP, CH, ROWS * WC), 1.0, 6.0, ((0, 2), (1, 16))),
        "branch_weight": draw_branch_weight(jax.random.fold_in(keys[13], 71), 0),
        "branch_first": normal_values(keys[4], (29, CH, CIN), (PIXELS ** 2 ** -1 * 2 ** -6), 12.0, ((1, 16),), jnp.float32),
        "branch_second": jnp.clip(jnp.exp(math.log(2.0) - 1.3862944 * jax.random.uniform(keys[5], (29, CH, CIN), jnp.float32) ** steps_of(keys[5], (29, CH, CIN), ((1, 16),), -0.2, 0.2)), 0.5, 2.0),
        "head_weight": normal_values(keys[6], (CH, 5 * CH), (5 * CH) ** -0.5, 0.15625, ((0, 16),), jnp.float32),
        "head_first": normal_values(keys[7], (CH, 5 * CH), (PIXELS ** 2 ** -1 * 2 ** -5), 24.0, ((0, 16),), jnp.float32),
        "head_second": jnp.clip(jnp.exp(math.log(8.0) - 1.3862944 * jax.random.uniform(keys[8], (CH, 5 * CH), jnp.float32) ** steps_of(keys[8], (CH, 5 * CH), ((0, 16),), -0.2, 0.2)), 2.0, 8.0),
        "norm_params": draw_norm_params(jax.random.fold_in(keys[13], 71), 0),
        "norm_first": normal_values(keys[10], (2, 6, CH), (PIXELS ** 2 ** -1 * 2 ** -5), 24.0, ((2, 16),), jnp.float32),
        "norm_second": jnp.clip(jnp.exp(math.log(4.0) - 1.3862944 * jax.random.uniform(keys[11], (2, 6, CH), jnp.float32) ** steps_of(keys[11], (2, 6, CH), ((2, 16),), -0.2, 0.2)), 1.0, 4.0),
        "running_stats": jnp.clip(jnp.exp(math.log(0.2) - 2.3025851 * jax.random.uniform(keys[12], (2, 6, CH), jnp.float32) ** steps_of(keys[12], (2, 6, CH), ((2, 16),), -0.2, 0.2)), 0.02, 0.2),
    }


@jax.custom_vjp
def low(v):
    return lax.optimization_barrier(v.astype(jnp.bfloat16)).astype(jnp.float32)

@jax.custom_vjp
def low_back(v):
    return v

def low_keep(v):
    return (low(v), None)

def low_pass(kept, grad):
    return (grad,)

def back_keep(v):
    return (v, None)

def back_low(kept, grad):
    return (low(grad),)
low.defvjp(low_keep, low_pass)
low_back.defvjp(back_keep, back_low)
dilations = (6, 12, 18)
epsilon = 1e-05
momentum = 0.1
first_decay = 0.9
second_decay = 0.999
conv_rate = 0.02
norm_rate = 0.4
weight_decay = 0.0001
adam_floor = 1e-08
highest = lax.Precision.HIGHEST

def tap_offsets():
    offsets = []
    for dilation in dilations:
        for row_step in range(3):
            for col_step in range(3):
                offsets.append(((row_step - 1) * dilation, (col_step - 1) * dilation))
    return offsets

def shift_slot(values_in, row_off, col_off):
    height = values_in.shape[-3]
    breadth = values_in.shape[-2]
    if abs(row_off) >= height or abs(col_off) >= breadth:
        return jnp.zeros_like(values_in)
    row_pad = abs(row_off)
    col_pad = abs(col_off)
    pad_widths = [(0, 0)] * (values_in.ndim - 3) + [(row_pad, row_pad), (col_pad, col_pad), (0, 0)]
    padded = jnp.pad(values_in, pad_widths)
    row_first = row_pad + row_off
    col_first = col_pad + col_off
    padded = lax.slice_in_dim(padded, row_first, row_first + height, axis=values_in.ndim - 3)
    return lax.slice_in_dim(padded, col_first, col_first + breadth, axis=values_in.ndim - 2)

def slot_inside(heights, slot_rows, columns):
    row_ids = jnp.arange(slot_rows, dtype=jnp.int32)[:, None]
    col_ids = jnp.arange(columns, dtype=jnp.int32)[None, :]
    extent = heights[..., None, None]
    return jnp.logical_and(row_ids < extent, col_ids < 2 * extent).astype(jnp.float32)

def adamw_update(parameter, gradient, moment_one, moment_two, step_rate, decay_rate):
    first_new = first_decay * moment_one + (1.0 - first_decay) * gradient
    second_new = second_decay * moment_two + (1.0 - second_decay) * gradient * gradient
    first_hat = first_new / (1.0 - first_decay ** STEP)
    second_hat = second_new / (1.0 - second_decay ** STEP)
    updated = parameter - step_rate * (first_hat / (jnp.sqrt(second_hat) + adam_floor) + decay_rate * parameter)
    return (first_new, second_new, updated)

def batch_norm(pre_value, inside_weights, overall, sum_axes, gain_row, shift_row):
    centre = lax.optimization_barrier(jnp.sum(pre_value * inside_weights, axis=sum_axes)) / overall
    variance = lax.optimization_barrier(jnp.sum(pre_value * pre_value * inside_weights, axis=sum_axes)) / overall - centre * centre
    normed = gain_row * (pre_value - centre) * lax.rsqrt(variance + epsilon) + shift_row
    return (normed, centre, variance)

def reference(features, scale_sizes, cotangent, branch_weight, branch_first, branch_second, head_weight, head_first, head_second, norm_params, norm_first, norm_second, running_stats):
    group_count, total_rows, columns, channels_in = features.shape
    image_count = scale_sizes.shape[1]
    slot_rows = total_rows // image_count
    tap_count = branch_weight.shape[0]
    channels = branch_weight.shape[1]
    inside = slot_inside(scale_sizes, slot_rows, columns)
    weighted = inside[..., None]
    image_areas = (2 * scale_sizes * scale_sizes).astype(jnp.float32)
    pixel_total = jnp.sum(inside)
    image_total = float(group_count * image_count)
    inputs = features.astype(jnp.float32).reshape(group_count, image_count, slot_rows, columns, channels_in)
    grad_out = jnp.transpose(cotangent.astype(jnp.float32), (0, 2, 1)).reshape(group_count, image_count, slot_rows, columns, channels)
    offsets = tap_offsets()

    def forward(pixels, conv_master, head_master, params):
        masked = pixels * weighted
        tap_values = low_back(jnp.einsum('gihwk,tck->gihwtc', masked, low(conv_master), precision=highest))
        branch_pre = [tap_values[..., 0, :]]
        for dilation_id in range(3):
            accumulated = jnp.zeros_like(branch_pre[0])
            for position in range(9):
                row_off, col_off = offsets[9 * dilation_id + position]
                accumulated = accumulated + shift_slot(tap_values[..., 1 + 9 * dilation_id + position, :], row_off, col_off)
            branch_pre.append(accumulated)
        activations = []
        centres = []
        variances = []
        for branch_id in range(4):
            normed, centre, variance = batch_norm(branch_pre[branch_id], weighted, pixel_total, (0, 1, 2, 3), params[0, branch_id], params[1, branch_id])
            activations.append(jax.nn.gelu(normed))
            centres.append(centre)
            variances.append(variance)
        pooled = lax.optimization_barrier(jnp.sum(tap_values[..., tap_count - 1, :] * weighted, axis=(2, 3))) / image_areas[..., None]
        pool_norm, centre, variance = batch_norm(pooled, 1.0, image_total, (0, 1), params[0, 4], params[1, 4])
        centres.append(centre)
        variances.append(variance)
        activations.append(jnp.broadcast_to(jax.nn.gelu(pool_norm)[:, :, None, None, :], branch_pre[0].shape))
        concat = low(jnp.stack(activations, axis=4))
        projection = low(head_master).reshape(channels, 5, channels)
        head_pre = low_back(jnp.einsum('gihwbc,obc->gihwo', concat, projection, precision=highest))
        head_norm, centre, variance = batch_norm(head_pre, weighted, pixel_total, (0, 1, 2, 3), params[0, 5], params[1, 5])
        centres.append(centre)
        variances.append(variance)
        result = weighted * jax.nn.gelu(head_norm)
        return (result, (jnp.stack(centres), jnp.stack(variances)))
    result, pullback, statistics = jax.vjp(forward, inputs, branch_weight, head_weight, norm_params, has_aux=True)
    input_back, branch_grads, head_grads, norm_grads = pullback(grad_out)
    centres, variances = statistics
    factors = jnp.where(jnp.arange(6) == 4, image_total / (image_total - 1.0), pixel_total / (pixel_total - 1.0))
    running_next = (1.0 - momentum) * running_stats + momentum * jnp.stack([centres, variances * factors[:, None]])
    head_output = jnp.transpose(result.reshape(group_count, total_rows * columns, channels), (0, 2, 1)).astype(jnp.bfloat16)
    input_grad = input_back.reshape(features.shape).astype(jnp.bfloat16)
    branch_means, branch_squares, branch_updated = adamw_update(branch_weight, branch_grads, branch_first, branch_second, conv_rate, weight_decay)
    head_means, head_squares, head_updated = adamw_update(head_weight, head_grads, head_first, head_second, conv_rate, weight_decay)
    norm_means, norm_squares, norm_updated = adamw_update(norm_params, norm_grads, norm_first, norm_second, norm_rate, 0.0)
    return (head_output, input_grad, branch_grads, branch_means, branch_squares, branch_updated, head_grads, head_means, head_squares, head_updated, norm_grads, norm_means, norm_squares, norm_updated, running_next)
```

```python
import functools

import jax
import jax.numpy as jnp
from jax import lax
from jax.experimental import pallas as pl
from jax.experimental.pallas import tpu as pltpu
from jax.sharding import Mesh, PartitionSpec as P

STEP = 10


dilations = (6, 12, 18)
epsilon = 1e-05
momentum = 0.1
first_decay = 0.9
second_decay = 0.999
conv_rate = 0.02
norm_rate = 0.4
weight_decay = 0.0001
adam_floor = 1e-08

LANES = 128
VMEM_LIMIT = 56 * 1024 * 1024
PLANE = ("z", "y", "c")
QUAD = ("y", "c")
SWAP = [(0, 1), (1, 0)]
PAIR = [(0, 1), (1, 0), (2, 3), (3, 2)]
MID = [(1, 2), (2, 1)]
OUTWARD = [(1, 0), (2, 3)]
INWARD = [(0, 1), (3, 2)]

bf16 = jnp.bfloat16
f32 = jnp.float32
barrier = lax.optimization_barrier


def gelu_back(pre_value, gradient):
    return jax.vjp(jax.nn.gelu, pre_value)[1](gradient)[0]


def adamw_update(parameter, gradient, moment_one, moment_two, step_rate, decay_rate):
    first_new = first_decay * moment_one + (1.0 - first_decay) * gradient
    second_new = second_decay * moment_two + (1.0 - second_decay) * gradient * gradient
    first_hat = first_new / (1.0 - first_decay**STEP)
    second_hat = second_new / (1.0 - second_decay**STEP)
    updated = parameter - step_rate * (
        first_hat / (jnp.sqrt(second_hat) + adam_floor) + decay_rate * parameter
    )
    return (first_new, second_new, updated)


def total_over(value, axes):
    count = 1
    for axis in axes:
        count *= lax.axis_size(axis)
    spread = jnp.broadcast_to(value[None], (count,) + value.shape)
    return jnp.sum(lax.all_to_all(spread, axes, 0, 0, tiled=True), axis=0)


def lane_masks(columns):
    lane = lax.broadcasted_iota(jnp.int32, (1, LANES), 1) % columns
    masks = {}
    for dilation in dilations:
        for off in (-dilation, dilation):
            moved = lane + off
            masks[off] = jnp.logical_and(moved >= 0, moved < columns)
    return masks


def forward_kernel(columns, split, sel_ref, x_ref, wz_ref, wx_ref, mask_ref, pre_ref, stat_ref, taps):
    step = pl.program_id(0)
    half = wz_ref.shape[0]
    block = x_ref.shape[0]
    sel = sel_ref[0]
    contract = (((1,), (1,)), ((), ()))
    pixels = x_ref[...]
    cols = pl.ds(pl.multiple_of(step * block, block), block)
    taps[pl.ds(pl.multiple_of(sel * half, 16), half), cols] = lax.dot_general(
        wz_ref[...], pixels, contract, preferred_element_type=f32
    )
    taps[pl.ds(pl.multiple_of((1 - sel) * half, 16), half), cols] = lax.dot_general(
        wx_ref[...], pixels, contract, preferred_element_type=f32
    )

    @pl.when(step == pl.num_programs(0) - 1)
    def _():
        total = taps.shape[1]
        tiles = total // LANES
        chans = pre_ref.shape[1]
        masks = lane_masks(columns)

        def rows_of(tap):
            first = tap * chans if tap <= split else (tap + 1) * chans
            return slice(first, first + chans)

        def tile(tap, at):
            return taps[rows_of(tap), at * LANES : (at + 1) * LANES]

        sums = [jnp.zeros((chans, LANES), f32) for _ in range(4)]
        squares = [jnp.zeros((chans, LANES), f32) for _ in range(4)]
        pooled = jnp.zeros((chans, LANES), f32)
        for at in range(tiles):
            lanes = slice(at * LANES, (at + 1) * LANES)
            weight = mask_ref[0:1, lanes]
            for branch in range(4):
                if branch == 0:
                    value = tile(0, at)
                else:
                    dilation = dilations[branch - 1]
                    jump = dilation * columns // LANES
                    value = None
                    for b in range(3):
                        part = None
                        for a in range(3):
                            source = at + (a - 1) * jump
                            if 0 <= source < tiles:
                                term = tile(1 + 9 * (branch - 1) + 3 * a + b, source)
                                part = term if part is None else part + term
                        off = (b - 1) * dilation
                        if off != 0:
                            part = pltpu.roll(part, (-off) % LANES, 1)
                            part = jnp.where(masks[off], part, 0.0)
                        value = part if value is None else value + part
                pre_ref[branch, :, lanes] = value
                weighted = value * weight
                sums[branch] = sums[branch] + weighted
                squares[branch] = squares[branch] + weighted * value
            pooled = pooled + tile(28, at)
        lane = lax.broadcasted_iota(jnp.int32, (chans, LANES), 1)
        for branch in range(4):
            one = jnp.sum(sums[branch], axis=1, keepdims=True)
            two = jnp.sum(squares[branch], axis=1, keepdims=True)
            row = jnp.where(lane == 0, one, jnp.where(lane == 1, two, 0.0))
            if branch == 0:
                row = jnp.where(lane == 2, jnp.sum(pooled, axis=1, keepdims=True), row)
            stat_ref[branch * chans : (branch + 1) * chans, :] = row


def forward_taps(pixels, mask_row, sel, wz, wx, columns, chans, split):
    total, depth = pixels.shape
    block = total // 4
    half = wz.shape[0]
    return pl.pallas_call(
        functools.partial(forward_kernel, columns, split),
        out_shape=(
            jax.ShapeDtypeStruct((4, chans, total), f32),
            jax.ShapeDtypeStruct((4 * chans, LANES), f32),
        ),
        grid_spec=pltpu.PrefetchScalarGridSpec(
            num_scalar_prefetch=1,
            grid=(4,),
            in_specs=[
                pl.BlockSpec((block, depth), lambda i, s: (i, 0)),
                pl.BlockSpec((half, depth), lambda i, s: (0, 0)),
                pl.BlockSpec((half, depth), lambda i, s: (0, 0)),
                pl.BlockSpec((8, total), lambda i, s: (0, 0)),
            ],
            out_specs=(
                pl.BlockSpec((4, chans, total), lambda i, s: (0, 0, 0)),
                pl.BlockSpec((4 * chans, LANES), lambda i, s: (0, 0)),
            ),
            scratch_shapes=[pltpu.VMEM((2 * half, total), f32)],
        ),
        compiler_params=pltpu.CompilerParams(vmem_limit_bytes=VMEM_LIMIT),
        cost_estimate=pl.CostEstimate(
            flops=4 * half * total * depth,
            bytes_accessed=2 * total * depth + 4 * half * depth + 16 * chans * total,
            transcendentals=0,
        ),
        name="atrous_forward",
    )(sel, pixels, wz, wx, mask_row)


def weight_kernel(columns, sel_ref, g_ref, x_ref, keep_ref, send_ref, taps_ref, total_ref):
    chans = g_ref.shape[0] // 5
    half = keep_ref.shape[0]
    start = half - chans

    @pl.when(pl.program_id(0) == 0)
    def _():
        tiles = g_ref.shape[1] // LANES
        masks = lane_masks(columns)
        for at in range(tiles):
            lanes = slice(at * LANES, (at + 1) * LANES)
            taps_ref[0:chans, lanes] = g_ref[0:chans, lanes]
            taps_ref[28 * chans : 29 * chans, lanes] = g_ref[4 * chans : 5 * chans, lanes]
            for j, dilation in enumerate(dilations):
                jump = dilation * columns // LANES
                grad = g_ref[(1 + j) * chans : (2 + j) * chans, lanes].astype(f32)
                for b in range(3):
                    off = (b - 1) * dilation
                    moved = grad
                    if off != 0:
                        moved = pltpu.roll(grad, off % LANES, 1)
                        moved = jnp.where(masks[-off], moved, 0.0)
                    moved = moved.astype(bf16)
                    for a in range(3):
                        tap = 1 + 9 * j + 3 * a + b
                        rows = slice(tap * chans, (tap + 1) * chans)
                        target = at + (a - 1) * jump
                        if 0 <= target < tiles:
                            taps_ref[rows, target * LANES : (target + 1) * LANES] = moved
                        source = at - (a - 1) * jump
                        if not 0 <= source < tiles:
                            taps_ref[rows, lanes] = jnp.zeros((chans, LANES), bf16)

    total_ref[...] = jnp.dot(taps_ref[...], x_ref[...], preferred_element_type=f32)
    sel = sel_ref[0]
    keep_ref[...] = total_ref[pl.ds(pl.multiple_of(sel * start, 16), half), :].astype(bf16)
    send_ref[...] = total_ref[pl.ds(pl.multiple_of((1 - sel) * start, 16), half), :].astype(bf16)


def weight_grads(grads, pixels, sel, columns, half):
    rows, total = grads.shape
    chans = rows // 5
    depth = pixels.shape[1]
    block = depth // 4
    return pl.pallas_call(
        functools.partial(weight_kernel, columns),
        out_shape=(
            jax.ShapeDtypeStruct((half, depth), bf16),
            jax.ShapeDtypeStruct((half, depth), bf16),
            jax.ShapeDtypeStruct((29 * chans, total), bf16),
        ),
        grid_spec=pltpu.PrefetchScalarGridSpec(
            num_scalar_prefetch=1,
            grid=(4,),
            in_specs=[
                pl.BlockSpec((rows, total), lambda i, s: (0, 0)),
                pl.BlockSpec((total, block), lambda i, s: (0, i)),
            ],
            out_specs=(
                pl.BlockSpec((half, block), lambda i, s: (0, i)),
                pl.BlockSpec((half, block), lambda i, s: (0, i)),
                pl.BlockSpec((29 * chans, total), lambda i, s: (0, 0)),
            ),
            scratch_shapes=[pltpu.VMEM((29 * chans, block), f32)],
        ),
        compiler_params=pltpu.CompilerParams(vmem_limit_bytes=VMEM_LIMIT),
        cost_estimate=pl.CostEstimate(
            flops=2 * 29 * chans * total * depth,
            bytes_accessed=2 * total * depth + 8 * half * depth,
            transcendentals=0,
        ),
        name="atrous_weight_grad",
    )(sel, grads, pixels)


def input_kernel(start, sel_ref, strip_ref, *refs):
    taps = refs[0:4]
    weights = refs[4:12]
    out_ref, total = refs[12], refs[13]
    half = weights[0].shape[0]
    contract = (((0,), (0,)), ((), ()))
    for slot in range(4):
        sel = sel_ref[slot]
        for which in range(2):
            first = sel * start if which == 0 else (1 - sel) * start
            part = lax.dot_general(
                taps[slot][pl.ds(pl.multiple_of(first, 16), half), :],
                weights[2 * slot + which][...],
                contract,
                preferred_element_type=f32,
            )
            if slot == 0 and which == 0:
                total[...] = part
            else:
                total[...] += part
    out_ref[0] = total[...].astype(bf16)


def input_grads(taps, weights, sels, strips, block):
    rows, total = taps[0].shape
    half, depth = weights[0].shape
    count = strips.shape[0]
    start = rows - half
    return pl.pallas_call(
        functools.partial(input_kernel, start),
        out_shape=jax.ShapeDtypeStruct((count, block, depth), bf16),
        grid_spec=pltpu.PrefetchScalarGridSpec(
            num_scalar_prefetch=2,
            grid=(count,),
            in_specs=[pl.BlockSpec((rows, block), lambda i, s, t: (0, t[i]))] * 4
            + [pl.BlockSpec((half, depth), lambda i, s, t: (0, 0))] * 8,
            out_specs=pl.BlockSpec((1, block, depth), lambda i, s, t: (i, 0, 0)),
            scratch_shapes=[pltpu.VMEM((block, depth), f32)],
        ),
        compiler_params=pltpu.CompilerParams(vmem_limit_bytes=VMEM_LIMIT),
        cost_estimate=pl.CostEstimate(
            flops=2 * 4 * rows * block * count * depth,
            bytes_accessed=16 * half * depth + 2 * count * block * depth,
            transcendentals=0,
        ),
        name="atrous_input_grad",
    )(sels, strips, *taps, *weights)


def local(
    features,
    scale_sizes,
    cotangent,
    branch_weight,
    branch_first,
    branch_second,
    head_weight,
    head_first,
    head_second,
    norm_params,
    norm_first,
    norm_second,
    running_stats,
):
    groups = lax.axis_size("dp")
    halves = groups == 2
    images = scale_sizes.shape[1]
    x_id, z_id = lax.axis_index("dp"), lax.axis_index("z")
    quad_id = lax.axis_index("y") * 2 + lax.axis_index("c")
    wide_id = z_id * 4 + quad_id
    strip_rows, columns, depth = features.shape[1:]
    strip = strip_rows * columns
    total = 4 * strip
    tap_count, chans = branch_weight.shape[:2]
    all_ch = chans * lax.axis_size("z") * 4
    split = (tap_count - 1) // 2
    half = (split + 1) * chans
    ends = jnp.logical_or(z_id == 0, z_id == 3)
    mid = jnp.logical_not(ends)

    height = lax.dynamic_index_in_dim(scale_sizes[0], z_id, 0, keepdims=False)
    pixel = jnp.arange(total, dtype=jnp.int32)
    inside = jnp.logical_and(pixel // columns < height, pixel % columns < 2 * height).astype(f32)
    own_inside = lax.dynamic_slice_in_dim(inside, quad_id * strip, strip, 0)
    area = (2 * height * height).astype(f32)
    mask_rows = jnp.broadcast_to(inside[None], (8, total))

    low_half = branch_weight[: split + 1]
    high_half = jnp.concatenate(
        [jnp.zeros_like(branch_weight[:1]), branch_weight[split + 1 :]], axis=0
    )
    own_w = [
        part.astype(bf16).reshape(half, depth) for part in (low_half, high_half)
    ]

    masked = features[0].reshape(strip, depth) * own_inside[:, None].astype(bf16)
    over_c = lax.ppermute(masked, "c", SWAP)
    over_y = lax.ppermute(masked, "y", SWAP)
    over_yc = lax.ppermute(over_y, "c", SWAP)

    def z_chain(block):
        near = lax.ppermute(block, "z", PAIR)
        mid_one = lax.ppermute(block, "z", MID)
        mid_two = lax.ppermute(near, "z", MID)
        out_one = lax.ppermute(mid_one, "z", OUTWARD)
        out_two = lax.ppermute(mid_two, "z", OUTWARD)
        second = jnp.where(mid, mid_one, out_one)
        out_two, second = barrier((out_two, second))
        third = jnp.where(mid, mid_two, out_two)
        return near, second, third

    if halves:
        mine = jnp.where(x_id == 0, own_w[0], own_w[1])
        slots = [(mine_z, lax.ppermute(mine_z, "dp", SWAP)) for mine_z in z_chain(mine)]
        sel = x_id.astype(jnp.int32)
    else:
        lows, highs = z_chain(own_w[0]), z_chain(own_w[1])
        slots = list(zip(lows, highs))
        sel = jnp.zeros((), jnp.int32)
    zero = jnp.zeros((), jnp.int32)
    slots = [tuple(own_w)] + slots
    sels = [zero, sel, sel, sel]
    order = jnp.stack(
        [
            z_id,
            jnp.array([1, 0, 3, 2], jnp.int32)[z_id],
            jnp.array([2, 2, 1, 1], jnp.int32)[z_id],
            jnp.array([3, 3, 0, 0], jnp.int32)[z_id],
        ]
    )
    place = (order[None, :] == jnp.arange(4, dtype=jnp.int32)[:, None]).astype(f32)

    def to_canon(by_slot):
        grown = place.reshape((4, 4) + (1,) * (by_slot.ndim - 1))
        return jnp.sum(grown * by_slot[None], axis=1)

    def to_slots(by_z):
        grown = place.reshape((4, 4) + (1,) * (by_z.ndim - 1))
        return jnp.sum(grown * by_z[:, None], axis=0)

    all_norm = lax.all_gather(norm_params, PLANE, axis=0).reshape(4, 4, 2, 6, chans)
    own_norm = lax.dynamic_index_in_dim(all_norm, quad_id, 1, keepdims=False)
    slot_norm = to_slots(own_norm)
    head_norm_params = jnp.transpose(all_norm[:, :, :, 5], (2, 0, 1, 3)).reshape(2, all_ch)
    gains, shifts = slot_norm[:, 0], slot_norm[:, 1]
    projection = lax.all_gather(head_weight.astype(bf16), PLANE, axis=0, tiled=True)
    projection = projection.reshape(all_ch, 5, 4, 4, chans)
    projection = jnp.stack(
        [lax.dynamic_index_in_dim(projection, order[slot], 2, keepdims=False) for slot in range(4)],
        axis=0,
    )
    projection = jnp.transpose(projection, (1, 3, 0, 2, 4))
    pixel_proj = projection[:, :, :, :4].reshape(all_ch, 4, 16 * chans)
    pixel_proj = jnp.pad(pixel_proj, ((0, 0), (0, 0), (0, 16))).reshape(all_ch, 4 * (16 * chans + 16))
    pool_proj = projection[:, :, :, 4].astype(f32).reshape(all_ch, 16 * chans)

    cot = lax.all_to_all(cotangent[0], PLANE, 1, 0, tiled=True)

    pixels = jnp.zeros((total, depth), bf16)
    for flip, part in enumerate((masked, over_c, over_y, over_yc)):
        pixels = lax.dynamic_update_slice_in_dim(
            pixels, part, jnp.bitwise_xor(quad_id, flip) * strip, 0
        )

    pre, stats = [], []
    for slot in range(4):
        pre_part, stat_part = forward_taps(
            pixels, mask_rows, sels[slot][None], *slots[slot], columns, chans, split
        )
        pre.append(pre_part)
        stats.append(stat_part)
    stats = jnp.stack(stats).reshape(4, 4, chans, LANES)
    pooled = stats[:, 0, :, 2] / area
    image_total = float(groups * images)
    partial = jnp.concatenate(
        [
            stats[..., 0],
            stats[..., 1],
            pooled[:, None],
            (pooled * pooled)[:, None],
            jnp.broadcast_to(area, (4, 1, chans)),
        ],
        axis=1,
    )
    sums = total_over(to_canon(partial), ("dp", "z"))
    pixel_total = sums[0, 10, 0]
    counts = jnp.concatenate([jnp.full((4,), 1.0, f32) * pixel_total, jnp.full((1,), image_total, f32)])
    firsts = jnp.concatenate([sums[:, 0:4], sums[:, 8:9]], axis=1)
    seconds = jnp.concatenate([sums[:, 4:8], sums[:, 9:10]], axis=1)
    centres = firsts / counts[None, :, None]
    variances = seconds / counts[None, :, None] - centres * centres
    inverses = lax.rsqrt(variances + epsilon)
    slot_centre, slot_inverse = to_slots(centres), to_slots(inverses)

    def branch_hat(slot):
        return (pre[slot] - slot_centre[slot, :4, :, None]) * slot_inverse[slot, :4, :, None]

    def branch_norm(slot):
        return (
            gains[slot, :4, :, None] * (pre[slot] - slot_centre[slot, :4, :, None])
        ) * slot_inverse[slot, :4, :, None] + shifts[slot, :4, :, None]

    pool_norm = gains[:, 4] * (pooled - slot_centre[:, 4]) * slot_inverse[:, 4] + shifts[:, 4]
    pool_hat = (pooled - slot_centre[:, 4]) * slot_inverse[:, 4]
    pool_act = jax.nn.gelu(pool_norm).astype(bf16)

    parts = [jax.nn.gelu(branch_norm(slot)).astype(bf16) for slot in range(4)]
    concat = jnp.stack(parts).reshape(4 * 4 * chans, 4, strip)
    concat = jnp.transpose(concat, (1, 0, 2))
    extra = jnp.pad(pool_act.reshape(1, 4 * chans), ((0, 15), (0, strip - 4 * chans)))
    concat = jnp.concatenate([concat, jnp.broadcast_to(extra[None], (4, 16, strip))], axis=1)
    concat = lax.all_to_all(concat, QUAD, 0, 0, tiled=True)
    all_pool = concat[:, 16 * chans, : 4 * chans].astype(f32).reshape(16 * chans)
    concat = concat.reshape(4 * (16 * chans + 16), strip)

    unit = jnp.dot(pixel_proj, concat, preferred_element_type=f32)
    unit = unit + jnp.sum(pool_proj * all_pool[None], axis=1)[:, None]
    weighted = own_inside[None]
    head_sums = total_over(
        jnp.stack([jnp.sum(unit * weighted, axis=1), jnp.sum(unit * unit * weighted, axis=1)]),
        ("dp",) + PLANE,
    )
    head_centre = head_sums[0] / pixel_total
    head_variance = head_sums[1] / pixel_total - head_centre * head_centre
    head_inverse = lax.rsqrt(head_variance + epsilon)
    head_gain, head_shift = head_norm_params[0], head_norm_params[1]
    head_hat = (unit - head_centre[:, None]) * head_inverse[:, None]
    head_norm = (head_gain[:, None] * (unit - head_centre[:, None])) * head_inverse[
        :, None
    ] + head_shift[:, None]
    head_values = (weighted * jax.nn.gelu(head_norm)).astype(bf16)
    head_output = lax.all_to_all(head_values, PLANE, 0, 1, tiled=True)[None]
    head_delta = gelu_back(head_norm, weighted * cot.astype(f32))
    head_moments = total_over(
        jnp.stack([jnp.sum(head_delta, axis=1), jnp.sum(head_delta * head_hat, axis=1)]),
        ("dp",) + PLANE,
    )
    unit_back = (
        weighted
        * (
            (head_gain * head_inverse)[:, None]
            * (
                head_delta
                - (head_moments[0][:, None] + head_hat * head_moments[1][:, None]) / pixel_total
            )
        )
    ).astype(bf16)
    row_sums = jnp.sum(unit_back.astype(f32), axis=1)

    concat_terms = lax.dot_general(
        pixel_proj, unit_back, (((0,), (0,)), ((), ())), preferred_element_type=f32
    ).astype(bf16)
    concat_terms = concat_terms.reshape(4, 16 * chans + 16, strip)[:, : 16 * chans]
    pool_terms = jnp.sum(pool_proj * row_sums[:, None], axis=0).reshape(4, 1, 4 * chans)
    pool_high = pool_terms.astype(bf16)
    pool_low = (pool_terms - pool_high.astype(f32)).astype(bf16)
    pool_rows = jnp.pad(
        jnp.concatenate([pool_high, pool_low], axis=1),
        ((0, 0), (0, 14), (0, strip - 4 * chans)),
    )
    concat_back = lax.all_to_all(
        jnp.concatenate([concat_terms, pool_rows], axis=1), QUAD, 0, 0, tiled=True
    )
    pool_back = jnp.sum(
        concat_back[:, 16 * chans : 16 * chans + 2, : 4 * chans].astype(f32), axis=(0, 1)
    ).reshape(4, chans)
    concat_back = jnp.transpose(concat_back[:, : 16 * chans], (1, 0, 2)).reshape(
        4, 4, chans, total
    )

    def branch_delta(slot):
        return gelu_back(branch_norm(slot), concat_back[slot].astype(f32))

    pool_delta = gelu_back(pool_norm, pool_back)
    moments = []
    for slot in range(4):
        delta = branch_delta(slot) * inside
        moments.append(
            jnp.stack([jnp.sum(delta, axis=2), jnp.sum(delta * branch_hat(slot), axis=2)])
        )
    moments = jnp.concatenate(
        [jnp.stack(moments), jnp.stack([pool_delta, pool_delta * pool_hat], axis=1)[:, :, None]],
        axis=2,
    )
    moments = total_over(to_canon(moments), ("dp", "z"))
    slot_moments = to_slots(moments)
    pool_grad = (
        gains[:, 4]
        * slot_inverse[:, 4]
        * (pool_delta - (slot_moments[:, 0, 4] + pool_hat * slot_moments[:, 1, 4]) / image_total)
    ) / area

    def branch_grad(slot):
        grad = inside * (
            (gains[slot, :4] * slot_inverse[slot, :4])[..., None]
            * (
                branch_delta(slot)
                - (
                    slot_moments[slot, 0, :4, :, None]
                    + branch_hat(slot) * slot_moments[slot, 1, :4, :, None]
                )
                / pixel_total
            )
        )
        spread = inside * pool_grad[slot][:, None]
        return jnp.concatenate([grad, spread[None]], axis=0).astype(bf16).reshape(5 * chans, total)

    keeps, sends, taps = [None] * 4, [None] * 4, [None] * 4
    for slot in (3, 2, 1, 0):
        grads = branch_grad(slot)
        keeps[slot], sends[slot], taps[slot] = weight_grads(
            grads, pixels, sel[None], columns, half
        )

    def add(*values):
        return sum(value.astype(f32) for value in values).astype(bf16)

    def z_sums(parts):
        first, near, second, third = parts
        mid_two = add(third, lax.ppermute(third, "z", INWARD))
        mid_one = add(second, lax.ppermute(second, "z", INWARD))
        near = add(near, lax.ppermute(mid_two, "z", MID))
        return add(first, lax.ppermute(near, "z", PAIR), lax.ppermute(mid_one, "z", MID))

    if halves:
        mixed = [None] * 4
        for slot in (3, 2, 1, 0):
            mixed[slot] = add(keeps[slot], lax.ppermute(sends[slot], "dp", SWAP))
        mine = z_sums(mixed)
        other = lax.ppermute(mine, "dp", SWAP)
        low_sum = jnp.where(x_id == 0, mine, other)
        high_sum = jnp.where(x_id == 0, other, mine)
    else:
        low_sum = lax.psum(z_sums(keeps), "dp")
        high_sum = lax.psum(z_sums(sends), "dp")
    branch_grads = jnp.concatenate(
        [
            low_sum.astype(f32).reshape(split + 1, chans, depth),
            high_sum.astype(f32).reshape(split + 1, chans, depth)[1:],
        ],
        axis=0,
    )

    flat_w = [part for slot in slots for part in slot]
    input_sel = jnp.stack(sels)
    cross = input_grads(
        taps, flat_w, input_sel, jnp.stack([quad_id ^ 3, quad_id ^ 1]), strip
    )
    cross = lax.ppermute(cross, "c", SWAP)
    own = input_grads(taps, flat_w, input_sel, jnp.stack([quad_id ^ 2, quad_id]), strip)
    far = add(own[0], cross[0])
    far = lax.ppermute(far, "y", SWAP)
    input_grad = (
        (own[1].astype(f32) + cross[1].astype(f32) + far.astype(f32)) * own_inside[:, None]
    ).astype(bf16)
    input_grad = input_grad.reshape(1, strip_rows, columns, depth)

    head_wgrad = lax.dot_general(
        unit_back, concat, (((1,), (1,)), ((), ())), preferred_element_type=f32
    )
    head_wgrad = head_wgrad.reshape(all_ch, 4, 16 * chans + 16)[:, :, : 16 * chans]
    head_wgrad = head_wgrad.reshape(all_ch, 4, 4, 4, chans)
    pool_wgrad = (row_sums[:, None] * all_pool[None]).reshape(all_ch, 4, 4, 1, chans)
    head_wgrad = jnp.concatenate([head_wgrad, pool_wgrad], axis=3).astype(bf16)
    spot = jnp.sum(place * jnp.arange(4, dtype=f32)[None], axis=1).astype(jnp.int32)
    head_wgrad = jnp.stack(
        [lax.dynamic_index_in_dim(head_wgrad, spot[at], 2, keepdims=False) for at in range(4)],
        axis=0,
    )
    head_wgrad = jnp.transpose(head_wgrad, (1, 3, 0, 2, 4)).reshape(all_ch, 5 * all_ch)
    head_grads = lax.psum_scatter(head_wgrad, PLANE, scatter_dimension=0, tiled=True)
    head_grads = lax.psum(head_grads.astype(f32), "dp")

    own_sums = lax.dynamic_index_in_dim(moments, z_id, 0, keepdims=False)
    own_head = lax.dynamic_slice_in_dim(head_moments, wide_id * chans, chans, 1)
    norm_grads = jnp.stack(
        [
            jnp.concatenate([own_sums[1], own_head[1][None]]),
            jnp.concatenate([own_sums[0], own_head[0][None]]),
        ]
    )
    own_centres = lax.dynamic_index_in_dim(centres, z_id, 0, keepdims=False)
    own_variances = lax.dynamic_index_in_dim(variances, z_id, 0, keepdims=False)
    head_stats = lax.dynamic_slice_in_dim(
        jnp.stack([head_centre, head_variance]), wide_id * chans, chans, 1
    )
    all_centres = jnp.concatenate([own_centres, head_stats[0][None]])
    all_variances = jnp.concatenate([own_variances, head_stats[1][None]])
    factors = jnp.where(
        jnp.arange(6) == 4, image_total / (image_total - 1.0), pixel_total / (pixel_total - 1.0)
    )
    running_next = (1.0 - momentum) * running_stats + momentum * jnp.stack(
        [all_centres, all_variances * factors[:, None]]
    )
    branch_means, branch_squares, branch_updated = adamw_update(
        branch_weight, branch_grads, branch_first, branch_second, conv_rate, weight_decay
    )
    head_means, head_squares, head_updated = adamw_update(
        head_weight, head_grads, head_first, head_second, conv_rate, weight_decay
    )
    norm_means, norm_squares, norm_updated = adamw_update(
        norm_params, norm_grads, norm_first, norm_second, norm_rate, 0.0
    )
    return (
        head_output,
        input_grad,
        branch_grads,
        branch_means,
        branch_squares,
        branch_updated,
        head_grads,
        head_means,
        head_squares,
        head_updated,
        norm_grads,
        norm_means,
        norm_squares,
        norm_updated,
        running_next,
    )


def solution(mesh):
    groups, wide = mesh.devices.shape
    fine = Mesh(mesh.devices.reshape(groups, 4, 2, wide // 8), ("dp",) + PLANE)
    placed = (
        P("dp", PLANE, None, None),
        P("dp", None),
        P("dp", PLANE, None),
        P(None, PLANE, None),
        P(None, PLANE, None),
        P(None, PLANE, None),
        P(PLANE, None),
        P(PLANE, None),
        P(PLANE, None),
        P(None, None, PLANE),
        P(None, None, PLANE),
        P(None, None, PLANE),
        P(None, None, PLANE),
    )
    return jax.shard_map(
        local,
        mesh=fine,
        in_specs=placed,
        out_specs=(
            P("dp", PLANE, None),
            P("dp", PLANE, None, None),
            P(None, PLANE, None),
            P(None, PLANE, None),
            P(None, PLANE, None),
            P(None, PLANE, None),
            P(PLANE, None),
            P(PLANE, None),
            P(PLANE, None),
            P(PLANE, None),
            P(None, None, PLANE),
            P(None, None, PLANE),
            P(None, None, PLANE),
            P(None, None, PLANE),
            P(None, None, PLANE),
        ),
        check_vma=False,
    )
```

```python
import functools

import jax
import jax.numpy as jnp
from jax import lax
from jax.experimental import pallas as pl
from jax.experimental.pallas import tpu as pltpu
from jax.sharding import Mesh, PartitionSpec as P

STEP = 10


dilations = (6, 12, 18)
epsilon = 1e-05
momentum = 0.1
first_decay = 0.9
second_decay = 0.999
conv_rate = 0.02
norm_rate = 0.4
weight_decay = 0.0001
adam_floor = 1e-08

LANES = 128
PLANE = ("z", "y", "c")
QUAD = ("y", "c")
SWAP = [(0, 1), (1, 0)]
PAIR = [(0, 1), (1, 0), (2, 3), (3, 2)]
MID = [(1, 2), (2, 1)]
OUTWARD = [(1, 0), (2, 3)]
INWARD = [(0, 1), (3, 2)]

bf16 = jnp.bfloat16
f32 = jnp.float32
barrier = lax.optimization_barrier


def adamw_update(parameter, gradient, moment_one, moment_two, step_rate, decay_rate):
    first_new = first_decay * moment_one + (1.0 - first_decay) * gradient
    second_new = second_decay * moment_two + (1.0 - second_decay) * gradient * gradient
    first_hat = first_new / (1.0 - first_decay**STEP)
    second_hat = second_new / (1.0 - second_decay**STEP)
    updated = parameter - step_rate * (
        first_hat / (jnp.sqrt(second_hat) + adam_floor) + decay_rate * parameter
    )
    return (first_new, second_new, updated)


def gelu_both(value):
    scale = (2.0 / jnp.pi) ** 0.5
    square = value * value
    bend = jnp.tanh(scale * (value + 0.044715 * (value * square)))
    lead = 0.5 * (1.0 + bend)
    slope = lead + 0.5 * value * (1.0 - bend * bend) * (scale * (1.0 + 3.0 * 0.044715 * square))
    return value * lead, slope


def tall(rows):
    fill = LANES - rows.shape[0]
    return jnp.concatenate([rows, jnp.zeros((fill, rows.shape[1]), rows.dtype)], axis=0).T


def put_lanes(shape, columns):
    lane = lax.broadcasted_iota(jnp.int32, shape, 1)
    total = jnp.zeros(shape, f32)
    for at, column in columns.items():
        total = jnp.where(lane == at, column, total)
    return total


def put_rows(shape, rows):
    row = lax.broadcasted_iota(jnp.int32, shape, 0)
    total = jnp.zeros(shape, f32)
    for at, value in rows.items():
        total = jnp.where(row == at, value, total)
    return total


def axes_size(axes):
    count = 1
    for axis in axes:
        count *= lax.axis_size(axis)
    return count


def call(
    kernel,
    name,
    grid,
    scalars,
    in_specs,
    out_specs,
    out_shape,
    scratch=(),
    aliases=None,
    flops=0,
    after=(),
    vmem=24,
):
    after = tuple(after)
    first = scalars + len(in_specs)

    def body(*refs):
        kernel(*refs[:first], *refs[first + len(after) :])

    run = pl.pallas_call(
        body,
        out_shape=out_shape,
        grid_spec=pltpu.PrefetchScalarGridSpec(
            num_scalar_prefetch=scalars,
            grid=grid,
            in_specs=list(in_specs) + [pl.BlockSpec(memory_space=pl.ANY)] * len(after),
            out_specs=out_specs,
            scratch_shapes=list(scratch),
        ),
        input_output_aliases=aliases or {},
        compiler_params=pltpu.CompilerParams(vmem_limit_bytes=vmem << 20),
        cost_estimate=pl.CostEstimate(flops=1, bytes_accessed=1, transcendentals=0),
        name=name,
    )
    return lambda *arrays: run(*arrays, *after)


def full(shape):
    return pl.BlockSpec(shape, lambda *_: (0,) * len(shape))


def add_kernel(*refs):
    total = refs[0][...].astype(f32)
    for ref in refs[1:-1]:
        total = total + ref[...].astype(f32)
    refs[-1][...] = total.astype(bf16)


def add(*values, after=()):
    rows, depth = values[0].shape
    parts = 4 if rows % 64 == 0 else 3
    spec = pl.BlockSpec((rows // parts, depth), lambda i: (i, 0))
    return call(
        add_kernel,
        "add",
        (parts,),
        0,
        [spec] * len(values),
        spec,
        jax.ShapeDtypeStruct((rows, depth), bf16),
        after=after,
    )(*values)


def pick_kernel(flag_ref, one_ref, two_ref, out_ref):
    @pl.when(flag_ref[0] == 1)
    def _():
        out_ref[...] = one_ref[...]

    @pl.when(flag_ref[0] != 1)
    def _():
        out_ref[...] = two_ref[...]


def pick(flag, one, two, after=()):
    rows, depth = one.shape
    spec = pl.BlockSpec((rows // 3, depth), lambda i, s: (i, 0))
    return call(
        pick_kernel,
        "pick",
        (3,),
        1,
        [spec, spec],
        spec,
        jax.ShapeDtypeStruct(one.shape, one.dtype),
        after=after,
    )(flag, one, two)


def held_kernel(in_ref, out_ref):
    del in_ref, out_ref


def held(value, after):
    anywhere = pl.BlockSpec(memory_space=pl.ANY)
    return call(
        held_kernel,
        "held",
        (1,),
        0,
        [anywhere],
        anywhere,
        jax.ShapeDtypeStruct(value.shape, value.dtype),
        aliases={0: 0},
        after=after,
    )(value)


def cast_kernel(sel_ref, in_ref, out_ref):
    taps, chans = in_ref.shape[:2]
    first = jnp.logical_and(sel_ref[0] == 1, pl.program_id(0) == 0)
    for tap in range(taps):
        value = in_ref[tap]
        if tap == 0:
            value = jnp.where(first, 0.0, value)
        out_ref[tap * chans : (tap + 1) * chans, :] = value.astype(bf16)


def cast_half(sel, weight, split):
    chans, depth = weight.shape[1:]
    parts = 3 if (split + 1) % 3 == 0 else 1
    block = (split + 1) // parts
    return call(
        cast_kernel,
        "cast",
        (parts,),
        1,
        [pl.BlockSpec((pl.Element(block), pl.Element(chans), pl.Element(depth)), lambda i, s: (s[0] * split + i * block, 0, 0))],
        pl.BlockSpec((block * chans, depth), lambda i, s: (i, 0)),
        jax.ShapeDtypeStruct(((split + 1) * chans, depth), bf16),
    )(sel, weight)


def mask_kernel(columns, cut, scalar_ref, in_ref, out_ref, low_ref, high_ref):
    block = in_ref.shape[0]
    step = pl.program_id(0)
    pixel = step * block + lax.broadcasted_iota(jnp.int32, (block, LANES), 0)
    row = pixel // columns + scalar_ref[1]
    height = scalar_ref[0]
    inside = jnp.logical_and(row < height, pixel % columns < 2 * height)
    for first in range(0, in_ref.shape[1], LANES):
        lanes = slice(first, first + LANES)
        out_ref[:, lanes] = jnp.where(inside, in_ref[:, lanes].astype(f32), 0.0).astype(bf16)

    @pl.when(step < cut)
    def _():
        low_ref[...] = out_ref[...]

    @pl.when(step >= cut)
    def _():
        high_ref[...] = out_ref[...]


def mask_strip(scalars, strip, columns, after):
    rows, depth = strip.shape
    block, cut = rows // 16, 7
    return call(
        functools.partial(mask_kernel, columns, cut),
        "mask",
        (16,),
        1,
        [pl.BlockSpec((block, depth), lambda i, s: (i, 0))],
        (
            pl.BlockSpec((block, depth), lambda i, s: (i, 0)),
            pl.BlockSpec((block, depth), lambda i, s: (jnp.minimum(i, cut - 1), 0)),
            pl.BlockSpec((block, depth), lambda i, s: (jnp.maximum(i - cut, 0), 0)),
        ),
        (
            jax.ShapeDtypeStruct((rows, depth), bf16),
            jax.ShapeDtypeStruct((cut * block, depth), bf16),
            jax.ShapeDtypeStruct((rows - cut * block, depth), bf16),
        ),
        after=after,
    )(scalars, strip)


def image_kernel(strip, places, spot_ref, *refs):
    *parts, out_ref, sems = refs
    copies = []
    for at, (which, first) in enumerate(places):
        rows = pl.ds(pl.multiple_of(spot_ref[which] * strip + first, 16), parts[at].shape[0])
        copies.append(pltpu.make_async_copy(parts[at], out_ref.at[rows, :], sems.at[at]))
    for copy in copies:
        copy.start()
    for copy in copies:
        copy.wait()


def image_of(spots, strip, parts, after):
    depth = parts[0][0].shape[1]
    places = []
    for which, strip_parts in enumerate(parts):
        first = 0
        for part in strip_parts:
            places.append((which, first))
            first += part.shape[0]
    flat = [part for strip_parts in parts for part in strip_parts]
    anywhere = pl.BlockSpec(memory_space=pl.ANY)
    return call(
        functools.partial(image_kernel, strip, places),
        "image",
        (1,),
        1,
        [anywhere] * len(flat),
        anywhere,
        jax.ShapeDtypeStruct((4 * strip, depth), bf16),
        [pltpu.SemaphoreType.DMA((len(flat),))],
        after=after,
    )(spots, *flat)


def head_grad_kernel(x_ref, back_ref, sum_ref, out_ref):
    channels = back_ref.shape[0]
    rows = x_ref.shape[0] // 4
    act = jnp.zeros((EXTRA, channels), f32)
    for quad in range(4):
        first = quad * rows + rows - EXTRA
        act = act + x_ref[first : first + EXTRA, :channels].astype(f32)
    out_ref[:, :channels] = (sum_ref[:, 0:1] * act[0:1, :]).astype(bf16)
    out_ref[:, channels:] = lax.dot_general(
        back_ref[...], x_ref[...], (((1,), (1,)), ((), ())), preferred_element_type=f32
    ).astype(bf16)


def head_weight_grads(concat, unit_back, row_sums, after):
    channels = unit_back.shape[0]
    arrays = (concat, unit_back, row_sums)
    shape = (channels, channels + concat.shape[0])
    return call(
        head_grad_kernel,
        "head_weight_grad",
        (1,),
        0,
        [full(array.shape) for array in arrays],
        full(shape),
        jax.ShapeDtypeStruct(shape, bf16),
        after=after,
    )(*arrays)


def strip_sum_kernel(columns, whole, scalar_ref, *refs):
    block = refs[0].shape[0]
    step = pl.program_id(0)
    pixel = step * block + lax.broadcasted_iota(jnp.int32, (block, LANES), 0)
    row = pixel // columns + scalar_ref[1]
    height = scalar_ref[0]
    inside = jnp.logical_and(row < height, pixel % columns < 2 * height)
    for at in range(4):

        @pl.when(step == at)
        def _():
            for first in range(0, refs[0].shape[1], LANES):
                lanes = slice(first, first + LANES)
                total = refs[whole + at][:, lanes].astype(f32)
                for ref in refs[:whole]:
                    total = total + ref[:, lanes].astype(f32)
                refs[-1][:, lanes] = jnp.where(inside, total, 0.0).astype(bf16)


def strip_sum(scalars, strips, parts, columns, after):
    rows, depth = strips[0].shape
    spec = pl.BlockSpec((rows // 4, depth), lambda i, s: (i, 0))
    return call(
        functools.partial(strip_sum_kernel, columns, len(strips)),
        "strip_sum",
        (4,),
        1,
        [spec] * len(strips) + [full((rows // 4, depth))] * 4,
        spec,
        jax.ShapeDtypeStruct((rows, depth), bf16),
        after=after,
    )(scalars, *strips, *parts)


def adam_kernel(start_ref, grad_ref, weight_ref, first_ref, second_ref, *rest):
    out_ref, mean_ref, square_ref, new_ref = rest[-4:]
    grad = grad_ref[...].astype(f32).reshape(out_ref.shape)
    mean, square, new = adamw_update(
        weight_ref[...], grad, first_ref[...], second_ref[...], conv_rate, weight_decay
    )
    out_ref[...] = grad
    mean_ref[...] = mean
    square_ref[...] = square
    new_ref[...] = new


def adam_taps(start, count, block, grads, weight, first, second, earlier, after):
    taps, chans, depth = weight.shape

    def piece(size, index):
        return pl.BlockSpec(tuple(pl.Element(n) for n in size), index)

    spec = piece((block, chans, depth), lambda i, s: (s[0] + i * block, 0, 0))
    anywhere = [pl.BlockSpec(memory_space=pl.ANY)] * len(earlier)
    return call(
        adam_kernel,
        "adamw",
        (count // block,),
        1,
        [piece((block * chans, depth), lambda i, s: ((s[1] + i * block) * chans, 0))]
        + [spec] * 3
        + anywhere,
        (spec,) * 4,
        (jax.ShapeDtypeStruct(weight.shape, f32),) * 4,
        aliases={5 + at: at for at in range(4)} if earlier else None,
        after=after,
    )(start, grads, weight, first, second, *earlier)


FIRST, SECOND, GAIN, SHIFT, AREA = 0, 8, 16, 24, 32
SUM_ROWS = 40
CENTRE, INVERSE, VARIANCE, COUNT, POOLED = 0, 8, 32, 40, 41
COEF_ROWS = 48
EXTRA = 16


def lane_masks(columns):
    lane = lax.broadcasted_iota(jnp.int32, (1, LANES), 1) % columns
    masks = {}
    for dilation in dilations:
        for off in (-dilation, dilation):
            moved = lane + off
            masks[off] = jnp.logical_and(moved >= 0, moved < columns)
    return masks


def forward_kernel(columns, split, scalar_ref, x_ref, wz_ref, wx_ref, mask_ref, *rest):
    pre_ref, stat_ref, taps = rest[-3:]
    step = pl.program_id(0)
    half = wz_ref.shape[0]
    block = x_ref.shape[0]
    sel = scalar_ref[0]
    contract = (((1,), (1,)), ((), ()))
    pixels = x_ref[...]
    cols = pl.ds(pl.multiple_of(step * block, block), block)
    taps[pl.ds(pl.multiple_of(sel * half, 16), half), cols] = lax.dot_general(
        wz_ref[...], pixels, contract, preferred_element_type=f32
    )
    taps[pl.ds(pl.multiple_of((1 - sel) * half, 16), half), cols] = lax.dot_general(
        wx_ref[...], pixels, contract, preferred_element_type=f32
    )

    @pl.when(step == pl.num_programs(0) - 1)
    def _():
        total = taps.shape[1]
        tiles = total // LANES
        chans = pre_ref.shape[2]
        masks = lane_masks(columns)

        def rows_of(tap):
            first = tap * chans if tap <= split else (tap + 1) * chans
            return slice(first, first + chans)

        def tile(tap, at):
            return taps[rows_of(tap), at * LANES : (at + 1) * LANES]

        sums = [jnp.zeros((chans, LANES), f32) for _ in range(4)]
        squares = [jnp.zeros((chans, LANES), f32) for _ in range(4)]
        pooled = jnp.zeros((chans, LANES), f32)
        for at in range(tiles):
            lanes = slice(at * LANES, (at + 1) * LANES)
            weight = mask_ref[0:1, lanes]
            for branch in range(4):
                if branch == 0:
                    value = tile(0, at)
                else:
                    dilation = dilations[branch - 1]
                    jump = dilation * columns // LANES
                    value = None
                    for b in range(3):
                        part = None
                        for a in range(3):
                            source = at + (a - 1) * jump
                            if 0 <= source < tiles:
                                term = tile(1 + 9 * (branch - 1) + 3 * a + b, source)
                                part = term if part is None else part + term
                        off = (b - 1) * dilation
                        if off != 0:
                            part = pltpu.roll(part, (-off) % LANES, 1)
                            part = jnp.where(masks[off], part, 0.0)
                        value = part if value is None else value + part
                pre_ref[0, branch, :, lanes] = value
                weighted = value * weight
                sums[branch] = sums[branch] + weighted
                squares[branch] = squares[branch] + weighted * value
            pooled = pooled + tile(28, at)
        height = jnp.full((1, 1), scalar_ref[2], jnp.int32).astype(f32)
        area = 2.0 * height * height
        pool = jnp.sum(pooled, axis=1, keepdims=True) / area
        columns_of = {FIRST + 4: pool, SECOND + 4: pool * pool, AREA: area}
        for branch in range(4):
            columns_of[FIRST + branch] = jnp.sum(sums[branch], axis=1, keepdims=True)
            columns_of[SECOND + branch] = jnp.sum(squares[branch], axis=1, keepdims=True)
        stat_ref[0] = put_lanes((chans, LANES), columns_of)


def forward_taps(pixels, mask_rows, scalars, wz, wx, earlier, columns, chans, split, after):
    total, depth = pixels.shape
    block = total // 4
    half = wz.shape[0]
    keep = [pl.BlockSpec(memory_space=pl.ANY)] * len(earlier)
    return call(
        functools.partial(forward_kernel, columns, split),
        "atrous_forward",
        (4,),
        1,
        [
            pl.BlockSpec((block, depth), lambda i, s: (i, 0)),
            full((half, depth)),
            full((half, depth)),
            full((8, total)),
        ]
        + keep,
        (
            pl.BlockSpec((1, 4, chans, total), lambda i, s: (s[1], 0, 0, 0)),
            pl.BlockSpec((1, chans, LANES), lambda i, s: (s[1], 0, 0)),
        ),
        (
            jax.ShapeDtypeStruct((4, 4, chans, total), f32),
            jax.ShapeDtypeStruct((4, chans, LANES), f32),
        ),
        [pltpu.VMEM((2 * half, total), f32)],
        {5: 0, 6: 1} if earlier else None,
        4 * half * total * depth,
        after,
        56,
    )(scalars, pixels, wz, wx, mask_rows, *earlier)


def pack_kernel(place_ref, stat_ref, norm_ref, out_ref, work):
    chans = norm_ref.shape[0]
    work[...] = jnp.zeros_like(work)
    for z in range(4):
        work[z * chans : (z + 1) * chans, :] = stat_ref[z]
    own = pl.ds(pl.multiple_of(place_ref[0] * chans, chans), chans)
    work[own, :] = work[own, :] + norm_ref[...]
    rows = work[...].T[:SUM_ROWS]
    for at in range(out_ref.shape[0]):
        out_ref[at] = rows


def pack_sums(place, stats, norm_cols, count, after):
    return call(
        pack_kernel,
        "branch_sums",
        (1,),
        1,
        [full(stats.shape), full(norm_cols.shape)],
        full((count, SUM_ROWS, LANES)),
        jax.ShapeDtypeStruct((count, SUM_ROWS, LANES), f32),
        [pltpu.VMEM((LANES, LANES), f32)],
        after=after,
    )(place, stats, norm_cols)


def pool_rows_of(rows_ref, own_width):
    def row(at):
        return rows_ref[at : at + 1, :]

    moved = row(POOLED) - row(CENTRE + 4)
    normed = row(GAIN + 4) * moved * row(INVERSE + 4) + row(SHIFT + 4)
    lane = lax.broadcasted_iota(jnp.int32, normed.shape, 1)
    return normed, moved * row(INVERSE + 4), lane < own_width


def act_kernel(image_total, quad_ref, parts_ref, own_ref, pre_ref, out_ref, col_ref, row_ref):
    chans = pre_ref.shape[2]

    @pl.when(pl.program_id(0) == 0)
    def _():
        sums = jnp.sum(parts_ref[...], axis=0)
        pixel_total = jnp.maximum(sums[AREA : AREA + 1], 1.0)
        index = lax.broadcasted_iota(jnp.int32, (8, LANES), 0)
        count = jnp.where(index == 4, image_total, pixel_total)
        centre = sums[FIRST : FIRST + 8] / count
        variance = sums[SECOND : SECOND + 8] / count - centre * centre
        inverse = lax.rsqrt(variance + epsilon)
        other = jnp.where(index == 0, pixel_total, jnp.where(index == 1, own_ref[0, 4:5, :], 0.0))
        rows = jnp.concatenate(
            [centre, inverse, sums[GAIN : GAIN + 8], sums[SHIFT : SHIFT + 8], variance, other],
            axis=0,
        )
        row_ref[...] = rows
        col_ref[...] = tall(rows)

    for z in range(4):
        span = slice(z * chans, (z + 1) * chans)
        for branch in range(4):
            moved = pre_ref[z, branch] - col_ref[span, CENTRE + branch : CENTRE + branch + 1]
            normed = (
                col_ref[span, GAIN + branch : GAIN + branch + 1]
                * moved
                * col_ref[span, INVERSE + branch : INVERSE + branch + 1]
                + col_ref[span, SHIFT + branch : SHIFT + branch + 1]
            )
            first = (4 * z + branch) * chans
            out_ref[0, first : first + chans, :] = gelu_both(normed)[0].astype(bf16)
    normed, _, valid = pool_rows_of(row_ref, 4 * chans)
    act = jnp.where(valid, gelu_both(normed)[0], 0.0)
    act = put_rows((EXTRA, LANES), {0: act + pltpu.roll(act, 4 * chans, 1)})
    lane = lax.broadcasted_iota(jnp.int32, act.shape, 1)
    for at in range(out_ref.shape[2] // LANES):
        owner = (lane + at * LANES) // (4 * chans)
        out_ref[0, 16 * chans :, at * LANES : (at + 1) * LANES] = jnp.where(
            owner == quad_ref[0], act, 0.0
        ).astype(bf16)


def activations(quad, parts, own, pre, image_total):
    chans, total = pre.shape[2:]
    strip = total // 4
    rows = 16 * chans + EXTRA
    return call(
        functools.partial(act_kernel, image_total),
        "branch_act",
        (4,),
        1,
        [
            full(parts.shape),
            full((1, SUM_ROWS, LANES)),
            pl.BlockSpec((4, 4, chans, strip), lambda i, s: (0, 0, 0, i)),
        ],
        (
            pl.BlockSpec((1, rows, strip), lambda i, s: (i, 0, 0)),
            full((LANES, LANES)),
            full((COEF_ROWS, LANES)),
        ),
        (
            jax.ShapeDtypeStruct((4, rows, strip), bf16),
            jax.ShapeDtypeStruct((LANES, LANES), f32),
            jax.ShapeDtypeStruct((COEF_ROWS, LANES), f32),
        ),
    )(quad, parts, own, pre)


def unit_kernel(x_ref, shared_ref, head_ref, mask_ref, unit_ref, out_ref):
    channels = shared_ref.shape[0]
    rows, strip = x_ref.shape[0] // 4, x_ref.shape[1]
    proj = shared_ref[:, channels + strip :]
    unit = jnp.dot(proj, x_ref[...], preferred_element_type=f32)
    act = jnp.zeros((EXTRA, channels), f32)
    for quad in range(4):
        first = quad * rows + rows - EXTRA
        act = act + x_ref[first : first + EXTRA, :channels].astype(f32)
    bias = shared_ref[:, :channels].astype(f32) * act[0:1, :]
    unit = unit + jnp.sum(bias, axis=1, keepdims=True)
    unit_ref[...] = unit
    weighted = unit * mask_ref[0:1, :]
    lane = lax.broadcasted_iota(jnp.int32, head_ref.shape, 1)
    one = jnp.sum(weighted, axis=1, keepdims=True)
    two = jnp.sum(weighted * unit, axis=1, keepdims=True)
    sums = jnp.where(lane == 0, one, jnp.where(lane == 1, two, head_ref[...])).T[:8]
    for at in range(out_ref.shape[0]):
        out_ref[at] = sums


def project(concat, shared, head_cols, strip_mask, count):
    channels, strip = shared.shape[0], concat.shape[1]
    arrays = (concat, shared, head_cols, strip_mask)
    return call(
        unit_kernel,
        "projection",
        (1,),
        0,
        [full(array.shape) for array in arrays],
        (full((channels, strip)), full((count, 8, channels))),
        (
            jax.ShapeDtypeStruct((channels, strip), f32),
            jax.ShapeDtypeStruct((count, 8, channels), f32),
        ),
    )(*arrays)


def head_kernel(parts_ref, unit_ref, shared_ref, mask_ref, row_ref, value_ref, delta_ref, col_ref, head_ref, out_ref):
    sums = jnp.sum(parts_ref[...], axis=0)
    pixel_total = row_ref[COUNT : COUNT + 1, 0:1]
    centre = sums[0:1] / pixel_total
    variance = sums[1:2] / pixel_total - centre * centre
    inverse = lax.rsqrt(variance + epsilon)
    rows = put_rows(
        sums.shape, {0: centre, 1: inverse, 2: sums[2:3], 3: sums[3:4], 4: variance}
    )
    head_ref[...] = rows
    columns = tall(rows)
    col_ref[...] = columns
    hat = (unit_ref[...] - columns[:, 0:1]) * columns[:, 1:2]
    normed = columns[:, 2:3] * hat + columns[:, 3:4]
    value, slope = gelu_both(normed)
    weight = mask_ref[0:1, :]
    value_ref[...] = (weight * value).astype(bf16)
    first = unit_ref.shape[0]
    cot = shared_ref[:, first : first + unit_ref.shape[1]].astype(f32)
    delta = slope * (weight * cot)
    delta_ref[...] = delta
    sums = put_lanes(
        columns.shape,
        {
            0: jnp.sum(delta, axis=1, keepdims=True),
            1: jnp.sum(delta * hat, axis=1, keepdims=True),
        },
    ).T[:8]
    for at in range(out_ref.shape[0]):
        out_ref[at] = sums


def head_norm(parts, unit, shared, strip_mask, coef_rows):
    channels, strip = unit.shape
    count = parts.shape[0]
    return call(
        head_kernel,
        "head_norm",
        (1,),
        0,
        [full(parts.shape), full(unit.shape), full(shared.shape), full((8, strip)), full(coef_rows.shape)],
        (
            full((channels, strip)),
            full((channels, strip)),
            full((channels, LANES)),
            full((8, channels)),
            full((count, 8, channels)),
        ),
        (
            jax.ShapeDtypeStruct((channels, strip), bf16),
            jax.ShapeDtypeStruct((channels, strip), f32),
            jax.ShapeDtypeStruct((channels, LANES), f32),
            jax.ShapeDtypeStruct((8, channels), f32),
            jax.ShapeDtypeStruct((count, 8, channels), f32),
        ),
    )(parts, unit, shared, strip_mask, coef_rows)


def unit_back_kernel(
    parts_ref, unit_ref, delta_ref, col_ref, mask_ref, row_ref, shared_ref, back_ref, out_ref, sum_ref, moment_ref
):
    sums = jnp.sum(parts_ref[...], axis=0)
    moment_ref[...] = sums
    moments = tall(sums)
    pixel_total = row_ref[COUNT : COUNT + 1, 0:1]
    inverse = col_ref[:, 1:2]
    hat = (unit_ref[...] - col_ref[:, 0:1]) * inverse
    back = mask_ref[0:1, :] * (
        (col_ref[:, 2:3] * inverse)
        * (delta_ref[...] - (moments[:, 0:1] + hat * moments[:, 1:2]) / pixel_total)
    )
    back = back.astype(bf16)
    back_ref[...] = back
    row_sums = jnp.sum(back.astype(f32), axis=1, keepdims=True)
    sum_ref[...] = jnp.broadcast_to(row_sums, sum_ref.shape)
    channels = shared_ref.shape[0]
    rows, width = out_ref.shape[1:]
    proj = shared_ref[:, channels + width :]
    terms = lax.dot_general(
        proj, back, (((0,), (0,)), ((), ())), preferred_element_type=f32
    )
    pool = jnp.sum(shared_ref[:, :channels].astype(f32) * row_sums, axis=0, keepdims=True)
    own = channels // 4
    for quad in range(4):
        first = quad * own // LANES * LANES
        part = pool[:, first : first + LANES]
        if quad * own != first:
            part = pltpu.roll(part, LANES - (quad * own - first), 1)
        lane = lax.broadcasted_iota(jnp.int32, part.shape, 1)
        part = jnp.where(lane < own, part, 0.0)
        high = part.astype(bf16).astype(f32)
        extra = put_rows((EXTRA, LANES), {0: high, 1: part - high})
        out_ref[quad, : rows - EXTRA, :] = terms[quad * rows : (quad + 1) * rows - EXTRA].astype(bf16)
        out_ref[quad, rows - EXTRA :, :LANES] = extra.astype(bf16)
        out_ref[quad, rows - EXTRA :, LANES:] = jnp.zeros((EXTRA, width - LANES), bf16)


def unit_backward(parts, unit, delta, cols, strip_mask, coef_rows, shared):
    channels, strip = unit.shape
    rows = (shared.shape[1] - channels - strip) // 4
    arrays = (parts, unit, delta, cols, strip_mask, coef_rows, shared)
    return call(
        unit_back_kernel,
        "unit_back",
        (1,),
        0,
        [full(array.shape) for array in arrays],
        (
            full((channels, strip)),
            full((4, rows, strip)),
            full((channels, LANES)),
            full((8, channels)),
        ),
        (
            jax.ShapeDtypeStruct((channels, strip), bf16),
            jax.ShapeDtypeStruct((4, rows, strip), bf16),
            jax.ShapeDtypeStruct((channels, LANES), f32),
            jax.ShapeDtypeStruct((8, channels), f32),
        ),
    )(*arrays)


def branch_kernel(x_ref, pre_ref, col_ref, row_ref, mask_ref, delta_ref, pool_ref, out_ref, sums, pooled):
    step = pl.program_id(0)
    chans = pre_ref.shape[2]

    @pl.when(step == 0)
    def _():
        sums[...] = jnp.zeros_like(sums)
        pooled[...] = jnp.zeros_like(pooled)

    def fold(value):
        total = value[:, :LANES]
        for at in range(1, value.shape[1] // LANES):
            total = total + value[:, at * LANES : (at + 1) * LANES]
        return total

    weight = mask_ref[0:1, :]
    for z in range(4):
        span = slice(z * chans, (z + 1) * chans)
        for branch in range(4):
            first = (4 * z + branch) * chans
            hat = (
                pre_ref[z, branch] - col_ref[span, CENTRE + branch : CENTRE + branch + 1]
            ) * col_ref[span, INVERSE + branch : INVERSE + branch + 1]
            normed = (
                col_ref[span, GAIN + branch : GAIN + branch + 1] * hat
                + col_ref[span, SHIFT + branch : SHIFT + branch + 1]
            )
            delta = gelu_both(normed)[1] * (
                weight * x_ref[0, first : first + chans, :].astype(f32)
            )
            delta_ref[z, branch] = delta
            sums[8 * z + branch] = sums[8 * z + branch] + fold(delta)
            sums[8 * z + 4 + branch] = sums[8 * z + 4 + branch] + fold(delta * hat)
    extra = x_ref[0, 16 * chans :, :LANES].astype(f32)
    pooled[...] = pooled[...] + jnp.broadcast_to(extra[0:1] + extra[1:2], pooled.shape)

    @pl.when(step == pl.num_programs(0) - 1)
    def _():
        normed, hat, valid = pool_rows_of(row_ref, 4 * chans)
        delta = jnp.where(valid, gelu_both(normed)[1] * pooled[0:1, :], 0.0)
        hat = jnp.where(valid, hat, 0.0)
        pool_ref[...] = put_rows(pool_ref.shape, {0: delta, 1: hat})
        found = []
        for z in range(4):
            columns = {}
            for branch in range(4):
                columns[branch] = jnp.sum(sums[8 * z + branch], axis=1, keepdims=True)
                columns[8 + branch] = jnp.sum(sums[8 * z + 4 + branch], axis=1, keepdims=True)
            found.append(put_lanes((chans, LANES), columns))
        found.append(jnp.zeros((LANES - 4 * chans, LANES), f32))
        rows = jnp.concatenate(found, axis=0).T[:16]
        index = lax.broadcasted_iota(jnp.int32, rows.shape, 0)
        rows = jnp.where(index == 4, delta, jnp.where(index == 12, delta * hat, rows))
        for at in range(out_ref.shape[0]):
            out_ref[at] = rows


def branch_backward(concat_back, pre, coef_cols, coef_rows, mask_rows, count):
    chans, total = pre.shape[2:]
    rows, strip = concat_back.shape[1:]
    spread = pl.BlockSpec((4, 4, chans, strip), lambda i: (0, 0, 0, i))
    return call(
        branch_kernel,
        "branch_back",
        (4,),
        0,
        [
            pl.BlockSpec((1, rows, strip), lambda i: (i, 0, 0)),
            spread,
            full(coef_cols.shape),
            full(coef_rows.shape),
            pl.BlockSpec((8, strip), lambda i: (0, i)),
        ],
        (spread, full((8, LANES)), full((count, 16, LANES))),
        (
            jax.ShapeDtypeStruct(pre.shape, f32),
            jax.ShapeDtypeStruct((8, LANES), f32),
            jax.ShapeDtypeStruct((count, 16, LANES), f32),
        ),
        [pltpu.VMEM((32, chans, LANES), f32), pltpu.VMEM((8, LANES), f32)],
    )(concat_back, pre, coef_cols, coef_rows, mask_rows)


def weight_kernel(
    columns, image_total, scalar_ref, parts_ref, pool_ref, col_ref, pre_ref, delta_ref, mask_ref, x_ref, keep_ref, send_ref, taps_ref, total_ref, moments
):
    chans = pre_ref.shape[2]
    half = keep_ref.shape[0]
    start = 29 * chans - half
    sel = scalar_ref[0]

    @pl.when(pl.program_id(0) == 0)
    def _():
        rows = jnp.concatenate([jnp.sum(parts_ref[...], axis=0), pool_ref[...]], axis=0)
        moments[...] = tall(rows)
        own = moments[pl.ds(pl.multiple_of(scalar_ref[1] * chans, chans), chans), :]
        coefs = col_ref[...]

        def coef(at):
            return coefs[:, at : at + 1]

        def moment(at):
            return own[:, at : at + 1]

        pixel_total = coef(COUNT)
        height = jnp.full((1, 1), scalar_ref[2], jnp.int32).astype(f32)
        area = 2.0 * height * height
        pool_grad = (
            coef(GAIN + 4)
            * coef(INVERSE + 4)
            * (moment(16) - (moment(4) + moment(17) * moment(12)) / image_total)
        ) / area
        tiles = pre_ref.shape[3] // LANES
        masks = lane_masks(columns)
        for at in range(tiles):
            lanes = slice(at * LANES, (at + 1) * LANES)
            weight = mask_ref[0:1, lanes]
            taps_ref[28 * chans : 29 * chans, lanes] = (weight * pool_grad).astype(bf16)
            for branch in range(4):
                hat = (pre_ref[0, branch, :, lanes] - coef(CENTRE + branch)) * coef(INVERSE + branch)
                grad = weight * (
                    (coef(GAIN + branch) * coef(INVERSE + branch))
                    * (
                        delta_ref[0, branch, :, lanes]
                        - (moment(branch) + hat * moment(8 + branch)) / pixel_total
                    )
                )
                if branch == 0:
                    taps_ref[0:chans, lanes] = grad.astype(bf16)
                    continue
                j, dilation = branch - 1, dilations[branch - 1]
                jump = dilation * columns // LANES
                for b in range(3):
                    off = (b - 1) * dilation
                    moved = grad
                    if off != 0:
                        moved = pltpu.roll(grad, off % LANES, 1)
                        moved = jnp.where(masks[-off], moved, 0.0)
                    moved = moved.astype(bf16)
                    for a in range(3):
                        tap = 1 + 9 * j + 3 * a + b
                        span = slice(tap * chans, (tap + 1) * chans)
                        target = at + (a - 1) * jump
                        if 0 <= target < tiles:
                            taps_ref[span, target * LANES : (target + 1) * LANES] = moved
                        source = at - (a - 1) * jump
                        if not 0 <= source < tiles:
                            taps_ref[span, lanes] = jnp.zeros((chans, LANES), bf16)

    total_ref[...] = jnp.dot(taps_ref[...], x_ref[...], preferred_element_type=f32)
    keep_ref[...] = total_ref[pl.ds(pl.multiple_of(sel * start, 16), half), :].astype(bf16)
    send_ref[...] = total_ref[pl.ds(pl.multiple_of((1 - sel) * start, 16), half), :].astype(bf16)


def weight_grads(
    scalars, parts, pool_rows, coef_cols, pre, delta, mask_rows, pixels, columns, half, image_total, after
):
    chans, total = pre.shape[2:]
    depth = pixels.shape[1]
    block = depth // 4
    own = pl.BlockSpec((1, 4, chans, total), lambda i, s: (s[1], 0, 0, 0))
    return call(
        functools.partial(weight_kernel, columns, image_total),
        "atrous_weight_grad",
        (4,),
        1,
        [
            full(parts.shape),
            full(pool_rows.shape),
            pl.BlockSpec((chans, LANES), lambda i, s: (s[1], 0)),
            own,
            own,
            full(mask_rows.shape),
            pl.BlockSpec((total, block), lambda i, s: (0, i)),
        ],
        (
            pl.BlockSpec((half, block), lambda i, s: (0, i)),
            pl.BlockSpec((half, block), lambda i, s: (0, i)),
            full((29 * chans, total)),
        ),
        (
            jax.ShapeDtypeStruct((half, depth), bf16),
            jax.ShapeDtypeStruct((half, depth), bf16),
            jax.ShapeDtypeStruct((29 * chans, total), bf16),
        ),
        [pltpu.VMEM((29 * chans, block), f32), pltpu.VMEM((LANES, LANES), f32)],
        flops=2 * 29 * chans * total * depth,
        after=after,
        vmem=56,
    )(scalars, parts, pool_rows, coef_cols, pre, delta, mask_rows, pixels)


def input_kernel(start, sel_ref, strip_ref, *refs):
    taps = refs[0:4]
    weights = refs[4:12]
    out_refs, total = refs[12:-1], refs[-1]
    half = weights[0].shape[0]
    contract = (((0,), (0,)), ((), ()))
    for slot in range(4):
        sel = sel_ref[slot]
        for which in range(2):
            first = sel * start if which == 0 else (1 - sel) * start
            part = lax.dot_general(
                taps[slot][pl.ds(pl.multiple_of(first, 16), half), :],
                weights[2 * slot + which][...],
                contract,
                preferred_element_type=f32,
            )
            if slot == 0 and which == 0:
                total[...] = part
            else:
                total[...] += part
    block = out_refs[0].shape[0]
    for at, out_ref in enumerate(out_refs):
        out_ref[...] = total[at * block : (at + 1) * block, :].astype(bf16)


def input_grads(taps, weights, sels, strip_id, block, parts, after=()):
    rows, total = taps[0].shape
    half, depth = weights[0].shape
    start = rows - half
    shape = (block // parts, depth)
    return call(
        functools.partial(input_kernel, start),
        "atrous_input_grad",
        (1,),
        2,
        [pl.BlockSpec((rows, block), lambda i, s, t: (0, t[0]))] * 4 + [full((half, depth))] * 8,
        (full(shape),) * parts,
        (jax.ShapeDtypeStruct(shape, bf16),) * parts,
        [pltpu.VMEM((block, depth), f32)],
        after=after,
        vmem=56,
    )(sels, strip_id, *taps, *weights)


def local(
    features,
    scale_sizes,
    cotangent,
    branch_weight,
    branch_first,
    branch_second,
    head_weight,
    head_first,
    head_second,
    norm_params,
    norm_first,
    norm_second,
    running_stats,
):
    groups = lax.axis_size("dp")
    halves = groups == 2
    images = scale_sizes.shape[1]
    image_total = float(groups * images)
    x_id, z_id = lax.axis_index("dp"), lax.axis_index("z")
    quad_id = lax.axis_index("y") * 2 + lax.axis_index("c")
    wide_id = z_id * 4 + quad_id
    strip_rows, columns, depth = features.shape[1:]
    strip = strip_rows * columns
    total = 4 * strip
    tap_count, chans = branch_weight.shape[:2]
    all_ch = chans * 16
    split = (tap_count - 1) // 2
    half = (split + 1) * chans
    cells, everyone = ("dp", "z"), ("dp",) + PLANE
    rows = 16 * chans + EXTRA

    def exchange(parts, axes):
        return lax.all_to_all(parts, axes, 0, 0, tiled=True)

    height = lax.dynamic_index_in_dim(scale_sizes[0], z_id, 0, keepdims=False)
    pixel = jnp.arange(total, dtype=jnp.int32)
    inside = jnp.logical_and(pixel // columns < height, pixel % columns < 2 * height).astype(f32)
    own_inside = lax.dynamic_slice_in_dim(inside, quad_id * strip, strip, 0)
    mask_rows = jnp.broadcast_to(inside[None], (8, total))
    strip_mask = jnp.broadcast_to(own_inside[None], (8, strip))

    low_half = branch_weight[: split + 1]
    high_half = jnp.concatenate(
        [jnp.zeros_like(branch_weight[:1]), branch_weight[split + 1 :]], axis=0
    )
    own_w = [part.astype(bf16).reshape(half, depth) for part in (low_half, high_half)]
    mid = jnp.logical_and(z_id >= 1, z_id <= 2).astype(jnp.int32)[None]

    def over_groups(block):
        return lax.ppermute(block, "dp", SWAP)

    def along(parts, pairs):
        return [lax.ppermute(part, "z", pairs) for part in parts]

    def hold(parts, after):
        return [held(part, after) for part in parts]

    def pair_of(parts):
        return (parts[0], over_groups(parts[0])) if halves else tuple(parts)

    def pick_all(ones, twos, after):
        return [pick(mid, one, two, after) for one, two in zip(ones, twos)]

    sel = x_id.astype(jnp.int32) if halves else jnp.zeros((), jnp.int32)
    zero = jnp.zeros((), jnp.int32)
    sending = [cast_half(sel[None], branch_weight, split)] if halves else own_w
    near, mid_one = along(sending, PAIR), along(sending, MID)

    own_place = jnp.stack([height, quad_id * strip_rows]).astype(jnp.int32)
    masked = mask_strip(own_place, features[0].reshape(strip, depth), columns, sending)

    masked, masked_low, masked_high = masked
    low_y, high_y = (lax.ppermute(part, "y", SWAP) for part in (masked_low, masked_high))
    over_c = lax.ppermute(masked, "c", SWAP)

    own_proj = head_weight.astype(bf16).reshape(chans, 5, 4, 4, chans)
    own_proj = jnp.transpose(own_proj, (0, 3, 2, 1, 4))
    pixel_proj = jnp.pad(
        own_proj[:, :, :, :4].reshape(chans, 4, 16 * chans), ((0, 0), (0, 0), (0, EXTRA))
    ).reshape(chans, 4 * rows)
    shared = jnp.concatenate(
        [
            jnp.broadcast_to(own_proj[:, :, :, 4].reshape(1, chans, all_ch), (16, chans, all_ch)),
            jnp.transpose(cotangent[0].reshape(chans, 16, strip), (1, 0, 2)),
            jnp.broadcast_to(pixel_proj[None], (16, chans, 4 * rows)),
        ],
        axis=2,
    )

    slots = [tuple(own_w)]
    near = hold(near, [masked, shared, *own_w])
    mid_two = along(near, MID)
    near = pair_of(near)
    mid_one = hold(mid_one, near[:1])
    out_one = along(mid_one, OUTWARD)
    low_y = held(low_y, mid_one)
    second = pick_all(mid_one, out_one, [low_y])
    second_pair = pair_of(second)
    mid_two = hold(mid_two, second)
    out_two = along(mid_two, OUTWARD)
    high_y = held(high_y, mid_two)
    low_yc, high_yc = (lax.ppermute(part, "c", SWAP) for part in (low_y, high_y))
    near = (near[0], held(near[1], (high_y,)))
    slots.append(near)
    spots = jnp.stack([jnp.bitwise_xor(quad_id, flip) for flip in range(4)]).astype(jnp.int32)
    parts = ((masked,), (over_c,), (low_y, high_y), (low_yc, high_yc))
    pixels = image_of(spots, strip, parts, near[1:])
    sels = [zero, sel, sel, sel]
    order = [
        z_id.astype(jnp.int32),
        jnp.bitwise_xor(z_id, 1).astype(jnp.int32),
        jnp.where(z_id <= 1, 2, 1).astype(jnp.int32),
        jnp.where(z_id <= 1, 3, 0).astype(jnp.int32),
    ]

    first_group = (x_id == 0).astype(f32)
    norm_cols = jnp.zeros((chans, LANES), f32)
    norm_cols = norm_cols.at[:, GAIN : GAIN + 5].set(jnp.transpose(norm_params[0, :5]))
    norm_cols = norm_cols.at[:, SHIFT : SHIFT + 5].set(jnp.transpose(norm_params[1, :5]))
    norm_cols = norm_cols * first_group
    head_cols = jnp.zeros((chans, LANES), f32).at[:, 2:4].set(jnp.transpose(norm_params[:, 5]))
    head_cols = lax.dynamic_update_slice_in_dim(
        jnp.zeros((all_ch, LANES), f32), head_cols * first_group, wide_id * chans, 0
    )
    def branch(slot, state, after):
        scalars = jnp.stack([sels[slot], order[slot], height])
        return forward_taps(
            pixels, mask_rows, scalars, *slots[slot], state, columns, chans, split, after
        )

    state = branch(0, (), ())
    state = branch(1, state, ())
    slots.append((second_pair[0], held(second_pair[1], [state[1]])))
    third = pick_all(mid_two, out_two, slots[2][1:])
    slots.append(pair_of(third))
    shared = exchange(held(shared, third), PLANE)
    shared = shared.reshape(all_ch, all_ch + strip + 4 * rows)
    state = branch(2, state, third)
    state = branch(3, state, ())
    pre, stats = state
    own_sums = pack_sums(order[0][None], stats, norm_cols, axes_size(cells), (shared,))
    quad = quad_id.astype(jnp.int32)[None]
    concat, coef_cols, coef_rows = activations(
        quad, exchange(own_sums, cells), own_sums, pre, image_total
    )
    concat = exchange(concat, QUAD).reshape(4 * rows, strip)

    unit, head_sums = project(concat, shared, head_cols, strip_mask, axes_size(everyone))
    head_values, head_delta, head_coefs, head_rows, head_sums = head_norm(
        exchange(head_sums, everyone), unit, shared, strip_mask, coef_rows
    )
    unit_back, concat_back, row_sums, head_moments = unit_backward(
        exchange(head_sums, everyone),
        unit,
        head_delta,
        head_coefs,
        strip_mask,
        coef_rows,
        shared,
    )

    delta, pool_rows, moments = branch_backward(
        exchange(concat_back, QUAD), pre, coef_cols, coef_rows, mask_rows, axes_size(cells)
    )
    moments = exchange(moments, cells)

    def weights_of(slot, after):
        return weight_grads(
            jnp.stack([sel, order[slot], height]),
            moments,
            pool_rows,
            coef_cols,
            pre,
            delta,
            mask_rows,
            pixels,
            columns,
            half,
            image_total,
            after,
        )

    def group_sum(keep, send, after):
        if halves:
            return [add(keep, over_groups(send), after=after)]
        return [keep, send]

    def swap_all(parts, axis):
        return [lax.ppermute(part, axis, SWAP) for part in parts]

    def add_all(*lists, after=()):
        return [add(*parts, after=after) for parts in zip(*lists)]

    flat_w = [part for slot in slots for part in slot]
    input_sel = jnp.stack(sels)

    def features_of(flip, parts, after):
        spot = jnp.bitwise_xor(quad_id, flip).astype(jnp.int32)[None]
        return input_grads(taps, flat_w, input_sel, spot, strip, parts, after)

    keep_c, send_c, taps_c = weights_of(3, ())
    own_parts = head_weight_grads(concat, unit_back, row_sums, (keep_c,))
    head_parts = exchange(own_parts.reshape(16, chans, all_ch + 4 * rows), PLANE)
    head_values = held(head_values.reshape(16, chans, strip), (keep_c,))
    head_values = exchange(head_values, PLANE)
    keep_b, send_b, taps_b = weights_of(2, (keep_c, own_parts))
    keep_a, send_a, taps_a = weights_of(1, (keep_b,))
    third = group_sum(keep_c, send_c, (keep_a,))
    keep_o, send_o, taps_o = weights_of(0, (*third, head_parts, head_values))
    taps = [taps_o, taps_a, taps_b, taps_c]
    far_cross = features_of(3, 4, ())
    second = group_sum(keep_b, send_b, far_cross[:1])
    mid_two = add_all(third, along(third, INWARD), after=second)
    (far,) = features_of(2, 1, mid_two)
    everywhere = jnp.stack([jnp.full_like(height, 1 << 20), zero])
    far = strip_sum(everywhere, (far,), swap_all(far_cross, "c"), columns, ())
    near = group_sum(keep_a, send_a, (far,))
    near = add_all(near, along(mid_two, MID))
    mid_one = add_all(second, along(second, INWARD), after=near)
    near_cross = features_of(1, 4, mid_one)
    (own_part,) = features_of(0, 1, near_cross[:1])

    head_parts = jnp.sum(held(head_parts, mid_one).astype(f32), axis=0)
    if halves:
        head_parts = head_parts + lax.ppermute(head_parts, "dp", SWAP)
    else:
        head_parts = lax.psum(head_parts, "dp")
    pool_part = head_parts[:, :all_ch].reshape(chans, 4, 4, 1, chans)
    pixel_part = head_parts[:, all_ch:].reshape(chans, 4, rows)[:, :, : 16 * chans]
    pixel_part = pixel_part.reshape(chans, 4, 4, 4, chans)
    head_grads = jnp.concatenate([pixel_part, pool_part], axis=3)
    head_grads = jnp.transpose(head_grads, (0, 3, 2, 1, 4)).reshape(chans, 5 * all_ch)

    mine = group_sum(keep_o, send_o, (own_part, head_grads))
    mine = add_all(mine, along(near, PAIR), along(mid_one, MID))
    state = (branch_weight, branch_first, branch_second)
    if halves:
        other = over_groups(mine[0])
    else:
        mine = [lax.psum(part, "dp") for part in mine]
    input_grad = strip_sum(
        own_place,
        (own_part, lax.ppermute(far, "y", SWAP)),
        swap_all(near_cross, "c"),
        columns,
        mine,
    ).reshape(1, strip_rows, columns, depth)
    start = jnp.stack([sel * split, zero])
    done = adam_taps(start, split + 1, 3, mine[0], *state, (), (input_grad,))
    start = jnp.stack([(1 - sel) * (split + 1), 1 - sel])
    done = adam_taps(start, split, 2, other if halves else mine[1], *state, done, ())
    branch_grads, branch_means, branch_squares, branch_updated = done

    head_output = jnp.transpose(head_values, (1, 0, 2)).reshape(1, chans, 16 * strip)
    def own_lanes(by_row):
        return lax.dynamic_slice_in_dim(by_row, z_id * chans, chans, 1)

    def own_head(by_row):
        return lax.dynamic_slice_in_dim(by_row, wide_id * chans, chans, 1)

    own_moments = own_lanes(jnp.sum(moments, axis=0))
    head_own = own_head(head_moments)
    norm_grads = jnp.stack(
        [
            jnp.concatenate([own_moments[8:13], head_own[1:2]]),
            jnp.concatenate([own_moments[0:5], head_own[0:1]]),
        ]
    )
    own_coefs, head_stats = own_lanes(coef_rows), own_head(head_rows)
    pixel_total = coef_rows[COUNT, 0]
    all_centres = jnp.concatenate([own_coefs[CENTRE : CENTRE + 5], head_stats[0:1]])
    all_variances = jnp.concatenate([own_coefs[VARIANCE : VARIANCE + 5], head_stats[4:5]])
    factors = jnp.where(
        jnp.arange(6) == 4, image_total / (image_total - 1.0), pixel_total / (pixel_total - 1.0)
    )
    running_next = (1.0 - momentum) * running_stats + momentum * jnp.stack(
        [all_centres, all_variances * factors[:, None]]
    )
    head_means, head_squares, head_updated = adamw_update(
        head_weight, head_grads, head_first, head_second, conv_rate, weight_decay
    )
    norm_means, norm_squares, norm_updated = adamw_update(
        norm_params, norm_grads, norm_first, norm_second, norm_rate, 0.0
    )
    return (
        head_output,
        input_grad,
        branch_grads,
        branch_means,
        branch_squares,
        branch_updated,
        head_grads,
        head_means,
        head_squares,
        head_updated,
        norm_grads,
        norm_means,
        norm_squares,
        norm_updated,
        running_next,
    )


def solution(mesh):
    groups, wide = mesh.devices.shape
    fine = Mesh(mesh.devices.reshape(groups, 4, 2, wide // 8), ("dp",) + PLANE)
    placed = (
        P("dp", PLANE, None, None),
        P("dp", None),
        P("dp", PLANE, None),
        P(None, PLANE, None),
        P(None, PLANE, None),
        P(None, PLANE, None),
        P(PLANE, None),
        P(PLANE, None),
        P(PLANE, None),
        P(None, None, PLANE),
        P(None, None, PLANE),
        P(None, None, PLANE),
        P(None, None, PLANE),
    )
    return jax.shard_map(
        local,
        mesh=fine,
        in_specs=placed,
        out_specs=(
            P("dp", PLANE, None),
            P("dp", PLANE, None, None),
            P(None, PLANE, None),
            P(None, PLANE, None),
            P(None, PLANE, None),
            P(None, PLANE, None),
            P(PLANE, None),
            P(PLANE, None),
            P(PLANE, None),
            P(PLANE, None),
            P(None, None, PLANE),
            P(None, None, PLANE),
            P(None, None, PLANE),
            P(None, None, PLANE),
            P(None, None, PLANE),
        ),
        check_vma=False,
    )
```

```python
import functools

import jax
import jax.numpy as jnp
from jax import lax
from jax.experimental import pallas as pl
from jax.experimental.pallas import tpu as pltpu
from jax.sharding import Mesh, PartitionSpec as P

STEP = 10


dilations = (6, 12, 18)
epsilon = 1e-05
momentum = 0.1
first_decay = 0.9
second_decay = 0.999
conv_rate = 0.02
norm_rate = 0.4
weight_decay = 0.0001
adam_floor = 1e-08

LANES = 128
PLANE = ("z", "y", "c")
QUAD = ("y", "c")
SWAP = [(0, 1), (1, 0)]
PAIR = [(0, 1), (1, 0), (2, 3), (3, 2)]
MID = [(1, 2), (2, 1)]
OUTWARD = [(1, 0), (2, 3)]
INWARD = [(0, 1), (3, 2)]

bf16 = jnp.bfloat16
f32 = jnp.float32
barrier = lax.optimization_barrier


def adamw_update(parameter, gradient, moment_one, moment_two, step_rate, decay_rate):
    first_new = first_decay * moment_one + (1.0 - first_decay) * gradient
    second_new = second_decay * moment_two + (1.0 - second_decay) * gradient * gradient
    first_hat = first_new / (1.0 - first_decay**STEP)
    second_hat = second_new / (1.0 - second_decay**STEP)
    updated = parameter - step_rate * (
        first_hat / (jnp.sqrt(second_hat) + adam_floor) + decay_rate * parameter
    )
    return (first_new, second_new, updated)


def gelu_both(value):
    scale = (2.0 / jnp.pi) ** 0.5
    square = value * value
    bend = jnp.tanh(scale * (value + 0.044715 * (value * square)))
    lead = 0.5 * (1.0 + bend)
    slope = lead + 0.5 * value * (1.0 - bend * bend) * (scale * (1.0 + 3.0 * 0.044715 * square))
    return value * lead, slope


def tall(rows):
    fill = LANES - rows.shape[0]
    return jnp.concatenate([rows, jnp.zeros((fill, rows.shape[1]), rows.dtype)], axis=0).T


def put_lanes(shape, columns):
    lane = lax.broadcasted_iota(jnp.int32, shape, 1)
    total = jnp.zeros(shape, f32)
    for at, column in columns.items():
        total = jnp.where(lane == at, column, total)
    return total


def put_rows(shape, rows):
    row = lax.broadcasted_iota(jnp.int32, shape, 0)
    total = jnp.zeros(shape, f32)
    for at, value in rows.items():
        total = jnp.where(row == at, value, total)
    return total


def axes_size(axes):
    count = 1
    for axis in axes:
        count *= lax.axis_size(axis)
    return count


def call(
    kernel,
    name,
    grid,
    scalars,
    in_specs,
    out_specs,
    out_shape,
    scratch=(),
    aliases=None,
    flops=0,
    after=(),
    vmem=24,
):
    after = tuple(after)
    first = scalars + len(in_specs)

    def body(*refs):
        kernel(*refs[:first], *refs[first + len(after) :])

    run = pl.pallas_call(
        body,
        out_shape=out_shape,
        grid_spec=pltpu.PrefetchScalarGridSpec(
            num_scalar_prefetch=scalars,
            grid=grid,
            in_specs=list(in_specs) + [pl.BlockSpec(memory_space=pl.ANY)] * len(after),
            out_specs=out_specs,
            scratch_shapes=list(scratch),
        ),
        input_output_aliases=aliases or {},
        compiler_params=pltpu.CompilerParams(vmem_limit_bytes=vmem << 20),
        cost_estimate=pl.CostEstimate(flops=1, bytes_accessed=1, transcendentals=0),
        name=name,
    )
    return lambda *arrays: run(*arrays, *after)


def full(shape):
    return pl.BlockSpec(shape, lambda *_: (0,) * len(shape))


def add_kernel(*refs):
    total = refs[0][...].astype(f32)
    for ref in refs[1:-1]:
        total = total + ref[...].astype(f32)
    refs[-1][...] = total.astype(bf16)


def add(*values, after=()):
    shape = values[0].shape
    return call(
        add_kernel,
        "add",
        (1,),
        0,
        [full(shape)] * len(values),
        full(shape),
        jax.ShapeDtypeStruct(shape, bf16),
        after=after,
        vmem=56,
    )(*values)


def pick_kernel(flag_ref, one_ref, two_ref, out_ref):
    @pl.when(flag_ref[0] == 1)
    def _():
        out_ref[...] = one_ref[...]

    @pl.when(flag_ref[0] != 1)
    def _():
        out_ref[...] = two_ref[...]


def pick(flag, one, two, after=()):
    rows, depth = one.shape
    spec = pl.BlockSpec((rows // 3, depth), lambda i, s: (i, 0))
    return call(
        pick_kernel,
        "pick",
        (3,),
        1,
        [spec, spec],
        spec,
        jax.ShapeDtypeStruct(one.shape, one.dtype),
        after=after,
    )(flag, one, two)


def held_kernel(in_ref, out_ref):
    del in_ref, out_ref


def held(value, after):
    anywhere = pl.BlockSpec(memory_space=pl.ANY)
    return call(
        held_kernel,
        "held",
        (1,),
        0,
        [anywhere],
        anywhere,
        jax.ShapeDtypeStruct(value.shape, value.dtype),
        aliases={0: 0},
        after=after,
        vmem=56,
    )(value)


def cast_kernel(sel_ref, in_ref, out_ref):
    taps, chans = in_ref.shape[:2]
    first = jnp.logical_and(sel_ref[0] == 1, pl.program_id(0) == 0)
    for tap in range(taps):
        value = in_ref[tap]
        if tap == 0:
            value = jnp.where(first, 0.0, value)
        out_ref[tap * chans : (tap + 1) * chans, :] = value.astype(bf16)


def cast_half(sel, weight, split, after):
    chans, depth = weight.shape[1:]
    parts = 3 if (split + 1) % 3 == 0 else 1
    block = (split + 1) // parts
    return call(
        cast_kernel,
        "cast",
        (parts,),
        1,
        [pl.BlockSpec((pl.Element(block), pl.Element(chans), pl.Element(depth)), lambda i, s: (s[0] * split + i * block, 0, 0))],
        pl.BlockSpec((block * chans, depth), lambda i, s: (i, 0)),
        jax.ShapeDtypeStruct(((split + 1) * chans, depth), bf16),
        after=after,
        vmem=56,
    )(sel, weight)


def mask_kernel(columns, scalar_ref, in_ref, out_ref, *part_refs):
    rows, depth = in_ref.shape
    pixel = lax.broadcasted_iota(jnp.int32, (rows, LANES), 0)
    row = pixel // columns + scalar_ref[HALF + 1] * (rows // columns)
    height = scalar_ref[HEIGHT]
    inside = jnp.logical_and(row < height, pixel % columns < 2 * height)
    for first in range(0, depth, LANES):
        lanes = slice(first, first + LANES)
        value = jnp.where(inside, in_ref[:, lanes].astype(f32), 0.0).astype(bf16)
        out_ref[:, lanes] = value
        start = 0
        for part_ref in part_refs:
            size = part_ref.shape[0]
            part_ref[:, lanes] = value[start : start + size]
            start += size


def mask_strip(scalars, strip, columns, after):
    rows, depth = strip.shape
    low = rows // 16 * 7
    shapes = ((rows, depth), (low, depth), (rows - low, depth))
    return call(
        functools.partial(mask_kernel, columns),
        "mask",
        (1,),
        1,
        [full((rows, depth))],
        tuple(full(shape) for shape in shapes),
        tuple(jax.ShapeDtypeStruct(shape, bf16) for shape in shapes),
        after=after,
        vmem=56,
    )(scalars, strip)


def image_kernel(strip, places, spot_ref, *refs):
    *parts, out_ref, sems = refs
    copies = []
    for at, (which, first) in enumerate(places):
        rows = pl.ds(pl.multiple_of(spot_ref[HALF + 1 + which] * strip + first, 16), parts[at].shape[0])
        copies.append(pltpu.make_async_copy(parts[at], out_ref.at[rows, :], sems.at[at]))
    for copy in copies:
        copy.start()
    for copy in copies:
        copy.wait()


def image_of(spots, strip, parts, after):
    depth = parts[0][0].shape[1]
    places = []
    for which, strip_parts in enumerate(parts):
        first = 0
        for part in strip_parts:
            places.append((which, first))
            first += part.shape[0]
    flat = [part for strip_parts in parts for part in strip_parts]
    anywhere = pl.BlockSpec(memory_space=pl.ANY)
    return call(
        functools.partial(image_kernel, strip, places),
        "image",
        (1,),
        1,
        [anywhere] * len(flat),
        full((4 * strip, depth)),
        jax.ShapeDtypeStruct((4 * strip, depth), bf16),
        [pltpu.SemaphoreType.DMA((len(flat),))],
        after=after,
        vmem=56,
    )(spots, *flat)


def head_grad_kernel(x_ref, back_ref, sum_ref, value_ref, out_ref):
    channels = back_ref.shape[0]
    rows = x_ref.shape[0] // 4
    act = jnp.zeros((EXTRA, channels), f32)
    for quad in range(4):
        first = quad * rows + rows - EXTRA
        act = act + x_ref[first : first + EXTRA, :channels].astype(f32)
    out_ref[:, :channels] = (sum_ref[:, 0:1] * act[0:1, :]).astype(bf16)
    strip = x_ref.shape[1]
    out_ref[:, channels : channels + strip] = value_ref[...]
    out_ref[:, channels + strip :] = lax.dot_general(
        back_ref[...], x_ref[...], (((1,), (1,)), ((), ())), preferred_element_type=f32
    ).astype(bf16)


def head_weight_grads(concat, unit_back, row_sums, values, after):
    channels = unit_back.shape[0]
    arrays = (concat, unit_back, row_sums, values)
    shape = (channels, channels + concat.shape[1] + concat.shape[0])
    return call(
        head_grad_kernel,
        "head_weight_grad",
        (1,),
        0,
        [full(array.shape) for array in arrays],
        full(shape),
        jax.ShapeDtypeStruct(shape, bf16),
        after=after,
        vmem=24,
    )(*arrays)


def strip_sum_kernel(columns, whole, masked, scalar_ref, *refs):
    block = refs[0].shape[0]
    step = pl.program_id(0)
    rows_all = refs[whole].shape[0] * (len(refs) - 1 - whole)
    pixel = step * block + lax.broadcasted_iota(jnp.int32, (block, LANES), 0)
    row = pixel // columns + scalar_ref[HALF + 1] * (rows_all // columns)
    height = scalar_ref[HEIGHT]
    inside = jnp.logical_and(row < height, pixel % columns < 2 * height)
    steps = refs[whole].shape[0] * (len(refs) - 1 - whole) // block
    count = steps // (len(refs) - 1 - whole)
    for at in range(steps):

        @pl.when(step == at)
        def _():
            part = refs[whole + at // count]
            rows = slice(at % count * block, (at % count + 1) * block)
            for first in range(0, refs[0].shape[1], LANES):
                lanes = slice(first, first + LANES)
                total = part[rows, lanes].astype(f32)
                for ref in refs[:whole]:
                    total = total + ref[:, lanes].astype(f32)
                if masked:
                    total = jnp.where(inside, total, 0.0)
                refs[-1][:, lanes] = total.astype(bf16)


def strip_sum(scalars, strips, parts, columns, masked, after):
    rows, depth = strips[0].shape
    spec = pl.BlockSpec((rows // 2, depth), lambda i, s: (i, 0))
    return call(
        functools.partial(strip_sum_kernel, columns, len(strips), masked),
        "strip_sum",
        (2,),
        1,
        [spec] * len(strips) + [full(part.shape) for part in parts],
        spec,
        jax.ShapeDtypeStruct((rows, depth), bf16),
        after=after,
        vmem=56,
    )(scalars, *strips, *parts)


def adam_kernel(start_ref, grad_ref, weight_ref, first_ref, second_ref, *rest):
    out_ref, mean_ref, square_ref, new_ref = rest[-4:]
    grad = grad_ref[...].astype(f32).reshape(out_ref.shape)
    mean, square, new = adamw_update(
        weight_ref[...], grad, first_ref[...], second_ref[...], conv_rate, weight_decay
    )
    out_ref[...] = grad
    mean_ref[...] = mean
    square_ref[...] = square
    new_ref[...] = new


def adam_taps(start, count, block, grads, weight, first, second, earlier, after):
    taps, chans, depth = weight.shape

    def piece(size, index):
        return pl.BlockSpec(tuple(pl.Element(n) for n in size), index)

    spec = piece((block, chans, depth), lambda i, s: (s[0] + i * block, 0, 0))
    anywhere = [pl.BlockSpec(memory_space=pl.ANY)] * len(earlier)
    return call(
        adam_kernel,
        "adamw",
        (count // block,),
        1,
        [piece((block * chans, depth), lambda i, s: ((s[1] + i * block) * chans, 0))]
        + [spec] * 3
        + anywhere,
        (spec,) * 4,
        (jax.ShapeDtypeStruct(weight.shape, f32),) * 4,
        aliases={5 + at: at for at in range(4)} if earlier else None,
        after=after,
        vmem=20,
    )(start, grads, weight, first, second, *earlier)


FIRST, SECOND, GAIN, SHIFT, AREA = 0, 8, 16, 24, 32
SUM_ROWS = 40
CENTRE, INVERSE, VARIANCE, COUNT, POOLED = 0, 8, 32, 40, 41
COEF_ROWS = 48
EXTRA = 16
HEIGHT, HALF = 8, 9


def lane_masks(columns):
    lane = lax.broadcasted_iota(jnp.int32, (1, LANES), 1) % columns
    masks = {}
    for dilation in dilations:
        for off in (-dilation, dilation):
            moved = lane + off
            masks[off] = jnp.logical_and(moved >= 0, moved < columns)
    return masks


def forward_kernel(columns, split, slot, scalar_ref, x_ref, wz_ref, wx_ref, mask_ref, *rest):
    pre_ref, stat_ref, taps = rest[-3:]
    step = pl.program_id(0)
    half = wz_ref.shape[0]
    block = x_ref.shape[0]
    sel = scalar_ref[slot]
    contract = (((1,), (1,)), ((), ()))
    pixels = x_ref[...]
    cols = pl.ds(pl.multiple_of(step * block, block), block)
    taps[pl.ds(pl.multiple_of(sel * half, 16), half), cols] = lax.dot_general(
        wz_ref[...], pixels, contract, preferred_element_type=f32
    )
    taps[pl.ds(pl.multiple_of((1 - sel) * half, 16), half), cols] = lax.dot_general(
        wx_ref[...], pixels, contract, preferred_element_type=f32
    )

    @pl.when(step == pl.num_programs(0) - 1)
    def _():
        total = taps.shape[1]
        tiles = total // LANES
        chans = pre_ref.shape[2]
        masks = lane_masks(columns)

        def rows_of(tap):
            first = tap * chans if tap <= split else (tap + 1) * chans
            return slice(first, first + chans)

        def tile(tap, at):
            return taps[rows_of(tap), at * LANES : (at + 1) * LANES]

        sums = [jnp.zeros((chans, LANES), f32) for _ in range(4)]
        squares = [jnp.zeros((chans, LANES), f32) for _ in range(4)]
        pooled = jnp.zeros((chans, LANES), f32)
        for at in range(tiles):
            lanes = slice(at * LANES, (at + 1) * LANES)
            weight = mask_ref[0:1, lanes]
            for branch in range(4):
                if branch == 0:
                    value = tile(0, at)
                else:
                    dilation = dilations[branch - 1]
                    jump = dilation * columns // LANES
                    value = None
                    for b in range(3):
                        part = None
                        for a in range(3):
                            source = at + (a - 1) * jump
                            if 0 <= source < tiles:
                                term = tile(1 + 9 * (branch - 1) + 3 * a + b, source)
                                part = term if part is None else part + term
                        off = (b - 1) * dilation
                        if off != 0:
                            part = pltpu.roll(part, (-off) % LANES, 1)
                            part = jnp.where(masks[off], part, 0.0)
                        value = part if value is None else value + part
                pre_ref[0, branch, :, lanes] = value
                weighted = value * weight
                sums[branch] = sums[branch] + weighted
                squares[branch] = squares[branch] + weighted * value
            pooled = pooled + tile(28, at)
        height = jnp.full((1, 1), scalar_ref[HEIGHT], jnp.int32).astype(f32)
        area = 2.0 * height * height
        pool = jnp.sum(pooled, axis=1, keepdims=True) / area
        columns_of = {FIRST + 4: pool, SECOND + 4: pool * pool, AREA: area}
        for branch in range(4):
            columns_of[FIRST + branch] = jnp.sum(sums[branch], axis=1, keepdims=True)
            columns_of[SECOND + branch] = jnp.sum(squares[branch], axis=1, keepdims=True)
        stat_ref[0] = put_lanes((chans, LANES), columns_of)


def forward_taps(slot, pixels, mask_rows, scalars, wz, wx, earlier, columns, chans, split, after):
    total, depth = pixels.shape
    block = total // 4
    half = wz.shape[0]
    keep = [pl.BlockSpec(memory_space=pl.ANY)] * len(earlier)
    return call(
        functools.partial(forward_kernel, columns, split, slot),
        "atrous_forward",
        (4,),
        1,
        [
            pl.BlockSpec((block, depth), lambda i, s: (i, 0)),
            full((half, depth)),
            full((half, depth)),
            full((8, total)),
        ]
        + keep,
        (
            pl.BlockSpec((1, 4, chans, total), lambda i, s: (s[4 + slot], 0, 0, 0)),
            pl.BlockSpec((1, chans, LANES), lambda i, s: (s[4 + slot], 0, 0)),
        ),
        (
            jax.ShapeDtypeStruct((4, 4, chans, total), f32),
            jax.ShapeDtypeStruct((4, chans, LANES), f32),
        ),
        [pltpu.VMEM((2 * half, total), f32)],
        {5: 0, 6: 1} if earlier else None,
        4 * half * total * depth,
        after,
        56,
    )(scalars, pixels, wz, wx, mask_rows, *earlier)


def pack_kernel(place_ref, stat_ref, norm_ref, out_ref, work):
    chans = norm_ref.shape[0]
    work[...] = jnp.zeros_like(work)
    for z in range(4):
        work[z * chans : (z + 1) * chans, :] = stat_ref[z]
    own = pl.ds(pl.multiple_of(place_ref[4] * chans, chans), chans)
    work[own, :] = work[own, :] + norm_ref[...]
    rows = work[...].T[:SUM_ROWS]
    for at in range(out_ref.shape[0]):
        out_ref[at] = rows


def pack_sums(place, stats, norm_cols, count, after):
    return call(
        pack_kernel,
        "branch_sums",
        (1,),
        1,
        [full(stats.shape), full(norm_cols.shape)],
        full((count, SUM_ROWS, LANES)),
        jax.ShapeDtypeStruct((count, SUM_ROWS, LANES), f32),
        [pltpu.VMEM((LANES, LANES), f32)],
        after=after,
        vmem=24,
    )(place, stats, norm_cols)


def pool_rows_of(rows_ref, own_width):
    def row(at):
        return rows_ref[at : at + 1, :]

    moved = row(POOLED) - row(CENTRE + 4)
    normed = row(GAIN + 4) * moved * row(INVERSE + 4) + row(SHIFT + 4)
    lane = lax.broadcasted_iota(jnp.int32, normed.shape, 1)
    return normed, moved * row(INVERSE + 4), lane < own_width


def act_kernel(image_total, quad_ref, parts_ref, own_ref, pre_ref, out_ref, col_ref, row_ref):
    chans = pre_ref.shape[2]

    @pl.when(pl.program_id(0) == 0)
    def _():
        sums = jnp.sum(parts_ref[...], axis=0)
        pixel_total = jnp.maximum(sums[AREA : AREA + 1], 1.0)
        index = lax.broadcasted_iota(jnp.int32, (8, LANES), 0)
        count = jnp.where(index == 4, image_total, pixel_total)
        centre = sums[FIRST : FIRST + 8] / count
        variance = sums[SECOND : SECOND + 8] / count - centre * centre
        inverse = lax.rsqrt(variance + epsilon)
        other = jnp.where(index == 0, pixel_total, jnp.where(index == 1, own_ref[0, 4:5, :], 0.0))
        rows = jnp.concatenate(
            [centre, inverse, sums[GAIN : GAIN + 8], sums[SHIFT : SHIFT + 8], variance, other],
            axis=0,
        )
        row_ref[...] = rows
        col_ref[...] = tall(rows)

    for z in range(4):
        span = slice(z * chans, (z + 1) * chans)
        for branch in range(4):
            moved = pre_ref[z, branch] - col_ref[span, CENTRE + branch : CENTRE + branch + 1]
            normed = (
                col_ref[span, GAIN + branch : GAIN + branch + 1]
                * moved
                * col_ref[span, INVERSE + branch : INVERSE + branch + 1]
                + col_ref[span, SHIFT + branch : SHIFT + branch + 1]
            )
            first = (4 * z + branch) * chans
            out_ref[0, first : first + chans, :] = gelu_both(normed)[0].astype(bf16)
    normed, _, valid = pool_rows_of(row_ref, 4 * chans)
    act = jnp.where(valid, gelu_both(normed)[0], 0.0)
    act = put_rows((EXTRA, LANES), {0: act + pltpu.roll(act, 4 * chans, 1)})
    lane = lax.broadcasted_iota(jnp.int32, act.shape, 1)
    for at in range(out_ref.shape[2] // LANES):
        owner = (lane + at * LANES) // (4 * chans)
        out_ref[0, 16 * chans :, at * LANES : (at + 1) * LANES] = jnp.where(
            owner == quad_ref[0], act, 0.0
        ).astype(bf16)


def activations(quad, parts, own, pre, image_total):
    chans, total = pre.shape[2:]
    strip = total // 4
    rows = 16 * chans + EXTRA
    return call(
        functools.partial(act_kernel, image_total),
        "branch_act",
        (4,),
        1,
        [
            full(parts.shape),
            full((1, SUM_ROWS, LANES)),
            pl.BlockSpec((4, 4, chans, strip), lambda i, s: (0, 0, 0, i)),
        ],
        (
            pl.BlockSpec((1, rows, strip), lambda i, s: (i, 0, 0)),
            full((LANES, LANES)),
            full((COEF_ROWS, LANES)),
        ),
        (
            jax.ShapeDtypeStruct((4, rows, strip), bf16),
            jax.ShapeDtypeStruct((LANES, LANES), f32),
            jax.ShapeDtypeStruct((COEF_ROWS, LANES), f32),
        ),
        vmem=24,
    )(quad, parts, own, pre)


def unit_kernel(x_ref, shared_ref, head_ref, mask_ref, unit_ref, out_ref):
    channels = shared_ref.shape[0]
    rows, strip = x_ref.shape[0] // 4, x_ref.shape[1]
    proj = shared_ref[:, channels + strip :]
    unit = jnp.dot(proj, x_ref[...], preferred_element_type=f32)
    act = jnp.zeros((EXTRA, channels), f32)
    for quad in range(4):
        first = quad * rows + rows - EXTRA
        act = act + x_ref[first : first + EXTRA, :channels].astype(f32)
    bias = shared_ref[:, :channels].astype(f32) * act[0:1, :]
    unit = unit + jnp.sum(bias, axis=1, keepdims=True)
    unit_ref[...] = unit
    weighted = unit * mask_ref[0:1, :]
    lane = lax.broadcasted_iota(jnp.int32, head_ref.shape, 1)
    one = jnp.sum(weighted, axis=1, keepdims=True)
    two = jnp.sum(weighted * unit, axis=1, keepdims=True)
    sums = jnp.where(lane == 0, one, jnp.where(lane == 1, two, head_ref[...])).T[:8]
    for at in range(out_ref.shape[0]):
        out_ref[at] = sums


def project(concat, shared, head_cols, strip_mask, count):
    channels, strip = shared.shape[0], concat.shape[1]
    arrays = (concat, shared, head_cols, strip_mask)
    return call(
        unit_kernel,
        "projection",
        (1,),
        0,
        [full(array.shape) for array in arrays],
        (full((channels, strip)), full((count, 8, channels))),
        (
            jax.ShapeDtypeStruct((channels, strip), f32),
            jax.ShapeDtypeStruct((count, 8, channels), f32),
        ),
        vmem=24,
    )(*arrays)


def head_kernel(parts_ref, unit_ref, shared_ref, mask_ref, row_ref, value_ref, delta_ref, col_ref, head_ref, out_ref):
    sums = jnp.sum(parts_ref[...], axis=0)
    pixel_total = row_ref[COUNT : COUNT + 1, 0:1]
    centre = sums[0:1] / pixel_total
    variance = sums[1:2] / pixel_total - centre * centre
    inverse = lax.rsqrt(variance + epsilon)
    rows = put_rows(
        sums.shape, {0: centre, 1: inverse, 2: sums[2:3], 3: sums[3:4], 4: variance}
    )
    head_ref[...] = rows
    columns = tall(rows)
    col_ref[...] = columns
    hat = (unit_ref[...] - columns[:, 0:1]) * columns[:, 1:2]
    normed = columns[:, 2:3] * hat + columns[:, 3:4]
    value, slope = gelu_both(normed)
    weight = mask_ref[0:1, :]
    value_ref[...] = (weight * value).astype(bf16)
    first = unit_ref.shape[0]
    cot = shared_ref[:, first : first + unit_ref.shape[1]].astype(f32)
    delta = slope * (weight * cot)
    delta_ref[...] = delta
    sums = put_lanes(
        columns.shape,
        {
            0: jnp.sum(delta, axis=1, keepdims=True),
            1: jnp.sum(delta * hat, axis=1, keepdims=True),
        },
    ).T[:8]
    for at in range(out_ref.shape[0]):
        out_ref[at] = sums


def head_norm(parts, unit, shared, strip_mask, coef_rows):
    channels, strip = unit.shape
    count = parts.shape[0]
    return call(
        head_kernel,
        "head_norm",
        (1,),
        0,
        [full(parts.shape), full(unit.shape), full(shared.shape), full((8, strip)), full(coef_rows.shape)],
        (
            full((channels, strip)),
            full((channels, strip)),
            full((channels, LANES)),
            full((8, channels)),
            full((count, 8, channels)),
        ),
        (
            jax.ShapeDtypeStruct((channels, strip), bf16),
            jax.ShapeDtypeStruct((channels, strip), f32),
            jax.ShapeDtypeStruct((channels, LANES), f32),
            jax.ShapeDtypeStruct((8, channels), f32),
            jax.ShapeDtypeStruct((count, 8, channels), f32),
        ),
        vmem=24,
    )(parts, unit, shared, strip_mask, coef_rows)


def unit_back_kernel(
    parts_ref, unit_ref, delta_ref, col_ref, mask_ref, row_ref, shared_ref, back_ref, out_ref, sum_ref, moment_ref
):
    sums = jnp.sum(parts_ref[...], axis=0)
    moment_ref[...] = sums
    moments = tall(sums)
    pixel_total = row_ref[COUNT : COUNT + 1, 0:1]
    inverse = col_ref[:, 1:2]
    hat = (unit_ref[...] - col_ref[:, 0:1]) * inverse
    back = mask_ref[0:1, :] * (
        (col_ref[:, 2:3] * inverse)
        * (delta_ref[...] - (moments[:, 0:1] + hat * moments[:, 1:2]) / pixel_total)
    )
    back = back.astype(bf16)
    back_ref[...] = back
    row_sums = jnp.sum(back.astype(f32), axis=1, keepdims=True)
    sum_ref[...] = jnp.broadcast_to(row_sums, sum_ref.shape)
    channels = shared_ref.shape[0]
    rows, width = out_ref.shape[1:]
    proj = shared_ref[:, channels + width :]
    terms = lax.dot_general(
        proj, back, (((0,), (0,)), ((), ())), preferred_element_type=f32
    )
    pool = jnp.sum(shared_ref[:, :channels].astype(f32) * row_sums, axis=0, keepdims=True)
    own = channels // 4
    for quad in range(4):
        first = quad * own // LANES * LANES
        part = pool[:, first : first + LANES]
        if quad * own != first:
            part = pltpu.roll(part, LANES - (quad * own - first), 1)
        lane = lax.broadcasted_iota(jnp.int32, part.shape, 1)
        part = jnp.where(lane < own, part, 0.0)
        high = part.astype(bf16).astype(f32)
        extra = put_rows((EXTRA, LANES), {0: high, 1: part - high})
        out_ref[quad, : rows - EXTRA, :] = terms[quad * rows : (quad + 1) * rows - EXTRA].astype(bf16)
        out_ref[quad, rows - EXTRA :, :LANES] = extra.astype(bf16)
        out_ref[quad, rows - EXTRA :, LANES:] = jnp.zeros((EXTRA, width - LANES), bf16)


def unit_backward(parts, unit, delta, cols, strip_mask, coef_rows, shared):
    channels, strip = unit.shape
    rows = (shared.shape[1] - channels - strip) // 4
    arrays = (parts, unit, delta, cols, strip_mask, coef_rows, shared)
    return call(
        unit_back_kernel,
        "unit_back",
        (1,),
        0,
        [full(array.shape) for array in arrays],
        (
            full((channels, strip)),
            full((4, rows, strip)),
            full((channels, LANES)),
            full((8, channels)),
        ),
        (
            jax.ShapeDtypeStruct((channels, strip), bf16),
            jax.ShapeDtypeStruct((4, rows, strip), bf16),
            jax.ShapeDtypeStruct((channels, LANES), f32),
            jax.ShapeDtypeStruct((8, channels), f32),
        ),
        vmem=24,
    )(*arrays)


def branch_kernel(x_ref, pre_ref, col_ref, row_ref, mask_ref, delta_ref, pool_ref, out_ref, sums, pooled):
    step = pl.program_id(0)
    chans = pre_ref.shape[2]

    @pl.when(step == 0)
    def _():
        sums[...] = jnp.zeros_like(sums)
        pooled[...] = jnp.zeros_like(pooled)

    def fold(value):
        total = value[:, :LANES]
        for at in range(1, value.shape[1] // LANES):
            total = total + value[:, at * LANES : (at + 1) * LANES]
        return total

    weight = mask_ref[0:1, :]
    for z in range(4):
        span = slice(z * chans, (z + 1) * chans)
        for branch in range(4):
            first = (4 * z + branch) * chans
            hat = (
                pre_ref[z, branch] - col_ref[span, CENTRE + branch : CENTRE + branch + 1]
            ) * col_ref[span, INVERSE + branch : INVERSE + branch + 1]
            normed = (
                col_ref[span, GAIN + branch : GAIN + branch + 1] * hat
                + col_ref[span, SHIFT + branch : SHIFT + branch + 1]
            )
            delta = gelu_both(normed)[1] * (
                weight * x_ref[0, first : first + chans, :].astype(f32)
            )
            delta_ref[z, branch] = delta
            sums[8 * z + branch] = sums[8 * z + branch] + fold(delta)
            sums[8 * z + 4 + branch] = sums[8 * z + 4 + branch] + fold(delta * hat)
    extra = x_ref[0, 16 * chans :, :LANES].astype(f32)
    pooled[...] = pooled[...] + jnp.broadcast_to(extra[0:1] + extra[1:2], pooled.shape)

    @pl.when(step == pl.num_programs(0) - 1)
    def _():
        normed, hat, valid = pool_rows_of(row_ref, 4 * chans)
        delta = jnp.where(valid, gelu_both(normed)[1] * pooled[0:1, :], 0.0)
        hat = jnp.where(valid, hat, 0.0)
        pool_ref[...] = put_rows(pool_ref.shape, {0: delta, 1: hat})
        found = []
        for z in range(4):
            columns = {}
            for branch in range(4):
                columns[branch] = jnp.sum(sums[8 * z + branch], axis=1, keepdims=True)
                columns[8 + branch] = jnp.sum(sums[8 * z + 4 + branch], axis=1, keepdims=True)
            found.append(put_lanes((chans, LANES), columns))
        found.append(jnp.zeros((LANES - 4 * chans, LANES), f32))
        rows = jnp.concatenate(found, axis=0).T[:16]
        index = lax.broadcasted_iota(jnp.int32, rows.shape, 0)
        rows = jnp.where(index == 4, delta, jnp.where(index == 12, delta * hat, rows))
        for at in range(out_ref.shape[0]):
            out_ref[at] = rows


def branch_backward(concat_back, pre, coef_cols, coef_rows, mask_rows, count, after):
    chans, total = pre.shape[2:]
    rows, strip = concat_back.shape[1:]
    spread = pl.BlockSpec((4, 4, chans, strip), lambda i: (0, 0, 0, i))
    return call(
        branch_kernel,
        "branch_back",
        (4,),
        0,
        [
            pl.BlockSpec((1, rows, strip), lambda i: (i, 0, 0)),
            spread,
            full(coef_cols.shape),
            full(coef_rows.shape),
            pl.BlockSpec((8, strip), lambda i: (0, i)),
        ],
        (spread, full((8, LANES)), full((count, 16, LANES))),
        (
            jax.ShapeDtypeStruct(pre.shape, f32),
            jax.ShapeDtypeStruct((8, LANES), f32),
            jax.ShapeDtypeStruct((count, 16, LANES), f32),
        ),
        [pltpu.VMEM((32, chans, LANES), f32), pltpu.VMEM((8, LANES), f32)],
        after=after,
        vmem=24,
    )(concat_back, pre, coef_cols, coef_rows, mask_rows)


def weight_kernel(columns, image_total, slots, scalar_ref, parts_ref, pool_ref, mask_ref, x_ref, *refs):
    count = len(slots)
    col_refs, pre_refs, delta_refs = refs[:count], refs[count : 2 * count], refs[2 * count : 3 * count]
    outs = refs[3 * count : 6 * count]
    total_ref, moments = refs[6 * count :]
    half = outs[0].shape[0]
    chans = pre_refs[0].shape[2]
    start = 29 * chans - half
    sel = scalar_ref[HALF]

    @pl.when(pl.program_id(0) == 0)
    def _():
        rows = jnp.concatenate([jnp.sum(parts_ref[...], axis=0), pool_ref[...]], axis=0)
        moments[...] = tall(rows)
        height = jnp.full((1, 1), scalar_ref[HEIGHT], jnp.int32).astype(f32)
        area = 2.0 * height * height
        masks = lane_masks(columns)
        for at, slot in enumerate(slots):
            own = moments[pl.ds(pl.multiple_of(scalar_ref[4 + slot] * chans, chans), chans), :]
            build_taps(
                own, col_refs[at][...], pre_refs[at], delta_refs[at], mask_ref, outs[3 * at + 2], masks, area, columns, image_total
            )

    for at in range(count):
        keep_ref, send_ref, taps_ref = outs[3 * at : 3 * at + 3]
        total_ref[...] = jnp.dot(taps_ref[...], x_ref[...], preferred_element_type=f32)
        keep_ref[...] = total_ref[pl.ds(pl.multiple_of(sel * start, 16), half), :].astype(bf16)
        send_ref[...] = total_ref[pl.ds(pl.multiple_of((1 - sel) * start, 16), half), :].astype(bf16)


def build_taps(own, coefs, pre_ref, delta_ref, mask_ref, taps_ref, masks, area, columns, image_total):
    chans = pre_ref.shape[2]

    def coef(at):
        return coefs[:, at : at + 1]

    def moment(at):
        return own[:, at : at + 1]

    pixel_total = coef(COUNT)
    pool_grad = (
        coef(GAIN + 4)
        * coef(INVERSE + 4)
        * (moment(16) - (moment(4) + moment(17) * moment(12)) / image_total)
    ) / area
    tiles = pre_ref.shape[3] // LANES
    for at in range(tiles):
        lanes = slice(at * LANES, (at + 1) * LANES)
        weight = mask_ref[0:1, lanes]
        taps_ref[28 * chans : 29 * chans, lanes] = (weight * pool_grad).astype(bf16)
        for branch in range(4):
            hat = (pre_ref[0, branch, :, lanes] - coef(CENTRE + branch)) * coef(INVERSE + branch)
            grad = weight * (
                (coef(GAIN + branch) * coef(INVERSE + branch))
                * (
                    delta_ref[0, branch, :, lanes]
                    - (moment(branch) + hat * moment(8 + branch)) / pixel_total
                )
            )
            if branch == 0:
                taps_ref[0:chans, lanes] = grad.astype(bf16)
                continue
            j, dilation = branch - 1, dilations[branch - 1]
            jump = dilation * columns // LANES
            for b in range(3):
                off = (b - 1) * dilation
                moved = grad
                if off != 0:
                    moved = pltpu.roll(grad, off % LANES, 1)
                    moved = jnp.where(masks[-off], moved, 0.0)
                moved = moved.astype(bf16)
                for a in range(3):
                    tap = 1 + 9 * j + 3 * a + b
                    span = slice(tap * chans, (tap + 1) * chans)
                    target = at + (a - 1) * jump
                    if 0 <= target < tiles:
                        taps_ref[span, target * LANES : (target + 1) * LANES] = moved
                    source = at - (a - 1) * jump
                    if not 0 <= source < tiles:
                        taps_ref[span, lanes] = jnp.zeros((chans, LANES), bf16)


def weight_grads(
    slots, scalars, parts, pool_rows, coef_cols, pre, delta, mask_rows, pixels, columns, half, image_total, after
):
    chans, total = pre.shape[2:]
    depth = pixels.shape[1]
    block = depth // 4
    count = len(slots)

    def cols(slot):
        return pl.BlockSpec((chans, LANES), lambda i, s: (s[4 + slot], 0))

    def own(slot):
        return pl.BlockSpec((1, 4, chans, total), lambda i, s: (s[4 + slot], 0, 0, 0))

    outs = call(
        functools.partial(weight_kernel, columns, image_total, slots),
        "atrous_weight_grad",
        (4,),
        1,
        [
            full(parts.shape),
            full(pool_rows.shape),
            full(mask_rows.shape),
            pl.BlockSpec((total, block), lambda i, s: (0, i)),
        ]
        + [cols(slot) for slot in slots]
        + [own(slot) for slot in slots] * 2,
        (
            pl.BlockSpec((half, block), lambda i, s: (0, i)),
            pl.BlockSpec((half, block), lambda i, s: (0, i)),
            full((29 * chans, total)),
        )
        * count,
        (
            jax.ShapeDtypeStruct((half, depth), bf16),
            jax.ShapeDtypeStruct((half, depth), bf16),
            jax.ShapeDtypeStruct((29 * chans, total), bf16),
        )
        * count,
        [pltpu.VMEM((29 * chans, block), f32), pltpu.VMEM((LANES, LANES), f32)],
        after=after,
        vmem=56,
    )(
        scalars,
        parts,
        pool_rows,
        mask_rows,
        pixels,
        *[coef_cols] * count,
        *[pre] * count,
        *[delta] * count,
    )
    return [outs[3 * at : 3 * at + 3] for at in range(count)]


def input_kernel(start, places, scalar_ref, *refs):
    taps, weights, outs = refs[0:4], refs[4:12], refs[12:15]
    all_weights, all_taps, result, weight_sems, tap_sems, out_sems = refs[15:]
    half, depth = weights[0].shape
    block = all_taps.shape[2]
    cut = depth // 2

    def tap_copies(strip):
        copies = []
        lanes = pl.ds(pl.multiple_of(scalar_ref[places[strip]] * block, LANES), block)
        for slot in range(4):
            sel = scalar_ref[slot]
            for which in range(2):
                first = sel * start if which == 0 else (1 - sel) * start
                at = 2 * slot + which
                copies.append(
                    pltpu.make_async_copy(
                        taps[slot].at[pl.ds(pl.multiple_of(first, 16), half), lanes],
                        all_taps.at[strip, pl.ds(at * half, half), :],
                        tap_sems.at[strip, at],
                    )
                )
        return copies

    def weight_copies(part):
        lanes = pl.ds(part * cut, cut)
        return [
            pltpu.make_async_copy(
                weights[at].at[:, lanes],
                all_weights.at[pl.ds(at * half, half), lanes],
                weight_sems.at[part, at],
            )
            for at in range(8)
        ]

    tap_lists = [tap_copies(0), tap_copies(1)]
    weight_lists = [weight_copies(0), weight_copies(1)]
    for copies in (tap_lists[0], weight_lists[0], weight_lists[1], tap_lists[1]):
        for copy in copies:
            copy.start()
    rows = outs[0].shape[0]
    out_lists = [
        [
            pltpu.make_async_copy(result.at[0, pl.ds(0, rows), :], outs[0], out_sems.at[0]),
            pltpu.make_async_copy(result.at[0, pl.ds(rows, rows), :], outs[1], out_sems.at[1]),
        ],
        [pltpu.make_async_copy(result.at[1], outs[2], out_sems.at[2])],
    ]
    for strip in range(2):
        for copy in tap_lists[strip]:
            copy.wait()
        for part in range(2):
            if strip == 0:
                for copy in weight_lists[part]:
                    copy.wait()
            lanes = slice(part * cut, (part + 1) * cut)
            result[strip, :, lanes] = lax.dot_general(
                all_taps[strip],
                all_weights[:, lanes],
                (((0,), (0,)), ((), ())),
                preferred_element_type=f32,
            ).astype(bf16)
        for copy in out_lists[strip]:
            copy.start()
    for copies in out_lists:
        for copy in copies:
            copy.wait()


def input_grads(flip, taps, weights, scalars, block, after):
    rows = taps[0].shape[0]
    half, depth = weights[0].shape
    shapes = ((block // 2, depth), (block // 2, depth), (block, depth))
    anywhere = pl.BlockSpec(memory_space=pl.ANY)
    low, high, own = call(
        functools.partial(input_kernel, rows - half, (HALF + 2 + flip, HALF + 1 + flip)),
        "atrous_input_grad",
        (1,),
        1,
        [anywhere] * 12,
        (anywhere,) * 3,
        tuple(jax.ShapeDtypeStruct(shape, bf16) for shape in shapes),
        [
            pltpu.VMEM((8 * half, depth), bf16),
            pltpu.VMEM((2, 8 * half, block), bf16),
            pltpu.VMEM((2, block, depth), bf16),
            pltpu.SemaphoreType.DMA((2, 8)),
            pltpu.SemaphoreType.DMA((2, 8)),
            pltpu.SemaphoreType.DMA((3,)),
        ],
        after=after,
        vmem=58,
    )(scalars, *taps, *weights)
    return [low, high], own


def local(
    features,
    scale_sizes,
    cotangent,
    branch_weight,
    branch_first,
    branch_second,
    head_weight,
    head_first,
    head_second,
    norm_params,
    norm_first,
    norm_second,
    running_stats,
):
    groups = lax.axis_size("dp")
    halves = groups == 2
    images = scale_sizes.shape[1]
    image_total = float(groups * images)
    x_id, z_id = lax.axis_index("dp"), lax.axis_index("z")
    quad_id = lax.axis_index("y") * 2 + lax.axis_index("c")
    wide_id = z_id * 4 + quad_id
    strip_rows, columns, depth = features.shape[1:]
    strip = strip_rows * columns
    total = 4 * strip
    tap_count, chans = branch_weight.shape[:2]
    all_ch = chans * 16
    split = (tap_count - 1) // 2
    half = (split + 1) * chans
    cells, everyone = ("dp", "z"), ("dp",) + PLANE
    rows = 16 * chans + EXTRA

    def exchange(parts, axes):
        return lax.all_to_all(parts, axes, 0, 0, tiled=True)

    height = lax.dynamic_index_in_dim(scale_sizes[0], z_id, 0, keepdims=False)
    pixel = jnp.arange(total, dtype=jnp.int32)
    inside = jnp.logical_and(pixel // columns < height, pixel % columns < 2 * height).astype(f32)
    own_inside = lax.dynamic_slice_in_dim(inside, quad_id * strip, strip, 0)
    mask_rows = jnp.broadcast_to(inside[None], (8, total))
    strip_mask = jnp.broadcast_to(own_inside[None], (8, strip))

    mid = jnp.logical_and(z_id >= 1, z_id <= 2).astype(jnp.int32)[None]

    sel = x_id.astype(jnp.int32) if halves else jnp.zeros((), jnp.int32)
    outer = z_id >= 2
    scalars = jnp.stack(
        [sel, sel, sel, sel]
        + [z_id, jnp.bitwise_xor(z_id, 1), jnp.where(outer, 1, 2), jnp.where(outer, 0, 3)]
        + [height, sel]
        + [jnp.bitwise_xor(quad_id, flip) for flip in range(4)]
    ).astype(jnp.int32)
    first_group = (x_id == 0).astype(f32)
    norm_cols = jnp.zeros((chans, LANES), f32)
    norm_cols = norm_cols.at[:, GAIN : GAIN + 5].set(jnp.transpose(norm_params[0, :5]))
    norm_cols = norm_cols.at[:, SHIFT : SHIFT + 5].set(jnp.transpose(norm_params[1, :5]))
    norm_cols = norm_cols * first_group
    head_cols = jnp.zeros((chans, LANES), f32).at[:, 2:4].set(jnp.transpose(norm_params[:, 5]))
    head_cols = lax.dynamic_update_slice_in_dim(
        jnp.zeros((all_ch, LANES), f32), head_cols * first_group, wide_id * chans, 0
    )
    def over_groups(block):
        return lax.ppermute(block, "dp", SWAP)

    def along(parts, pairs):
        return [lax.ppermute(part, "z", pairs) for part in parts]

    def hold(parts, after):
        return [held(part, after) for part in parts]

    def pair_of(parts):
        return (parts[0], over_groups(parts[0])) if halves else tuple(parts)

    def pick_all(ones, twos, after):
        return [pick(mid, one, two, after) for one, two in zip(ones, twos)]

    zero = jnp.zeros((), jnp.int32)
    mine_w = cast_half(sel[None], branch_weight, split, ())
    other_w = cast_half(1 - sel[None], branch_weight, split, (mine_w,))
    sending = [mine_w] if halves else [mine_w, other_w]
    near, mid_one = along(sending, PAIR), along(sending, MID)

    own_strip = features[0].reshape(strip, depth)
    masked, *masked_parts = mask_strip(scalars, own_strip, columns, sending)
    low_y, high_y = (lax.ppermute(part, "y", SWAP) for part in masked_parts)
    over_c = lax.ppermute(masked, "c", SWAP)

    own_proj = head_weight.astype(bf16).reshape(chans, 5, 4, 4, chans)
    own_proj = jnp.transpose(own_proj, (0, 3, 2, 1, 4))
    pixel_proj = jnp.pad(
        own_proj[:, :, :, :4].reshape(chans, 4, 16 * chans), ((0, 0), (0, 0), (0, EXTRA))
    ).reshape(chans, 4 * rows)
    shared = jnp.concatenate(
        [
            jnp.broadcast_to(own_proj[:, :, :, 4].reshape(1, chans, all_ch), (16, chans, all_ch)),
            jnp.transpose(cotangent[0].reshape(chans, 16, strip), (1, 0, 2)),
            jnp.broadcast_to(pixel_proj[None], (16, chans, 4 * rows)),
        ],
        axis=2,
    )

    slots = [(mine_w, other_w)]
    near = hold(near, [masked, mask_rows, scalars])
    mid_two = along(near, MID)
    near = pair_of(near)
    mid_one = hold(mid_one, near[:1])
    out_one = along(mid_one, OUTWARD)
    low_y = held(low_y, mid_one)
    mid_two = hold(mid_two, [low_y, other_w, shared, strip_mask, norm_cols, head_cols])
    out_two = along(mid_two, OUTWARD)
    second = pick_all(mid_one, out_one, mid_two)
    second_pair = pair_of(second)
    high_y = held(high_y, second)
    low_yc, high_yc = (lax.ppermute(part, "c", SWAP) for part in (low_y, high_y))
    near = (near[0], held(near[1], (high_y,)))
    slots.append(near)
    parts = ((masked,), (over_c,), (low_y, high_y), (low_yc, high_yc))
    pixels = image_of(scalars, strip, parts, near[1:])

    def branch(slot, state, after):
        return forward_taps(
            slot, pixels, mask_rows, scalars, *slots[slot], state, columns, chans, split, after
        )

    state = branch(0, (), ())
    slots.append((second_pair[0], held(second_pair[1], [state[1]])))
    third = pick_all(mid_two, out_two, slots[2][1:])
    slots.append(pair_of(third))
    shared = exchange(held(shared, third), PLANE)
    shared = shared.reshape(all_ch, all_ch + strip + 4 * rows)
    state = branch(1, state, third)
    state = branch(2, state, ())
    state = branch(3, state, ())
    pre, stats = state
    own_sums = pack_sums(scalars, stats, norm_cols, axes_size(cells), (shared,))
    quad = quad_id.astype(jnp.int32)[None]
    concat, coef_cols, coef_rows = activations(
        quad, exchange(own_sums, cells), own_sums, pre, image_total
    )
    concat = exchange(concat, QUAD).reshape(4 * rows, strip)

    unit, head_sums = project(concat, shared, head_cols, strip_mask, axes_size(everyone))
    head_values, head_delta, head_coefs, head_rows, head_sums = head_norm(
        exchange(head_sums, everyone), unit, shared, strip_mask, coef_rows
    )
    unit_back, concat_back, row_sums, head_moments = unit_backward(
        exchange(head_sums, everyone),
        unit,
        head_delta,
        head_coefs,
        strip_mask,
        coef_rows,
        shared,
    )

    delta, pool_rows, moments = branch_backward(
        exchange(concat_back, QUAD), pre, coef_cols, coef_rows, mask_rows, axes_size(cells), ()
    )
    moments = exchange(moments, cells)

    def weights_of(slots, after):
        return weight_grads(
            slots,
            scalars,
            moments,
            pool_rows,
            coef_cols,
            pre,
            delta,
            mask_rows,
            pixels,
            columns,
            half,
            image_total,
            after,
        )

    def group_sums(slot, after, *lists):
        if halves:
            return [add(slot[0], over_groups(slot[1]), *(parts[0] for parts in lists), after=after)]
        return [add(*parts, after=after) for parts in zip(slot[:2], *lists)]

    def swap_all(parts, axis):
        return [lax.ppermute(part, axis, SWAP) for part in parts]

    def add_all(*lists, after=()):
        return [add(*parts, after=after) for parts in zip(*lists)]

    flat_w = [part for slot in slots for part in slot]

    def features_of(flip, after):
        return input_grads(flip, taps, flat_w, scalars, strip, after)

    ((keep_c, send_c, taps_c),) = weights_of((3,), ())
    head_parts = head_weight_grads(concat, unit_back, row_sums, head_values, (taps_c,))
    head_parts = exchange(head_parts.reshape(16, chans, all_ch + strip + 4 * rows), PLANE)
    slot_b, slot_a, slot_o = weights_of((2, 1, 0), (taps_c,))
    taps = [slot_o[2], slot_a[2], slot_b[2], taps_c]
    third = group_sums((keep_c, send_c), (slot_o[2], head_parts))
    far_cross, far = features_of(2, third)
    mid_two = add_all(third, along(third, INWARD), after=(far,))
    second = group_sums(slot_b, mid_two)
    far = strip_sum(scalars, (far,), swap_all(far_cross, "c"), columns, False, second)
    near = group_sums(slot_a, (far,), along(mid_two, MID))
    mid_one = add_all(second, along(second, INWARD), after=near)

    head_output = head_parts[:, :, all_ch : all_ch + strip]
    head_output = jnp.transpose(head_output, (1, 0, 2)).reshape(1, chans, 16 * strip)
    head_parts = jnp.sum(head_parts.astype(f32), axis=0)
    pool_part = head_parts[:, :all_ch].reshape(chans, 4, 4, 1, chans)
    pixel_part = head_parts[:, all_ch + strip :].reshape(chans, 4, rows)[:, :, : 16 * chans]
    pixel_part = pixel_part.reshape(chans, 4, 4, 4, chans)
    head_grads = jnp.concatenate([pixel_part, pool_part], axis=3)
    head_grads = jnp.transpose(head_grads, (0, 3, 2, 1, 4)).reshape(chans, 5 * all_ch)
    near_cross, own_part = features_of(0, (*mid_one, head_grads))
    if halves:
        head_grads = head_grads + lax.ppermute(head_grads, "dp", SWAP)
    else:
        head_grads = lax.psum(head_grads, "dp")
    mine = group_sums(slot_o, (own_part, head_grads), along(near, PAIR), along(mid_one, MID))
    state = (branch_weight, branch_first, branch_second)
    if halves:
        other = over_groups(mine[0])
    else:
        mine = [lax.psum(part, "dp") for part in mine]
    input_grad = strip_sum(
        scalars,
        (own_part, lax.ppermute(far, "y", SWAP)),
        swap_all(near_cross, "c"),
        columns,
        True,
        mine,
    ).reshape(1, strip_rows, columns, depth)
    start = jnp.stack([sel * split, zero])
    done = adam_taps(start, split + 1, 3, mine[0], *state, (), (input_grad,))
    start = jnp.stack([(1 - sel) * (split + 1), 1 - sel])
    done = adam_taps(start, split, 2, other if halves else mine[1], *state, done, ())
    branch_grads, branch_means, branch_squares, branch_updated = done

    def own_lanes(by_row):
        return lax.dynamic_slice_in_dim(by_row, z_id * chans, chans, 1)

    def own_head(by_row):
        return lax.dynamic_slice_in_dim(by_row, wide_id * chans, chans, 1)

    own_moments = own_lanes(jnp.sum(moments, axis=0))
    head_own = own_head(head_moments)
    norm_grads = jnp.stack(
        [
            jnp.concatenate([own_moments[8:13], head_own[1:2]]),
            jnp.concatenate([own_moments[0:5], head_own[0:1]]),
        ]
    )
    own_coefs, head_stats = own_lanes(coef_rows), own_head(head_rows)
    pixel_total = coef_rows[COUNT, 0]
    all_centres = jnp.concatenate([own_coefs[CENTRE : CENTRE + 5], head_stats[0:1]])
    all_variances = jnp.concatenate([own_coefs[VARIANCE : VARIANCE + 5], head_stats[4:5]])
    factors = jnp.where(
        jnp.arange(6) == 4, image_total / (image_total - 1.0), pixel_total / (pixel_total - 1.0)
    )
    running_next = (1.0 - momentum) * running_stats + momentum * jnp.stack(
        [all_centres, all_variances * factors[:, None]]
    )
    head_means, head_squares, head_updated = adamw_update(
        head_weight, head_grads, head_first, head_second, conv_rate, weight_decay
    )
    norm_means, norm_squares, norm_updated = adamw_update(
        norm_params, norm_grads, norm_first, norm_second, norm_rate, 0.0
    )
    return (
        head_output,
        input_grad,
        branch_grads,
        branch_means,
        branch_squares,
        branch_updated,
        head_grads,
        head_means,
        head_squares,
        head_updated,
        norm_grads,
        norm_means,
        norm_squares,
        norm_updated,
        running_next,
    )


def solution(mesh):
    groups, wide = mesh.devices.shape
    fine = Mesh(mesh.devices.reshape(groups, 4, 2, wide // 8), ("dp",) + PLANE)
    placed = (
        P("dp", PLANE, None, None),
        P("dp", None),
        P("dp", PLANE, None),
        P(None, PLANE, None),
        P(None, PLANE, None),
        P(None, PLANE, None),
        P(PLANE, None),
        P(PLANE, None),
        P(PLANE, None),
        P(None, None, PLANE),
        P(None, None, PLANE),
        P(None, None, PLANE),
        P(None, None, PLANE),
    )
    return jax.shard_map(
        local,
        mesh=fine,
        in_specs=placed,
        out_specs=(
            P("dp", PLANE, None),
            P("dp", PLANE, None, None),
            P(None, PLANE, None),
            P(None, PLANE, None),
            P(None, PLANE, None),
            P(None, PLANE, None),
            P(PLANE, None),
            P(PLANE, None),
            P(PLANE, None),
            P(PLANE, None),
            P(None, None, PLANE),
            P(None, None, PLANE),
            P(None, None, PLANE),
            P(None, None, PLANE),
            P(None, None, PLANE),
        ),
        check_vma=False,
    )
```

```python
import functools

import jax
import jax.numpy as jnp
from jax import lax
from jax.experimental import pallas as pl
from jax.experimental.pallas import tpu as pltpu
from jax.sharding import Mesh, PartitionSpec as P

STEP = 10


dilations = (6, 12, 18)
epsilon = 1e-05
momentum = 0.1
first_decay = 0.9
second_decay = 0.999
conv_rate = 0.02
norm_rate = 0.4
weight_decay = 0.0001
adam_floor = 1e-08

LANES = 128
PLANE = ("z", "y", "c")
QUAD = ("y", "c")
SWAP = [(0, 1), (1, 0)]
PAIR = [(0, 1), (1, 0), (2, 3), (3, 2)]
MID = [(1, 2), (2, 1)]
OUTWARD = [(1, 0), (2, 3)]
INWARD = [(0, 1), (3, 2)]

bf16 = jnp.bfloat16
f32 = jnp.float32
barrier = lax.optimization_barrier


def adamw_update(parameter, gradient, moment_one, moment_two, step_rate, decay_rate):
    first_new = first_decay * moment_one + (1.0 - first_decay) * gradient
    second_new = second_decay * moment_two + (1.0 - second_decay) * gradient * gradient
    first_hat = first_new / (1.0 - first_decay**STEP)
    second_hat = second_new / (1.0 - second_decay**STEP)
    updated = parameter - step_rate * (
        first_hat / (jnp.sqrt(second_hat) + adam_floor) + decay_rate * parameter
    )
    return (first_new, second_new, updated)


def gelu_both(value):
    scale = (2.0 / jnp.pi) ** 0.5
    square = value * value
    bend = jnp.tanh(scale * (value + 0.044715 * (value * square)))
    lead = 0.5 * (1.0 + bend)
    slope = lead + 0.5 * value * (1.0 - bend * bend) * (scale * (1.0 + 3.0 * 0.044715 * square))
    return value * lead, slope


def tall(rows):
    fill = LANES - rows.shape[0]
    return jnp.concatenate([rows, jnp.zeros((fill, rows.shape[1]), rows.dtype)], axis=0).T


def put_lanes(shape, columns):
    lane = lax.broadcasted_iota(jnp.int32, shape, 1)
    total = jnp.zeros(shape, f32)
    for at, column in columns.items():
        total = jnp.where(lane == at, column, total)
    return total


def put_rows(shape, rows):
    row = lax.broadcasted_iota(jnp.int32, shape, 0)
    total = jnp.zeros(shape, f32)
    for at, value in rows.items():
        total = jnp.where(row == at, value, total)
    return total


def axes_size(axes):
    count = 1
    for axis in axes:
        count *= lax.axis_size(axis)
    return count


def call(
    kernel,
    name,
    grid,
    scalars,
    in_specs,
    out_specs,
    out_shape,
    scratch=(),
    aliases=None,
    flops=0,
    after=(),
    vmem=24,
):
    after = tuple(after)
    first = scalars + len(in_specs)

    def body(*refs):
        kernel(*refs[:first], *refs[first + len(after) :])

    run = pl.pallas_call(
        body,
        out_shape=out_shape,
        grid_spec=pltpu.PrefetchScalarGridSpec(
            num_scalar_prefetch=scalars,
            grid=grid,
            in_specs=list(in_specs) + [pl.BlockSpec(memory_space=pl.ANY)] * len(after),
            out_specs=out_specs,
            scratch_shapes=list(scratch),
        ),
        input_output_aliases=aliases or {},
        compiler_params=pltpu.CompilerParams(vmem_limit_bytes=vmem << 20),
        cost_estimate=pl.CostEstimate(flops=1, bytes_accessed=1, transcendentals=0),
        name=name,
    )
    return lambda *arrays: run(*arrays, *after)


def full(shape):
    return pl.BlockSpec(shape, lambda *_: (0,) * len(shape))


def add_kernel(*refs):
    total = refs[0][...].astype(f32)
    for ref in refs[1:-1]:
        total = total + ref[...].astype(f32)
    refs[-1][...] = total.astype(bf16)


def add(*values, after=()):
    first = held(values[0], after) if after else values[0]
    total = first.astype(f32)
    for value in values[1:]:
        total = total + value.astype(f32)
    return barrier(total.astype(bf16))


def pick_kernel(flag_ref, one_ref, two_ref, out_ref):
    @pl.when(flag_ref[0] == 1)
    def _():
        out_ref[...] = one_ref[...]

    @pl.when(flag_ref[0] != 1)
    def _():
        out_ref[...] = two_ref[...]


def pick(flag, one, two, after=()):
    rows, depth = one.shape
    spec = pl.BlockSpec((rows // 3, depth), lambda i, s: (i, 0))
    return call(
        pick_kernel,
        "pick",
        (3,),
        1,
        [spec, spec],
        spec,
        jax.ShapeDtypeStruct(one.shape, one.dtype),
        after=after,
    )(flag, one, two)


def held_kernel(in_ref, out_ref):
    del in_ref, out_ref


def held(value, after):
    anywhere = pl.BlockSpec(memory_space=pl.ANY)
    return call(
        held_kernel,
        "held",
        (1,),
        0,
        [anywhere],
        anywhere,
        jax.ShapeDtypeStruct(value.shape, value.dtype),
        aliases={0: 0},
        after=after,
        vmem=56,
    )(value)


def cast_kernel(sel_ref, in_ref, out_ref):
    taps, chans = in_ref.shape[:2]
    first = jnp.logical_and(sel_ref[0] == 1, pl.program_id(0) == 0)
    for tap in range(taps):
        value = in_ref[tap]
        if tap == 0:
            value = jnp.where(first, 0.0, value)
        out_ref[tap * chans : (tap + 1) * chans, :] = value.astype(bf16)


def cast_half(sel, weight, split, after):
    chans, depth = weight.shape[1:]
    parts = 3 if (split + 1) % 3 == 0 else 1
    block = (split + 1) // parts
    return call(
        cast_kernel,
        "cast",
        (parts,),
        1,
        [pl.BlockSpec((pl.Element(block), pl.Element(chans), pl.Element(depth)), lambda i, s: (s[0] * split + i * block, 0, 0))],
        pl.BlockSpec((block * chans, depth), lambda i, s: (i, 0)),
        jax.ShapeDtypeStruct(((split + 1) * chans, depth), bf16),
        after=after,
        vmem=56,
    )(sel, weight)


def mask_kernel(columns, scalar_ref, in_ref, out_ref, *part_refs):
    rows, depth = in_ref.shape
    pixel = lax.broadcasted_iota(jnp.int32, (rows, LANES), 0)
    row = pixel // columns + scalar_ref[HALF + 1] * (rows // columns)
    height = scalar_ref[HEIGHT]
    inside = jnp.logical_and(row < height, pixel % columns < 2 * height)
    for first in range(0, depth, LANES):
        lanes = slice(first, first + LANES)
        value = jnp.where(inside, in_ref[:, lanes].astype(f32), 0.0).astype(bf16)
        out_ref[:, lanes] = value
        start = 0
        for part_ref in part_refs:
            size = part_ref.shape[0]
            part_ref[:, lanes] = value[start : start + size]
            start += size


def mask_strip(scalars, strip, columns, after):
    rows, depth = strip.shape
    low = rows // 16 * 7
    shapes = ((rows, depth), (low, depth), (rows - low, depth))
    return call(
        functools.partial(mask_kernel, columns),
        "mask",
        (1,),
        1,
        [full((rows, depth))],
        tuple(full(shape) for shape in shapes),
        tuple(jax.ShapeDtypeStruct(shape, bf16) for shape in shapes),
        after=after,
        vmem=56,
    )(scalars, strip)


def image_kernel(strip, places, spot_ref, *refs):
    *parts, out_ref, sems = refs
    copies = []
    for at, (which, first) in enumerate(places):
        rows = pl.ds(pl.multiple_of(spot_ref[HALF + 1 + which] * strip + first, 16), parts[at].shape[0])
        copies.append(pltpu.make_async_copy(parts[at], out_ref.at[rows, :], sems.at[at]))
    for copy in copies:
        copy.start()
    for copy in copies:
        copy.wait()


def image_of(spots, strip, parts, after):
    depth = parts[0][0].shape[1]
    places = []
    for which, strip_parts in enumerate(parts):
        first = 0
        for part in strip_parts:
            places.append((which, first))
            first += part.shape[0]
    flat = [part for strip_parts in parts for part in strip_parts]
    anywhere = pl.BlockSpec(memory_space=pl.ANY)
    return call(
        functools.partial(image_kernel, strip, places),
        "image",
        (1,),
        1,
        [anywhere] * len(flat),
        full((4 * strip, depth)),
        jax.ShapeDtypeStruct((4 * strip, depth), bf16),
        [pltpu.SemaphoreType.DMA((len(flat),))],
        after=after,
        vmem=56,
    )(spots, *flat)


def head_grad_kernel(x_ref, back_ref, sum_ref, value_ref, out_ref):
    channels = back_ref.shape[0]
    rows = x_ref.shape[0] // 4
    act = jnp.zeros((EXTRA, channels), f32)
    for quad in range(4):
        first = quad * rows + rows - EXTRA
        act = act + x_ref[first : first + EXTRA, :channels].astype(f32)
    out_ref[:, :channels] = (sum_ref[:, 0:1] * act[0:1, :]).astype(bf16)
    strip = x_ref.shape[1]
    out_ref[:, channels : channels + strip] = value_ref[...]
    out_ref[:, channels + strip :] = lax.dot_general(
        back_ref[...], x_ref[...], (((1,), (1,)), ((), ())), preferred_element_type=f32
    ).astype(bf16)


def head_weight_grads(concat, unit_back, row_sums, values, after):
    channels = unit_back.shape[0]
    arrays = (concat, unit_back, row_sums, values)
    shape = (channels, channels + concat.shape[1] + concat.shape[0])
    return call(
        head_grad_kernel,
        "head_weight_grad",
        (1,),
        0,
        [full(array.shape) for array in arrays],
        full(shape),
        jax.ShapeDtypeStruct(shape, bf16),
        after=after,
        vmem=24,
    )(*arrays)


def strip_sum_kernel(columns, whole, masked, scalar_ref, *refs):
    block = refs[0].shape[0]
    step = pl.program_id(0)
    rows_all = refs[whole].shape[0] * (len(refs) - 1 - whole)
    pixel = step * block + lax.broadcasted_iota(jnp.int32, (block, LANES), 0)
    row = pixel // columns + scalar_ref[HALF + 1] * (rows_all // columns)
    height = scalar_ref[HEIGHT]
    inside = jnp.logical_and(row < height, pixel % columns < 2 * height)
    steps = refs[whole].shape[0] * (len(refs) - 1 - whole) // block
    count = steps // (len(refs) - 1 - whole)
    for at in range(steps):

        @pl.when(step == at)
        def _():
            part = refs[whole + at // count]
            rows = slice(at % count * block, (at % count + 1) * block)
            for first in range(0, refs[0].shape[1], LANES):
                lanes = slice(first, first + LANES)
                total = part[rows, lanes].astype(f32)
                for ref in refs[:whole]:
                    total = total + ref[:, lanes].astype(f32)
                if masked:
                    total = jnp.where(inside, total, 0.0)
                refs[-1][:, lanes] = total.astype(bf16)


def strip_sum(scalars, strips, parts, columns, masked, after):
    rows, depth = strips[0].shape
    spec = pl.BlockSpec((rows // 2, depth), lambda i, s: (i, 0))
    return call(
        functools.partial(strip_sum_kernel, columns, len(strips), masked),
        "strip_sum",
        (2,),
        1,
        [spec] * len(strips) + [full(part.shape) for part in parts],
        spec,
        jax.ShapeDtypeStruct((rows, depth), bf16),
        after=after,
        vmem=56,
    )(scalars, *strips, *parts)


def adam_kernel(start_ref, grad_ref, weight_ref, first_ref, second_ref, *rest):
    out_ref, mean_ref, square_ref, new_ref = rest[-4:]
    grad = grad_ref[...].astype(f32).reshape(out_ref.shape)
    mean, square, new = adamw_update(
        weight_ref[...], grad, first_ref[...], second_ref[...], conv_rate, weight_decay
    )
    out_ref[...] = grad
    mean_ref[...] = mean
    square_ref[...] = square
    new_ref[...] = new


def adam_taps(start, count, block, grads, weight, first, second, earlier, after):
    taps, chans, depth = weight.shape

    def piece(size, index):
        return pl.BlockSpec(tuple(pl.Element(n) for n in size), index)

    spec = piece((block, chans, depth), lambda i, s: (s[0] + i * block, 0, 0))
    anywhere = [pl.BlockSpec(memory_space=pl.ANY)] * len(earlier)
    return call(
        adam_kernel,
        "adamw",
        (count // block,),
        1,
        [piece((block * chans, depth), lambda i, s: ((s[1] + i * block) * chans, 0))]
        + [spec] * 3
        + anywhere,
        (spec,) * 4,
        (jax.ShapeDtypeStruct(weight.shape, f32),) * 4,
        aliases={5 + at: at for at in range(4)} if earlier else None,
        after=after,
        vmem=20,
    )(start, grads, weight, first, second, *earlier)


FIRST, SECOND, GAIN, SHIFT, AREA = 0, 8, 16, 24, 32
SUM_ROWS = 40
CENTRE, INVERSE, VARIANCE, COUNT, POOLED = 0, 8, 32, 40, 41
COEF_ROWS = 48
EXTRA = 16
HEIGHT, HALF = 8, 9


def lane_masks(columns):
    lane = lax.broadcasted_iota(jnp.int32, (1, LANES), 1) % columns
    masks = {}
    for dilation in dilations:
        for off in (-dilation, dilation):
            moved = lane + off
            masks[off] = jnp.logical_and(moved >= 0, moved < columns)
    return masks


def forward_kernel(columns, split, slot, scalar_ref, x_ref, wz_ref, wx_ref, mask_ref, *rest):
    pre_ref, stat_ref, taps = rest[-3:]
    step = pl.program_id(0)
    half = wz_ref.shape[0]
    block = x_ref.shape[0]
    sel = scalar_ref[slot]
    contract = (((1,), (1,)), ((), ()))
    pixels = x_ref[...]
    cols = pl.ds(pl.multiple_of(step * block, block), block)
    taps[pl.ds(pl.multiple_of(sel * half, 16), half), cols] = lax.dot_general(
        wz_ref[...], pixels, contract, preferred_element_type=f32
    )
    taps[pl.ds(pl.multiple_of((1 - sel) * half, 16), half), cols] = lax.dot_general(
        wx_ref[...], pixels, contract, preferred_element_type=f32
    )

    @pl.when(step == pl.num_programs(0) - 1)
    def _():
        total = taps.shape[1]
        tiles = total // LANES
        chans = pre_ref.shape[2]
        masks = lane_masks(columns)

        def rows_of(tap):
            first = tap * chans if tap <= split else (tap + 1) * chans
            return slice(first, first + chans)

        def tile(tap, at):
            return taps[rows_of(tap), at * LANES : (at + 1) * LANES]

        sums = [jnp.zeros((chans, LANES), f32) for _ in range(4)]
        squares = [jnp.zeros((chans, LANES), f32) for _ in range(4)]
        pooled = jnp.zeros((chans, LANES), f32)
        for at in range(tiles):
            lanes = slice(at * LANES, (at + 1) * LANES)
            weight = mask_ref[0:1, lanes]
            for branch in range(4):
                if branch == 0:
                    value = tile(0, at)
                else:
                    dilation = dilations[branch - 1]
                    jump = dilation * columns // LANES
                    value = None
                    for b in range(3):
                        part = None
                        for a in range(3):
                            source = at + (a - 1) * jump
                            if 0 <= source < tiles:
                                term = tile(1 + 9 * (branch - 1) + 3 * a + b, source)
                                part = term if part is None else part + term
                        off = (b - 1) * dilation
                        if off != 0:
                            part = pltpu.roll(part, (-off) % LANES, 1)
                            part = jnp.where(masks[off], part, 0.0)
                        value = part if value is None else value + part
                pre_ref[0, branch, :, lanes] = value
                weighted = value * weight
                sums[branch] = sums[branch] + weighted
                squares[branch] = squares[branch] + weighted * value
            pooled = pooled + tile(28, at)
        height = jnp.full((1, 1), scalar_ref[HEIGHT], jnp.int32).astype(f32)
        area = 2.0 * height * height
        pool = jnp.sum(pooled, axis=1, keepdims=True) / area
        columns_of = {FIRST + 4: pool, SECOND + 4: pool * pool, AREA: area}
        for branch in range(4):
            columns_of[FIRST + branch] = jnp.sum(sums[branch], axis=1, keepdims=True)
            columns_of[SECOND + branch] = jnp.sum(squares[branch], axis=1, keepdims=True)
        stat_ref[0] = put_lanes((chans, LANES), columns_of)


def forward_taps(slot, pixels, mask_rows, scalars, wz, wx, earlier, columns, chans, split, after):
    total, depth = pixels.shape
    block = total // 4
    half = wz.shape[0]
    keep = [pl.BlockSpec(memory_space=pl.ANY)] * len(earlier)
    return call(
        functools.partial(forward_kernel, columns, split, slot),
        "atrous_forward",
        (4,),
        1,
        [
            pl.BlockSpec((block, depth), lambda i, s: (i, 0)),
            full((half, depth)),
            full((half, depth)),
            full((8, total)),
        ]
        + keep,
        (
            pl.BlockSpec((1, 4, chans, total), lambda i, s: (s[4 + slot], 0, 0, 0)),
            pl.BlockSpec((1, chans, LANES), lambda i, s: (s[4 + slot], 0, 0)),
        ),
        (
            jax.ShapeDtypeStruct((4, 4, chans, total), f32),
            jax.ShapeDtypeStruct((4, chans, LANES), f32),
        ),
        [pltpu.VMEM((2 * half, total), f32)],
        {5: 0, 6: 1} if earlier else None,
        4 * half * total * depth,
        after,
        56,
    )(scalars, pixels, wz, wx, mask_rows, *earlier)


def pack_kernel(place_ref, stat_ref, norm_ref, out_ref, work):
    chans = norm_ref.shape[0]
    work[...] = jnp.zeros_like(work)
    for z in range(4):
        work[z * chans : (z + 1) * chans, :] = stat_ref[z]
    own = pl.ds(pl.multiple_of(place_ref[4] * chans, chans), chans)
    work[own, :] = work[own, :] + norm_ref[...]
    rows = work[...].T[:SUM_ROWS]
    for at in range(out_ref.shape[0]):
        out_ref[at] = rows


def pack_sums(place, stats, norm_cols, count, after):
    return call(
        pack_kernel,
        "branch_sums",
        (1,),
        1,
        [full(stats.shape), full(norm_cols.shape)],
        full((count, SUM_ROWS, LANES)),
        jax.ShapeDtypeStruct((count, SUM_ROWS, LANES), f32),
        [pltpu.VMEM((LANES, LANES), f32)],
        after=after,
        vmem=24,
    )(place, stats, norm_cols)


def pool_rows_of(rows_ref, own_width):
    def row(at):
        return rows_ref[at : at + 1, :]

    moved = row(POOLED) - row(CENTRE + 4)
    normed = row(GAIN + 4) * moved * row(INVERSE + 4) + row(SHIFT + 4)
    lane = lax.broadcasted_iota(jnp.int32, normed.shape, 1)
    return normed, moved * row(INVERSE + 4), lane < own_width


def act_kernel(image_total, quad_ref, parts_ref, own_ref, pre_ref, out_ref, col_ref, row_ref):
    chans = pre_ref.shape[2]

    @pl.when(pl.program_id(0) == 0)
    def _():
        sums = jnp.sum(parts_ref[...], axis=0)
        pixel_total = jnp.maximum(sums[AREA : AREA + 1], 1.0)
        index = lax.broadcasted_iota(jnp.int32, (8, LANES), 0)
        count = jnp.where(index == 4, image_total, pixel_total)
        centre = sums[FIRST : FIRST + 8] / count
        variance = sums[SECOND : SECOND + 8] / count - centre * centre
        inverse = lax.rsqrt(variance + epsilon)
        other = jnp.where(index == 0, pixel_total, jnp.where(index == 1, own_ref[0, 4:5, :], 0.0))
        rows = jnp.concatenate(
            [centre, inverse, sums[GAIN : GAIN + 8], sums[SHIFT : SHIFT + 8], variance, other],
            axis=0,
        )
        row_ref[...] = rows
        col_ref[...] = tall(rows)

    for z in range(4):
        span = slice(z * chans, (z + 1) * chans)
        for branch in range(4):
            moved = pre_ref[z, branch] - col_ref[span, CENTRE + branch : CENTRE + branch + 1]
            normed = (
                col_ref[span, GAIN + branch : GAIN + branch + 1]
                * moved
                * col_ref[span, INVERSE + branch : INVERSE + branch + 1]
                + col_ref[span, SHIFT + branch : SHIFT + branch + 1]
            )
            first = (4 * z + branch) * chans
            out_ref[0, first : first + chans, :] = gelu_both(normed)[0].astype(bf16)
    normed, _, valid = pool_rows_of(row_ref, 4 * chans)
    act = jnp.where(valid, gelu_both(normed)[0], 0.0)
    act = put_rows((EXTRA, LANES), {0: act + pltpu.roll(act, 4 * chans, 1)})
    lane = lax.broadcasted_iota(jnp.int32, act.shape, 1)
    for at in range(out_ref.shape[2] // LANES):
        owner = (lane + at * LANES) // (4 * chans)
        out_ref[0, 16 * chans :, at * LANES : (at + 1) * LANES] = jnp.where(
            owner == quad_ref[0], act, 0.0
        ).astype(bf16)


def activations(quad, parts, own, pre, image_total):
    chans, total = pre.shape[2:]
    strip = total // 4
    rows = 16 * chans + EXTRA
    return call(
        functools.partial(act_kernel, image_total),
        "branch_act",
        (4,),
        1,
        [
            full(parts.shape),
            full((1, SUM_ROWS, LANES)),
            pl.BlockSpec((4, 4, chans, strip), lambda i, s: (0, 0, 0, i)),
        ],
        (
            pl.BlockSpec((1, rows, strip), lambda i, s: (i, 0, 0)),
            full((LANES, LANES)),
            full((COEF_ROWS, LANES)),
        ),
        (
            jax.ShapeDtypeStruct((4, rows, strip), bf16),
            jax.ShapeDtypeStruct((LANES, LANES), f32),
            jax.ShapeDtypeStruct((COEF_ROWS, LANES), f32),
        ),
        vmem=24,
    )(quad, parts, own, pre)


def unit_kernel(x_ref, shared_ref, head_ref, mask_ref, unit_ref, out_ref):
    channels = shared_ref.shape[0]
    rows, strip = x_ref.shape[0] // 4, x_ref.shape[1]
    proj = shared_ref[:, channels + strip :]
    unit = jnp.dot(proj, x_ref[...], preferred_element_type=f32)
    act = jnp.zeros((EXTRA, channels), f32)
    for quad in range(4):
        first = quad * rows + rows - EXTRA
        act = act + x_ref[first : first + EXTRA, :channels].astype(f32)
    bias = shared_ref[:, :channels].astype(f32) * act[0:1, :]
    unit = unit + jnp.sum(bias, axis=1, keepdims=True)
    unit_ref[...] = unit
    weighted = unit * mask_ref[0:1, :]
    lane = lax.broadcasted_iota(jnp.int32, head_ref.shape, 1)
    one = jnp.sum(weighted, axis=1, keepdims=True)
    two = jnp.sum(weighted * unit, axis=1, keepdims=True)
    sums = jnp.where(lane == 0, one, jnp.where(lane == 1, two, head_ref[...])).T[:8]
    for at in range(out_ref.shape[0]):
        out_ref[at] = sums


def project(concat, shared, head_cols, strip_mask, count):
    channels, strip = shared.shape[0], concat.shape[1]
    arrays = (concat, shared, head_cols, strip_mask)
    return call(
        unit_kernel,
        "projection",
        (1,),
        0,
        [full(array.shape) for array in arrays],
        (full((channels, strip)), full((count, 8, channels))),
        (
            jax.ShapeDtypeStruct((channels, strip), f32),
            jax.ShapeDtypeStruct((count, 8, channels), f32),
        ),
        vmem=24,
    )(*arrays)


def head_kernel(parts_ref, unit_ref, shared_ref, mask_ref, row_ref, value_ref, delta_ref, col_ref, head_ref, out_ref):
    sums = jnp.sum(parts_ref[...], axis=0)
    pixel_total = row_ref[COUNT : COUNT + 1, 0:1]
    centre = sums[0:1] / pixel_total
    variance = sums[1:2] / pixel_total - centre * centre
    inverse = lax.rsqrt(variance + epsilon)
    rows = put_rows(
        sums.shape, {0: centre, 1: inverse, 2: sums[2:3], 3: sums[3:4], 4: variance}
    )
    head_ref[...] = rows
    columns = tall(rows)
    col_ref[...] = columns
    hat = (unit_ref[...] - columns[:, 0:1]) * columns[:, 1:2]
    normed = columns[:, 2:3] * hat + columns[:, 3:4]
    value, slope = gelu_both(normed)
    weight = mask_ref[0:1, :]
    value_ref[...] = (weight * value).astype(bf16)
    first = unit_ref.shape[0]
    cot = shared_ref[:, first : first + unit_ref.shape[1]].astype(f32)
    delta = slope * (weight * cot)
    delta_ref[...] = delta
    sums = put_lanes(
        columns.shape,
        {
            0: jnp.sum(delta, axis=1, keepdims=True),
            1: jnp.sum(delta * hat, axis=1, keepdims=True),
        },
    ).T[:8]
    for at in range(out_ref.shape[0]):
        out_ref[at] = sums


def head_norm(parts, unit, shared, strip_mask, coef_rows):
    channels, strip = unit.shape
    count = parts.shape[0]
    return call(
        head_kernel,
        "head_norm",
        (1,),
        0,
        [full(parts.shape), full(unit.shape), full(shared.shape), full((8, strip)), full(coef_rows.shape)],
        (
            full((channels, strip)),
            full((channels, strip)),
            full((channels, LANES)),
            full((8, channels)),
            full((count, 8, channels)),
        ),
        (
            jax.ShapeDtypeStruct((channels, strip), bf16),
            jax.ShapeDtypeStruct((channels, strip), f32),
            jax.ShapeDtypeStruct((channels, LANES), f32),
            jax.ShapeDtypeStruct((8, channels), f32),
            jax.ShapeDtypeStruct((count, 8, channels), f32),
        ),
        vmem=24,
    )(parts, unit, shared, strip_mask, coef_rows)


def unit_back_kernel(
    parts_ref, unit_ref, delta_ref, col_ref, mask_ref, row_ref, shared_ref, back_ref, out_ref, sum_ref, moment_ref
):
    sums = jnp.sum(parts_ref[...], axis=0)
    moment_ref[...] = sums
    moments = tall(sums)
    pixel_total = row_ref[COUNT : COUNT + 1, 0:1]
    inverse = col_ref[:, 1:2]
    hat = (unit_ref[...] - col_ref[:, 0:1]) * inverse
    back = mask_ref[0:1, :] * (
        (col_ref[:, 2:3] * inverse)
        * (delta_ref[...] - (moments[:, 0:1] + hat * moments[:, 1:2]) / pixel_total)
    )
    back = back.astype(bf16)
    back_ref[...] = back
    row_sums = jnp.sum(back.astype(f32), axis=1, keepdims=True)
    sum_ref[...] = jnp.broadcast_to(row_sums, sum_ref.shape)
    channels = shared_ref.shape[0]
    rows, width = out_ref.shape[1:]
    proj = shared_ref[:, channels + width :]
    terms = lax.dot_general(
        proj, back, (((0,), (0,)), ((), ())), preferred_element_type=f32
    )
    pool = jnp.sum(shared_ref[:, :channels].astype(f32) * row_sums, axis=0, keepdims=True)
    own = channels // 4
    for quad in range(4):
        first = quad * own // LANES * LANES
        part = pool[:, first : first + LANES]
        if quad * own != first:
            part = pltpu.roll(part, LANES - (quad * own - first), 1)
        lane = lax.broadcasted_iota(jnp.int32, part.shape, 1)
        part = jnp.where(lane < own, part, 0.0)
        high = part.astype(bf16).astype(f32)
        extra = put_rows((EXTRA, LANES), {0: high, 1: part - high})
        out_ref[quad, : rows - EXTRA, :] = terms[quad * rows : (quad + 1) * rows - EXTRA].astype(bf16)
        out_ref[quad, rows - EXTRA :, :LANES] = extra.astype(bf16)
        out_ref[quad, rows - EXTRA :, LANES:] = jnp.zeros((EXTRA, width - LANES), bf16)


def unit_backward(parts, unit, delta, cols, strip_mask, coef_rows, shared):
    channels, strip = unit.shape
    rows = (shared.shape[1] - channels - strip) // 4
    arrays = (parts, unit, delta, cols, strip_mask, coef_rows, shared)
    return call(
        unit_back_kernel,
        "unit_back",
        (1,),
        0,
        [full(array.shape) for array in arrays],
        (
            full((channels, strip)),
            full((4, rows, strip)),
            full((channels, LANES)),
            full((8, channels)),
        ),
        (
            jax.ShapeDtypeStruct((channels, strip), bf16),
            jax.ShapeDtypeStruct((4, rows, strip), bf16),
            jax.ShapeDtypeStruct((channels, LANES), f32),
            jax.ShapeDtypeStruct((8, channels), f32),
        ),
        vmem=24,
    )(*arrays)


def branch_kernel(x_ref, pre_ref, col_ref, row_ref, mask_ref, delta_ref, pool_ref, out_ref, sums, pooled):
    step = pl.program_id(0)
    chans = pre_ref.shape[2]

    @pl.when(step == 0)
    def _():
        sums[...] = jnp.zeros_like(sums)
        pooled[...] = jnp.zeros_like(pooled)

    def fold(value):
        total = value[:, :LANES]
        for at in range(1, value.shape[1] // LANES):
            total = total + value[:, at * LANES : (at + 1) * LANES]
        return total

    weight = mask_ref[0:1, :]
    for z in range(4):
        span = slice(z * chans, (z + 1) * chans)
        for branch in range(4):
            first = (4 * z + branch) * chans
            hat = (
                pre_ref[z, branch] - col_ref[span, CENTRE + branch : CENTRE + branch + 1]
            ) * col_ref[span, INVERSE + branch : INVERSE + branch + 1]
            normed = (
                col_ref[span, GAIN + branch : GAIN + branch + 1] * hat
                + col_ref[span, SHIFT + branch : SHIFT + branch + 1]
            )
            delta = gelu_both(normed)[1] * (
                weight * x_ref[0, first : first + chans, :].astype(f32)
            )
            delta_ref[z, branch] = delta
            sums[8 * z + branch] = sums[8 * z + branch] + fold(delta)
            sums[8 * z + 4 + branch] = sums[8 * z + 4 + branch] + fold(delta * hat)
    extra = x_ref[0, 16 * chans :, :LANES].astype(f32)
    pooled[...] = pooled[...] + jnp.broadcast_to(extra[0:1] + extra[1:2], pooled.shape)

    @pl.when(step == pl.num_programs(0) - 1)
    def _():
        normed, hat, valid = pool_rows_of(row_ref, 4 * chans)
        delta = jnp.where(valid, gelu_both(normed)[1] * pooled[0:1, :], 0.0)
        hat = jnp.where(valid, hat, 0.0)
        pool_ref[...] = put_rows(pool_ref.shape, {0: delta, 1: hat})
        found = []
        for z in range(4):
            columns = {}
            for branch in range(4):
                columns[branch] = jnp.sum(sums[8 * z + branch], axis=1, keepdims=True)
                columns[8 + branch] = jnp.sum(sums[8 * z + 4 + branch], axis=1, keepdims=True)
            found.append(put_lanes((chans, LANES), columns))
        found.append(jnp.zeros((LANES - 4 * chans, LANES), f32))
        rows = jnp.concatenate(found, axis=0).T[:16]
        index = lax.broadcasted_iota(jnp.int32, rows.shape, 0)
        rows = jnp.where(index == 4, delta, jnp.where(index == 12, delta * hat, rows))
        for at in range(out_ref.shape[0]):
            out_ref[at] = rows


def branch_backward(concat_back, pre, coef_cols, coef_rows, mask_rows, count, after):
    chans, total = pre.shape[2:]
    rows, strip = concat_back.shape[1:]
    spread = pl.BlockSpec((4, 4, chans, strip), lambda i: (0, 0, 0, i))
    return call(
        branch_kernel,
        "branch_back",
        (4,),
        0,
        [
            pl.BlockSpec((1, rows, strip), lambda i: (i, 0, 0)),
            spread,
            full(coef_cols.shape),
            full(coef_rows.shape),
            pl.BlockSpec((8, strip), lambda i: (0, i)),
        ],
        (spread, full((8, LANES)), full((count, 16, LANES))),
        (
            jax.ShapeDtypeStruct(pre.shape, f32),
            jax.ShapeDtypeStruct((8, LANES), f32),
            jax.ShapeDtypeStruct((count, 16, LANES), f32),
        ),
        [pltpu.VMEM((32, chans, LANES), f32), pltpu.VMEM((8, LANES), f32)],
        after=after,
        vmem=24,
    )(concat_back, pre, coef_cols, coef_rows, mask_rows)


def weight_kernel(columns, image_total, slots, scalar_ref, parts_ref, pool_ref, mask_ref, x_ref, *refs):
    count = len(slots)
    col_refs, pre_refs, delta_refs = refs[:count], refs[count : 2 * count], refs[2 * count : 3 * count]
    outs = refs[3 * count : 6 * count]
    total_ref, moments = refs[6 * count :]
    half = outs[0].shape[0]
    chans = pre_refs[0].shape[2]
    start = 29 * chans - half
    sel = scalar_ref[HALF]

    @pl.when(pl.program_id(0) == 0)
    def _():
        rows = jnp.concatenate([jnp.sum(parts_ref[...], axis=0), pool_ref[...]], axis=0)
        moments[...] = tall(rows)
        height = jnp.full((1, 1), scalar_ref[HEIGHT], jnp.int32).astype(f32)
        area = 2.0 * height * height
        masks = lane_masks(columns)
        for at, slot in enumerate(slots):
            own = moments[pl.ds(pl.multiple_of(scalar_ref[4 + slot] * chans, chans), chans), :]
            build_taps(
                own, col_refs[at][...], pre_refs[at], delta_refs[at], mask_ref, outs[3 * at + 2], masks, area, columns, image_total
            )

    for at in range(count):
        keep_ref, send_ref, taps_ref = outs[3 * at : 3 * at + 3]
        total_ref[...] = jnp.dot(taps_ref[...], x_ref[...], preferred_element_type=f32)
        keep_ref[...] = total_ref[pl.ds(pl.multiple_of(sel * start, 16), half), :].astype(bf16)
        send_ref[...] = total_ref[pl.ds(pl.multiple_of((1 - sel) * start, 16), half), :].astype(bf16)


def build_taps(own, coefs, pre_ref, delta_ref, mask_ref, taps_ref, masks, area, columns, image_total):
    chans = pre_ref.shape[2]

    def coef(at):
        return coefs[:, at : at + 1]

    def moment(at):
        return own[:, at : at + 1]

    pixel_total = coef(COUNT)
    pool_grad = (
        coef(GAIN + 4)
        * coef(INVERSE + 4)
        * (moment(16) - (moment(4) + moment(17) * moment(12)) / image_total)
    ) / area
    tiles = pre_ref.shape[3] // LANES
    for at in range(tiles):
        lanes = slice(at * LANES, (at + 1) * LANES)
        weight = mask_ref[0:1, lanes]
        taps_ref[28 * chans : 29 * chans, lanes] = (weight * pool_grad).astype(bf16)
        for branch in range(4):
            hat = (pre_ref[0, branch, :, lanes] - coef(CENTRE + branch)) * coef(INVERSE + branch)
            grad = weight * (
                (coef(GAIN + branch) * coef(INVERSE + branch))
                * (
                    delta_ref[0, branch, :, lanes]
                    - (moment(branch) + hat * moment(8 + branch)) / pixel_total
                )
            )
            if branch == 0:
                taps_ref[0:chans, lanes] = grad.astype(bf16)
                continue
            j, dilation = branch - 1, dilations[branch - 1]
            jump = dilation * columns // LANES
            for b in range(3):
                off = (b - 1) * dilation
                moved = grad
                if off != 0:
                    moved = pltpu.roll(grad, off % LANES, 1)
                    moved = jnp.where(masks[-off], moved, 0.0)
                moved = moved.astype(bf16)
                for a in range(3):
                    tap = 1 + 9 * j + 3 * a + b
                    span = slice(tap * chans, (tap + 1) * chans)
                    target = at + (a - 1) * jump
                    if 0 <= target < tiles:
                        taps_ref[span, target * LANES : (target + 1) * LANES] = moved
                    source = at - (a - 1) * jump
                    if not 0 <= source < tiles:
                        taps_ref[span, lanes] = jnp.zeros((chans, LANES), bf16)


def weight_grads(
    slots, scalars, parts, pool_rows, coef_cols, pre, delta, mask_rows, pixels, columns, half, image_total, after
):
    chans, total = pre.shape[2:]
    depth = pixels.shape[1]
    block = depth // 4
    count = len(slots)

    def cols(slot):
        return pl.BlockSpec((chans, LANES), lambda i, s: (s[4 + slot], 0))

    def own(slot):
        return pl.BlockSpec((1, 4, chans, total), lambda i, s: (s[4 + slot], 0, 0, 0))

    outs = call(
        functools.partial(weight_kernel, columns, image_total, slots),
        "atrous_weight_grad",
        (4,),
        1,
        [
            full(parts.shape),
            full(pool_rows.shape),
            full(mask_rows.shape),
            pl.BlockSpec((total, block), lambda i, s: (0, i)),
        ]
        + [cols(slot) for slot in slots]
        + [own(slot) for slot in slots] * 2,
        (
            pl.BlockSpec((half, block), lambda i, s: (0, i)),
            pl.BlockSpec((half, block), lambda i, s: (0, i)),
            full((29 * chans, total)),
        )
        * count,
        (
            jax.ShapeDtypeStruct((half, depth), bf16),
            jax.ShapeDtypeStruct((half, depth), bf16),
            jax.ShapeDtypeStruct((29 * chans, total), bf16),
        )
        * count,
        [pltpu.VMEM((29 * chans, block), f32), pltpu.VMEM((LANES, LANES), f32)],
        after=after,
        vmem=28 if slots[0] == 3 else 56,
    )(
        scalars,
        parts,
        pool_rows,
        mask_rows,
        pixels,
        *[coef_cols] * count,
        *[pre] * count,
        *[delta] * count,
    )
    return [outs[3 * at : 3 * at + 3] for at in range(count)]


def input_kernel(start, places, scalar_ref, *refs):
    taps, weights, outs = refs[0:4], refs[4:12], refs[12:15]
    all_weights, all_taps, result, weight_sems, tap_sems, out_sems = refs[15:]
    half, depth = weights[0].shape
    block = all_taps.shape[2]
    cut = depth // 2

    def tap_copies(strip):
        copies = []
        lanes = pl.ds(pl.multiple_of(scalar_ref[places[strip]] * block, LANES), block)
        for slot in range(4):
            sel = scalar_ref[slot]
            for which in range(2):
                first = sel * start if which == 0 else (1 - sel) * start
                at = 2 * slot + which
                copies.append(
                    pltpu.make_async_copy(
                        taps[slot].at[pl.ds(pl.multiple_of(first, 16), half), lanes],
                        all_taps.at[strip, pl.ds(at * half, half), :],
                        tap_sems.at[strip, at],
                    )
                )
        return copies

    def weight_copies(part):
        lanes = pl.ds(part * cut, cut)
        return [
            pltpu.make_async_copy(
                weights[at].at[:, lanes],
                all_weights.at[pl.ds(at * half, half), lanes],
                weight_sems.at[part, at],
            )
            for at in range(8)
        ]

    tap_lists = [tap_copies(0), tap_copies(1)]
    weight_lists = [weight_copies(0), weight_copies(1)]
    for copies in (tap_lists[0], weight_lists[0], weight_lists[1], tap_lists[1]):
        for copy in copies:
            copy.start()
    rows = outs[0].shape[0]
    out_lists = [
        [
            pltpu.make_async_copy(result.at[0, pl.ds(0, rows), :], outs[0], out_sems.at[0]),
            pltpu.make_async_copy(result.at[0, pl.ds(rows, rows), :], outs[1], out_sems.at[1]),
        ],
        [pltpu.make_async_copy(result.at[1], outs[2], out_sems.at[2])],
    ]
    for strip in range(2):
        for copy in tap_lists[strip]:
            copy.wait()
        for part in range(2):
            if strip == 0:
                for copy in weight_lists[part]:
                    copy.wait()
            lanes = slice(part * cut, (part + 1) * cut)
            result[strip, :, lanes] = lax.dot_general(
                all_taps[strip],
                all_weights[:, lanes],
                (((0,), (0,)), ((), ())),
                preferred_element_type=f32,
            ).astype(bf16)
        for copy in out_lists[strip]:
            copy.start()
    for copies in out_lists:
        for copy in copies:
            copy.wait()


def input_grads(flip, taps, weights, scalars, block, after):
    rows = taps[0].shape[0]
    half, depth = weights[0].shape
    shapes = ((block // 2, depth), (block // 2, depth), (block, depth))
    anywhere = pl.BlockSpec(memory_space=pl.ANY)
    low, high, own = call(
        functools.partial(input_kernel, rows - half, (HALF + 2 + flip, HALF + 1 + flip)),
        "atrous_input_grad",
        (1,),
        1,
        [anywhere] * 12,
        (anywhere,) * 3,
        tuple(jax.ShapeDtypeStruct(shape, bf16) for shape in shapes),
        [
            pltpu.VMEM((8 * half, depth), bf16),
            pltpu.VMEM((2, 8 * half, block), bf16),
            pltpu.VMEM((2, block, depth), bf16),
            pltpu.SemaphoreType.DMA((2, 8)),
            pltpu.SemaphoreType.DMA((2, 8)),
            pltpu.SemaphoreType.DMA((3,)),
        ],
        after=after,
        vmem=58,
    )(scalars, *taps, *weights)
    return [low, high], own


def local(
    features,
    scale_sizes,
    cotangent,
    branch_weight,
    branch_first,
    branch_second,
    head_weight,
    head_first,
    head_second,
    norm_params,
    norm_first,
    norm_second,
    running_stats,
):
    groups = lax.axis_size("dp")
    halves = groups == 2
    images = scale_sizes.shape[1]
    image_total = float(groups * images)
    x_id, z_id = lax.axis_index("dp"), lax.axis_index("z")
    quad_id = lax.axis_index("y") * 2 + lax.axis_index("c")
    wide_id = z_id * 4 + quad_id
    strip_rows, columns, depth = features.shape[1:]
    strip = strip_rows * columns
    total = 4 * strip
    tap_count, chans = branch_weight.shape[:2]
    all_ch = chans * 16
    split = (tap_count - 1) // 2
    half = (split + 1) * chans
    cells, everyone = ("dp", "z"), ("dp",) + PLANE
    rows = 16 * chans + EXTRA

    def exchange(parts, axes):
        return lax.all_to_all(parts, axes, 0, 0, tiled=True)

    height = lax.dynamic_index_in_dim(scale_sizes[0], z_id, 0, keepdims=False)
    pixel = jnp.arange(total, dtype=jnp.int32)
    inside = jnp.logical_and(pixel // columns < height, pixel % columns < 2 * height).astype(f32)
    own_inside = lax.dynamic_slice_in_dim(inside, quad_id * strip, strip, 0)
    mask_rows = jnp.broadcast_to(inside[None], (8, total))
    strip_mask = jnp.broadcast_to(own_inside[None], (8, strip))

    mid = jnp.logical_and(z_id >= 1, z_id <= 2).astype(jnp.int32)[None]

    sel = x_id.astype(jnp.int32) if halves else jnp.zeros((), jnp.int32)
    outer = z_id >= 2
    scalars = jnp.stack(
        [sel, sel, sel, sel]
        + [z_id, jnp.bitwise_xor(z_id, 1), jnp.where(outer, 1, 2), jnp.where(outer, 0, 3)]
        + [height, sel]
        + [jnp.bitwise_xor(quad_id, flip) for flip in range(4)]
    ).astype(jnp.int32)
    first_group = (x_id == 0).astype(f32)
    norm_cols = jnp.zeros((chans, LANES), f32)
    norm_cols = norm_cols.at[:, GAIN : GAIN + 5].set(jnp.transpose(norm_params[0, :5]))
    norm_cols = norm_cols.at[:, SHIFT : SHIFT + 5].set(jnp.transpose(norm_params[1, :5]))
    norm_cols = norm_cols * first_group
    head_cols = jnp.zeros((chans, LANES), f32).at[:, 2:4].set(jnp.transpose(norm_params[:, 5]))
    head_cols = lax.dynamic_update_slice_in_dim(
        jnp.zeros((all_ch, LANES), f32), head_cols * first_group, wide_id * chans, 0
    )
    def over_groups(block):
        return lax.ppermute(block, "dp", SWAP)

    def along(parts, pairs):
        return [lax.ppermute(part, "z", pairs) for part in parts]

    def hold(parts, after):
        return [held(part, after) for part in parts]

    def pair_of(parts):
        return (parts[0], over_groups(parts[0])) if halves else tuple(parts)

    def pick_all(ones, twos, after):
        return [pick(mid, one, two, after) for one, two in zip(ones, twos)]

    zero = jnp.zeros((), jnp.int32)
    mine_w = cast_half(sel[None], branch_weight, split, ())
    other_w = cast_half(1 - sel[None], branch_weight, split, (mine_w,))
    sending = [mine_w] if halves else [mine_w, other_w]
    near, mid_one = along(sending, PAIR), along(sending, MID)

    own_strip = features[0].reshape(strip, depth)
    masked, *masked_parts = mask_strip(scalars, own_strip, columns, sending)
    low_y, high_y = (lax.ppermute(part, "y", SWAP) for part in masked_parts)
    over_c = lax.ppermute(masked, "c", SWAP)

    own_proj = head_weight.astype(bf16).reshape(chans, 5, 4, 4, chans)
    own_proj = jnp.transpose(own_proj, (0, 3, 2, 1, 4))
    pixel_proj = jnp.pad(
        own_proj[:, :, :, :4].reshape(chans, 4, 16 * chans), ((0, 0), (0, 0), (0, EXTRA))
    ).reshape(chans, 4 * rows)
    shared = jnp.concatenate(
        [
            jnp.broadcast_to(own_proj[:, :, :, 4].reshape(1, chans, all_ch), (16, chans, all_ch)),
            jnp.transpose(cotangent[0].reshape(chans, 16, strip), (1, 0, 2)),
            jnp.broadcast_to(pixel_proj[None], (16, chans, 4 * rows)),
        ],
        axis=2,
    )

    slots = [(mine_w, other_w)]
    near = hold(near, [masked, mask_rows, scalars])
    mid_two = along(near, MID)
    near = pair_of(near)
    mid_one = hold(mid_one, near[:1])
    out_one = along(mid_one, OUTWARD)
    low_y = held(low_y, mid_one)
    mid_two = hold(mid_two, [low_y, other_w, shared, strip_mask, norm_cols, head_cols])
    out_two = along(mid_two, OUTWARD)
    second = pick_all(mid_one, out_one, mid_two)
    second_pair = pair_of(second)
    high_y = held(high_y, second)
    low_yc, high_yc = (lax.ppermute(part, "c", SWAP) for part in (low_y, high_y))
    near = (near[0], held(near[1], (high_y,)))
    slots.append(near)
    parts = ((masked,), (over_c,), (low_y, high_y), (low_yc, high_yc))
    pixels = image_of(scalars, strip, parts, near[1:])

    def branch(slot, state, after):
        return forward_taps(
            slot, pixels, mask_rows, scalars, *slots[slot], state, columns, chans, split, after
        )

    state = branch(0, (), ())
    slots.append((second_pair[0], held(second_pair[1], [state[1]])))
    third = pick_all(mid_two, out_two, slots[2][1:])
    slots.append(pair_of(third))
    shared = exchange(held(shared, third), PLANE)
    shared = shared.reshape(all_ch, all_ch + strip + 4 * rows)
    state = branch(1, state, third)
    state = branch(2, state, ())
    state = branch(3, state, ())
    pre, stats = state
    own_sums = pack_sums(scalars, stats, norm_cols, axes_size(cells), (shared,))
    quad = quad_id.astype(jnp.int32)[None]
    concat, coef_cols, coef_rows = activations(
        quad, exchange(own_sums, cells), own_sums, pre, image_total
    )
    concat = exchange(concat, QUAD).reshape(4 * rows, strip)

    unit, head_sums = project(concat, shared, head_cols, strip_mask, axes_size(everyone))
    head_values, head_delta, head_coefs, head_rows, head_sums = head_norm(
        exchange(head_sums, everyone), unit, shared, strip_mask, coef_rows
    )
    unit_back, concat_back, row_sums, head_moments = unit_backward(
        exchange(head_sums, everyone),
        unit,
        head_delta,
        head_coefs,
        strip_mask,
        coef_rows,
        shared,
    )

    delta, pool_rows, moments = branch_backward(
        exchange(concat_back, QUAD), pre, coef_cols, coef_rows, mask_rows, axes_size(cells), ()
    )
    moments = exchange(moments, cells)

    def weights_of(slots, after):
        return weight_grads(
            slots,
            scalars,
            moments,
            pool_rows,
            coef_cols,
            pre,
            delta,
            mask_rows,
            pixels,
            columns,
            half,
            image_total,
            after,
        )

    def group_sums(slot, after, *lists):
        if halves:
            return [add(slot[0], over_groups(slot[1]), *(parts[0] for parts in lists), after=after)]
        return [add(*parts, after=after) for parts in zip(slot[:2], *lists)]

    def swap_all(parts, axis):
        return [lax.ppermute(part, axis, SWAP) for part in parts]

    def add_all(*lists, after=()):
        return [add(*parts, after=after) for parts in zip(*lists)]

    flat_w = [part for slot in slots for part in slot]

    def features_of(flip, after):
        return input_grads(flip, taps, flat_w, scalars, strip, after)

    ((keep_c, send_c, taps_c),) = weights_of((3,), ())
    head_parts = head_weight_grads(concat, unit_back, row_sums, head_values, (taps_c,))
    head_parts = exchange(head_parts.reshape(16, chans, all_ch + strip + 4 * rows), PLANE)
    slot_b, slot_a, slot_o = weights_of((2, 1, 0), (taps_c,))
    taps = [slot_o[2], slot_a[2], slot_b[2], taps_c]
    third = group_sums((keep_c, send_c), (slot_o[2], head_parts))
    far_cross, far = features_of(2, third)
    mid_two = add_all(third, along(third, INWARD), after=(far,))
    second = group_sums(slot_b, mid_two)
    far = strip_sum(scalars, (far,), swap_all(far_cross, "c"), columns, False, second)
    near = group_sums(slot_a, (far,), along(mid_two, MID))
    mid_one = add_all(second, along(second, INWARD), after=near)

    head_output = head_parts[:, :, all_ch : all_ch + strip]
    head_output = jnp.transpose(head_output, (1, 0, 2)).reshape(1, chans, 16 * strip)
    head_parts = jnp.sum(head_parts.astype(f32), axis=0)
    pool_part = head_parts[:, :all_ch].reshape(chans, 4, 4, 1, chans)
    pixel_part = head_parts[:, all_ch + strip :].reshape(chans, 4, rows)[:, :, : 16 * chans]
    pixel_part = pixel_part.reshape(chans, 4, 4, 4, chans)
    head_grads = jnp.concatenate([pixel_part, pool_part], axis=3)
    head_grads = jnp.transpose(head_grads, (0, 3, 2, 1, 4)).reshape(chans, 5 * all_ch)
    near_cross, own_part = features_of(0, (*mid_one, head_grads))
    if halves:
        head_grads = head_grads + lax.ppermute(head_grads, "dp", SWAP)
    else:
        head_grads = lax.psum(head_grads, "dp")
    mine = group_sums(slot_o, (own_part, head_grads), along(near, PAIR), along(mid_one, MID))
    state = (branch_weight, branch_first, branch_second)
    if halves:
        other = over_groups(mine[0])
    else:
        mine = [lax.psum(part, "dp") for part in mine]
    cross = swap_all(near_cross, "c")
    total = held(own_part, mine).astype(f32) + jnp.concatenate(cross, axis=0).astype(f32)
    total = total + lax.ppermute(far, "y", SWAP).astype(f32)
    input_grad = (total * own_inside[:, None]).astype(bf16)
    input_grad = input_grad.reshape(1, strip_rows, columns, depth)
    start = jnp.stack([sel * split, zero])
    done = adam_taps(start, split + 1, 3, mine[0], *state, (), (input_grad,))
    start = jnp.stack([(1 - sel) * (split + 1), 1 - sel])
    done = adam_taps(start, split, 2, other if halves else mine[1], *state, done, ())
    branch_grads, branch_means, branch_squares, branch_updated = done

    def own_lanes(by_row):
        return lax.dynamic_slice_in_dim(by_row, z_id * chans, chans, 1)

    def own_head(by_row):
        return lax.dynamic_slice_in_dim(by_row, wide_id * chans, chans, 1)

    own_moments = own_lanes(jnp.sum(moments, axis=0))
    head_own = own_head(head_moments)
    norm_grads = jnp.stack(
        [
            jnp.concatenate([own_moments[8:13], head_own[1:2]]),
            jnp.concatenate([own_moments[0:5], head_own[0:1]]),
        ]
    )
    own_coefs, head_stats = own_lanes(coef_rows), own_head(head_rows)
    pixel_total = coef_rows[COUNT, 0]
    all_centres = jnp.concatenate([own_coefs[CENTRE : CENTRE + 5], head_stats[0:1]])
    all_variances = jnp.concatenate([own_coefs[VARIANCE : VARIANCE + 5], head_stats[4:5]])
    factors = jnp.where(
        jnp.arange(6) == 4, image_total / (image_total - 1.0), pixel_total / (pixel_total - 1.0)
    )
    running_next = (1.0 - momentum) * running_stats + momentum * jnp.stack(
        [all_centres, all_variances * factors[:, None]]
    )
    head_means, head_squares, head_updated = adamw_update(
        head_weight, head_grads, head_first, head_second, conv_rate, weight_decay
    )
    norm_means, norm_squares, norm_updated = adamw_update(
        norm_params, norm_grads, norm_first, norm_second, norm_rate, 0.0
    )
    return (
        head_output,
        input_grad,
        branch_grads,
        branch_means,
        branch_squares,
        branch_updated,
        head_grads,
        head_means,
        head_squares,
        head_updated,
        norm_grads,
        norm_means,
        norm_squares,
        norm_updated,
        running_next,
    )


def solution(mesh):
    groups, wide = mesh.devices.shape
    fine = Mesh(mesh.devices.reshape(groups, 4, 2, wide // 8), ("dp",) + PLANE)
    placed = (
        P("dp", PLANE, None, None),
        P("dp", None),
        P("dp", PLANE, None),
        P(None, PLANE, None),
        P(None, PLANE, None),
        P(None, PLANE, None),
        P(PLANE, None),
        P(PLANE, None),
        P(PLANE, None),
        P(None, None, PLANE),
        P(None, None, PLANE),
        P(None, None, PLANE),
        P(None, None, PLANE),
    )
    return jax.shard_map(
        local,
        mesh=fine,
        in_specs=placed,
        out_specs=(
            P("dp", PLANE, None),
            P("dp", PLANE, None, None),
            P(None, PLANE, None),
            P(None, PLANE, None),
            P(None, PLANE, None),
            P(None, PLANE, None),
            P(PLANE, None),
            P(PLANE, None),
            P(PLANE, None),
            P(PLANE, None),
            P(None, None, PLANE),
            P(None, None, PLANE),
            P(None, None, PLANE),
            P(None, None, PLANE),
            P(None, None, PLANE),
        ),
        check_vma=False,
    )
```

```python
import functools

import jax
import jax.numpy as jnp
from jax import lax
from jax.experimental import pallas as pl
from jax.experimental.pallas import tpu as pltpu
from jax.sharding import Mesh, PartitionSpec as P

STEP = 10


dilations = (6, 12, 18)
epsilon = 1e-05
momentum = 0.1
first_decay = 0.9
second_decay = 0.999
conv_rate = 0.02
norm_rate = 0.4
weight_decay = 0.0001
adam_floor = 1e-08

LANES = 128
PLANE = ("z", "y", "c")
QUAD = ("y", "c")
SWAP = [(0, 1), (1, 0)]
PAIR = [(0, 1), (1, 0), (2, 3), (3, 2)]
MID = [(1, 2), (2, 1)]
OUTWARD = [(1, 0), (2, 3)]
INWARD = [(0, 1), (3, 2)]

bf16 = jnp.bfloat16
f32 = jnp.float32
barrier = lax.optimization_barrier


def adamw_update(parameter, gradient, moment_one, moment_two, step_rate, decay_rate):
    first_new = first_decay * moment_one + (1.0 - first_decay) * gradient
    second_new = second_decay * moment_two + (1.0 - second_decay) * gradient * gradient
    first_hat = first_new / (1.0 - first_decay**STEP)
    second_hat = second_new / (1.0 - second_decay**STEP)
    updated = parameter - step_rate * (
        first_hat / (jnp.sqrt(second_hat) + adam_floor) + decay_rate * parameter
    )
    return (first_new, second_new, updated)


def gelu_both(value):
    scale = (2.0 / jnp.pi) ** 0.5
    square = value * value
    bend = jnp.tanh(scale * (value + 0.044715 * (value * square)))
    lead = 0.5 * (1.0 + bend)
    slope = lead + 0.5 * value * (1.0 - bend * bend) * (scale * (1.0 + 3.0 * 0.044715 * square))
    return value * lead, slope


def tall(rows):
    fill = LANES - rows.shape[0]
    return jnp.concatenate([rows, jnp.zeros((fill, rows.shape[1]), rows.dtype)], axis=0).T


def stacked(rows, count):
    found = {}
    for at in range(count):
        found[2 * at] = rows[at : at + 1, :LANES]
        found[2 * at + 1] = rows[at : at + 1, LANES:]
    return put_rows((8, LANES), found)[: 2 * count]


def unstacked(rows):
    found = {}
    for at in range(rows.shape[0] // 2):
        found[at] = jnp.concatenate([rows[2 * at : 2 * at + 1], rows[2 * at + 1 : 2 * at + 2]], axis=1)
    return put_rows((8, 2 * LANES), found)


def beside(left, right, width):
    lane = lax.broadcasted_iota(jnp.int32, left.shape, 1)
    return jnp.where(lane < width, left, pltpu.roll(right, width, 1))


def put_lanes(shape, columns):
    lane = lax.broadcasted_iota(jnp.int32, shape, 1)
    total = jnp.zeros(shape, f32)
    for at, column in columns.items():
        total = jnp.where(lane == at, column, total)
    return total


def put_rows(shape, rows):
    row = lax.broadcasted_iota(jnp.int32, shape, 0)
    total = jnp.zeros(shape, f32)
    for at, value in rows.items():
        total = jnp.where(row == at, value, total)
    return total


def axes_size(axes):
    count = 1
    for axis in axes:
        count *= lax.axis_size(axis)
    return count


def call(
    kernel,
    name,
    grid,
    scalars,
    in_specs,
    out_specs,
    out_shape,
    scratch=(),
    aliases=None,
    flops=0,
    after=(),
    vmem=24,
):
    after = tuple(after)
    first = scalars + len(in_specs)

    def body(*refs):
        kernel(*refs[:first], *refs[first + len(after) :])

    run = pl.pallas_call(
        body,
        out_shape=out_shape,
        grid_spec=pltpu.PrefetchScalarGridSpec(
            num_scalar_prefetch=scalars,
            grid=grid,
            in_specs=list(in_specs) + [pl.BlockSpec(memory_space=pl.ANY)] * len(after),
            out_specs=out_specs,
            scratch_shapes=list(scratch),
        ),
        input_output_aliases=aliases or {},
        compiler_params=pltpu.CompilerParams(vmem_limit_bytes=vmem << 20),
        cost_estimate=pl.CostEstimate(flops=1, bytes_accessed=1, transcendentals=0),
        name=name,
    )
    return lambda *arrays: run(*arrays, *after)


def full(shape):
    return pl.BlockSpec(shape, lambda *_: (0,) * len(shape))


def add_kernel(*refs):
    total = refs[0][...].astype(f32)
    for ref in refs[1:-1]:
        total = total + ref[...].astype(f32)
    refs[-1][...] = total.astype(bf16)


def add(*values, after=()):
    first = held(values[0], after) if after else values[0]
    total = first.astype(f32)
    for value in values[1:]:
        total = total + value.astype(f32)
    return barrier(total.astype(bf16))


def pick_kernel(flag_ref, one_ref, two_ref, out_ref):
    @pl.when(flag_ref[0] == 1)
    def _():
        out_ref[...] = one_ref[...]

    @pl.when(flag_ref[0] != 1)
    def _():
        out_ref[...] = two_ref[...]


def pick(flag, one, two, after=()):
    rows, depth = one.shape
    spec = pl.BlockSpec((rows // 3, depth), lambda i, s: (i, 0))
    return call(
        pick_kernel,
        "pick",
        (3,),
        1,
        [spec, spec],
        spec,
        jax.ShapeDtypeStruct(one.shape, one.dtype),
        after=after,
    )(flag, one, two)


def held_kernel(in_ref, out_ref):
    del in_ref, out_ref


def held(value, after):
    anywhere = pl.BlockSpec(memory_space=pl.ANY)
    return call(
        held_kernel,
        "held",
        (1,),
        0,
        [anywhere],
        anywhere,
        jax.ShapeDtypeStruct(value.shape, value.dtype),
        aliases={0: 0},
        after=after,
        vmem=56,
    )(value)


def cast_kernel(sel_ref, in_ref, out_ref):
    taps, chans = in_ref.shape[:2]
    first = jnp.logical_and(sel_ref[0] == 1, pl.program_id(0) == 0)
    for tap in range(taps):
        value = in_ref[tap]
        if tap == 0:
            value = jnp.where(first, 0.0, value)
        out_ref[tap * chans : (tap + 1) * chans, :] = value.astype(bf16)


def cast_half(sel, weight, split, after):
    chans, depth = weight.shape[1:]
    parts = 3 if (split + 1) % 3 == 0 else 1
    block = (split + 1) // parts
    return call(
        cast_kernel,
        "cast",
        (parts,),
        1,
        [pl.BlockSpec((pl.Element(block), pl.Element(chans), pl.Element(depth)), lambda i, s: (s[0] * split + i * block, 0, 0))],
        pl.BlockSpec((block * chans, depth), lambda i, s: (i, 0)),
        jax.ShapeDtypeStruct(((split + 1) * chans, depth), bf16),
        after=after,
        vmem=56,
    )(sel, weight)


def mask_kernel(columns, scalar_ref, in_ref, out_ref, *part_refs):
    rows, depth = in_ref.shape
    pixel = lax.broadcasted_iota(jnp.int32, (rows, LANES), 0)
    row = pixel // columns + scalar_ref[HALF + 1] * (rows // columns)
    height = scalar_ref[HEIGHT]
    inside = jnp.logical_and(row < height, pixel % columns < 2 * height)
    for first in range(0, depth, LANES):
        lanes = slice(first, first + LANES)
        value = jnp.where(inside, in_ref[:, lanes].astype(f32), 0.0).astype(bf16)
        out_ref[:, lanes] = value
        start = 0
        for part_ref in part_refs:
            size = part_ref.shape[0]
            part_ref[:, lanes] = value[start : start + size]
            start += size


def mask_strip(scalars, strip, columns, after):
    rows, depth = strip.shape
    low = rows // 16 * 7
    shapes = ((rows, depth), (low, depth), (rows - low, depth))
    return call(
        functools.partial(mask_kernel, columns),
        "mask",
        (1,),
        1,
        [full((rows, depth))],
        tuple(full(shape) for shape in shapes),
        tuple(jax.ShapeDtypeStruct(shape, bf16) for shape in shapes),
        after=after,
        vmem=56,
    )(scalars, strip)


def image_kernel(strip, places, spot_ref, *refs):
    *parts, out_ref, sems = refs
    copies = []
    for at, (which, first) in enumerate(places):
        rows = pl.ds(pl.multiple_of(spot_ref[HALF + 1 + which] * strip + first, 16), parts[at].shape[0])
        copies.append(pltpu.make_async_copy(parts[at], out_ref.at[rows, :], sems.at[at]))
    for copy in copies:
        copy.start()
    for copy in copies:
        copy.wait()


def image_of(spots, strip, parts, after):
    depth = parts[0][0].shape[1]
    places = []
    for which, strip_parts in enumerate(parts):
        first = 0
        for part in strip_parts:
            places.append((which, first))
            first += part.shape[0]
    flat = [part for strip_parts in parts for part in strip_parts]
    anywhere = pl.BlockSpec(memory_space=pl.ANY)
    return call(
        functools.partial(image_kernel, strip, places),
        "image",
        (1,),
        1,
        [anywhere] * len(flat),
        full((4 * strip, depth)),
        jax.ShapeDtypeStruct((4 * strip, depth), bf16),
        [pltpu.SemaphoreType.DMA((len(flat),))],
        after=after,
        vmem=56,
    )(spots, *flat)


def head_grad_kernel(x_ref, back_ref, sum_ref, value_ref, out_ref):
    channels = back_ref.shape[0]
    rows = x_ref.shape[0] // 4
    act = jnp.zeros((EXTRA, channels), f32)
    for quad in range(4):
        first = quad * rows + rows - EXTRA
        act = act + x_ref[first : first + EXTRA, :channels].astype(f32)
    out_ref[:, :channels] = (sum_ref[:, 0:1] * act[0:1, :]).astype(bf16)
    strip = x_ref.shape[1]
    out_ref[:, channels : channels + strip] = value_ref[...]
    out_ref[:, channels + strip :] = lax.dot_general(
        back_ref[...], x_ref[...], (((1,), (1,)), ((), ())), preferred_element_type=f32
    ).astype(bf16)


def head_weight_grads(concat, unit_back, row_sums, values, after):
    channels = unit_back.shape[0]
    arrays = (concat, unit_back, row_sums, values)
    shape = (channels, channels + concat.shape[1] + concat.shape[0])
    return call(
        head_grad_kernel,
        "head_weight_grad",
        (1,),
        0,
        [full(array.shape) for array in arrays],
        full(shape),
        jax.ShapeDtypeStruct(shape, bf16),
        after=after,
        vmem=24,
    )(*arrays)


def strip_sum_kernel(columns, whole, masked, scalar_ref, *refs):
    block = refs[0].shape[0]
    step = pl.program_id(0)
    rows_all = refs[whole].shape[0] * (len(refs) - 1 - whole)
    pixel = step * block + lax.broadcasted_iota(jnp.int32, (block, LANES), 0)
    row = pixel // columns + scalar_ref[HALF + 1] * (rows_all // columns)
    height = scalar_ref[HEIGHT]
    inside = jnp.logical_and(row < height, pixel % columns < 2 * height)
    steps = refs[whole].shape[0] * (len(refs) - 1 - whole) // block
    count = steps // (len(refs) - 1 - whole)
    for at in range(steps):

        @pl.when(step == at)
        def _():
            part = refs[whole + at // count]
            rows = slice(at % count * block, (at % count + 1) * block)
            for first in range(0, refs[0].shape[1], LANES):
                lanes = slice(first, first + LANES)
                total = part[rows, lanes].astype(f32)
                for ref in refs[:whole]:
                    total = total + ref[:, lanes].astype(f32)
                if masked:
                    total = jnp.where(inside, total, 0.0)
                refs[-1][:, lanes] = total.astype(bf16)


def strip_sum(scalars, strips, parts, columns, masked, after):
    rows, depth = strips[0].shape
    spec = pl.BlockSpec((rows // 2, depth), lambda i, s: (i, 0))
    return call(
        functools.partial(strip_sum_kernel, columns, len(strips), masked),
        "strip_sum",
        (2,),
        1,
        [spec] * len(strips) + [full(part.shape) for part in parts],
        spec,
        jax.ShapeDtypeStruct((rows, depth), bf16),
        after=after,
        vmem=56,
    )(scalars, *strips, *parts)


def adam_kernel(start_ref, grad_ref, weight_ref, first_ref, second_ref, *rest):
    out_ref, mean_ref, square_ref, new_ref = rest[-4:]
    grad = grad_ref[...].astype(f32).reshape(out_ref.shape)
    mean, square, new = adamw_update(
        weight_ref[...], grad, first_ref[...], second_ref[...], conv_rate, weight_decay
    )
    out_ref[...] = grad
    mean_ref[...] = mean
    square_ref[...] = square
    new_ref[...] = new


def adam_taps(start, count, block, grads, weight, first, second, earlier, after):
    taps, chans, depth = weight.shape

    def piece(size, index):
        return pl.BlockSpec(tuple(pl.Element(n) for n in size), index)

    spec = piece((block, chans, depth), lambda i, s: (s[0] + i * block, 0, 0))
    anywhere = [pl.BlockSpec(memory_space=pl.ANY)] * len(earlier)
    return call(
        adam_kernel,
        "adamw",
        (count // block,),
        1,
        [piece((block * chans, depth), lambda i, s: ((s[1] + i * block) * chans, 0))]
        + [spec] * 3
        + anywhere,
        (spec,) * 4,
        (jax.ShapeDtypeStruct(weight.shape, f32),) * 4,
        aliases={5 + at: at for at in range(4)} if earlier else None,
        after=after,
        vmem=20,
    )(start, grads, weight, first, second, *earlier)


FIRST, SECOND, GAIN, SHIFT, AREA = 0, 8, 16, 24, 5
SUM_ROWS = 16
CENTRE, INVERSE, VARIANCE, COUNT, POOLED = 0, 8, 32, 40, 41
COEF_ROWS = 48
EXTRA = 16
HEIGHT, HALF = 8, 9


def lane_masks(columns):
    lane = lax.broadcasted_iota(jnp.int32, (1, LANES), 1) % columns
    masks = {}
    for dilation in dilations:
        for off in (-dilation, dilation):
            moved = lane + off
            masks[off] = jnp.logical_and(moved >= 0, moved < columns)
    return masks


def forward_kernel(columns, split, slot, scalar_ref, x_ref, wz_ref, wx_ref, mask_ref, *rest):
    pre_ref, stat_ref, taps = rest[-3:]
    step = pl.program_id(0)
    half = wz_ref.shape[0]
    block = x_ref.shape[0]
    sel = scalar_ref[slot]
    contract = (((1,), (1,)), ((), ()))
    pixels = x_ref[...]
    cols = pl.ds(pl.multiple_of(step * block, block), block)
    taps[pl.ds(pl.multiple_of(sel * half, 16), half), cols] = lax.dot_general(
        wz_ref[...], pixels, contract, preferred_element_type=f32
    )
    taps[pl.ds(pl.multiple_of((1 - sel) * half, 16), half), cols] = lax.dot_general(
        wx_ref[...], pixels, contract, preferred_element_type=f32
    )

    @pl.when(step == pl.num_programs(0) - 1)
    def _():
        total = taps.shape[1]
        tiles = total // LANES
        chans = pre_ref.shape[2]
        masks = lane_masks(columns)

        def rows_of(tap):
            first = tap * chans if tap <= split else (tap + 1) * chans
            return slice(first, first + chans)

        def tile(tap, at):
            return taps[rows_of(tap), at * LANES : (at + 1) * LANES]

        sums = [jnp.zeros((chans, LANES), f32) for _ in range(4)]
        squares = [jnp.zeros((chans, LANES), f32) for _ in range(4)]
        pooled = jnp.zeros((chans, LANES), f32)
        for at in range(tiles):
            lanes = slice(at * LANES, (at + 1) * LANES)
            weight = mask_ref[0:1, lanes]
            for branch in range(4):
                if branch == 0:
                    value = tile(0, at)
                else:
                    dilation = dilations[branch - 1]
                    jump = dilation * columns // LANES
                    value = None
                    for b in range(3):
                        part = None
                        for a in range(3):
                            source = at + (a - 1) * jump
                            if 0 <= source < tiles:
                                term = tile(1 + 9 * (branch - 1) + 3 * a + b, source)
                                part = term if part is None else part + term
                        off = (b - 1) * dilation
                        if off != 0:
                            part = pltpu.roll(part, (-off) % LANES, 1)
                            part = jnp.where(masks[off], part, 0.0)
                        value = part if value is None else value + part
                pre_ref[0, branch, :, lanes] = value
                weighted = value * weight
                sums[branch] = sums[branch] + weighted
                squares[branch] = squares[branch] + weighted * value
            pooled = pooled + tile(28, at)
        height = jnp.full((1, 1), scalar_ref[HEIGHT], jnp.int32).astype(f32)
        area = 2.0 * height * height
        pool = jnp.sum(pooled, axis=1, keepdims=True) / area
        columns_of = {FIRST + 4: pool, SECOND + 4: pool * pool, AREA: area}
        for branch in range(4):
            columns_of[FIRST + branch] = jnp.sum(sums[branch], axis=1, keepdims=True)
            columns_of[SECOND + branch] = jnp.sum(squares[branch], axis=1, keepdims=True)
        stat_ref[0] = put_lanes((chans, LANES), columns_of)


def forward_taps(slot, pixels, mask_rows, scalars, wz, wx, earlier, columns, chans, split, after):
    total, depth = pixels.shape
    block = total // 4
    half = wz.shape[0]
    keep = [pl.BlockSpec(memory_space=pl.ANY)] * len(earlier)
    return call(
        functools.partial(forward_kernel, columns, split, slot),
        "atrous_forward",
        (4,),
        1,
        [
            pl.BlockSpec((block, depth), lambda i, s: (i, 0)),
            full((half, depth)),
            full((half, depth)),
            full((8, total)),
        ]
        + keep,
        (
            pl.BlockSpec((1, 4, chans, total), lambda i, s: (s[4 + slot], 0, 0, 0)),
            pl.BlockSpec((1, chans, LANES), lambda i, s: (s[4 + slot], 0, 0)),
        ),
        (
            jax.ShapeDtypeStruct((4, 4, chans, total), f32),
            jax.ShapeDtypeStruct((4, chans, LANES), f32),
        ),
        [pltpu.VMEM((2 * half, total), f32)],
        {5: 0, 6: 1} if earlier else None,
        4 * half * total * depth,
        after,
        56,
    )(scalars, pixels, wz, wx, mask_rows, *earlier)


def pack_kernel(place_ref, stat_ref, norm_ref, out_ref, work):
    chans = norm_ref.shape[0]
    work[...] = jnp.zeros_like(work)
    for z in range(4):
        work[z * chans : (z + 1) * chans, :] = stat_ref[z]
    own = pl.ds(pl.multiple_of(place_ref[4] * chans, chans), chans)
    work[own, :] = work[own, :] + norm_ref[...]
    rows = work[...].T
    rows = beside(rows[:SUM_ROWS], rows[SUM_ROWS : 2 * SUM_ROWS], 4 * chans)
    for at in range(out_ref.shape[0]):
        out_ref[at] = rows


def pack_sums(place, stats, norm_cols, count, after):
    return call(
        pack_kernel,
        "branch_sums",
        (1,),
        1,
        [full(stats.shape), full(norm_cols.shape)],
        full((count, SUM_ROWS, LANES)),
        jax.ShapeDtypeStruct((count, SUM_ROWS, LANES), f32),
        [pltpu.VMEM((LANES, LANES), f32)],
        after=after,
        vmem=24,
    )(place, stats, norm_cols)


def pool_rows_of(rows_ref, own_width):
    def row(at):
        return rows_ref[at : at + 1, :]

    moved = row(POOLED) - row(CENTRE + 4)
    normed = row(GAIN + 4) * moved * row(INVERSE + 4) + row(SHIFT + 4)
    lane = lax.broadcasted_iota(jnp.int32, normed.shape, 1)
    return normed, moved * row(INVERSE + 4), lane < own_width


def act_kernel(image_total, quad_ref, parts_ref, own_ref, pre_ref, out_ref, col_ref, row_ref):
    chans = pre_ref.shape[2]

    @pl.when(pl.program_id(0) == 0)
    def _():
        sums = jnp.sum(parts_ref[...], axis=0)
        affine = pltpu.roll(sums, LANES - 4 * chans, 1)
        pixel_total = jnp.maximum(sums[AREA : AREA + 1], 1.0)
        index = lax.broadcasted_iota(jnp.int32, (8, LANES), 0)
        count = jnp.where(index == 4, image_total, pixel_total)
        centre = sums[FIRST : FIRST + 8] / count
        variance = sums[SECOND : SECOND + 8] / count - centre * centre
        inverse = lax.rsqrt(variance + epsilon)
        other = jnp.where(index == 0, pixel_total, jnp.where(index == 1, own_ref[0, 4:5, :], 0.0))
        rows = jnp.concatenate(
            [centre, inverse, affine[:8], affine[8:16], variance, other],
            axis=0,
        )
        row_ref[...] = rows
        col_ref[...] = tall(rows)

    for z in range(4):
        span = slice(z * chans, (z + 1) * chans)
        for branch in range(4):
            moved = pre_ref[z, branch] - col_ref[span, CENTRE + branch : CENTRE + branch + 1]
            normed = (
                col_ref[span, GAIN + branch : GAIN + branch + 1]
                * moved
                * col_ref[span, INVERSE + branch : INVERSE + branch + 1]
                + col_ref[span, SHIFT + branch : SHIFT + branch + 1]
            )
            first = (4 * z + branch) * chans
            out_ref[0, first : first + chans, :] = gelu_both(normed)[0].astype(bf16)
    normed, _, valid = pool_rows_of(row_ref, 4 * chans)
    act = jnp.where(valid, gelu_both(normed)[0], 0.0)
    act = put_rows((EXTRA, LANES), {0: act + pltpu.roll(act, 4 * chans, 1)})
    lane = lax.broadcasted_iota(jnp.int32, act.shape, 1)
    for at in range(out_ref.shape[2] // LANES):
        owner = (lane + at * LANES) // (4 * chans)
        out_ref[0, 16 * chans :, at * LANES : (at + 1) * LANES] = jnp.where(
            owner == quad_ref[0], act, 0.0
        ).astype(bf16)


def activations(quad, parts, own, pre, image_total):
    chans, total = pre.shape[2:]
    strip = total // 4
    rows = 16 * chans + EXTRA
    return call(
        functools.partial(act_kernel, image_total),
        "branch_act",
        (4,),
        1,
        [
            full(parts.shape),
            full((1, SUM_ROWS, LANES)),
            pl.BlockSpec((4, 4, chans, strip), lambda i, s: (0, 0, 0, i)),
        ],
        (
            pl.BlockSpec((1, rows, strip), lambda i, s: (i, 0, 0)),
            full((LANES, LANES)),
            full((COEF_ROWS, LANES)),
        ),
        (
            jax.ShapeDtypeStruct((4, rows, strip), bf16),
            jax.ShapeDtypeStruct((LANES, LANES), f32),
            jax.ShapeDtypeStruct((COEF_ROWS, LANES), f32),
        ),
        vmem=24,
    )(quad, parts, own, pre)


def unit_kernel(x_ref, shared_ref, head_ref, mask_ref, unit_ref, out_ref):
    channels = shared_ref.shape[0]
    rows, strip = x_ref.shape[0] // 4, x_ref.shape[1]
    proj = shared_ref[:, channels + strip :]
    unit = jnp.dot(proj, x_ref[...], preferred_element_type=f32)
    act = jnp.zeros((EXTRA, channels), f32)
    for quad in range(4):
        first = quad * rows + rows - EXTRA
        act = act + x_ref[first : first + EXTRA, :channels].astype(f32)
    bias = shared_ref[:, :channels].astype(f32) * act[0:1, :]
    unit = unit + jnp.sum(bias, axis=1, keepdims=True)
    unit_ref[...] = unit
    weighted = unit * mask_ref[0:1, :]
    lane = lax.broadcasted_iota(jnp.int32, head_ref.shape, 1)
    one = jnp.sum(weighted, axis=1, keepdims=True)
    two = jnp.sum(weighted * unit, axis=1, keepdims=True)
    sums = jnp.where(lane == 0, one, jnp.where(lane == 1, two, head_ref[...])).T[:8]
    sums = stacked(sums, 4)
    for at in range(out_ref.shape[0]):
        out_ref[at] = sums


def project(concat, shared, head_cols, strip_mask, count):
    channels, strip = shared.shape[0], concat.shape[1]
    arrays = (concat, shared, head_cols, strip_mask)
    return call(
        unit_kernel,
        "projection",
        (1,),
        0,
        [full(array.shape) for array in arrays],
        (full((channels, strip)), full((count, 8, LANES))),
        (
            jax.ShapeDtypeStruct((channels, strip), f32),
            jax.ShapeDtypeStruct((count, 8, LANES), f32),
        ),
        vmem=24,
    )(*arrays)


def head_kernel(parts_ref, unit_ref, shared_ref, mask_ref, row_ref, value_ref, delta_ref, col_ref, head_ref, out_ref):
    sums = unstacked(jnp.sum(parts_ref[...], axis=0))
    pixel_total = row_ref[COUNT : COUNT + 1, 0:1]
    centre = sums[0:1] / pixel_total
    variance = sums[1:2] / pixel_total - centre * centre
    inverse = lax.rsqrt(variance + epsilon)
    rows = put_rows(
        sums.shape, {0: centre, 1: inverse, 2: sums[2:3], 3: sums[3:4], 4: variance}
    )
    head_ref[...] = rows
    columns = tall(rows)
    col_ref[...] = columns
    hat = (unit_ref[...] - columns[:, 0:1]) * columns[:, 1:2]
    normed = columns[:, 2:3] * hat + columns[:, 3:4]
    value, slope = gelu_both(normed)
    weight = mask_ref[0:1, :]
    value_ref[...] = (weight * value).astype(bf16)
    first = unit_ref.shape[0]
    cot = shared_ref[:, first : first + unit_ref.shape[1]].astype(f32)
    delta = slope * (weight * cot)
    delta_ref[...] = delta
    sums = put_lanes(
        columns.shape,
        {
            0: jnp.sum(delta, axis=1, keepdims=True),
            1: jnp.sum(delta * hat, axis=1, keepdims=True),
        },
    ).T[:8]
    sums = stacked(sums, 2)
    for at in range(out_ref.shape[0]):
        out_ref[at] = sums


def head_norm(parts, unit, shared, strip_mask, coef_rows):
    channels, strip = unit.shape
    count = parts.shape[0]
    return call(
        head_kernel,
        "head_norm",
        (1,),
        0,
        [full(parts.shape), full(unit.shape), full(shared.shape), full((8, strip)), full(coef_rows.shape)],
        (
            full((channels, strip)),
            full((channels, strip)),
            full((channels, LANES)),
            full((8, channels)),
            full((count, 4, LANES)),
        ),
        (
            jax.ShapeDtypeStruct((channels, strip), bf16),
            jax.ShapeDtypeStruct((channels, strip), f32),
            jax.ShapeDtypeStruct((channels, LANES), f32),
            jax.ShapeDtypeStruct((8, channels), f32),
            jax.ShapeDtypeStruct((count, 4, LANES), f32),
        ),
        vmem=24,
    )(parts, unit, shared, strip_mask, coef_rows)


def unit_back_kernel(
    parts_ref, unit_ref, delta_ref, col_ref, mask_ref, row_ref, shared_ref, back_ref, out_ref, sum_ref, moment_ref
):
    sums = unstacked(jnp.sum(parts_ref[...], axis=0))
    moment_ref[...] = sums
    moments = tall(sums)
    pixel_total = row_ref[COUNT : COUNT + 1, 0:1]
    inverse = col_ref[:, 1:2]
    hat = (unit_ref[...] - col_ref[:, 0:1]) * inverse
    back = mask_ref[0:1, :] * (
        (col_ref[:, 2:3] * inverse)
        * (delta_ref[...] - (moments[:, 0:1] + hat * moments[:, 1:2]) / pixel_total)
    )
    back = back.astype(bf16)
    back_ref[...] = back
    row_sums = jnp.sum(back.astype(f32), axis=1, keepdims=True)
    sum_ref[...] = jnp.broadcast_to(row_sums, sum_ref.shape)
    channels = shared_ref.shape[0]
    rows, width = out_ref.shape[1:]
    proj = shared_ref[:, channels + width :]
    terms = lax.dot_general(
        proj, back, (((0,), (0,)), ((), ())), preferred_element_type=f32
    )
    pool = jnp.sum(shared_ref[:, :channels].astype(f32) * row_sums, axis=0, keepdims=True)
    own = channels // 4
    for quad in range(4):
        first = quad * own // LANES * LANES
        part = pool[:, first : first + LANES]
        if quad * own != first:
            part = pltpu.roll(part, LANES - (quad * own - first), 1)
        lane = lax.broadcasted_iota(jnp.int32, part.shape, 1)
        part = jnp.where(lane < own, part, 0.0)
        high = part.astype(bf16).astype(f32)
        extra = put_rows((EXTRA, LANES), {0: high, 1: part - high})
        out_ref[quad, : rows - EXTRA, :] = terms[quad * rows : (quad + 1) * rows - EXTRA].astype(bf16)
        out_ref[quad, rows - EXTRA :, :LANES] = extra.astype(bf16)
        out_ref[quad, rows - EXTRA :, LANES:] = jnp.zeros((EXTRA, width - LANES), bf16)


def unit_backward(parts, unit, delta, cols, strip_mask, coef_rows, shared):
    channels, strip = unit.shape
    rows = (shared.shape[1] - channels - strip) // 4
    arrays = (parts, unit, delta, cols, strip_mask, coef_rows, shared)
    return call(
        unit_back_kernel,
        "unit_back",
        (1,),
        0,
        [full(array.shape) for array in arrays],
        (
            full((channels, strip)),
            full((4, rows, strip)),
            full((channels, LANES)),
            full((8, channels)),
        ),
        (
            jax.ShapeDtypeStruct((channels, strip), bf16),
            jax.ShapeDtypeStruct((4, rows, strip), bf16),
            jax.ShapeDtypeStruct((channels, LANES), f32),
            jax.ShapeDtypeStruct((8, channels), f32),
        ),
        vmem=24,
    )(*arrays)


def branch_kernel(x_ref, pre_ref, col_ref, row_ref, mask_ref, delta_ref, pool_ref, out_ref, sums, pooled):
    step = pl.program_id(0)
    chans = pre_ref.shape[2]

    @pl.when(step == 0)
    def _():
        sums[...] = jnp.zeros_like(sums)
        pooled[...] = jnp.zeros_like(pooled)

    def fold(value):
        total = value[:, :LANES]
        for at in range(1, value.shape[1] // LANES):
            total = total + value[:, at * LANES : (at + 1) * LANES]
        return total

    weight = mask_ref[0:1, :]
    for z in range(4):
        span = slice(z * chans, (z + 1) * chans)
        for branch in range(4):
            first = (4 * z + branch) * chans
            hat = (
                pre_ref[z, branch] - col_ref[span, CENTRE + branch : CENTRE + branch + 1]
            ) * col_ref[span, INVERSE + branch : INVERSE + branch + 1]
            normed = (
                col_ref[span, GAIN + branch : GAIN + branch + 1] * hat
                + col_ref[span, SHIFT + branch : SHIFT + branch + 1]
            )
            delta = gelu_both(normed)[1] * (
                weight * x_ref[0, first : first + chans, :].astype(f32)
            )
            delta_ref[z, branch] = delta
            sums[8 * z + branch] = sums[8 * z + branch] + fold(delta)
            sums[8 * z + 4 + branch] = sums[8 * z + 4 + branch] + fold(delta * hat)
    extra = x_ref[0, 16 * chans :, :LANES].astype(f32)
    pooled[...] = pooled[...] + jnp.broadcast_to(extra[0:1] + extra[1:2], pooled.shape)

    @pl.when(step == pl.num_programs(0) - 1)
    def _():
        normed, hat, valid = pool_rows_of(row_ref, 4 * chans)
        delta = jnp.where(valid, gelu_both(normed)[1] * pooled[0:1, :], 0.0)
        hat = jnp.where(valid, hat, 0.0)
        pool_ref[...] = put_rows(pool_ref.shape, {0: delta, 1: hat})
        found = []
        for z in range(4):
            columns = {}
            for branch in range(4):
                columns[branch] = jnp.sum(sums[8 * z + branch], axis=1, keepdims=True)
                columns[8 + branch] = jnp.sum(sums[8 * z + 4 + branch], axis=1, keepdims=True)
            found.append(put_lanes((chans, LANES), columns))
        found.append(jnp.zeros((LANES - 4 * chans, LANES), f32))
        rows = jnp.concatenate(found, axis=0).T[:16]
        index = lax.broadcasted_iota(jnp.int32, rows.shape, 0)
        rows = jnp.where(index == 4, delta, jnp.where(index == 12, delta * hat, rows))
        rows = beside(rows[:8], rows[8:16], 4 * chans)
        for at in range(out_ref.shape[0]):
            out_ref[at] = rows


def branch_backward(concat_back, pre, coef_cols, coef_rows, mask_rows, count, after):
    chans, total = pre.shape[2:]
    rows, strip = concat_back.shape[1:]
    spread = pl.BlockSpec((4, 4, chans, strip), lambda i: (0, 0, 0, i))
    return call(
        branch_kernel,
        "branch_back",
        (4,),
        0,
        [
            pl.BlockSpec((1, rows, strip), lambda i: (i, 0, 0)),
            spread,
            full(coef_cols.shape),
            full(coef_rows.shape),
            pl.BlockSpec((8, strip), lambda i: (0, i)),
        ],
        (spread, full((8, LANES)), full((count, 8, LANES))),
        (
            jax.ShapeDtypeStruct(pre.shape, f32),
            jax.ShapeDtypeStruct((8, LANES), f32),
            jax.ShapeDtypeStruct((count, 8, LANES), f32),
        ),
        [pltpu.VMEM((32, chans, LANES), f32), pltpu.VMEM((8, LANES), f32)],
        after=after,
        vmem=24,
    )(concat_back, pre, coef_cols, coef_rows, mask_rows)


def weight_kernel(columns, image_total, slots, scalar_ref, parts_ref, pool_ref, mask_ref, x_ref, *refs):
    count = len(slots)
    col_refs, pre_refs, delta_refs = refs[:count], refs[count : 2 * count], refs[2 * count : 3 * count]
    outs = refs[3 * count : 6 * count]
    total_ref, moments = refs[6 * count :]
    half = outs[0].shape[0]
    chans = pre_refs[0].shape[2]
    start = 29 * chans - half
    sel = scalar_ref[HALF]

    @pl.when(pl.program_id(0) == 0)
    def _():
        sums = jnp.sum(parts_ref[...], axis=0)
        second = pltpu.roll(sums, LANES // 2, 1)
        moments[...] = tall(jnp.concatenate([sums, second, pool_ref[...]], axis=0))
        height = jnp.full((1, 1), scalar_ref[HEIGHT], jnp.int32).astype(f32)
        area = 2.0 * height * height
        masks = lane_masks(columns)
        for at, slot in enumerate(slots):
            own = moments[pl.ds(pl.multiple_of(scalar_ref[4 + slot] * chans, chans), chans), :]
            build_taps(
                own, col_refs[at][...], pre_refs[at], delta_refs[at], mask_ref, outs[3 * at + 2], masks, area, columns, image_total
            )

    for at in range(count):
        keep_ref, send_ref, taps_ref = outs[3 * at : 3 * at + 3]
        total_ref[...] = jnp.dot(taps_ref[...], x_ref[...], preferred_element_type=f32)
        keep_ref[...] = total_ref[pl.ds(pl.multiple_of(sel * start, 16), half), :].astype(bf16)
        send_ref[...] = total_ref[pl.ds(pl.multiple_of((1 - sel) * start, 16), half), :].astype(bf16)


def build_taps(own, coefs, pre_ref, delta_ref, mask_ref, taps_ref, masks, area, columns, image_total):
    chans = pre_ref.shape[2]

    def coef(at):
        return coefs[:, at : at + 1]

    def moment(at):
        return own[:, at : at + 1]

    pixel_total = coef(COUNT)
    pool_grad = (
        coef(GAIN + 4)
        * coef(INVERSE + 4)
        * (moment(16) - (moment(4) + moment(17) * moment(12)) / image_total)
    ) / area
    tiles = pre_ref.shape[3] // LANES
    for at in range(tiles):
        lanes = slice(at * LANES, (at + 1) * LANES)
        weight = mask_ref[0:1, lanes]
        taps_ref[28 * chans : 29 * chans, lanes] = (weight * pool_grad).astype(bf16)
        for branch in range(4):
            hat = (pre_ref[0, branch, :, lanes] - coef(CENTRE + branch)) * coef(INVERSE + branch)
            grad = weight * (
                (coef(GAIN + branch) * coef(INVERSE + branch))
                * (
                    delta_ref[0, branch, :, lanes]
                    - (moment(branch) + hat * moment(8 + branch)) / pixel_total
                )
            )
            if branch == 0:
                taps_ref[0:chans, lanes] = grad.astype(bf16)
                continue
            j, dilation = branch - 1, dilations[branch - 1]
            jump = dilation * columns // LANES
            for b in range(3):
                off = (b - 1) * dilation
                moved = grad
                if off != 0:
                    moved = pltpu.roll(grad, off % LANES, 1)
                    moved = jnp.where(masks[-off], moved, 0.0)
                moved = moved.astype(bf16)
                for a in range(3):
                    tap = 1 + 9 * j + 3 * a + b
                    span = slice(tap * chans, (tap + 1) * chans)
                    target = at + (a - 1) * jump
                    if 0 <= target < tiles:
                        taps_ref[span, target * LANES : (target + 1) * LANES] = moved
                    source = at - (a - 1) * jump
                    if not 0 <= source < tiles:
                        taps_ref[span, lanes] = jnp.zeros((chans, LANES), bf16)


def weight_grads(
    slots, scalars, parts, pool_rows, coef_cols, pre, delta, mask_rows, pixels, columns, half, image_total, after
):
    chans, total = pre.shape[2:]
    depth = pixels.shape[1]
    block = depth // 4
    count = len(slots)

    def cols(slot):
        return pl.BlockSpec((chans, LANES), lambda i, s: (s[4 + slot], 0))

    def own(slot):
        return pl.BlockSpec((1, 4, chans, total), lambda i, s: (s[4 + slot], 0, 0, 0))

    outs = call(
        functools.partial(weight_kernel, columns, image_total, slots),
        "atrous_weight_grad",
        (4,),
        1,
        [
            full(parts.shape),
            full(pool_rows.shape),
            full(mask_rows.shape),
            pl.BlockSpec((total, block), lambda i, s: (0, i)),
        ]
        + [cols(slot) for slot in slots]
        + [own(slot) for slot in slots] * 2,
        (
            pl.BlockSpec((half, block), lambda i, s: (0, i)),
            pl.BlockSpec((half, block), lambda i, s: (0, i)),
            full((29 * chans, total)),
        )
        * count,
        (
            jax.ShapeDtypeStruct((half, depth), bf16),
            jax.ShapeDtypeStruct((half, depth), bf16),
            jax.ShapeDtypeStruct((29 * chans, total), bf16),
        )
        * count,
        [pltpu.VMEM((29 * chans, block), f32), pltpu.VMEM((LANES, LANES), f32)],
        after=after,
        vmem=28 if slots[0] == 3 else 56,
    )(
        scalars,
        parts,
        pool_rows,
        mask_rows,
        pixels,
        *[coef_cols] * count,
        *[pre] * count,
        *[delta] * count,
    )
    return [outs[3 * at : 3 * at + 3] for at in range(count)]


def input_kernel(start, places, scalar_ref, *refs):
    taps, weights, outs = refs[0:4], refs[4:12], refs[12:15]
    all_weights, all_taps, result, weight_sems, tap_sems, out_sems = refs[15:]
    half, depth = weights[0].shape
    block = all_taps.shape[2]
    cut = depth // 2

    def tap_copies(strip):
        copies = []
        lanes = pl.ds(pl.multiple_of(scalar_ref[places[strip]] * block, LANES), block)
        for slot in range(4):
            sel = scalar_ref[slot]
            for which in range(2):
                first = sel * start if which == 0 else (1 - sel) * start
                at = 2 * slot + which
                copies.append(
                    pltpu.make_async_copy(
                        taps[slot].at[pl.ds(pl.multiple_of(first, 16), half), lanes],
                        all_taps.at[strip, pl.ds(at * half, half), :],
                        tap_sems.at[strip, at],
                    )
                )
        return copies

    def weight_copies(part):
        lanes = pl.ds(part * cut, cut)
        return [
            pltpu.make_async_copy(
                weights[at].at[:, lanes],
                all_weights.at[pl.ds(at * half, half), lanes],
                weight_sems.at[part, at],
            )
            for at in range(8)
        ]

    tap_lists = [tap_copies(0), tap_copies(1)]
    weight_lists = [weight_copies(0), weight_copies(1)]
    for copies in (tap_lists[0], weight_lists[0], weight_lists[1], tap_lists[1]):
        for copy in copies:
            copy.start()
    rows = outs[0].shape[0]
    out_lists = [
        [
            pltpu.make_async_copy(result.at[0, pl.ds(0, rows), :], outs[0], out_sems.at[0]),
            pltpu.make_async_copy(result.at[0, pl.ds(rows, rows), :], outs[1], out_sems.at[1]),
        ],
        [pltpu.make_async_copy(result.at[1], outs[2], out_sems.at[2])],
    ]
    for strip in range(2):
        for copy in tap_lists[strip]:
            copy.wait()
        for part in range(2):
            if strip == 0:
                for copy in weight_lists[part]:
                    copy.wait()
            lanes = slice(part * cut, (part + 1) * cut)
            result[strip, :, lanes] = lax.dot_general(
                all_taps[strip],
                all_weights[:, lanes],
                (((0,), (0,)), ((), ())),
                preferred_element_type=f32,
            ).astype(bf16)
        for copy in out_lists[strip]:
            copy.start()
    for copies in out_lists:
        for copy in copies:
            copy.wait()


def input_grads(flip, taps, weights, scalars, block, after):
    rows = taps[0].shape[0]
    half, depth = weights[0].shape
    shapes = ((block // 2, depth), (block // 2, depth), (block, depth))
    anywhere = pl.BlockSpec(memory_space=pl.ANY)
    low, high, own = call(
        functools.partial(input_kernel, rows - half, (HALF + 2 + flip, HALF + 1 + flip)),
        "atrous_input_grad",
        (1,),
        1,
        [anywhere] * 12,
        (anywhere,) * 3,
        tuple(jax.ShapeDtypeStruct(shape, bf16) for shape in shapes),
        [
            pltpu.VMEM((8 * half, depth), bf16),
            pltpu.VMEM((2, 8 * half, block), bf16),
            pltpu.VMEM((2, block, depth), bf16),
            pltpu.SemaphoreType.DMA((2, 8)),
            pltpu.SemaphoreType.DMA((2, 8)),
            pltpu.SemaphoreType.DMA((3,)),
        ],
        after=after,
        vmem=58,
    )(scalars, *taps, *weights)
    return [low, high], own


def local(
    features,
    scale_sizes,
    cotangent,
    branch_weight,
    branch_first,
    branch_second,
    head_weight,
    head_first,
    head_second,
    norm_params,
    norm_first,
    norm_second,
    running_stats,
):
    groups = lax.axis_size("dp")
    halves = groups == 2
    images = scale_sizes.shape[1]
    image_total = float(groups * images)
    x_id, z_id = lax.axis_index("dp"), lax.axis_index("z")
    quad_id = lax.axis_index("y") * 2 + lax.axis_index("c")
    wide_id = z_id * 4 + quad_id
    strip_rows, columns, depth = features.shape[1:]
    strip = strip_rows * columns
    total = 4 * strip
    tap_count, chans = branch_weight.shape[:2]
    all_ch = chans * 16
    split = (tap_count - 1) // 2
    half = (split + 1) * chans
    cells, everyone = ("dp", "z"), ("dp",) + PLANE
    rows = 16 * chans + EXTRA

    def exchange(parts, axes):
        return lax.all_to_all(parts, axes, 0, 0, tiled=True)

    height = lax.dynamic_index_in_dim(scale_sizes[0], z_id, 0, keepdims=False)
    pixel = jnp.arange(total, dtype=jnp.int32)
    inside = jnp.logical_and(pixel // columns < height, pixel % columns < 2 * height).astype(f32)
    own_inside = lax.dynamic_slice_in_dim(inside, quad_id * strip, strip, 0)
    mask_rows = jnp.broadcast_to(inside[None], (8, total))
    strip_mask = jnp.broadcast_to(own_inside[None], (8, strip))

    mid = jnp.logical_and(z_id >= 1, z_id <= 2).astype(jnp.int32)[None]

    sel = x_id.astype(jnp.int32) if halves else jnp.zeros((), jnp.int32)
    outer = z_id >= 2
    scalars = jnp.stack(
        [sel, sel, sel, sel]
        + [z_id, jnp.bitwise_xor(z_id, 1), jnp.where(outer, 1, 2), jnp.where(outer, 0, 3)]
        + [height, sel]
        + [jnp.bitwise_xor(quad_id, flip) for flip in range(4)]
    ).astype(jnp.int32)
    first_group = (x_id == 0).astype(f32)
    norm_cols = jnp.zeros((chans, LANES), f32)
    norm_cols = norm_cols.at[:, GAIN : GAIN + 5].set(jnp.transpose(norm_params[0, :5]))
    norm_cols = norm_cols.at[:, SHIFT : SHIFT + 5].set(jnp.transpose(norm_params[1, :5]))
    norm_cols = norm_cols * first_group
    head_cols = jnp.zeros((chans, LANES), f32).at[:, 2:4].set(jnp.transpose(norm_params[:, 5]))
    head_cols = lax.dynamic_update_slice_in_dim(
        jnp.zeros((all_ch, LANES), f32), head_cols * first_group, wide_id * chans, 0
    )
    def over_groups(block):
        return lax.ppermute(block, "dp", SWAP)

    def along(parts, pairs):
        return [lax.ppermute(part, "z", pairs) for part in parts]

    def hold(parts, after):
        return [held(part, after) for part in parts]

    def pair_of(parts):
        return (parts[0], over_groups(parts[0])) if halves else tuple(parts)

    def pick_all(ones, twos, after):
        return [pick(mid, one, two, after) for one, two in zip(ones, twos)]

    zero = jnp.zeros((), jnp.int32)
    mine_w = cast_half(sel[None], branch_weight, split, ())
    other_w = cast_half(1 - sel[None], branch_weight, split, (mine_w,))
    sending = [mine_w] if halves else [mine_w, other_w]
    near, mid_one = along(sending, PAIR), along(sending, MID)

    own_strip = features[0].reshape(strip, depth)
    masked, *masked_parts = mask_strip(scalars, own_strip, columns, sending)
    low_y, high_y = (lax.ppermute(part, "y", SWAP) for part in masked_parts)
    over_c = lax.ppermute(masked, "c", SWAP)

    own_proj = head_weight.astype(bf16).reshape(chans, 5, 4, 4, chans)
    own_proj = jnp.transpose(own_proj, (0, 3, 2, 1, 4))
    pixel_proj = jnp.pad(
        own_proj[:, :, :, :4].reshape(chans, 4, 16 * chans), ((0, 0), (0, 0), (0, EXTRA))
    ).reshape(chans, 4 * rows)
    shared = jnp.concatenate(
        [
            jnp.broadcast_to(own_proj[:, :, :, 4].reshape(1, chans, all_ch), (16, chans, all_ch)),
            jnp.transpose(cotangent[0].reshape(chans, 16, strip), (1, 0, 2)),
            jnp.broadcast_to(pixel_proj[None], (16, chans, 4 * rows)),
        ],
        axis=2,
    )

    slots = [(mine_w, other_w)]
    near = hold(near, [masked, mask_rows, scalars])
    mid_two = along(near, MID)
    near = pair_of(near)
    mid_one = hold(mid_one, near[:1])
    out_one = along(mid_one, OUTWARD)
    low_y = held(low_y, mid_one)
    mid_two = hold(mid_two, [low_y, other_w, shared, strip_mask, norm_cols, head_cols])
    out_two = along(mid_two, OUTWARD)
    second = pick_all(mid_one, out_one, mid_two)
    second_pair = pair_of(second)
    high_y = held(high_y, second)
    low_yc, high_yc = (lax.ppermute(part, "c", SWAP) for part in (low_y, high_y))
    near = (near[0], held(near[1], (high_y,)))
    slots.append(near)
    parts = ((masked,), (over_c,), (low_y, high_y), (low_yc, high_yc))
    pixels = image_of(scalars, strip, parts, near[1:])

    def branch(slot, state, after):
        return forward_taps(
            slot, pixels, mask_rows, scalars, *slots[slot], state, columns, chans, split, after
        )

    state = branch(0, (), ())
    slots.append((second_pair[0], held(second_pair[1], [state[1]])))
    third = pick_all(mid_two, out_two, slots[2][1:])
    slots.append(pair_of(third))
    shared = exchange(held(shared, third), PLANE)
    shared = shared.reshape(all_ch, all_ch + strip + 4 * rows)
    state = branch(1, state, third)
    state = branch(2, state, ())
    state = branch(3, state, ())
    pre, stats = state
    own_sums = pack_sums(scalars, stats, norm_cols, axes_size(cells), (shared,))
    quad = quad_id.astype(jnp.int32)[None]
    concat, coef_cols, coef_rows = activations(
        quad, exchange(own_sums, cells), own_sums, pre, image_total
    )
    concat = exchange(concat, QUAD).reshape(4 * rows, strip)

    unit, head_sums = project(concat, shared, head_cols, strip_mask, axes_size(everyone))
    head_values, head_delta, head_coefs, head_rows, head_sums = head_norm(
        exchange(head_sums, everyone), unit, shared, strip_mask, coef_rows
    )
    unit_back, concat_back, row_sums, head_moments = unit_backward(
        exchange(head_sums, everyone),
        unit,
        head_delta,
        head_coefs,
        strip_mask,
        coef_rows,
        shared,
    )

    delta, pool_rows, moments = branch_backward(
        exchange(concat_back, QUAD), pre, coef_cols, coef_rows, mask_rows, axes_size(cells), ()
    )
    moments = exchange(moments, cells)

    def weights_of(slots, after):
        return weight_grads(
            slots,
            scalars,
            moments,
            pool_rows,
            coef_cols,
            pre,
            delta,
            mask_rows,
            pixels,
            columns,
            half,
            image_total,
            after,
        )

    def group_sums(slot, after, *lists):
        if halves:
            return [add(slot[0], over_groups(slot[1]), *(parts[0] for parts in lists), after=after)]
        return [add(*parts, after=after) for parts in zip(slot[:2], *lists)]

    def swap_all(parts, axis):
        return [lax.ppermute(part, axis, SWAP) for part in parts]

    def add_all(*lists, after=()):
        return [add(*parts, after=after) for parts in zip(*lists)]

    flat_w = [part for slot in slots for part in slot]

    def features_of(flip, after):
        return input_grads(flip, taps, flat_w, scalars, strip, after)

    ((keep_c, send_c, taps_c),) = weights_of((3,), ())
    head_parts = head_weight_grads(concat, unit_back, row_sums, head_values, (taps_c,))
    head_parts = exchange(head_parts.reshape(16, chans, all_ch + strip + 4 * rows), PLANE)
    slot_b, slot_a, slot_o = weights_of((2, 1, 0), (taps_c,))
    taps = [slot_o[2], slot_a[2], slot_b[2], taps_c]
    third = group_sums((keep_c, send_c), (slot_o[2], head_parts))
    far_cross, far = features_of(2, third)
    mid_two = add_all(third, along(third, INWARD), after=(far,))
    second = group_sums(slot_b, mid_two)
    far = strip_sum(scalars, (far,), swap_all(far_cross, "c"), columns, False, second)
    near = group_sums(slot_a, (far,), along(mid_two, MID))
    mid_one = add_all(second, along(second, INWARD), after=near)

    head_output = head_parts[:, :, all_ch : all_ch + strip]
    head_output = jnp.transpose(head_output, (1, 0, 2)).reshape(1, chans, 16 * strip)
    head_parts = jnp.sum(head_parts.astype(f32), axis=0)
    pool_part = head_parts[:, :all_ch].reshape(chans, 4, 4, 1, chans)
    pixel_part = head_parts[:, all_ch + strip :].reshape(chans, 4, rows)[:, :, : 16 * chans]
    pixel_part = pixel_part.reshape(chans, 4, 4, 4, chans)
    head_grads = jnp.concatenate([pixel_part, pool_part], axis=3)
    head_grads = jnp.transpose(head_grads, (0, 3, 2, 1, 4)).reshape(chans, 5 * all_ch)
    near_cross, own_part = features_of(0, (*mid_one, head_grads))
    if halves:
        head_grads = head_grads + lax.ppermute(head_grads, "dp", SWAP)
    else:
        head_grads = lax.psum(head_grads, "dp")
    mine = group_sums(slot_o, (own_part, head_grads), along(near, PAIR), along(mid_one, MID))
    state = (branch_weight, branch_first, branch_second)
    if halves:
        other = over_groups(mine[0])
    else:
        mine = [lax.psum(part, "dp") for part in mine]
    cross = swap_all(near_cross, "c")
    total = held(own_part, mine).astype(f32) + jnp.concatenate(cross, axis=0).astype(f32)
    total = total + lax.ppermute(far, "y", SWAP).astype(f32)
    input_grad = (total * own_inside[:, None]).astype(bf16)
    input_grad = input_grad.reshape(1, strip_rows, columns, depth)
    start = jnp.stack([sel * split, zero])
    done = adam_taps(start, split + 1, 3, mine[0], *state, (), (input_grad,))
    start = jnp.stack([(1 - sel) * (split + 1), 1 - sel])
    done = adam_taps(start, split, 2, other if halves else mine[1], *state, done, ())
    branch_grads, branch_means, branch_squares, branch_updated = done

    def own_lanes(by_row):
        return lax.dynamic_slice_in_dim(by_row, z_id * chans, chans, 1)

    def own_head(by_row):
        return lax.dynamic_slice_in_dim(by_row, wide_id * chans, chans, 1)

    moments = jnp.sum(moments, axis=0)
    own_firsts, own_seconds = own_lanes(moments), own_lanes(moments[:, 4 * chans :])
    head_own = own_head(head_moments)
    norm_grads = jnp.stack(
        [
            jnp.concatenate([own_seconds[0:5], head_own[1:2]]),
            jnp.concatenate([own_firsts[0:5], head_own[0:1]]),
        ]
    )
    own_coefs, head_stats = own_lanes(coef_rows), own_head(head_rows)
    pixel_total = coef_rows[COUNT, 0]
    all_centres = jnp.concatenate([own_coefs[CENTRE : CENTRE + 5], head_stats[0:1]])
    all_variances = jnp.concatenate([own_coefs[VARIANCE : VARIANCE + 5], head_stats[4:5]])
    factors = jnp.where(
        jnp.arange(6) == 4, image_total / (image_total - 1.0), pixel_total / (pixel_total - 1.0)
    )
    running_next = (1.0 - momentum) * running_stats + momentum * jnp.stack(
        [all_centres, all_variances * factors[:, None]]
    )
    head_means, head_squares, head_updated = adamw_update(
        head_weight, head_grads, head_first, head_second, conv_rate, weight_decay
    )
    norm_means, norm_squares, norm_updated = adamw_update(
        norm_params, norm_grads, norm_first, norm_second, norm_rate, 0.0
    )
    return (
        head_output,
        input_grad,
        branch_grads,
        branch_means,
        branch_squares,
        branch_updated,
        head_grads,
        head_means,
        head_squares,
        head_updated,
        norm_grads,
        norm_means,
        norm_squares,
        norm_updated,
        running_next,
    )


def solution(mesh):
    groups, wide = mesh.devices.shape
    fine = Mesh(mesh.devices.reshape(groups, 4, 2, wide // 8), ("dp",) + PLANE)
    placed = (
        P("dp", PLANE, None, None),
        P("dp", None),
        P("dp", PLANE, None),
        P(None, PLANE, None),
        P(None, PLANE, None),
        P(None, PLANE, None),
        P(PLANE, None),
        P(PLANE, None),
        P(PLANE, None),
        P(None, None, PLANE),
        P(None, None, PLANE),
        P(None, None, PLANE),
        P(None, None, PLANE),
    )
    return jax.shard_map(
        local,
        mesh=fine,
        in_specs=placed,
        out_specs=(
            P("dp", PLANE, None),
            P("dp", PLANE, None, None),
            P(None, PLANE, None),
            P(None, PLANE, None),
            P(None, PLANE, None),
            P(None, PLANE, None),
            P(PLANE, None),
            P(PLANE, None),
            P(PLANE, None),
            P(PLANE, None),
            P(None, None, PLANE),
            P(None, None, PLANE),
            P(None, None, PLANE),
            P(None, None, PLANE),
            P(None, None, PLANE),
        ),
        check_vma=False,
    )
```

```python
import functools

import jax
import jax.numpy as jnp
from jax import lax
from jax.experimental import pallas as pl
from jax.experimental.pallas import tpu as pltpu
from jax.sharding import Mesh, PartitionSpec as P

STEP = 10


dilations = (6, 12, 18)
epsilon = 1e-05
momentum = 0.1
first_decay = 0.9
second_decay = 0.999
conv_rate = 0.02
norm_rate = 0.4
weight_decay = 0.0001
adam_floor = 1e-08

LANES = 128
PLANE = ("z", "y", "c")
QUAD = ("y", "c")
SWAP = [(0, 1), (1, 0)]
PAIR = [(0, 1), (1, 0), (2, 3), (3, 2)]
MID = [(1, 2), (2, 1)]
OUTWARD = [(1, 0), (2, 3)]
INWARD = [(0, 1), (3, 2)]

bf16 = jnp.bfloat16
f32 = jnp.float32
barrier = lax.optimization_barrier


def adamw_update(parameter, gradient, moment_one, moment_two, step_rate, decay_rate):
    first_new = first_decay * moment_one + (1.0 - first_decay) * gradient
    second_new = second_decay * moment_two + (1.0 - second_decay) * gradient * gradient
    first_hat = first_new / (1.0 - first_decay**STEP)
    second_hat = second_new / (1.0 - second_decay**STEP)
    updated = parameter - step_rate * (
        first_hat / (jnp.sqrt(second_hat) + adam_floor) + decay_rate * parameter
    )
    return (first_new, second_new, updated)


def gelu_both(value):
    scale = (2.0 / jnp.pi) ** 0.5
    square = value * value
    bend = jnp.tanh(scale * (value + 0.044715 * (value * square)))
    lead = 0.5 * (1.0 + bend)
    slope = lead + 0.5 * value * (1.0 - bend * bend) * (scale * (1.0 + 3.0 * 0.044715 * square))
    return value * lead, slope


def tall(rows):
    fill = LANES - rows.shape[0]
    return jnp.concatenate([rows, jnp.zeros((fill, rows.shape[1]), rows.dtype)], axis=0).T


def stacked(rows, count):
    found = {}
    for at in range(count):
        found[2 * at] = rows[at : at + 1, :LANES]
        found[2 * at + 1] = rows[at : at + 1, LANES:]
    return put_rows((8, LANES), found)[: 2 * count]


def unstacked(rows):
    found = {}
    for at in range(rows.shape[0] // 2):
        found[at] = jnp.concatenate([rows[2 * at : 2 * at + 1], rows[2 * at + 1 : 2 * at + 2]], axis=1)
    return put_rows((8, 2 * LANES), found)


def beside(left, right, width):
    lane = lax.broadcasted_iota(jnp.int32, left.shape, 1)
    return jnp.where(lane < width, left, pltpu.roll(right, width, 1))


def put_lanes(shape, columns):
    lane = lax.broadcasted_iota(jnp.int32, shape, 1)
    total = jnp.zeros(shape, f32)
    for at, column in columns.items():
        total = jnp.where(lane == at, column, total)
    return total


def put_rows(shape, rows):
    row = lax.broadcasted_iota(jnp.int32, shape, 0)
    total = jnp.zeros(shape, f32)
    for at, value in rows.items():
        total = jnp.where(row == at, value, total)
    return total


def axes_size(axes):
    count = 1
    for axis in axes:
        count *= lax.axis_size(axis)
    return count


def call(
    kernel,
    name,
    grid,
    scalars,
    in_specs,
    out_specs,
    out_shape,
    scratch=(),
    aliases=None,
    flops=0,
    after=(),
    vmem=24,
):
    after = tuple(after)
    first = scalars + len(in_specs)

    def body(*refs):
        kernel(*refs[:first], *refs[first + len(after) :])

    run = pl.pallas_call(
        body,
        out_shape=out_shape,
        grid_spec=pltpu.PrefetchScalarGridSpec(
            num_scalar_prefetch=scalars,
            grid=grid,
            in_specs=list(in_specs) + [pl.BlockSpec(memory_space=pl.ANY)] * len(after),
            out_specs=out_specs,
            scratch_shapes=list(scratch),
        ),
        input_output_aliases=aliases or {},
        compiler_params=pltpu.CompilerParams(vmem_limit_bytes=vmem << 20),
        cost_estimate=pl.CostEstimate(flops=1, bytes_accessed=1, transcendentals=0),
        name=name,
    )
    return lambda *arrays: run(*arrays, *after)


def full(shape):
    return pl.BlockSpec(shape, lambda *_: (0,) * len(shape))


def add_kernel(*refs):
    total = refs[0][...].astype(f32)
    for ref in refs[1:-1]:
        total = total + ref[...].astype(f32)
    refs[-1][...] = total.astype(bf16)


def add(*values, after=()):
    first = held(values[0], after) if after else values[0]
    total = first.astype(f32)
    for value in values[1:]:
        total = total + value.astype(f32)
    return barrier(total.astype(bf16))


def pick_kernel(flag_ref, one_ref, two_ref, out_ref):
    @pl.when(flag_ref[0] == 1)
    def _():
        out_ref[...] = one_ref[...]

    @pl.when(flag_ref[0] != 1)
    def _():
        out_ref[...] = two_ref[...]


def pick(flag, one, two, after=()):
    rows, depth = one.shape
    spec = pl.BlockSpec((rows // 3, depth), lambda i, s: (i, 0))
    return call(
        pick_kernel,
        "pick",
        (3,),
        1,
        [spec, spec],
        spec,
        jax.ShapeDtypeStruct(one.shape, one.dtype),
        after=after,
    )(flag, one, two)


def held_kernel(in_ref, out_ref):
    del in_ref, out_ref


def held(value, after):
    anywhere = pl.BlockSpec(memory_space=pl.ANY)
    return call(
        held_kernel,
        "held",
        (1,),
        0,
        [anywhere],
        anywhere,
        jax.ShapeDtypeStruct(value.shape, value.dtype),
        aliases={0: 0},
        after=after,
        vmem=56,
    )(value)


def cast_kernel(sel_ref, in_ref, out_ref):
    taps, chans = in_ref.shape[:2]
    first = jnp.logical_and(sel_ref[0] == 1, pl.program_id(0) == 0)
    for tap in range(taps):
        value = in_ref[tap]
        if tap == 0:
            value = jnp.where(first, 0.0, value)
        out_ref[tap * chans : (tap + 1) * chans, :] = value.astype(bf16)


def cast_half(sel, weight, split, after):
    chans, depth = weight.shape[1:]
    parts = 3 if (split + 1) % 3 == 0 else 1
    block = (split + 1) // parts
    return call(
        cast_kernel,
        "cast",
        (parts,),
        1,
        [pl.BlockSpec((pl.Element(block), pl.Element(chans), pl.Element(depth)), lambda i, s: (s[0] * split + i * block, 0, 0))],
        pl.BlockSpec((block * chans, depth), lambda i, s: (i, 0)),
        jax.ShapeDtypeStruct(((split + 1) * chans, depth), bf16),
        after=after,
        vmem=56,
    )(sel, weight)


def mask_kernel(columns, scalar_ref, in_ref, out_ref, *part_refs):
    rows, depth = in_ref.shape
    pixel = lax.broadcasted_iota(jnp.int32, (rows, LANES), 0)
    row = pixel // columns + scalar_ref[HALF + 1] * (rows // columns)
    height = scalar_ref[HEIGHT]
    inside = jnp.logical_and(row < height, pixel % columns < 2 * height)
    for first in range(0, depth, LANES):
        lanes = slice(first, first + LANES)
        value = jnp.where(inside, in_ref[:, lanes].astype(f32), 0.0).astype(bf16)
        out_ref[:, lanes] = value
        start = 0
        for part_ref in part_refs:
            size = part_ref.shape[0]
            part_ref[:, lanes] = value[start : start + size]
            start += size


def mask_strip(scalars, strip, columns, after):
    rows, depth = strip.shape
    low = rows // 16 * 7
    shapes = ((rows, depth), (low, depth), (rows - low, depth))
    return call(
        functools.partial(mask_kernel, columns),
        "mask",
        (1,),
        1,
        [full((rows, depth))],
        tuple(full(shape) for shape in shapes),
        tuple(jax.ShapeDtypeStruct(shape, bf16) for shape in shapes),
        after=after,
        vmem=56,
    )(scalars, strip)


def image_kernel(strip, places, spot_ref, *refs):
    *parts, out_ref, sems = refs
    copies = []
    for at, (which, first) in enumerate(places):
        rows = pl.ds(pl.multiple_of(spot_ref[HALF + 1 + which] * strip + first, 16), parts[at].shape[0])
        copies.append(pltpu.make_async_copy(parts[at], out_ref.at[rows, :], sems.at[at]))
    for copy in copies:
        copy.start()
    for copy in copies:
        copy.wait()


def image_of(spots, strip, parts, after):
    depth = parts[0][0].shape[1]
    places = []
    for which, strip_parts in enumerate(parts):
        first = 0
        for part in strip_parts:
            places.append((which, first))
            first += part.shape[0]
    flat = [part for strip_parts in parts for part in strip_parts]
    anywhere = pl.BlockSpec(memory_space=pl.ANY)
    return call(
        functools.partial(image_kernel, strip, places),
        "image",
        (1,),
        1,
        [anywhere] * len(flat),
        full((4 * strip, depth)),
        jax.ShapeDtypeStruct((4 * strip, depth), bf16),
        [pltpu.SemaphoreType.DMA((len(flat),))],
        after=after,
        vmem=56,
    )(spots, *flat)


def head_grad_kernel(x_ref, back_ref, sum_ref, value_ref, out_ref):
    channels = back_ref.shape[0]
    rows = x_ref.shape[0] // 4
    act = jnp.zeros((EXTRA, channels), f32)
    for quad in range(4):
        first = quad * rows + rows - EXTRA
        act = act + x_ref[first : first + EXTRA, :channels].astype(f32)
    out_ref[:, :channels] = (sum_ref[:, 0:1] * act[0:1, :]).astype(bf16)
    strip = x_ref.shape[1]
    out_ref[:, channels : channels + strip] = value_ref[...]
    out_ref[:, channels + strip :] = lax.dot_general(
        back_ref[...], x_ref[...], (((1,), (1,)), ((), ())), preferred_element_type=f32
    ).astype(bf16)


def head_weight_grads(concat, unit_back, row_sums, values, after):
    channels = unit_back.shape[0]
    arrays = (concat, unit_back, row_sums, values)
    shape = (channels, channels + concat.shape[1] + concat.shape[0])
    return call(
        head_grad_kernel,
        "head_weight_grad",
        (1,),
        0,
        [full(array.shape) for array in arrays],
        full(shape),
        jax.ShapeDtypeStruct(shape, bf16),
        after=after,
        vmem=24,
    )(*arrays)


def strip_sum_kernel(columns, whole, masked, scalar_ref, *refs):
    block = refs[0].shape[0]
    step = pl.program_id(0)
    rows_all = refs[whole].shape[0] * (len(refs) - 1 - whole)
    pixel = step * block + lax.broadcasted_iota(jnp.int32, (block, LANES), 0)
    row = pixel // columns + scalar_ref[HALF + 1] * (rows_all // columns)
    height = scalar_ref[HEIGHT]
    inside = jnp.logical_and(row < height, pixel % columns < 2 * height)
    steps = refs[whole].shape[0] * (len(refs) - 1 - whole) // block
    count = steps // (len(refs) - 1 - whole)
    for at in range(steps):

        @pl.when(step == at)
        def _():
            part = refs[whole + at // count]
            rows = slice(at % count * block, (at % count + 1) * block)
            for first in range(0, refs[0].shape[1], LANES):
                lanes = slice(first, first + LANES)
                total = part[rows, lanes].astype(f32)
                for ref in refs[:whole]:
                    total = total + ref[:, lanes].astype(f32)
                if masked:
                    total = jnp.where(inside, total, 0.0)
                refs[-1][:, lanes] = total.astype(bf16)


def strip_sum(scalars, strips, parts, columns, masked, after):
    rows, depth = strips[0].shape
    spec = pl.BlockSpec((rows // 2, depth), lambda i, s: (i, 0))
    return call(
        functools.partial(strip_sum_kernel, columns, len(strips), masked),
        "strip_sum",
        (2,),
        1,
        [spec] * len(strips) + [full(part.shape) for part in parts],
        spec,
        jax.ShapeDtypeStruct((rows, depth), bf16),
        after=after,
        vmem=56,
    )(scalars, *strips, *parts)


def adam_kernel(start_ref, grad_ref, weight_ref, first_ref, second_ref, *rest):
    out_ref, mean_ref, square_ref, new_ref = rest[-4:]
    grad = grad_ref[...].astype(f32).reshape(out_ref.shape)
    mean, square, new = adamw_update(
        weight_ref[...], grad, first_ref[...], second_ref[...], conv_rate, weight_decay
    )
    out_ref[...] = grad
    mean_ref[...] = mean
    square_ref[...] = square
    new_ref[...] = new


def adam_taps(start, count, block, grads, weight, first, second, earlier, after):
    taps, chans, depth = weight.shape

    def piece(size, index):
        return pl.BlockSpec(tuple(pl.Element(n) for n in size), index)

    spec = piece((block, chans, depth), lambda i, s: (s[0] + i * block, 0, 0))
    anywhere = [pl.BlockSpec(memory_space=pl.ANY)] * len(earlier)
    return call(
        adam_kernel,
        "adamw",
        (count // block,),
        1,
        [piece((block * chans, depth), lambda i, s: ((s[1] + i * block) * chans, 0))]
        + [spec] * 3
        + anywhere,
        (spec,) * 4,
        (jax.ShapeDtypeStruct(weight.shape, f32),) * 4,
        aliases={5 + at: at for at in range(4)} if earlier else None,
        after=after,
        vmem=20,
    )(start, grads, weight, first, second, *earlier)


FIRST, SECOND, GAIN, SHIFT, AREA = 0, 8, 16, 24, 5
SUM_ROWS = 8
CENTRE, INVERSE, VARIANCE, COUNT, POOLED = 0, 8, 32, 40, 41
COEF_ROWS = 48
EXTRA = 16
TERMS = 64
HEIGHT, HALF = 8, 9


def lane_masks(columns):
    lane = lax.broadcasted_iota(jnp.int32, (1, LANES), 1) % columns
    masks = {}
    for dilation in dilations:
        for off in (-dilation, dilation):
            moved = lane + off
            masks[off] = jnp.logical_and(moved >= 0, moved < columns)
    return masks


def forward_kernel(columns, split, slot, scalar_ref, x_ref, wz_ref, wx_ref, mask_ref, *rest):
    pre_ref, stat_ref, taps = rest[-3:]
    step = pl.program_id(0)
    half = wz_ref.shape[0]
    block = x_ref.shape[0]
    sel = scalar_ref[slot]
    contract = (((1,), (1,)), ((), ()))
    pixels = x_ref[...]
    cols = pl.ds(pl.multiple_of(step * block, block), block)
    taps[pl.ds(pl.multiple_of(sel * half, 16), half), cols] = lax.dot_general(
        wz_ref[...], pixels, contract, preferred_element_type=f32
    )
    taps[pl.ds(pl.multiple_of((1 - sel) * half, 16), half), cols] = lax.dot_general(
        wx_ref[...], pixels, contract, preferred_element_type=f32
    )

    @pl.when(step == pl.num_programs(0) - 1)
    def _():
        total = taps.shape[1]
        tiles = total // LANES
        chans = pre_ref.shape[2]
        masks = lane_masks(columns)

        def rows_of(tap):
            first = tap * chans if tap <= split else (tap + 1) * chans
            return slice(first, first + chans)

        def tile(tap, at):
            return taps[rows_of(tap), at * LANES : (at + 1) * LANES]

        sums = [jnp.zeros((chans, LANES), f32) for _ in range(4)]
        squares = [jnp.zeros((chans, LANES), f32) for _ in range(4)]
        pooled = jnp.zeros((chans, LANES), f32)
        for at in range(tiles):
            lanes = slice(at * LANES, (at + 1) * LANES)
            weight = mask_ref[0:1, lanes]
            for branch in range(4):
                if branch == 0:
                    value = tile(0, at)
                else:
                    dilation = dilations[branch - 1]
                    jump = dilation * columns // LANES
                    value = None
                    for b in range(3):
                        part = None
                        for a in range(3):
                            source = at + (a - 1) * jump
                            if 0 <= source < tiles:
                                term = tile(1 + 9 * (branch - 1) + 3 * a + b, source)
                                part = term if part is None else part + term
                        off = (b - 1) * dilation
                        if off != 0:
                            part = pltpu.roll(part, (-off) % LANES, 1)
                            part = jnp.where(masks[off], part, 0.0)
                        value = part if value is None else value + part
                pre_ref[0, branch, :, lanes] = value
                weighted = value * weight
                sums[branch] = sums[branch] + weighted
                squares[branch] = squares[branch] + weighted * value
            pooled = pooled + tile(28, at)
        height = jnp.full((1, 1), scalar_ref[HEIGHT], jnp.int32).astype(f32)
        area = 2.0 * height * height
        pool = jnp.sum(pooled, axis=1, keepdims=True) / area
        columns_of = {FIRST + 4: pool, SECOND + 4: pool * pool, AREA: area}
        for branch in range(4):
            columns_of[FIRST + branch] = jnp.sum(sums[branch], axis=1, keepdims=True)
            columns_of[SECOND + branch] = jnp.sum(squares[branch], axis=1, keepdims=True)
        stat_ref[0] = put_lanes((chans, LANES), columns_of)


def forward_taps(slot, pixels, mask_rows, scalars, wz, wx, earlier, columns, chans, split, after):
    total, depth = pixels.shape
    block = total // 4
    half = wz.shape[0]
    keep = [pl.BlockSpec(memory_space=pl.ANY)] * len(earlier)
    return call(
        functools.partial(forward_kernel, columns, split, slot),
        "atrous_forward",
        (4,),
        1,
        [
            pl.BlockSpec((block, depth), lambda i, s: (i, 0)),
            full((half, depth)),
            full((half, depth)),
            full((8, total)),
        ]
        + keep,
        (
            pl.BlockSpec((1, 4, chans, total), lambda i, s: (s[4 + slot], 0, 0, 0)),
            pl.BlockSpec((1, chans, LANES), lambda i, s: (s[4 + slot], 0, 0)),
        ),
        (
            jax.ShapeDtypeStruct((4, 4, chans, total), f32),
            jax.ShapeDtypeStruct((4, chans, LANES), f32),
        ),
        [pltpu.VMEM((2 * half, total), f32)],
        {5: 0, 6: 1} if earlier else None,
        4 * half * total * depth,
        after,
        56,
    )(scalars, pixels, wz, wx, mask_rows, *earlier)


def pack_kernel(stat_ref, out_ref, work):
    chans = stat_ref.shape[1]
    work[...] = jnp.zeros_like(work)
    for z in range(4):
        work[z * chans : (z + 1) * chans, :] = stat_ref[z]
    rows = work[...].T
    rows = beside(rows[:8], rows[8:16], 4 * chans)
    for at in range(out_ref.shape[0]):
        out_ref[at] = rows


def pack_sums(stats, count, after):
    return call(
        pack_kernel,
        "branch_sums",
        (1,),
        0,
        [full(stats.shape)],
        full((count, SUM_ROWS, LANES)),
        jax.ShapeDtypeStruct((count, SUM_ROWS, LANES), f32),
        [pltpu.VMEM((LANES, LANES), f32)],
        after=after,
        vmem=24,
    )(stats)


def term_sum(block, which, norm, start):
    first = start + 3 * (6 * which + norm)
    return block[:, first : first + 1] + block[:, first + 1 : first + 2] + block[:, first + 2 : first + 3]


def pool_rows_of(rows_ref, own_width):
    def row(at):
        return rows_ref[at : at + 1, :]

    moved = row(POOLED) - row(CENTRE + 4)
    normed = row(GAIN + 4) * moved * row(INVERSE + 4) + row(SHIFT + 4)
    lane = lax.broadcasted_iota(jnp.int32, normed.shape, 1)
    return normed, moved * row(INVERSE + 4), lane < own_width


def act_kernel(image_total, quad_ref, parts_ref, own_ref, term_ref, pre_ref, out_ref, col_ref, row_ref):
    chans = pre_ref.shape[2]

    @pl.when(pl.program_id(0) == 0)
    def _():
        sums = jnp.sum(parts_ref[...], axis=0)
        second = pltpu.roll(sums, LANES - 4 * chans, 1)
        found = []
        for z in range(4):
            place = pl.multiple_of((4 * z + quad_ref[0]) * chans, chans)
            block = term_ref[pl.ds(place, chans), :].astype(f32)
            columns = {}
            for norm in range(5):
                columns[norm] = term_sum(block, 0, norm, LANES - TERMS)
                columns[8 + norm] = term_sum(block, 1, norm, LANES - TERMS)
            found.append(put_lanes((chans, LANES), columns))
        found.append(jnp.zeros((LANES - 4 * chans, LANES), f32))
        affine = jnp.concatenate(found, axis=0).T
        pixel_total = jnp.maximum(sums[AREA : AREA + 1], 1.0)
        index = lax.broadcasted_iota(jnp.int32, (8, LANES), 0)
        count = jnp.where(index == 4, image_total, pixel_total)
        centre = sums / count
        variance = second / count - centre * centre
        inverse = lax.rsqrt(variance + epsilon)
        other = jnp.where(index == 0, pixel_total, jnp.where(index == 1, own_ref[0, 4:5, :], 0.0))
        rows = jnp.concatenate(
            [centre, inverse, affine[:8], affine[8:16], variance, other],
            axis=0,
        )
        row_ref[...] = rows
        col_ref[...] = tall(rows)

    for z in range(4):
        span = slice(z * chans, (z + 1) * chans)
        for branch in range(4):
            moved = pre_ref[z, branch] - col_ref[span, CENTRE + branch : CENTRE + branch + 1]
            normed = (
                col_ref[span, GAIN + branch : GAIN + branch + 1]
                * moved
                * col_ref[span, INVERSE + branch : INVERSE + branch + 1]
                + col_ref[span, SHIFT + branch : SHIFT + branch + 1]
            )
            first = (4 * z + branch) * chans
            out_ref[0, first : first + chans, :] = gelu_both(normed)[0].astype(bf16)
    normed, _, valid = pool_rows_of(row_ref, 4 * chans)
    act = jnp.where(valid, gelu_both(normed)[0], 0.0)
    act = put_rows((EXTRA, LANES), {0: act + pltpu.roll(act, 4 * chans, 1)})
    lane = lax.broadcasted_iota(jnp.int32, act.shape, 1)
    for at in range(out_ref.shape[2] // LANES):
        owner = (lane + at * LANES) // (4 * chans)
        out_ref[0, 16 * chans :, at * LANES : (at + 1) * LANES] = jnp.where(
            owner == quad_ref[0], act, 0.0
        ).astype(bf16)


def activations(quad, parts, own, shared, pre, image_total):
    chans, total = pre.shape[2:]
    strip = total // 4
    rows = 16 * chans + EXTRA
    return call(
        functools.partial(act_kernel, image_total),
        "branch_act",
        (4,),
        1,
        [
            full(parts.shape),
            full((1, SUM_ROWS, LANES)),
            pl.BlockSpec((shared.shape[0], LANES), lambda i, s: (0, shared.shape[1] // LANES - 1)),
            pl.BlockSpec((4, 4, chans, strip), lambda i, s: (0, 0, 0, i)),
        ],
        (
            pl.BlockSpec((1, rows, strip), lambda i, s: (i, 0, 0)),
            full((LANES, LANES)),
            full((COEF_ROWS, LANES)),
        ),
        (
            jax.ShapeDtypeStruct((4, rows, strip), bf16),
            jax.ShapeDtypeStruct((LANES, LANES), f32),
            jax.ShapeDtypeStruct((COEF_ROWS, LANES), f32),
        ),
        vmem=24,
    )(quad, parts, own, shared, pre)


def unit_kernel(x_ref, shared_ref, mask_ref, unit_ref, out_ref):
    channels = shared_ref.shape[0]
    rows, strip = x_ref.shape[0] // 4, x_ref.shape[1]
    proj = shared_ref[:, channels + strip : shared_ref.shape[1] - TERMS]
    unit = jnp.dot(proj, x_ref[...], preferred_element_type=f32)
    act = jnp.zeros((EXTRA, channels), f32)
    for quad in range(4):
        first = quad * rows + rows - EXTRA
        act = act + x_ref[first : first + EXTRA, :channels].astype(f32)
    bias = shared_ref[:, :channels].astype(f32) * act[0:1, :]
    unit = unit + jnp.sum(bias, axis=1, keepdims=True)
    unit_ref[...] = unit
    weighted = unit * mask_ref[0:1, :]
    one = jnp.sum(weighted, axis=1, keepdims=True)
    two = jnp.sum(weighted * unit, axis=1, keepdims=True)
    sums = put_lanes((channels, LANES), {0: one, 1: two}).T[:8]
    sums = stacked(sums, 2)
    for at in range(out_ref.shape[0]):
        out_ref[at] = sums


def project(concat, shared, strip_mask, count):
    channels, strip = shared.shape[0], concat.shape[1]
    arrays = (concat, shared, strip_mask)
    return call(
        unit_kernel,
        "projection",
        (1,),
        0,
        [full(array.shape) for array in arrays],
        (full((channels, strip)), full((count, 4, LANES))),
        (
            jax.ShapeDtypeStruct((channels, strip), f32),
            jax.ShapeDtypeStruct((count, 4, LANES), f32),
        ),
        vmem=24,
    )(*arrays)


def head_kernel(parts_ref, unit_ref, shared_ref, mask_ref, row_ref, value_ref, delta_ref, col_ref, head_ref, out_ref):
    sums = unstacked(jnp.sum(parts_ref[...], axis=0))
    pixel_total = row_ref[COUNT : COUNT + 1, 0:1]
    centre = sums[0:1] / pixel_total
    variance = sums[1:2] / pixel_total - centre * centre
    inverse = lax.rsqrt(variance + epsilon)
    rows = put_rows(
        sums.shape, {0: centre, 1: inverse, 4: variance}
    )
    head_ref[...] = rows
    columns = tall(rows)
    width = shared_ref.shape[1]
    block = shared_ref[:, width - LANES :].astype(f32)
    lane = lax.broadcasted_iota(jnp.int32, columns.shape, 1)
    gain = term_sum(block, 0, 5, LANES - TERMS)
    shift = term_sum(block, 1, 5, LANES - TERMS)
    columns = jnp.where(lane == 2, gain, jnp.where(lane == 3, shift, columns))
    col_ref[...] = columns
    hat = (unit_ref[...] - columns[:, 0:1]) * columns[:, 1:2]
    normed = columns[:, 2:3] * hat + columns[:, 3:4]
    value, slope = gelu_both(normed)
    weight = mask_ref[0:1, :]
    value_ref[...] = (weight * value).astype(bf16)
    first = unit_ref.shape[0]
    cot = shared_ref[:, first : first + unit_ref.shape[1]].astype(f32)
    delta = slope * (weight * cot)
    delta_ref[...] = delta
    sums = put_lanes(
        columns.shape,
        {
            0: jnp.sum(delta, axis=1, keepdims=True),
            1: jnp.sum(delta * hat, axis=1, keepdims=True),
        },
    ).T[:8]
    sums = stacked(sums, 2)
    for at in range(out_ref.shape[0]):
        out_ref[at] = sums


def head_norm(parts, unit, shared, strip_mask, coef_rows):
    channels, strip = unit.shape
    count = parts.shape[0]
    return call(
        head_kernel,
        "head_norm",
        (1,),
        0,
        [full(parts.shape), full(unit.shape), full(shared.shape), full((8, strip)), full(coef_rows.shape)],
        (
            full((channels, strip)),
            full((channels, strip)),
            full((channels, LANES)),
            full((8, channels)),
            full((count, 4, LANES)),
        ),
        (
            jax.ShapeDtypeStruct((channels, strip), bf16),
            jax.ShapeDtypeStruct((channels, strip), f32),
            jax.ShapeDtypeStruct((channels, LANES), f32),
            jax.ShapeDtypeStruct((8, channels), f32),
            jax.ShapeDtypeStruct((count, 4, LANES), f32),
        ),
        vmem=24,
    )(parts, unit, shared, strip_mask, coef_rows)


def unit_back_kernel(
    parts_ref, unit_ref, delta_ref, col_ref, mask_ref, row_ref, shared_ref, back_ref, out_ref, sum_ref, moment_ref
):
    sums = unstacked(jnp.sum(parts_ref[...], axis=0))
    moment_ref[...] = sums
    moments = tall(sums)
    pixel_total = row_ref[COUNT : COUNT + 1, 0:1]
    inverse = col_ref[:, 1:2]
    hat = (unit_ref[...] - col_ref[:, 0:1]) * inverse
    back = mask_ref[0:1, :] * (
        (col_ref[:, 2:3] * inverse)
        * (delta_ref[...] - (moments[:, 0:1] + hat * moments[:, 1:2]) / pixel_total)
    )
    back = back.astype(bf16)
    back_ref[...] = back
    row_sums = jnp.sum(back.astype(f32), axis=1, keepdims=True)
    sum_ref[...] = jnp.broadcast_to(row_sums, sum_ref.shape)
    channels = shared_ref.shape[0]
    rows, width = out_ref.shape[1:]
    proj = shared_ref[:, channels + width : shared_ref.shape[1] - TERMS]
    terms = lax.dot_general(
        proj, back, (((0,), (0,)), ((), ())), preferred_element_type=f32
    )
    pool = jnp.sum(shared_ref[:, :channels].astype(f32) * row_sums, axis=0, keepdims=True)
    own = channels // 4
    for quad in range(4):
        first = quad * own // LANES * LANES
        part = pool[:, first : first + LANES]
        if quad * own != first:
            part = pltpu.roll(part, LANES - (quad * own - first), 1)
        lane = lax.broadcasted_iota(jnp.int32, part.shape, 1)
        part = jnp.where(lane < own, part, 0.0)
        high = part.astype(bf16).astype(f32)
        extra = put_rows((EXTRA, LANES), {0: high, 1: part - high})
        out_ref[quad, : rows - EXTRA, :] = terms[quad * rows : (quad + 1) * rows - EXTRA].astype(bf16)
        out_ref[quad, rows - EXTRA :, :LANES] = extra.astype(bf16)
        out_ref[quad, rows - EXTRA :, LANES:] = jnp.zeros((EXTRA, width - LANES), bf16)


def unit_backward(parts, unit, delta, cols, strip_mask, coef_rows, shared):
    channels, strip = unit.shape
    rows = (shared.shape[1] - channels - strip - TERMS) // 4
    arrays = (parts, unit, delta, cols, strip_mask, coef_rows, shared)
    return call(
        unit_back_kernel,
        "unit_back",
        (1,),
        0,
        [full(array.shape) for array in arrays],
        (
            full((channels, strip)),
            full((4, rows, strip)),
            full((channels, LANES)),
            full((8, channels)),
        ),
        (
            jax.ShapeDtypeStruct((channels, strip), bf16),
            jax.ShapeDtypeStruct((4, rows, strip), bf16),
            jax.ShapeDtypeStruct((channels, LANES), f32),
            jax.ShapeDtypeStruct((8, channels), f32),
        ),
        vmem=24,
    )(*arrays)


def branch_kernel(x_ref, pre_ref, col_ref, row_ref, mask_ref, delta_ref, pool_ref, out_ref, sums, pooled):
    step = pl.program_id(0)
    chans = pre_ref.shape[2]

    @pl.when(step == 0)
    def _():
        sums[...] = jnp.zeros_like(sums)
        pooled[...] = jnp.zeros_like(pooled)

    def fold(value):
        total = value[:, :LANES]
        for at in range(1, value.shape[1] // LANES):
            total = total + value[:, at * LANES : (at + 1) * LANES]
        return total

    weight = mask_ref[0:1, :]
    for z in range(4):
        span = slice(z * chans, (z + 1) * chans)
        for branch in range(4):
            first = (4 * z + branch) * chans
            hat = (
                pre_ref[z, branch] - col_ref[span, CENTRE + branch : CENTRE + branch + 1]
            ) * col_ref[span, INVERSE + branch : INVERSE + branch + 1]
            normed = (
                col_ref[span, GAIN + branch : GAIN + branch + 1] * hat
                + col_ref[span, SHIFT + branch : SHIFT + branch + 1]
            )
            delta = gelu_both(normed)[1] * (
                weight * x_ref[0, first : first + chans, :].astype(f32)
            )
            delta_ref[z, branch] = delta
            sums[8 * z + branch] = sums[8 * z + branch] + fold(delta)
            sums[8 * z + 4 + branch] = sums[8 * z + 4 + branch] + fold(delta * hat)
    extra = x_ref[0, 16 * chans :, :LANES].astype(f32)
    pooled[...] = pooled[...] + jnp.broadcast_to(extra[0:1] + extra[1:2], pooled.shape)

    @pl.when(step == pl.num_programs(0) - 1)
    def _():
        normed, hat, valid = pool_rows_of(row_ref, 4 * chans)
        delta = jnp.where(valid, gelu_both(normed)[1] * pooled[0:1, :], 0.0)
        hat = jnp.where(valid, hat, 0.0)
        pool_ref[...] = put_rows(pool_ref.shape, {0: delta, 1: hat})
        found = []
        for z in range(4):
            columns = {}
            for branch in range(4):
                columns[branch] = jnp.sum(sums[8 * z + branch], axis=1, keepdims=True)
                columns[8 + branch] = jnp.sum(sums[8 * z + 4 + branch], axis=1, keepdims=True)
            found.append(put_lanes((chans, LANES), columns))
        found.append(jnp.zeros((LANES - 4 * chans, LANES), f32))
        rows = jnp.concatenate(found, axis=0).T[:16]
        index = lax.broadcasted_iota(jnp.int32, rows.shape, 0)
        rows = jnp.where(index == 4, delta, jnp.where(index == 12, delta * hat, rows))
        rows = beside(rows[:8], rows[8:16], 4 * chans)
        for at in range(out_ref.shape[0]):
            out_ref[at] = rows


def branch_backward(concat_back, pre, coef_cols, coef_rows, mask_rows, count, after):
    chans, total = pre.shape[2:]
    rows, strip = concat_back.shape[1:]
    spread = pl.BlockSpec((4, 4, chans, strip), lambda i: (0, 0, 0, i))
    return call(
        branch_kernel,
        "branch_back",
        (4,),
        0,
        [
            pl.BlockSpec((1, rows, strip), lambda i: (i, 0, 0)),
            spread,
            full(coef_cols.shape),
            full(coef_rows.shape),
            pl.BlockSpec((8, strip), lambda i: (0, i)),
        ],
        (spread, full((8, LANES)), full((count, 8, LANES))),
        (
            jax.ShapeDtypeStruct(pre.shape, f32),
            jax.ShapeDtypeStruct((8, LANES), f32),
            jax.ShapeDtypeStruct((count, 8, LANES), f32),
        ),
        [pltpu.VMEM((32, chans, LANES), f32), pltpu.VMEM((8, LANES), f32)],
        after=after,
        vmem=24,
    )(concat_back, pre, coef_cols, coef_rows, mask_rows)


def weight_kernel(columns, image_total, slots, scalar_ref, parts_ref, pool_ref, mask_ref, x_ref, *refs):
    count = len(slots)
    col_refs, pre_refs, delta_refs = refs[:count], refs[count : 2 * count], refs[2 * count : 3 * count]
    outs = refs[3 * count : 6 * count]
    total_ref, moments = refs[6 * count :]
    half = outs[0].shape[0]
    chans = pre_refs[0].shape[2]
    start = 29 * chans - half
    sel = scalar_ref[HALF]

    @pl.when(pl.program_id(0) == 0)
    def _():
        sums = jnp.sum(parts_ref[...], axis=0)
        second = pltpu.roll(sums, LANES // 2, 1)
        moments[...] = tall(jnp.concatenate([sums, second, pool_ref[...]], axis=0))
        height = jnp.full((1, 1), scalar_ref[HEIGHT], jnp.int32).astype(f32)
        area = 2.0 * height * height
        masks = lane_masks(columns)
        for at, slot in enumerate(slots):
            own = moments[pl.ds(pl.multiple_of(scalar_ref[4 + slot] * chans, chans), chans), :]
            build_taps(
                own, col_refs[at][...], pre_refs[at], delta_refs[at], mask_ref, outs[3 * at + 2], masks, area, columns, image_total
            )

    for at in range(count):
        keep_ref, send_ref, taps_ref = outs[3 * at : 3 * at + 3]
        total_ref[...] = jnp.dot(taps_ref[...], x_ref[...], preferred_element_type=f32)
        keep_ref[...] = total_ref[pl.ds(pl.multiple_of(sel * start, 16), half), :].astype(bf16)
        send_ref[...] = total_ref[pl.ds(pl.multiple_of((1 - sel) * start, 16), half), :].astype(bf16)


def build_taps(own, coefs, pre_ref, delta_ref, mask_ref, taps_ref, masks, area, columns, image_total):
    chans = pre_ref.shape[2]

    def coef(at):
        return coefs[:, at : at + 1]

    def moment(at):
        return own[:, at : at + 1]

    pixel_total = coef(COUNT)
    pool_grad = (
        coef(GAIN + 4)
        * coef(INVERSE + 4)
        * (moment(16) - (moment(4) + moment(17) * moment(12)) / image_total)
    ) / area
    tiles = pre_ref.shape[3] // LANES
    for at in range(tiles):
        lanes = slice(at * LANES, (at + 1) * LANES)
        weight = mask_ref[0:1, lanes]
        taps_ref[28 * chans : 29 * chans, lanes] = (weight * pool_grad).astype(bf16)
        for branch in range(4):
            hat = (pre_ref[0, branch, :, lanes] - coef(CENTRE + branch)) * coef(INVERSE + branch)
            grad = weight * (
                (coef(GAIN + branch) * coef(INVERSE + branch))
                * (
                    delta_ref[0, branch, :, lanes]
                    - (moment(branch) + hat * moment(8 + branch)) / pixel_total
                )
            )
            if branch == 0:
                taps_ref[0:chans, lanes] = grad.astype(bf16)
                continue
            j, dilation = branch - 1, dilations[branch - 1]
            jump = dilation * columns // LANES
            for b in range(3):
                off = (b - 1) * dilation
                moved = grad
                if off != 0:
                    moved = pltpu.roll(grad, off % LANES, 1)
                    moved = jnp.where(masks[-off], moved, 0.0)
                moved = moved.astype(bf16)
                for a in range(3):
                    tap = 1 + 9 * j + 3 * a + b
                    span = slice(tap * chans, (tap + 1) * chans)
                    target = at + (a - 1) * jump
                    if 0 <= target < tiles:
                        taps_ref[span, target * LANES : (target + 1) * LANES] = moved
                    source = at - (a - 1) * jump
                    if not 0 <= source < tiles:
                        taps_ref[span, lanes] = jnp.zeros((chans, LANES), bf16)


def weight_grads(
    slots, scalars, parts, pool_rows, coef_cols, pre, delta, mask_rows, pixels, columns, half, image_total, after
):
    chans, total = pre.shape[2:]
    depth = pixels.shape[1]
    block = depth // 4
    count = len(slots)

    def cols(slot):
        return pl.BlockSpec((chans, LANES), lambda i, s: (s[4 + slot], 0))

    def own(slot):
        return pl.BlockSpec((1, 4, chans, total), lambda i, s: (s[4 + slot], 0, 0, 0))

    outs = call(
        functools.partial(weight_kernel, columns, image_total, slots),
        "atrous_weight_grad",
        (4,),
        1,
        [
            full(parts.shape),
            full(pool_rows.shape),
            full(mask_rows.shape),
            pl.BlockSpec((total, block), lambda i, s: (0, i)),
        ]
        + [cols(slot) for slot in slots]
        + [own(slot) for slot in slots] * 2,
        (
            pl.BlockSpec((half, block), lambda i, s: (0, i)),
            pl.BlockSpec((half, block), lambda i, s: (0, i)),
            full((29 * chans, total)),
        )
        * count,
        (
            jax.ShapeDtypeStruct((half, depth), bf16),
            jax.ShapeDtypeStruct((half, depth), bf16),
            jax.ShapeDtypeStruct((29 * chans, total), bf16),
        )
        * count,
        [pltpu.VMEM((29 * chans, block), f32), pltpu.VMEM((LANES, LANES), f32)],
        after=after,
        vmem=28 if slots[0] == 3 else 56,
    )(
        scalars,
        parts,
        pool_rows,
        mask_rows,
        pixels,
        *[coef_cols] * count,
        *[pre] * count,
        *[delta] * count,
    )
    return [outs[3 * at : 3 * at + 3] for at in range(count)]


def input_kernel(start, places, scalar_ref, *refs):
    taps, weights, outs = refs[0:4], refs[4:12], refs[12:15]
    all_weights, all_taps, result, weight_sems, tap_sems, out_sems = refs[15:]
    half, depth = weights[0].shape
    block = all_taps.shape[2]
    cut = depth // 2

    def tap_copies(strip):
        copies = []
        lanes = pl.ds(pl.multiple_of(scalar_ref[places[strip]] * block, LANES), block)
        for slot in range(4):
            sel = scalar_ref[slot]
            for which in range(2):
                first = sel * start if which == 0 else (1 - sel) * start
                at = 2 * slot + which
                copies.append(
                    pltpu.make_async_copy(
                        taps[slot].at[pl.ds(pl.multiple_of(first, 16), half), lanes],
                        all_taps.at[strip, pl.ds(at * half, half), :],
                        tap_sems.at[strip, at],
                    )
                )
        return copies

    def weight_copies(part):
        lanes = pl.ds(part * cut, cut)
        return [
            pltpu.make_async_copy(
                weights[at].at[:, lanes],
                all_weights.at[pl.ds(at * half, half), lanes],
                weight_sems.at[part, at],
            )
            for at in range(8)
        ]

    tap_lists = [tap_copies(0), tap_copies(1)]
    weight_lists = [weight_copies(0), weight_copies(1)]
    for copies in (tap_lists[0], weight_lists[0], weight_lists[1], tap_lists[1]):
        for copy in copies:
            copy.start()
    rows = outs[0].shape[0]
    out_lists = [
        [
            pltpu.make_async_copy(result.at[0, pl.ds(0, rows), :], outs[0], out_sems.at[0]),
            pltpu.make_async_copy(result.at[0, pl.ds(rows, rows), :], outs[1], out_sems.at[1]),
        ],
        [pltpu.make_async_copy(result.at[1], outs[2], out_sems.at[2])],
    ]
    for strip in range(2):
        for copy in tap_lists[strip]:
            copy.wait()
        for part in range(2):
            if strip == 0:
                for copy in weight_lists[part]:
                    copy.wait()
            lanes = slice(part * cut, (part + 1) * cut)
            result[strip, :, lanes] = lax.dot_general(
                all_taps[strip],
                all_weights[:, lanes],
                (((0,), (0,)), ((), ())),
                preferred_element_type=f32,
            ).astype(bf16)
        for copy in out_lists[strip]:
            copy.start()
    for copies in out_lists:
        for copy in copies:
            copy.wait()


def input_grads(flip, taps, weights, scalars, block, after):
    rows = taps[0].shape[0]
    half, depth = weights[0].shape
    shapes = ((block // 2, depth), (block // 2, depth), (block, depth))
    anywhere = pl.BlockSpec(memory_space=pl.ANY)
    low, high, own = call(
        functools.partial(input_kernel, rows - half, (HALF + 2 + flip, HALF + 1 + flip)),
        "atrous_input_grad",
        (1,),
        1,
        [anywhere] * 12,
        (anywhere,) * 3,
        tuple(jax.ShapeDtypeStruct(shape, bf16) for shape in shapes),
        [
            pltpu.VMEM((8 * half, depth), bf16),
            pltpu.VMEM((2, 8 * half, block), bf16),
            pltpu.VMEM((2, block, depth), bf16),
            pltpu.SemaphoreType.DMA((2, 8)),
            pltpu.SemaphoreType.DMA((2, 8)),
            pltpu.SemaphoreType.DMA((3,)),
        ],
        after=after,
        vmem=58,
    )(scalars, *taps, *weights)
    return [low, high], own


def local(
    features,
    scale_sizes,
    cotangent,
    branch_weight,
    branch_first,
    branch_second,
    head_weight,
    head_first,
    head_second,
    norm_params,
    norm_first,
    norm_second,
    running_stats,
):
    groups = lax.axis_size("dp")
    halves = groups == 2
    images = scale_sizes.shape[1]
    image_total = float(groups * images)
    x_id, z_id = lax.axis_index("dp"), lax.axis_index("z")
    quad_id = lax.axis_index("y") * 2 + lax.axis_index("c")
    wide_id = z_id * 4 + quad_id
    strip_rows, columns, depth = features.shape[1:]
    strip = strip_rows * columns
    total = 4 * strip
    tap_count, chans = branch_weight.shape[:2]
    all_ch = chans * 16
    split = (tap_count - 1) // 2
    half = (split + 1) * chans
    cells, everyone = ("dp", "z"), ("dp",) + PLANE
    rows = 16 * chans + EXTRA

    def exchange(parts, axes):
        return lax.all_to_all(parts, axes, 0, 0, tiled=True)

    height = lax.dynamic_index_in_dim(scale_sizes[0], z_id, 0, keepdims=False)
    pixel = jnp.arange(total, dtype=jnp.int32)
    inside = jnp.logical_and(pixel // columns < height, pixel % columns < 2 * height).astype(f32)
    own_inside = lax.dynamic_slice_in_dim(inside, quad_id * strip, strip, 0)
    mask_rows = jnp.broadcast_to(inside[None], (8, total))
    strip_mask = jnp.broadcast_to(own_inside[None], (8, strip))

    mid = jnp.logical_and(z_id >= 1, z_id <= 2).astype(jnp.int32)[None]

    sel = x_id.astype(jnp.int32) if halves else jnp.zeros((), jnp.int32)
    outer = z_id >= 2
    scalars = jnp.stack(
        [sel, sel, sel, sel]
        + [z_id, jnp.bitwise_xor(z_id, 1), jnp.where(outer, 1, 2), jnp.where(outer, 0, 3)]
        + [height, sel]
        + [jnp.bitwise_xor(quad_id, flip) for flip in range(4)]
    ).astype(jnp.int32)
    def over_groups(block):
        return lax.ppermute(block, "dp", SWAP)

    def along(parts, pairs):
        return [lax.ppermute(part, "z", pairs) for part in parts]

    def hold(parts, after):
        return [held(part, after) for part in parts]

    def pair_of(parts):
        return (parts[0], over_groups(parts[0])) if halves else tuple(parts)

    def pick_all(ones, twos, after):
        return [pick(mid, one, two, after) for one, two in zip(ones, twos)]

    zero = jnp.zeros((), jnp.int32)
    mine_w = cast_half(sel[None], branch_weight, split, ())
    other_w = cast_half(1 - sel[None], branch_weight, split, (mine_w,))
    sending = [mine_w] if halves else [mine_w, other_w]
    near, mid_one = along(sending, PAIR), along(sending, MID)

    own_strip = features[0].reshape(strip, depth)
    masked, *masked_parts = mask_strip(scalars, own_strip, columns, sending)
    low_y, high_y = (lax.ppermute(part, "y", SWAP) for part in masked_parts)
    over_c = lax.ppermute(masked, "c", SWAP)

    own_proj = head_weight.astype(bf16).reshape(chans, 5, 4, 4, chans)
    own_proj = jnp.transpose(own_proj, (0, 3, 2, 1, 4))
    pixel_proj = jnp.pad(
        own_proj[:, :, :, :4].reshape(chans, 4, 16 * chans), ((0, 0), (0, 0), (0, EXTRA))
    ).reshape(chans, 4 * rows)
    value = jnp.transpose(norm_params.reshape(12, chans))
    terms = []
    for _ in range(3):
        terms.append(barrier(value.astype(bf16)))
        value = value - terms[-1].astype(f32)
    terms = jnp.pad(jnp.stack(terms, axis=2).reshape(chans, 36), ((0, 0), (0, TERMS - 36)))
    shared = jnp.concatenate(
        [
            jnp.broadcast_to(own_proj[:, :, :, 4].reshape(1, chans, all_ch), (16, chans, all_ch)),
            jnp.transpose(cotangent[0].reshape(chans, 16, strip), (1, 0, 2)),
            jnp.broadcast_to(pixel_proj[None], (16, chans, 4 * rows)),
            jnp.broadcast_to(terms[None], (16, chans, TERMS)),
        ],
        axis=2,
    )

    slots = [(mine_w, other_w)]
    near = hold(near, [masked, mask_rows, scalars])
    mid_two = along(near, MID)
    near = pair_of(near)
    mid_one = hold(mid_one, near[:1])
    out_one = along(mid_one, OUTWARD)
    low_y = held(low_y, mid_one)
    mid_two = hold(mid_two, [low_y, other_w, shared, strip_mask])
    out_two = along(mid_two, OUTWARD)
    second = pick_all(mid_one, out_one, mid_two)
    second_pair = pair_of(second)
    high_y = held(high_y, second)
    low_yc, high_yc = (lax.ppermute(part, "c", SWAP) for part in (low_y, high_y))
    near = (near[0], held(near[1], (high_y,)))
    slots.append(near)
    parts = ((masked,), (over_c,), (low_y, high_y), (low_yc, high_yc))
    pixels = image_of(scalars, strip, parts, near[1:])

    def branch(slot, state, after):
        return forward_taps(
            slot, pixels, mask_rows, scalars, *slots[slot], state, columns, chans, split, after
        )

    state = branch(0, (), ())
    slots.append((second_pair[0], held(second_pair[1], [state[1]])))
    third = pick_all(mid_two, out_two, slots[2][1:])
    slots.append(pair_of(third))
    shared = exchange(held(shared, third), PLANE)
    shared = shared.reshape(all_ch, all_ch + strip + 4 * rows + TERMS)
    state = branch(1, state, third)
    state = branch(2, state, ())
    state = branch(3, state, ())
    pre, stats = state
    own_sums = pack_sums(stats, axes_size(cells), (shared,))
    quad = quad_id.astype(jnp.int32)[None]
    concat, coef_cols, coef_rows = activations(
        quad, exchange(own_sums, cells), own_sums, shared, pre, image_total
    )
    concat = exchange(concat, QUAD).reshape(4 * rows, strip)

    unit, head_sums = project(concat, shared, strip_mask, axes_size(everyone))
    head_values, head_delta, head_coefs, head_rows, head_sums = head_norm(
        exchange(head_sums, everyone), unit, shared, strip_mask, coef_rows
    )
    unit_back, concat_back, row_sums, head_moments = unit_backward(
        exchange(head_sums, everyone),
        unit,
        head_delta,
        head_coefs,
        strip_mask,
        coef_rows,
        shared,
    )

    delta, pool_rows, moments = branch_backward(
        exchange(concat_back, QUAD), pre, coef_cols, coef_rows, mask_rows, axes_size(cells), ()
    )
    moments = exchange(moments, cells)

    def weights_of(slots, after):
        return weight_grads(
            slots,
            scalars,
            moments,
            pool_rows,
            coef_cols,
            pre,
            delta,
            mask_rows,
            pixels,
            columns,
            half,
            image_total,
            after,
        )

    def group_sums(slot, after, *lists):
        if halves:
            return [add(slot[0], over_groups(slot[1]), *(parts[0] for parts in lists), after=after)]
        return [add(*parts, after=after) for parts in zip(slot[:2], *lists)]

    def swap_all(parts, axis):
        return [lax.ppermute(part, axis, SWAP) for part in parts]

    def add_all(*lists, after=()):
        return [add(*parts, after=after) for parts in zip(*lists)]

    flat_w = [part for slot in slots for part in slot]

    def features_of(flip, after):
        return input_grads(flip, taps, flat_w, scalars, strip, after)

    ((keep_c, send_c, taps_c),) = weights_of((3,), ())
    head_parts = head_weight_grads(concat, unit_back, row_sums, head_values, (taps_c,))
    head_parts = exchange(head_parts.reshape(16, chans, all_ch + strip + 4 * rows), PLANE)
    slot_b, slot_a, slot_o = weights_of((2, 1, 0), (taps_c,))
    taps = [slot_o[2], slot_a[2], slot_b[2], taps_c]
    third = group_sums((keep_c, send_c), (slot_o[2], head_parts))
    far_cross, far = features_of(2, third)
    second = group_sums(slot_b, (far,))
    mid_two = add_all(third, along(third, INWARD), after=second)
    far = strip_sum(scalars, (far,), swap_all(far_cross, "c"), columns, False, mid_two)
    near = group_sums(slot_a, (far,), along(mid_two, MID))
    mid_one = add_all(second, along(second, INWARD), after=near)

    head_output = head_parts[:, :, all_ch : all_ch + strip]
    head_output = jnp.transpose(head_output, (1, 0, 2)).reshape(1, chans, 16 * strip)
    head_parts = jnp.sum(head_parts.astype(f32), axis=0)
    pool_part = head_parts[:, :all_ch].reshape(chans, 4, 4, 1, chans)
    pixel_part = head_parts[:, all_ch + strip :].reshape(chans, 4, rows)[:, :, : 16 * chans]
    pixel_part = pixel_part.reshape(chans, 4, 4, 4, chans)
    head_grads = jnp.concatenate([pixel_part, pool_part], axis=3)
    head_grads = jnp.transpose(head_grads, (0, 3, 2, 1, 4)).reshape(chans, 5 * all_ch)
    near_cross, own_part = features_of(0, (*mid_one, head_grads))
    if halves:
        head_grads = head_grads + lax.ppermute(head_grads, "dp", SWAP)
    else:
        head_grads = lax.psum(head_grads, "dp")
    mine = group_sums(slot_o, (own_part, head_grads), along(near, PAIR), along(mid_one, MID))
    state = (branch_weight, branch_first, branch_second)
    if halves:
        other = over_groups(mine[0])
    else:
        mine = [lax.psum(part, "dp") for part in mine]
    cross = swap_all(near_cross, "c")
    total = held(own_part, mine).astype(f32) + jnp.concatenate(cross, axis=0).astype(f32)
    total = total + lax.ppermute(far, "y", SWAP).astype(f32)
    input_grad = (total * own_inside[:, None]).astype(bf16)
    input_grad = input_grad.reshape(1, strip_rows, columns, depth)
    start = jnp.stack([sel * split, zero])
    done = adam_taps(start, split + 1, 3, mine[0], *state, (), (input_grad,))
    start = jnp.stack([(1 - sel) * (split + 1), 1 - sel])
    done = adam_taps(start, split, 2, other if halves else mine[1], *state, done, ())
    branch_grads, branch_means, branch_squares, branch_updated = done

    def own_lanes(by_row):
        return lax.dynamic_slice_in_dim(by_row, z_id * chans, chans, 1)

    def own_head(by_row):
        return lax.dynamic_slice_in_dim(by_row, wide_id * chans, chans, 1)

    moments = jnp.sum(moments, axis=0)
    own_firsts, own_seconds = own_lanes(moments), own_lanes(moments[:, 4 * chans :])
    head_own = own_head(head_moments)
    norm_grads = jnp.stack(
        [
            jnp.concatenate([own_seconds[0:5], head_own[1:2]]),
            jnp.concatenate([own_firsts[0:5], head_own[0:1]]),
        ]
    )
    own_coefs, head_stats = own_lanes(coef_rows), own_head(head_rows)
    pixel_total = coef_rows[COUNT, 0]
    all_centres = jnp.concatenate([own_coefs[CENTRE : CENTRE + 5], head_stats[0:1]])
    all_variances = jnp.concatenate([own_coefs[VARIANCE : VARIANCE + 5], head_stats[4:5]])
    factors = jnp.where(
        jnp.arange(6) == 4, image_total / (image_total - 1.0), pixel_total / (pixel_total - 1.0)
    )
    running_next = (1.0 - momentum) * running_stats + momentum * jnp.stack(
        [all_centres, all_variances * factors[:, None]]
    )
    head_means, head_squares, head_updated = adamw_update(
        head_weight, head_grads, head_first, head_second, conv_rate, weight_decay
    )
    norm_means, norm_squares, norm_updated = adamw_update(
        norm_params, norm_grads, norm_first, norm_second, norm_rate, 0.0
    )
    return (
        head_output,
        input_grad,
        branch_grads,
        branch_means,
        branch_squares,
        branch_updated,
        head_grads,
        head_means,
        head_squares,
        head_updated,
        norm_grads,
        norm_means,
        norm_squares,
        norm_updated,
        running_next,
    )


def solution(mesh):
    groups, wide = mesh.devices.shape
    fine = Mesh(mesh.devices.reshape(groups, 4, 2, wide // 8), ("dp",) + PLANE)
    placed = (
        P("dp", PLANE, None, None),
        P("dp", None),
        P("dp", PLANE, None),
        P(None, PLANE, None),
        P(None, PLANE, None),
        P(None, PLANE, None),
        P(PLANE, None),
        P(PLANE, None),
        P(PLANE, None),
        P(None, None, PLANE),
        P(None, None, PLANE),
        P(None, None, PLANE),
        P(None, None, PLANE),
    )
    return jax.shard_map(
        local,
        mesh=fine,
        in_specs=placed,
        out_specs=(
            P("dp", PLANE, None),
            P("dp", PLANE, None, None),
            P(None, PLANE, None),
            P(None, PLANE, None),
            P(None, PLANE, None),
            P(None, PLANE, None),
            P(PLANE, None),
            P(PLANE, None),
            P(PLANE, None),
            P(PLANE, None),
            P(None, None, PLANE),
            P(None, None, PLANE),
            P(None, None, PLANE),
            P(None, None, PLANE),
            P(None, None, PLANE),
        ),
        check_vma=False,
    )
```

```python
import functools

import jax
import jax.numpy as jnp
from jax import lax
from jax.experimental import pallas as pl
from jax.experimental.pallas import tpu as pltpu
from jax.sharding import Mesh, PartitionSpec as P

STEP = 10


dilations = (6, 12, 18)
epsilon = 1e-05
momentum = 0.1
first_decay = 0.9
second_decay = 0.999
conv_rate = 0.02
norm_rate = 0.4
weight_decay = 0.0001
adam_floor = 1e-08

LANES = 128
PLANE = ("z", "y", "c")
QUAD = ("y", "c")
SWAP = [(0, 1), (1, 0)]
PAIR = [(0, 1), (1, 0), (2, 3), (3, 2)]
MID = [(1, 2), (2, 1)]
OUTWARD = [(1, 0), (2, 3)]
INWARD = [(0, 1), (3, 2)]

bf16 = jnp.bfloat16
f32 = jnp.float32
barrier = lax.optimization_barrier


def adamw_update(parameter, gradient, moment_one, moment_two, step_rate, decay_rate):
    first_new = first_decay * moment_one + (1.0 - first_decay) * gradient
    second_new = second_decay * moment_two + (1.0 - second_decay) * gradient * gradient
    first_hat = first_new / (1.0 - first_decay**STEP)
    second_hat = second_new / (1.0 - second_decay**STEP)
    updated = parameter - step_rate * (
        first_hat / (jnp.sqrt(second_hat) + adam_floor) + decay_rate * parameter
    )
    return (first_new, second_new, updated)


def gelu_both(value):
    scale = (2.0 / jnp.pi) ** 0.5
    square = value * value
    bend = jnp.tanh(scale * (value + 0.044715 * (value * square)))
    lead = 0.5 * (1.0 + bend)
    slope = lead + 0.5 * value * (1.0 - bend * bend) * (scale * (1.0 + 3.0 * 0.044715 * square))
    return value * lead, slope


def tall(rows):
    fill = LANES - rows.shape[0]
    return jnp.concatenate([rows, jnp.zeros((fill, rows.shape[1]), rows.dtype)], axis=0).T


def stacked(rows, count):
    found = {}
    for at in range(count):
        found[2 * at] = rows[at : at + 1, :LANES]
        found[2 * at + 1] = rows[at : at + 1, LANES:]
    return put_rows((8, LANES), found)[: 2 * count]


def unstacked(rows):
    found = {}
    for at in range(rows.shape[0] // 2):
        found[at] = jnp.concatenate([rows[2 * at : 2 * at + 1], rows[2 * at + 1 : 2 * at + 2]], axis=1)
    return put_rows((8, 2 * LANES), found)


def beside(left, right, width):
    lane = lax.broadcasted_iota(jnp.int32, left.shape, 1)
    return jnp.where(lane < width, left, pltpu.roll(right, width, 1))


def put_lanes(shape, columns):
    lane = lax.broadcasted_iota(jnp.int32, shape, 1)
    total = jnp.zeros(shape, f32)
    for at, column in columns.items():
        total = jnp.where(lane == at, column, total)
    return total


def put_rows(shape, rows):
    row = lax.broadcasted_iota(jnp.int32, shape, 0)
    total = jnp.zeros(shape, f32)
    for at, value in rows.items():
        total = jnp.where(row == at, value, total)
    return total


def axes_size(axes):
    count = 1
    for axis in axes:
        count *= lax.axis_size(axis)
    return count


def call(
    kernel,
    name,
    grid,
    scalars,
    in_specs,
    out_specs,
    out_shape,
    scratch=(),
    aliases=None,
    flops=0,
    after=(),
    vmem=24,
):
    after = tuple(after)
    first = scalars + len(in_specs)

    def body(*refs):
        kernel(*refs[:first], *refs[first + len(after) :])

    run = pl.pallas_call(
        body,
        out_shape=out_shape,
        grid_spec=pltpu.PrefetchScalarGridSpec(
            num_scalar_prefetch=scalars,
            grid=grid,
            in_specs=list(in_specs) + [pl.BlockSpec(memory_space=pl.ANY)] * len(after),
            out_specs=out_specs,
            scratch_shapes=list(scratch),
        ),
        input_output_aliases=aliases or {},
        compiler_params=pltpu.CompilerParams(vmem_limit_bytes=vmem << 20),
        cost_estimate=pl.CostEstimate(flops=1, bytes_accessed=1, transcendentals=0),
        name=name,
    )
    return lambda *arrays: run(*arrays, *after)


def full(shape):
    return pl.BlockSpec(shape, lambda *_: (0,) * len(shape))


def add_kernel(*refs):
    total = refs[0][...].astype(f32)
    for ref in refs[1:-1]:
        total = total + ref[...].astype(f32)
    refs[-1][...] = total.astype(bf16)


def add(*values, after=()):
    first = held(values[0], after) if after else values[0]
    total = first.astype(f32)
    for value in values[1:]:
        total = total + value.astype(f32)
    return barrier(total.astype(bf16))


def pick_kernel(flag_ref, one_ref, two_ref, out_ref):
    @pl.when(flag_ref[0] == 1)
    def _():
        out_ref[...] = one_ref[...]

    @pl.when(flag_ref[0] != 1)
    def _():
        out_ref[...] = two_ref[...]


def pick(flag, one, two, after=()):
    rows, depth = one.shape
    spec = pl.BlockSpec((rows // 3, depth), lambda i, s: (i, 0))
    return call(
        pick_kernel,
        "pick",
        (3,),
        1,
        [spec, spec],
        spec,
        jax.ShapeDtypeStruct(one.shape, one.dtype),
        after=after,
    )(flag, one, two)


def held_kernel(in_ref, out_ref):
    del in_ref, out_ref


def held(value, after):
    anywhere = pl.BlockSpec(memory_space=pl.ANY)
    return call(
        held_kernel,
        "held",
        (1,),
        0,
        [anywhere],
        anywhere,
        jax.ShapeDtypeStruct(value.shape, value.dtype),
        aliases={0: 0},
        after=after,
        vmem=56,
    )(value)


def cast_kernel(sel_ref, in_ref, out_ref):
    taps, chans = in_ref.shape[:2]
    first = jnp.logical_and(sel_ref[0] == 1, pl.program_id(0) == 0)
    for tap in range(taps):
        value = in_ref[tap]
        if tap == 0:
            value = jnp.where(first, 0.0, value)
        out_ref[tap * chans : (tap + 1) * chans, :] = value.astype(bf16)


def cast_half(sel, weight, split, after):
    chans, depth = weight.shape[1:]
    parts = 3 if (split + 1) % 3 == 0 else 1
    block = (split + 1) // parts
    return call(
        cast_kernel,
        "cast",
        (parts,),
        1,
        [pl.BlockSpec((pl.Element(block), pl.Element(chans), pl.Element(depth)), lambda i, s: (s[0] * split + i * block, 0, 0))],
        pl.BlockSpec((block * chans, depth), lambda i, s: (i, 0)),
        jax.ShapeDtypeStruct(((split + 1) * chans, depth), bf16),
        after=after,
        vmem=56,
    )(sel, weight)


def mask_kernel(columns, strip, scalar_ref, in_ref, *out_refs):
    rows, depth = in_ref.shape
    pixel = lax.broadcasted_iota(jnp.int32, (rows, LANES), 0)
    row = pixel // columns + scalar_ref[HALF + 1] * (strip // columns)
    height = scalar_ref[HEIGHT]
    inside = jnp.logical_and(row < height, pixel % columns < 2 * height)
    for first in range(0, depth, LANES):
        lanes = slice(first, first + LANES)
        value = jnp.where(inside, in_ref[:, lanes].astype(f32), 0.0).astype(bf16)
        for out_ref in out_refs:
            out_ref[:, lanes] = value[rows - out_ref.shape[0] :]


def mask_strip(scalars, strip, columns, count, lasts, after):
    rows, depth = strip.shape
    return call(
        functools.partial(mask_kernel, columns, rows),
        "mask",
        (1,),
        1,
        [pl.BlockSpec((count, depth), lambda i, s: (0, 0))],
        tuple(full((last, depth)) for last in lasts),
        tuple(jax.ShapeDtypeStruct((last, depth), bf16) for last in lasts),
        after=after,
        vmem=56,
    )(scalars, strip)


def image_kernel(strip, places, spot_ref, *refs):
    *parts, out_ref, sems = refs
    copies = []
    for at, (which, first) in enumerate(places):
        rows = pl.ds(pl.multiple_of(spot_ref[HALF + 1 + which] * strip + first, 16), parts[at].shape[0])
        copies.append(pltpu.make_async_copy(parts[at], out_ref.at[rows, :], sems.at[at]))
    for copy in copies:
        copy.start()
    for copy in copies:
        copy.wait()


def image_of(spots, strip, parts, after):
    depth = parts[0][0].shape[1]
    places = []
    for which, strip_parts in enumerate(parts):
        first = 0
        for part in strip_parts:
            places.append((which, first))
            first += part.shape[0]
    flat = [part for strip_parts in parts for part in strip_parts]
    anywhere = pl.BlockSpec(memory_space=pl.ANY)
    return call(
        functools.partial(image_kernel, strip, places),
        "image",
        (1,),
        1,
        [anywhere] * len(flat),
        full((4 * strip, depth)),
        jax.ShapeDtypeStruct((4 * strip, depth), bf16),
        [pltpu.SemaphoreType.DMA((len(flat),))],
        after=after,
        vmem=56,
    )(spots, *flat)


def head_grad_kernel(x_ref, back_ref, sum_ref, value_ref, out_ref):
    channels = back_ref.shape[0]
    rows = x_ref.shape[0] // 4
    act = jnp.zeros((EXTRA, channels), f32)
    for quad in range(4):
        first = quad * rows + rows - EXTRA
        act = act + x_ref[first : first + EXTRA, :channels].astype(f32)
    out_ref[:, :channels] = (sum_ref[:, 0:1] * act[0:1, :]).astype(bf16)
    strip = x_ref.shape[1]
    out_ref[:, channels : channels + strip] = value_ref[...]
    out_ref[:, channels + strip :] = lax.dot_general(
        back_ref[...], x_ref[...], (((1,), (1,)), ((), ())), preferred_element_type=f32
    ).astype(bf16)


def head_weight_grads(concat, unit_back, row_sums, values, after):
    channels = unit_back.shape[0]
    arrays = (concat, unit_back, row_sums, values)
    shape = (channels, channels + concat.shape[1] + concat.shape[0])
    return call(
        head_grad_kernel,
        "head_weight_grad",
        (1,),
        0,
        [full(array.shape) for array in arrays],
        full(shape),
        jax.ShapeDtypeStruct(shape, bf16),
        after=after,
        vmem=24,
    )(*arrays)


def strip_sum_kernel(columns, whole, masked, scalar_ref, *refs):
    block = refs[0].shape[0]
    step = pl.program_id(0)
    rows_all = refs[whole].shape[0] * (len(refs) - 1 - whole)
    pixel = step * block + lax.broadcasted_iota(jnp.int32, (block, LANES), 0)
    row = pixel // columns + scalar_ref[HALF + 1] * (rows_all // columns)
    height = scalar_ref[HEIGHT]
    inside = jnp.logical_and(row < height, pixel % columns < 2 * height)
    steps = refs[whole].shape[0] * (len(refs) - 1 - whole) // block
    count = steps // (len(refs) - 1 - whole)
    for at in range(steps):

        @pl.when(step == at)
        def _():
            part = refs[whole + at // count]
            rows = slice(at % count * block, (at % count + 1) * block)
            for first in range(0, refs[0].shape[1], LANES):
                lanes = slice(first, first + LANES)
                total = part[rows, lanes].astype(f32)
                for ref in refs[:whole]:
                    total = total + ref[:, lanes].astype(f32)
                if masked:
                    total = jnp.where(inside, total, 0.0)
                refs[-1][:, lanes] = total.astype(bf16)


def strip_sum(scalars, strips, parts, columns, masked, after):
    rows, depth = strips[0].shape
    spec = pl.BlockSpec((rows // 2, depth), lambda i, s: (i, 0))
    return call(
        functools.partial(strip_sum_kernel, columns, len(strips), masked),
        "strip_sum",
        (2,),
        1,
        [spec] * len(strips) + [full(part.shape) for part in parts],
        spec,
        jax.ShapeDtypeStruct((rows, depth), bf16),
        after=after,
        vmem=56,
    )(scalars, *strips, *parts)


def adam_kernel(start_ref, grad_ref, weight_ref, first_ref, second_ref, *rest):
    out_ref, mean_ref, square_ref, new_ref = rest[-4:]
    grad = grad_ref[...].astype(f32).reshape(out_ref.shape)
    mean, square, new = adamw_update(
        weight_ref[...], grad, first_ref[...], second_ref[...], conv_rate, weight_decay
    )
    out_ref[...] = grad
    mean_ref[...] = mean
    square_ref[...] = square
    new_ref[...] = new


def adam_taps(start, count, block, grads, weight, first, second, earlier, after):
    taps, chans, depth = weight.shape

    def piece(size, index):
        return pl.BlockSpec(tuple(pl.Element(n) for n in size), index)

    spec = piece((block, chans, depth), lambda i, s: (s[0] + i * block, 0, 0))
    anywhere = [pl.BlockSpec(memory_space=pl.ANY)] * len(earlier)
    return call(
        adam_kernel,
        "adamw",
        (count // block,),
        1,
        [piece((block * chans, depth), lambda i, s: ((s[1] + i * block) * chans, 0))]
        + [spec] * 3
        + anywhere,
        (spec,) * 4,
        (jax.ShapeDtypeStruct(weight.shape, f32),) * 4,
        aliases={5 + at: at for at in range(4)} if earlier else None,
        after=after,
        vmem=36,
    )(start, grads, weight, first, second, *earlier)


FIRST, SECOND, GAIN, SHIFT, AREA = 0, 8, 16, 24, 5
SUM_ROWS = 8
CENTRE, INVERSE, VARIANCE, COUNT, POOLED = 0, 8, 32, 40, 41
COEF_ROWS = 48
EXTRA = 16
TERMS = 64
HEIGHT, HALF = 8, 9


def lane_masks(columns):
    lane = lax.broadcasted_iota(jnp.int32, (1, LANES), 1) % columns
    masks = {}
    for dilation in dilations:
        for off in (-dilation, dilation):
            moved = lane + off
            masks[off] = jnp.logical_and(moved >= 0, moved < columns)
    return masks


def forward_kernel(columns, split, slot, scalar_ref, x_ref, wz_ref, wx_ref, mask_ref, *rest):
    pre_ref, stat_ref, taps = rest[-3:]
    step = pl.program_id(0)
    half = wz_ref.shape[0]
    block = x_ref.shape[0]
    sel = scalar_ref[slot]
    contract = (((1,), (1,)), ((), ()))
    pixels = x_ref[...]
    cols = pl.ds(pl.multiple_of(step * block, block), block)
    taps[pl.ds(pl.multiple_of(sel * half, 16), half), cols] = lax.dot_general(
        wz_ref[...], pixels, contract, preferred_element_type=f32
    )
    taps[pl.ds(pl.multiple_of((1 - sel) * half, 16), half), cols] = lax.dot_general(
        wx_ref[...], pixels, contract, preferred_element_type=f32
    )

    @pl.when(step == pl.num_programs(0) - 1)
    def _():
        total = taps.shape[1]
        tiles = total // LANES
        chans = pre_ref.shape[2]
        masks = lane_masks(columns)

        def rows_of(tap):
            first = tap * chans if tap <= split else (tap + 1) * chans
            return slice(first, first + chans)

        def tile(tap, at):
            return taps[rows_of(tap), at * LANES : (at + 1) * LANES]

        sums = [jnp.zeros((chans, LANES), f32) for _ in range(4)]
        squares = [jnp.zeros((chans, LANES), f32) for _ in range(4)]
        pooled = jnp.zeros((chans, LANES), f32)
        for at in range(tiles):
            lanes = slice(at * LANES, (at + 1) * LANES)
            weight = mask_ref[0:1, lanes]
            for branch in range(4):
                if branch == 0:
                    value = tile(0, at)
                else:
                    dilation = dilations[branch - 1]
                    jump = dilation * columns // LANES
                    value = None
                    for b in range(3):
                        part = None
                        for a in range(3):
                            source = at + (a - 1) * jump
                            if 0 <= source < tiles:
                                term = tile(1 + 9 * (branch - 1) + 3 * a + b, source)
                                part = term if part is None else part + term
                        off = (b - 1) * dilation
                        if off != 0:
                            part = pltpu.roll(part, (-off) % LANES, 1)
                            part = jnp.where(masks[off], part, 0.0)
                        value = part if value is None else value + part
                pre_ref[0, branch, :, lanes] = value
                weighted = value * weight
                sums[branch] = sums[branch] + weighted
                squares[branch] = squares[branch] + weighted * value
            pooled = pooled + tile(28, at)
        height = jnp.full((1, 1), scalar_ref[HEIGHT], jnp.int32).astype(f32)
        area = 2.0 * height * height
        pool = jnp.sum(pooled, axis=1, keepdims=True) / area
        columns_of = {FIRST + 4: pool, SECOND + 4: pool * pool, AREA: area}
        for branch in range(4):
            columns_of[FIRST + branch] = jnp.sum(sums[branch], axis=1, keepdims=True)
            columns_of[SECOND + branch] = jnp.sum(squares[branch], axis=1, keepdims=True)
        stat_ref[0] = put_lanes((chans, LANES), columns_of)


def forward_taps(slot, pixels, mask_rows, scalars, wz, wx, earlier, columns, chans, split, after):
    total, depth = pixels.shape
    block = total // 4
    half = wz.shape[0]
    keep = [pl.BlockSpec(memory_space=pl.ANY)] * len(earlier)
    return call(
        functools.partial(forward_kernel, columns, split, slot),
        "atrous_forward",
        (4,),
        1,
        [
            pl.BlockSpec((block, depth), lambda i, s: (i, 0)),
            full((half, depth)),
            full((half, depth)),
            full((8, total)),
        ]
        + keep,
        (
            pl.BlockSpec((1, 4, chans, total), lambda i, s: (s[4 + slot], 0, 0, 0)),
            pl.BlockSpec((1, chans, LANES), lambda i, s: (s[4 + slot], 0, 0)),
        ),
        (
            jax.ShapeDtypeStruct((4, 4, chans, total), f32),
            jax.ShapeDtypeStruct((4, chans, LANES), f32),
        ),
        [pltpu.VMEM((2 * half, total), f32)],
        {5: 0, 6: 1} if earlier else None,
        4 * half * total * depth,
        after,
        56,
    )(scalars, pixels, wz, wx, mask_rows, *earlier)


def pack_kernel(stat_ref, out_ref, work):
    chans = stat_ref.shape[1]
    work[...] = jnp.zeros_like(work)
    for z in range(4):
        work[z * chans : (z + 1) * chans, :] = stat_ref[z]
    rows = work[...].T
    rows = beside(rows[:8], rows[8:16], 4 * chans)
    for at in range(out_ref.shape[0]):
        out_ref[at] = rows


def pack_sums(stats, count, after):
    return call(
        pack_kernel,
        "branch_sums",
        (1,),
        0,
        [full(stats.shape)],
        full((count, SUM_ROWS, LANES)),
        jax.ShapeDtypeStruct((count, SUM_ROWS, LANES), f32),
        [pltpu.VMEM((LANES, LANES), f32)],
        after=after,
        vmem=24,
    )(stats)


def term_sum(block, which, norm, start):
    first = start + 3 * (6 * which + norm)
    return block[:, first : first + 1] + block[:, first + 1 : first + 2] + block[:, first + 2 : first + 3]


def pool_rows_of(rows_ref, own_width):
    def row(at):
        return rows_ref[at : at + 1, :]

    moved = row(POOLED) - row(CENTRE + 4)
    normed = row(GAIN + 4) * moved * row(INVERSE + 4) + row(SHIFT + 4)
    lane = lax.broadcasted_iota(jnp.int32, normed.shape, 1)
    return normed, moved * row(INVERSE + 4), lane < own_width


def act_kernel(image_total, quad_ref, parts_ref, own_ref, term_ref, pre_ref, out_ref, col_ref, row_ref):
    chans = pre_ref.shape[2]

    @pl.when(pl.program_id(0) == 0)
    def _():
        sums = jnp.sum(parts_ref[...], axis=0)
        second = pltpu.roll(sums, LANES - 4 * chans, 1)
        found = []
        for z in range(4):
            place = pl.multiple_of((4 * z + quad_ref[0]) * chans, chans)
            block = term_ref[pl.ds(place, chans), :].astype(f32)
            columns = {}
            for norm in range(5):
                columns[norm] = term_sum(block, 0, norm, LANES - TERMS)
                columns[8 + norm] = term_sum(block, 1, norm, LANES - TERMS)
            found.append(put_lanes((chans, LANES), columns))
        found.append(jnp.zeros((LANES - 4 * chans, LANES), f32))
        affine = jnp.concatenate(found, axis=0).T
        pixel_total = jnp.maximum(sums[AREA : AREA + 1], 1.0)
        index = lax.broadcasted_iota(jnp.int32, (8, LANES), 0)
        count = jnp.where(index == 4, image_total, pixel_total)
        centre = sums / count
        variance = second / count - centre * centre
        inverse = lax.rsqrt(variance + epsilon)
        other = jnp.where(index == 0, pixel_total, jnp.where(index == 1, own_ref[0, 4:5, :], 0.0))
        rows = jnp.concatenate(
            [centre, inverse, affine[:8], affine[8:16], variance, other],
            axis=0,
        )
        row_ref[...] = rows
        col_ref[...] = tall(rows)

    for z in range(4):
        span = slice(z * chans, (z + 1) * chans)
        for branch in range(4):
            moved = pre_ref[z, branch] - col_ref[span, CENTRE + branch : CENTRE + branch + 1]
            normed = (
                col_ref[span, GAIN + branch : GAIN + branch + 1]
                * moved
                * col_ref[span, INVERSE + branch : INVERSE + branch + 1]
                + col_ref[span, SHIFT + branch : SHIFT + branch + 1]
            )
            first = (4 * z + branch) * chans
            out_ref[0, first : first + chans, :] = gelu_both(normed)[0].astype(bf16)
    normed, _, valid = pool_rows_of(row_ref, 4 * chans)
    act = jnp.where(valid, gelu_both(normed)[0], 0.0)
    act = put_rows((EXTRA, LANES), {0: act + pltpu.roll(act, 4 * chans, 1)})
    lane = lax.broadcasted_iota(jnp.int32, act.shape, 1)
    for at in range(out_ref.shape[2] // LANES):
        owner = (lane + at * LANES) // (4 * chans)
        out_ref[0, 16 * chans :, at * LANES : (at + 1) * LANES] = jnp.where(
            owner == quad_ref[0], act, 0.0
        ).astype(bf16)


def activations(quad, parts, own, shared, pre, image_total):
    chans, total = pre.shape[2:]
    strip = total // 4
    rows = 16 * chans + EXTRA
    return call(
        functools.partial(act_kernel, image_total),
        "branch_act",
        (4,),
        1,
        [
            full(parts.shape),
            full((1, SUM_ROWS, LANES)),
            pl.BlockSpec((shared.shape[0], LANES), lambda i, s: (0, shared.shape[1] // LANES - 1)),
            pl.BlockSpec((4, 4, chans, strip), lambda i, s: (0, 0, 0, i)),
        ],
        (
            pl.BlockSpec((1, rows, strip), lambda i, s: (i, 0, 0)),
            full((LANES, LANES)),
            full((COEF_ROWS, LANES)),
        ),
        (
            jax.ShapeDtypeStruct((4, rows, strip), bf16),
            jax.ShapeDtypeStruct((LANES, LANES), f32),
            jax.ShapeDtypeStruct((COEF_ROWS, LANES), f32),
        ),
        vmem=24,
    )(quad, parts, own, shared, pre)


def unit_kernel(x_ref, shared_ref, mask_ref, unit_ref, out_ref):
    channels = shared_ref.shape[0]
    rows, strip = x_ref.shape[0] // 4, x_ref.shape[1]
    proj = shared_ref[:, channels + strip : shared_ref.shape[1] - TERMS]
    unit = jnp.dot(proj, x_ref[...], preferred_element_type=f32)
    act = jnp.zeros((EXTRA, channels), f32)
    for quad in range(4):
        first = quad * rows + rows - EXTRA
        act = act + x_ref[first : first + EXTRA, :channels].astype(f32)
    bias = shared_ref[:, :channels].astype(f32) * act[0:1, :]
    unit = unit + jnp.sum(bias, axis=1, keepdims=True)
    unit_ref[...] = unit
    weighted = unit * mask_ref[0:1, :]
    one = jnp.sum(weighted, axis=1, keepdims=True)
    two = jnp.sum(weighted * unit, axis=1, keepdims=True)
    sums = put_lanes((channels, LANES), {0: one, 1: two}).T[:8]
    sums = stacked(sums, 2)
    for at in range(out_ref.shape[0]):
        out_ref[at] = sums


def project(concat, shared, strip_mask, count):
    channels, strip = shared.shape[0], concat.shape[1]
    arrays = (concat, shared, strip_mask)
    return call(
        unit_kernel,
        "projection",
        (1,),
        0,
        [full(array.shape) for array in arrays],
        (full((channels, strip)), full((count, 4, LANES))),
        (
            jax.ShapeDtypeStruct((channels, strip), f32),
            jax.ShapeDtypeStruct((count, 4, LANES), f32),
        ),
        vmem=24,
    )(*arrays)


def head_kernel(parts_ref, unit_ref, shared_ref, mask_ref, row_ref, value_ref, delta_ref, col_ref, head_ref, out_ref):
    sums = unstacked(jnp.sum(parts_ref[...], axis=0))
    pixel_total = row_ref[COUNT : COUNT + 1, 0:1]
    centre = sums[0:1] / pixel_total
    variance = sums[1:2] / pixel_total - centre * centre
    inverse = lax.rsqrt(variance + epsilon)
    rows = put_rows(
        sums.shape, {0: centre, 1: inverse, 4: variance}
    )
    head_ref[...] = rows
    columns = tall(rows)
    width = shared_ref.shape[1]
    block = shared_ref[:, width - LANES :].astype(f32)
    lane = lax.broadcasted_iota(jnp.int32, columns.shape, 1)
    gain = term_sum(block, 0, 5, LANES - TERMS)
    shift = term_sum(block, 1, 5, LANES - TERMS)
    columns = jnp.where(lane == 2, gain, jnp.where(lane == 3, shift, columns))
    col_ref[...] = columns
    hat = (unit_ref[...] - columns[:, 0:1]) * columns[:, 1:2]
    normed = columns[:, 2:3] * hat + columns[:, 3:4]
    value, slope = gelu_both(normed)
    weight = mask_ref[0:1, :]
    value_ref[...] = (weight * value).astype(bf16)
    first = unit_ref.shape[0]
    cot = shared_ref[:, first : first + unit_ref.shape[1]].astype(f32)
    delta = slope * (weight * cot)
    delta_ref[...] = delta
    sums = put_lanes(
        columns.shape,
        {
            0: jnp.sum(delta, axis=1, keepdims=True),
            1: jnp.sum(delta * hat, axis=1, keepdims=True),
        },
    ).T[:8]
    sums = stacked(sums, 2)
    for at in range(out_ref.shape[0]):
        out_ref[at] = sums


def head_norm(parts, unit, shared, strip_mask, coef_rows):
    channels, strip = unit.shape
    count = parts.shape[0]
    return call(
        head_kernel,
        "head_norm",
        (1,),
        0,
        [full(parts.shape), full(unit.shape), full(shared.shape), full((8, strip)), full(coef_rows.shape)],
        (
            full((channels, strip)),
            full((channels, strip)),
            full((channels, LANES)),
            full((8, channels)),
            full((count, 4, LANES)),
        ),
        (
            jax.ShapeDtypeStruct((channels, strip), bf16),
            jax.ShapeDtypeStruct((channels, strip), f32),
            jax.ShapeDtypeStruct((channels, LANES), f32),
            jax.ShapeDtypeStruct((8, channels), f32),
            jax.ShapeDtypeStruct((count, 4, LANES), f32),
        ),
        vmem=24,
    )(parts, unit, shared, strip_mask, coef_rows)


def unit_back_kernel(
    parts_ref, unit_ref, delta_ref, col_ref, mask_ref, row_ref, shared_ref, back_ref, out_ref, sum_ref, moment_ref
):
    sums = unstacked(jnp.sum(parts_ref[...], axis=0))
    moment_ref[...] = sums
    moments = tall(sums)
    pixel_total = row_ref[COUNT : COUNT + 1, 0:1]
    inverse = col_ref[:, 1:2]
    hat = (unit_ref[...] - col_ref[:, 0:1]) * inverse
    back = mask_ref[0:1, :] * (
        (col_ref[:, 2:3] * inverse)
        * (delta_ref[...] - (moments[:, 0:1] + hat * moments[:, 1:2]) / pixel_total)
    )
    back = back.astype(bf16)
    back_ref[...] = back
    row_sums = jnp.sum(back.astype(f32), axis=1, keepdims=True)
    sum_ref[...] = jnp.broadcast_to(row_sums, sum_ref.shape)
    channels = shared_ref.shape[0]
    rows, width = out_ref.shape[1:]
    proj = shared_ref[:, channels + width : shared_ref.shape[1] - TERMS]
    terms = lax.dot_general(
        proj, back, (((0,), (0,)), ((), ())), preferred_element_type=f32
    )
    pool = jnp.sum(shared_ref[:, :channels].astype(f32) * row_sums, axis=0, keepdims=True)
    own = channels // 4
    for quad in range(4):
        first = quad * own // LANES * LANES
        part = pool[:, first : first + LANES]
        if quad * own != first:
            part = pltpu.roll(part, LANES - (quad * own - first), 1)
        lane = lax.broadcasted_iota(jnp.int32, part.shape, 1)
        part = jnp.where(lane < own, part, 0.0)
        high = part.astype(bf16).astype(f32)
        extra = put_rows((EXTRA, LANES), {0: high, 1: part - high})
        out_ref[quad, : rows - EXTRA, :] = terms[quad * rows : (quad + 1) * rows - EXTRA].astype(bf16)
        out_ref[quad, rows - EXTRA :, :LANES] = extra.astype(bf16)
        out_ref[quad, rows - EXTRA :, LANES:] = jnp.zeros((EXTRA, width - LANES), bf16)


def unit_backward(parts, unit, delta, cols, strip_mask, coef_rows, shared):
    channels, strip = unit.shape
    rows = (shared.shape[1] - channels - strip - TERMS) // 4
    arrays = (parts, unit, delta, cols, strip_mask, coef_rows, shared)
    return call(
        unit_back_kernel,
        "unit_back",
        (1,),
        0,
        [full(array.shape) for array in arrays],
        (
            full((channels, strip)),
            full((4, rows, strip)),
            full((channels, LANES)),
            full((8, channels)),
        ),
        (
            jax.ShapeDtypeStruct((channels, strip), bf16),
            jax.ShapeDtypeStruct((4, rows, strip), bf16),
            jax.ShapeDtypeStruct((channels, LANES), f32),
            jax.ShapeDtypeStruct((8, channels), f32),
        ),
        vmem=24,
    )(*arrays)


def branch_kernel(x_ref, pre_ref, col_ref, row_ref, mask_ref, delta_ref, pool_ref, out_ref, sums, pooled):
    step = pl.program_id(0)
    chans = pre_ref.shape[2]

    @pl.when(step == 0)
    def _():
        sums[...] = jnp.zeros_like(sums)
        pooled[...] = jnp.zeros_like(pooled)

    def fold(value):
        total = value[:, :LANES]
        for at in range(1, value.shape[1] // LANES):
            total = total + value[:, at * LANES : (at + 1) * LANES]
        return total

    weight = mask_ref[0:1, :]
    for z in range(4):
        span = slice(z * chans, (z + 1) * chans)
        for branch in range(4):
            first = (4 * z + branch) * chans
            hat = (
                pre_ref[z, branch] - col_ref[span, CENTRE + branch : CENTRE + branch + 1]
            ) * col_ref[span, INVERSE + branch : INVERSE + branch + 1]
            normed = (
                col_ref[span, GAIN + branch : GAIN + branch + 1] * hat
                + col_ref[span, SHIFT + branch : SHIFT + branch + 1]
            )
            delta = gelu_both(normed)[1] * (
                weight * x_ref[0, first : first + chans, :].astype(f32)
            )
            delta_ref[z, branch] = delta
            sums[8 * z + branch] = sums[8 * z + branch] + fold(delta)
            sums[8 * z + 4 + branch] = sums[8 * z + 4 + branch] + fold(delta * hat)
    extra = x_ref[0, 16 * chans :, :LANES].astype(f32)
    pooled[...] = pooled[...] + jnp.broadcast_to(extra[0:1] + extra[1:2], pooled.shape)

    @pl.when(step == pl.num_programs(0) - 1)
    def _():
        normed, hat, valid = pool_rows_of(row_ref, 4 * chans)
        delta = jnp.where(valid, gelu_both(normed)[1] * pooled[0:1, :], 0.0)
        hat = jnp.where(valid, hat, 0.0)
        pool_ref[...] = put_rows(pool_ref.shape, {0: delta, 1: hat})
        found = []
        for z in range(4):
            columns = {}
            for branch in range(4):
                columns[branch] = jnp.sum(sums[8 * z + branch], axis=1, keepdims=True)
                columns[8 + branch] = jnp.sum(sums[8 * z + 4 + branch], axis=1, keepdims=True)
            found.append(put_lanes((chans, LANES), columns))
        found.append(jnp.zeros((LANES - 4 * chans, LANES), f32))
        rows = jnp.concatenate(found, axis=0).T[:16]
        index = lax.broadcasted_iota(jnp.int32, rows.shape, 0)
        rows = jnp.where(index == 4, delta, jnp.where(index == 12, delta * hat, rows))
        rows = beside(rows[:8], rows[8:16], 4 * chans)
        for at in range(out_ref.shape[0]):
            out_ref[at] = rows


def branch_backward(concat_back, pre, coef_cols, coef_rows, mask_rows, count, after):
    chans, total = pre.shape[2:]
    rows, strip = concat_back.shape[1:]
    spread = pl.BlockSpec((4, 4, chans, strip), lambda i: (0, 0, 0, i))
    return call(
        branch_kernel,
        "branch_back",
        (4,),
        0,
        [
            pl.BlockSpec((1, rows, strip), lambda i: (i, 0, 0)),
            spread,
            full(coef_cols.shape),
            full(coef_rows.shape),
            pl.BlockSpec((8, strip), lambda i: (0, i)),
        ],
        (spread, full((8, LANES)), full((count, 8, LANES))),
        (
            jax.ShapeDtypeStruct(pre.shape, f32),
            jax.ShapeDtypeStruct((8, LANES), f32),
            jax.ShapeDtypeStruct((count, 8, LANES), f32),
        ),
        [pltpu.VMEM((32, chans, LANES), f32), pltpu.VMEM((8, LANES), f32)],
        after=after,
        vmem=24,
    )(concat_back, pre, coef_cols, coef_rows, mask_rows)


def weight_kernel(columns, image_total, slots, scalar_ref, parts_ref, pool_ref, mask_ref, x_ref, *refs):
    count = len(slots)
    col_refs, pre_refs, delta_refs = refs[:count], refs[count : 2 * count], refs[2 * count : 3 * count]
    outs = refs[3 * count : 6 * count]
    total_ref, moments = refs[6 * count :]
    half = outs[0].shape[0]
    chans = pre_refs[0].shape[2]
    start = 29 * chans - half
    sel = scalar_ref[HALF]

    @pl.when(pl.program_id(0) == 0)
    def _():
        sums = jnp.sum(parts_ref[...], axis=0)
        second = pltpu.roll(sums, LANES // 2, 1)
        moments[...] = tall(jnp.concatenate([sums, second, pool_ref[...]], axis=0))
        height = jnp.full((1, 1), scalar_ref[HEIGHT], jnp.int32).astype(f32)
        area = 2.0 * height * height
        masks = lane_masks(columns)
        for at, slot in enumerate(slots):
            own = moments[pl.ds(pl.multiple_of(scalar_ref[4 + slot] * chans, chans), chans), :]
            build_taps(
                own, col_refs[at][...], pre_refs[at], delta_refs[at], mask_ref, outs[3 * at + 2], masks, area, columns, image_total
            )

    for at in range(count):
        keep_ref, send_ref, taps_ref = outs[3 * at : 3 * at + 3]
        total_ref[...] = jnp.dot(taps_ref[...], x_ref[...], preferred_element_type=f32)
        keep_ref[...] = total_ref[pl.ds(pl.multiple_of(sel * start, 16), half), :].astype(bf16)
        send_ref[...] = total_ref[pl.ds(pl.multiple_of((1 - sel) * start, 16), half), :].astype(bf16)


def build_taps(own, coefs, pre_ref, delta_ref, mask_ref, taps_ref, masks, area, columns, image_total):
    chans = pre_ref.shape[2]

    def coef(at):
        return coefs[:, at : at + 1]

    def moment(at):
        return own[:, at : at + 1]

    pixel_total = coef(COUNT)
    pool_grad = (
        coef(GAIN + 4)
        * coef(INVERSE + 4)
        * (moment(16) - (moment(4) + moment(17) * moment(12)) / image_total)
    ) / area
    tiles = pre_ref.shape[3] // LANES
    for at in range(tiles):
        lanes = slice(at * LANES, (at + 1) * LANES)
        weight = mask_ref[0:1, lanes]
        taps_ref[28 * chans : 29 * chans, lanes] = (weight * pool_grad).astype(bf16)
        for branch in range(4):
            hat = (pre_ref[0, branch, :, lanes] - coef(CENTRE + branch)) * coef(INVERSE + branch)
            grad = weight * (
                (coef(GAIN + branch) * coef(INVERSE + branch))
                * (
                    delta_ref[0, branch, :, lanes]
                    - (moment(branch) + hat * moment(8 + branch)) / pixel_total
                )
            )
            if branch == 0:
                taps_ref[0:chans, lanes] = grad.astype(bf16)
                continue
            j, dilation = branch - 1, dilations[branch - 1]
            jump = dilation * columns // LANES
            for b in range(3):
                off = (b - 1) * dilation
                moved = grad
                if off != 0:
                    moved = pltpu.roll(grad, off % LANES, 1)
                    moved = jnp.where(masks[-off], moved, 0.0)
                moved = moved.astype(bf16)
                for a in range(3):
                    tap = 1 + 9 * j + 3 * a + b
                    span = slice(tap * chans, (tap + 1) * chans)
                    target = at + (a - 1) * jump
                    if 0 <= target < tiles:
                        taps_ref[span, target * LANES : (target + 1) * LANES] = moved
                    source = at - (a - 1) * jump
                    if not 0 <= source < tiles:
                        taps_ref[span, lanes] = jnp.zeros((chans, LANES), bf16)


def weight_grads(
    slots, scalars, parts, pool_rows, coef_cols, pre, delta, mask_rows, pixels, columns, half, image_total, after
):
    chans, total = pre.shape[2:]
    depth = pixels.shape[1]
    block = depth // 4
    count = len(slots)

    def cols(slot):
        return pl.BlockSpec((chans, LANES), lambda i, s: (s[4 + slot], 0))

    def own(slot):
        return pl.BlockSpec((1, 4, chans, total), lambda i, s: (s[4 + slot], 0, 0, 0))

    outs = call(
        functools.partial(weight_kernel, columns, image_total, slots),
        "atrous_weight_grad",
        (4,),
        1,
        [
            full(parts.shape),
            full(pool_rows.shape),
            full(mask_rows.shape),
            pl.BlockSpec((total, block), lambda i, s: (0, i)),
        ]
        + [cols(slot) for slot in slots]
        + [own(slot) for slot in slots] * 2,
        (
            pl.BlockSpec((half, block), lambda i, s: (0, i)),
            pl.BlockSpec((half, block), lambda i, s: (0, i)),
            full((29 * chans, total)),
        )
        * count,
        (
            jax.ShapeDtypeStruct((half, depth), bf16),
            jax.ShapeDtypeStruct((half, depth), bf16),
            jax.ShapeDtypeStruct((29 * chans, total), bf16),
        )
        * count,
        [pltpu.VMEM((29 * chans, block), f32), pltpu.VMEM((LANES, LANES), f32)],
        after=after,
        vmem=28 if slots[0] == 3 else 56,
    )(
        scalars,
        parts,
        pool_rows,
        mask_rows,
        pixels,
        *[coef_cols] * count,
        *[pre] * count,
        *[delta] * count,
    )
    return [outs[3 * at : 3 * at + 3] for at in range(count)]


def input_kernel(start, places, scalar_ref, *refs):
    taps, weights, outs = refs[0:4], refs[4:12], refs[12:15]
    all_weights, all_taps, result, weight_sems, tap_sems, out_sems = refs[15:]
    half, depth = weights[0].shape
    block = all_taps.shape[2]
    cut = depth // 2

    def tap_copies(strip):
        copies = []
        lanes = pl.ds(pl.multiple_of(scalar_ref[places[strip]] * block, LANES), block)
        for slot in range(4):
            sel = scalar_ref[slot]
            for which in range(2):
                first = sel * start if which == 0 else (1 - sel) * start
                at = 2 * slot + which
                copies.append(
                    pltpu.make_async_copy(
                        taps[slot].at[pl.ds(pl.multiple_of(first, 16), half), lanes],
                        all_taps.at[strip, pl.ds(at * half, half), :],
                        tap_sems.at[strip, at],
                    )
                )
        return copies

    def weight_copies(part):
        lanes = pl.ds(part * cut, cut)
        return [
            pltpu.make_async_copy(
                weights[at].at[:, lanes],
                all_weights.at[pl.ds(at * half, half), lanes],
                weight_sems.at[part, at],
            )
            for at in range(8)
        ]

    tap_lists = [tap_copies(0), tap_copies(1)]
    weight_lists = [weight_copies(0), weight_copies(1)]
    for copies in (tap_lists[0], weight_lists[0], weight_lists[1], tap_lists[1]):
        for copy in copies:
            copy.start()
    rows = outs[0].shape[0]
    out_lists = [
        [
            pltpu.make_async_copy(result.at[0, pl.ds(0, rows), :], outs[0], out_sems.at[0]),
            pltpu.make_async_copy(result.at[0, pl.ds(rows, rows), :], outs[1], out_sems.at[1]),
        ],
        [pltpu.make_async_copy(result.at[1], outs[2], out_sems.at[2])],
    ]
    for strip in range(2):
        for copy in tap_lists[strip]:
            copy.wait()
        for part in range(2):
            if strip == 0:
                for copy in weight_lists[part]:
                    copy.wait()
            lanes = slice(part * cut, (part + 1) * cut)
            result[strip, :, lanes] = lax.dot_general(
                all_taps[strip],
                all_weights[:, lanes],
                (((0,), (0,)), ((), ())),
                preferred_element_type=f32,
            ).astype(bf16)
        for copy in out_lists[strip]:
            copy.start()
    for copies in out_lists:
        for copy in copies:
            copy.wait()


def input_grads(flip, taps, weights, scalars, block, after):
    rows = taps[0].shape[0]
    half, depth = weights[0].shape
    shapes = ((block // 2, depth), (block // 2, depth), (block, depth))
    anywhere = pl.BlockSpec(memory_space=pl.ANY)
    low, high, own = call(
        functools.partial(input_kernel, rows - half, (HALF + 2 + flip, HALF + 1 + flip)),
        "atrous_input_grad",
        (1,),
        1,
        [anywhere] * 12,
        (anywhere,) * 3,
        tuple(jax.ShapeDtypeStruct(shape, bf16) for shape in shapes),
        [
            pltpu.VMEM((8 * half, depth), bf16),
            pltpu.VMEM((2, 8 * half, block), bf16),
            pltpu.VMEM((2, block, depth), bf16),
            pltpu.SemaphoreType.DMA((2, 8)),
            pltpu.SemaphoreType.DMA((2, 8)),
            pltpu.SemaphoreType.DMA((3,)),
        ],
        after=after,
        vmem=58,
    )(scalars, *taps, *weights)
    return [low, high], own


def local(
    features,
    scale_sizes,
    cotangent,
    branch_weight,
    branch_first,
    branch_second,
    head_weight,
    head_first,
    head_second,
    norm_params,
    norm_first,
    norm_second,
    running_stats,
):
    groups = lax.axis_size("dp")
    halves = groups == 2
    images = scale_sizes.shape[1]
    image_total = float(groups * images)
    x_id, z_id = lax.axis_index("dp"), lax.axis_index("z")
    quad_id = lax.axis_index("y") * 2 + lax.axis_index("c")
    wide_id = z_id * 4 + quad_id
    strip_rows, columns, depth = features.shape[1:]
    strip = strip_rows * columns
    total = 4 * strip
    tap_count, chans = branch_weight.shape[:2]
    all_ch = chans * 16
    split = (tap_count - 1) // 2
    half = (split + 1) * chans
    cells, everyone = ("dp", "z"), ("dp",) + PLANE
    rows = 16 * chans + EXTRA

    def exchange(parts, axes):
        return lax.all_to_all(parts, axes, 0, 0, tiled=True)

    height = lax.dynamic_index_in_dim(scale_sizes[0], z_id, 0, keepdims=False)
    pixel = jnp.arange(total, dtype=jnp.int32)
    inside = jnp.logical_and(pixel // columns < height, pixel % columns < 2 * height).astype(f32)
    own_inside = lax.dynamic_slice_in_dim(inside, quad_id * strip, strip, 0)
    mask_rows = jnp.broadcast_to(inside[None], (8, total))
    strip_mask = jnp.broadcast_to(own_inside[None], (8, strip))

    mid = jnp.logical_and(z_id >= 1, z_id <= 2).astype(jnp.int32)[None]

    sel = x_id.astype(jnp.int32) if halves else jnp.zeros((), jnp.int32)
    outer = z_id >= 2
    scalars = jnp.stack(
        [sel, sel, sel, sel]
        + [z_id, jnp.bitwise_xor(z_id, 1), jnp.where(outer, 1, 2), jnp.where(outer, 0, 3)]
        + [height, sel]
        + [jnp.bitwise_xor(quad_id, flip) for flip in range(4)]
    ).astype(jnp.int32)
    def over_groups(block):
        return lax.ppermute(block, "dp", SWAP)

    def along(parts, pairs):
        return [lax.ppermute(part, "z", pairs) for part in parts]

    def hold(parts, after):
        return [held(part, after) for part in parts]

    def pair_of(parts):
        return (parts[0], over_groups(parts[0])) if halves else tuple(parts)

    def pick_all(ones, twos, after):
        return [pick(mid, one, two, after) for one, two in zip(ones, twos)]

    zero = jnp.zeros((), jnp.int32)
    mine_w = cast_half(sel[None], branch_weight, split, ())
    other_w = cast_half(1 - sel[None], branch_weight, split, (mine_w,))
    sending = [mine_w] if halves else [mine_w, other_w]
    near, mid_one = along(sending, PAIR), along(sending, MID)

    own_strip = features[0].reshape(strip, depth)
    cut = strip // 16 * 7
    (masked_low,) = mask_strip(scalars, own_strip, columns, cut, (cut,), sending)
    masked, masked_high = mask_strip(
        scalars, own_strip, columns, strip, (strip, strip - cut), (masked_low,)
    )
    masked_parts = masked_low, masked_high
    low_y, high_y = (lax.ppermute(part, "y", SWAP) for part in masked_parts)
    over_c = lax.ppermute(masked, "c", SWAP)

    own_proj = head_weight.astype(bf16).reshape(chans, 5, 4, 4, chans)
    own_proj = jnp.transpose(own_proj, (0, 3, 2, 1, 4))
    pixel_proj = jnp.pad(
        own_proj[:, :, :, :4].reshape(chans, 4, 16 * chans), ((0, 0), (0, 0), (0, EXTRA))
    ).reshape(chans, 4 * rows)
    value = jnp.transpose(norm_params.reshape(12, chans))
    terms = []
    for _ in range(3):
        terms.append(barrier(value.astype(bf16)))
        value = value - terms[-1].astype(f32)
    terms = jnp.pad(jnp.stack(terms, axis=2).reshape(chans, 36), ((0, 0), (0, TERMS - 36)))
    shared = jnp.concatenate(
        [
            jnp.broadcast_to(own_proj[:, :, :, 4].reshape(1, chans, all_ch), (16, chans, all_ch)),
            jnp.transpose(cotangent[0].reshape(chans, 16, strip), (1, 0, 2)),
            jnp.broadcast_to(pixel_proj[None], (16, chans, 4 * rows)),
            jnp.broadcast_to(terms[None], (16, chans, TERMS)),
        ],
        axis=2,
    )

    slots = [(mine_w, other_w)]
    near = hold(near, [masked, mask_rows, scalars])
    mid_two = along(near, MID)
    near = pair_of(near)
    mid_one = hold(mid_one, near[:1])
    out_one = along(mid_one, OUTWARD)
    low_y = held(low_y, mid_one)
    mid_two = hold(mid_two, [low_y, other_w, shared, strip_mask])
    out_two = along(mid_two, OUTWARD)
    second = pick_all(mid_one, out_one, mid_two)
    second_pair = pair_of(second)
    high_y = held(high_y, second)
    low_yc, high_yc = (lax.ppermute(part, "c", SWAP) for part in (low_y, high_y))
    near = (near[0], held(near[1], (high_y,)))
    slots.append(near)
    parts = ((masked,), (over_c,), (low_y, high_y), (low_yc, high_yc))
    pixels = image_of(scalars, strip, parts, near[1:])

    def branch(slot, state, after):
        return forward_taps(
            slot, pixels, mask_rows, scalars, *slots[slot], state, columns, chans, split, after
        )

    state = branch(0, (), ())
    slots.append((second_pair[0], held(second_pair[1], [state[1]])))
    third = pick_all(mid_two, out_two, slots[2][1:])
    slots.append(pair_of(third))
    shared = exchange(held(shared, third), PLANE)
    shared = shared.reshape(all_ch, all_ch + strip + 4 * rows + TERMS)
    state = branch(1, state, third)
    state = branch(2, state, ())
    state = branch(3, state, ())
    pre, stats = state
    own_sums = pack_sums(stats, axes_size(cells), (shared,))
    quad = quad_id.astype(jnp.int32)[None]
    concat, coef_cols, coef_rows = activations(
        quad, exchange(own_sums, cells), own_sums, shared, pre, image_total
    )
    concat = exchange(concat, QUAD).reshape(4 * rows, strip)

    unit, head_sums = project(concat, shared, strip_mask, axes_size(everyone))
    head_values, head_delta, head_coefs, head_rows, head_sums = head_norm(
        exchange(head_sums, everyone), unit, shared, strip_mask, coef_rows
    )
    unit_back, concat_back, row_sums, head_moments = unit_backward(
        exchange(head_sums, everyone),
        unit,
        head_delta,
        head_coefs,
        strip_mask,
        coef_rows,
        shared,
    )

    delta, pool_rows, moments = branch_backward(
        exchange(concat_back, QUAD), pre, coef_cols, coef_rows, mask_rows, axes_size(cells), ()
    )
    moments = exchange(moments, cells)

    def weights_of(slots, after):
        return weight_grads(
            slots,
            scalars,
            moments,
            pool_rows,
            coef_cols,
            pre,
            delta,
            mask_rows,
            pixels,
            columns,
            half,
            image_total,
            after,
        )

    def group_sums(slot, after, *lists):
        if halves:
            return [add(slot[0], over_groups(slot[1]), *(parts[0] for parts in lists), after=after)]
        return [add(*parts, after=after) for parts in zip(slot[:2], *lists)]

    def swap_all(parts, axis):
        return [lax.ppermute(part, axis, SWAP) for part in parts]

    def add_all(*lists, after=()):
        return [add(*parts, after=after) for parts in zip(*lists)]

    flat_w = [part for slot in slots for part in slot]

    def features_of(flip, after):
        return input_grads(flip, taps, flat_w, scalars, strip, after)

    ((keep_c, send_c, taps_c),) = weights_of((3,), ())
    head_parts = head_weight_grads(concat, unit_back, row_sums, head_values, (taps_c,))
    head_parts = exchange(head_parts.reshape(16, chans, all_ch + strip + 4 * rows), PLANE)
    slot_b, slot_a, slot_o = weights_of((2, 1, 0), (taps_c,))
    taps = [slot_o[2], slot_a[2], slot_b[2], taps_c]
    third = group_sums((keep_c, send_c), (slot_o[2], head_parts))
    far_cross, far = features_of(2, third)
    second = group_sums(slot_b, (far,))
    mid_two = add_all(third, along(third, INWARD), after=second)
    far = strip_sum(scalars, (far,), swap_all(far_cross, "c"), columns, False, mid_two)
    near = group_sums(slot_a, (far,), along(mid_two, MID))
    mid_one = add_all(second, along(second, INWARD), after=near)

    head_output = head_parts[:, :, all_ch : all_ch + strip]
    head_output = jnp.transpose(head_output, (1, 0, 2)).reshape(1, chans, 16 * strip)
    head_parts = jnp.sum(head_parts.astype(f32), axis=0)
    pool_part = head_parts[:, :all_ch].reshape(chans, 4, 4, 1, chans)
    pixel_part = head_parts[:, all_ch + strip :].reshape(chans, 4, rows)[:, :, : 16 * chans]
    pixel_part = pixel_part.reshape(chans, 4, 4, 4, chans)
    head_grads = jnp.concatenate([pixel_part, pool_part], axis=3)
    head_grads = jnp.transpose(head_grads, (0, 3, 2, 1, 4)).reshape(chans, 5 * all_ch)
    near_cross, own_part = features_of(0, (*mid_one, head_grads))
    if halves:
        head_grads = head_grads + lax.ppermute(head_grads, "dp", SWAP)
    else:
        head_grads = lax.psum(head_grads, "dp")
    mine = group_sums(slot_o, (own_part, head_grads), along(near, PAIR), along(mid_one, MID))
    state = (branch_weight, branch_first, branch_second)
    if halves:
        other = over_groups(mine[0])
    else:
        mine = [lax.psum(part, "dp") for part in mine]
    cross = swap_all(near_cross, "c")
    total = held(own_part, mine).astype(f32) + jnp.concatenate(cross, axis=0).astype(f32)
    total = total + lax.ppermute(far, "y", SWAP).astype(f32)
    input_grad = (total * own_inside[:, None]).astype(bf16)
    input_grad = input_grad.reshape(1, strip_rows, columns, depth)
    start = jnp.stack([sel * split, zero])
    done = adam_taps(start, split + 1, 5, mine[0], *state, (), (input_grad,))
    start = jnp.stack([(1 - sel) * (split + 1), 1 - sel])
    done = adam_taps(start, split, 7, other if halves else mine[1], *state, done, ())
    branch_grads, branch_means, branch_squares, branch_updated = done

    def own_lanes(by_row):
        return lax.dynamic_slice_in_dim(by_row, z_id * chans, chans, 1)

    def own_head(by_row):
        return lax.dynamic_slice_in_dim(by_row, wide_id * chans, chans, 1)

    moments = jnp.sum(moments, axis=0)
    own_firsts, own_seconds = own_lanes(moments), own_lanes(moments[:, 4 * chans :])
    head_own = own_head(head_moments)
    norm_grads = jnp.stack(
        [
            jnp.concatenate([own_seconds[0:5], head_own[1:2]]),
            jnp.concatenate([own_firsts[0:5], head_own[0:1]]),
        ]
    )
    own_coefs, head_stats = own_lanes(coef_rows), own_head(head_rows)
    pixel_total = coef_rows[COUNT, 0]
    all_centres = jnp.concatenate([own_coefs[CENTRE : CENTRE + 5], head_stats[0:1]])
    all_variances = jnp.concatenate([own_coefs[VARIANCE : VARIANCE + 5], head_stats[4:5]])
    factors = jnp.where(
        jnp.arange(6) == 4, image_total / (image_total - 1.0), pixel_total / (pixel_total - 1.0)
    )
    running_next = (1.0 - momentum) * running_stats + momentum * jnp.stack(
        [all_centres, all_variances * factors[:, None]]
    )
    head_means, head_squares, head_updated = adamw_update(
        head_weight, head_grads, head_first, head_second, conv_rate, weight_decay
    )
    norm_means, norm_squares, norm_updated = adamw_update(
        norm_params, norm_grads, norm_first, norm_second, norm_rate, 0.0
    )
    return (
        head_output,
        input_grad,
        branch_grads,
        branch_means,
        branch_squares,
        branch_updated,
        head_grads,
        head_means,
        head_squares,
        head_updated,
        norm_grads,
        norm_means,
        norm_squares,
        norm_updated,
        running_next,
    )


def solution(mesh):
    groups, wide = mesh.devices.shape
    fine = Mesh(mesh.devices.reshape(groups, 4, 2, wide // 8), ("dp",) + PLANE)
    placed = (
        P("dp", PLANE, None, None),
        P("dp", None),
        P("dp", PLANE, None),
        P(None, PLANE, None),
        P(None, PLANE, None),
        P(None, PLANE, None),
        P(PLANE, None),
        P(PLANE, None),
        P(PLANE, None),
        P(None, None, PLANE),
        P(None, None, PLANE),
        P(None, None, PLANE),
        P(None, None, PLANE),
    )
    return jax.shard_map(
        local,
        mesh=fine,
        in_specs=placed,
        out_specs=(
            P("dp", PLANE, None),
            P("dp", PLANE, None, None),
            P(None, PLANE, None),
            P(None, PLANE, None),
            P(None, PLANE, None),
            P(None, PLANE, None),
            P(PLANE, None),
            P(PLANE, None),
            P(PLANE, None),
            P(PLANE, None),
            P(None, None, PLANE),
            P(None, None, PLANE),
            P(None, None, PLANE),
            P(None, None, PLANE),
            P(None, None, PLANE),
        ),
        check_vma=False,
    )
```

```python
import functools

import jax
import jax.numpy as jnp
from jax import lax
from jax.experimental import pallas as pl
from jax.experimental.pallas import tpu as pltpu
from jax.sharding import Mesh, PartitionSpec as P

STEP = 10


dilations = (6, 12, 18)
epsilon = 1e-05
momentum = 0.1
first_decay = 0.9
second_decay = 0.999
conv_rate = 0.02
norm_rate = 0.4
weight_decay = 0.0001
adam_floor = 1e-08

LANES = 128
PLANE = ("z", "y", "c")
QUAD = ("y", "c")
SWAP = [(0, 1), (1, 0)]
PAIR = [(0, 1), (1, 0), (2, 3), (3, 2)]
MID = [(1, 2), (2, 1)]
OUTWARD = [(1, 0), (2, 3)]
INWARD = [(0, 1), (3, 2)]

bf16 = jnp.bfloat16
f32 = jnp.float32
barrier = lax.optimization_barrier


def adamw_update(parameter, gradient, moment_one, moment_two, step_rate, decay_rate):
    first_new = first_decay * moment_one + (1.0 - first_decay) * gradient
    second_new = second_decay * moment_two + (1.0 - second_decay) * gradient * gradient
    first_hat = first_new / (1.0 - first_decay**STEP)
    second_hat = second_new / (1.0 - second_decay**STEP)
    updated = parameter - step_rate * (
        first_hat / (jnp.sqrt(second_hat) + adam_floor) + decay_rate * parameter
    )
    return (first_new, second_new, updated)


def gelu_both(value):
    scale = (2.0 / jnp.pi) ** 0.5
    square = value * value
    bend = jnp.tanh(scale * (value + 0.044715 * (value * square)))
    lead = 0.5 * (1.0 + bend)
    slope = lead + 0.5 * value * (1.0 - bend * bend) * (scale * (1.0 + 3.0 * 0.044715 * square))
    return value * lead, slope


def tall(rows):
    fill = LANES - rows.shape[0]
    return jnp.concatenate([rows, jnp.zeros((fill, rows.shape[1]), rows.dtype)], axis=0).T


def stacked(rows, count):
    found = {}
    for at in range(count):
        found[2 * at] = rows[at : at + 1, :LANES]
        found[2 * at + 1] = rows[at : at + 1, LANES:]
    return put_rows((8, LANES), found)[: 2 * count]


def unstacked(rows):
    found = {}
    for at in range(rows.shape[0] // 2):
        found[at] = jnp.concatenate([rows[2 * at : 2 * at + 1], rows[2 * at + 1 : 2 * at + 2]], axis=1)
    return put_rows((8, 2 * LANES), found)


def beside(left, right, width):
    lane = lax.broadcasted_iota(jnp.int32, left.shape, 1)
    return jnp.where(lane < width, left, pltpu.roll(right, width, 1))


def put_lanes(shape, columns):
    lane = lax.broadcasted_iota(jnp.int32, shape, 1)
    total = jnp.zeros(shape, f32)
    for at, column in columns.items():
        total = jnp.where(lane == at, column, total)
    return total


def put_rows(shape, rows):
    row = lax.broadcasted_iota(jnp.int32, shape, 0)
    total = jnp.zeros(shape, f32)
    for at, value in rows.items():
        total = jnp.where(row == at, value, total)
    return total


def axes_size(axes):
    count = 1
    for axis in axes:
        count *= lax.axis_size(axis)
    return count


def call(
    kernel,
    name,
    grid,
    scalars,
    in_specs,
    out_specs,
    out_shape,
    scratch=(),
    aliases=None,
    flops=0,
    after=(),
    vmem=24,
):
    after = tuple(after)
    first = scalars + len(in_specs)

    def body(*refs):
        kernel(*refs[:first], *refs[first + len(after) :])

    run = pl.pallas_call(
        body,
        out_shape=out_shape,
        grid_spec=pltpu.PrefetchScalarGridSpec(
            num_scalar_prefetch=scalars,
            grid=grid,
            in_specs=list(in_specs) + [pl.BlockSpec(memory_space=pl.ANY)] * len(after),
            out_specs=out_specs,
            scratch_shapes=list(scratch),
        ),
        input_output_aliases=aliases or {},
        compiler_params=pltpu.CompilerParams(vmem_limit_bytes=vmem << 20),
        cost_estimate=pl.CostEstimate(flops=1, bytes_accessed=1, transcendentals=0),
        name=name,
    )
    return lambda *arrays: run(*arrays, *after)


def full(shape):
    return pl.BlockSpec(shape, lambda *_: (0,) * len(shape))


def add_kernel(*refs):
    total = refs[0][...].astype(f32)
    for ref in refs[1:-1]:
        total = total + ref[...].astype(f32)
    refs[-1][...] = total.astype(bf16)


def add(*values, after=()):
    first = held(values[0], after) if after else values[0]
    total = first.astype(f32)
    for value in values[1:]:
        total = total + value.astype(f32)
    return barrier(total.astype(bf16))


def pick_kernel(flag_ref, one_ref, two_ref, out_ref):
    @pl.when(flag_ref[0] == 1)
    def _():
        out_ref[...] = one_ref[...]

    @pl.when(flag_ref[0] != 1)
    def _():
        out_ref[...] = two_ref[...]


def pick(flag, one, two, after=()):
    rows, depth = one.shape
    spec = pl.BlockSpec((rows // 3, depth), lambda i, s: (i, 0))
    return call(
        pick_kernel,
        "pick",
        (3,),
        1,
        [spec, spec],
        spec,
        jax.ShapeDtypeStruct(one.shape, one.dtype),
        after=after,
    )(flag, one, two)


def held_kernel(in_ref, out_ref):
    del in_ref, out_ref


def held(value, after):
    anywhere = pl.BlockSpec(memory_space=pl.ANY)
    return call(
        held_kernel,
        "held",
        (1,),
        0,
        [anywhere],
        anywhere,
        jax.ShapeDtypeStruct(value.shape, value.dtype),
        aliases={0: 0},
        after=after,
        vmem=56,
    )(value)


def cast_kernel(sel_ref, in_ref, out_ref):
    taps, chans = in_ref.shape[:2]
    first = jnp.logical_and(sel_ref[0] == 1, pl.program_id(0) == 0)
    for tap in range(taps):
        value = in_ref[tap]
        if tap == 0:
            value = jnp.where(first, 0.0, value)
        out_ref[tap * chans : (tap + 1) * chans, :] = value.astype(bf16)


def cast_half(sel, weight, split, after):
    chans, depth = weight.shape[1:]
    parts = 3 if (split + 1) % 3 == 0 else 1
    block = (split + 1) // parts
    return call(
        cast_kernel,
        "cast",
        (parts,),
        1,
        [pl.BlockSpec((pl.Element(block), pl.Element(chans), pl.Element(depth)), lambda i, s: (s[0] * split + i * block, 0, 0))],
        pl.BlockSpec((block * chans, depth), lambda i, s: (i, 0)),
        jax.ShapeDtypeStruct(((split + 1) * chans, depth), bf16),
        after=after,
        vmem=56,
    )(sel, weight)


def mask_kernel(columns, strip, scalar_ref, in_ref, *out_refs):
    rows, depth = in_ref.shape
    pixel = lax.broadcasted_iota(jnp.int32, (rows, LANES), 0)
    row = pixel // columns + scalar_ref[HALF + 1] * (strip // columns)
    height = scalar_ref[HEIGHT]
    inside = jnp.logical_and(row < height, pixel % columns < 2 * height)
    for first in range(0, depth, LANES):
        lanes = slice(first, first + LANES)
        value = jnp.where(inside, in_ref[:, lanes].astype(f32), 0.0).astype(bf16)
        for out_ref in out_refs:
            out_ref[:, lanes] = value[rows - out_ref.shape[0] :]


def mask_strip(scalars, strip, columns, count, lasts, after):
    rows, depth = strip.shape
    return call(
        functools.partial(mask_kernel, columns, rows),
        "mask",
        (1,),
        1,
        [pl.BlockSpec((count, depth), lambda i, s: (0, 0))],
        tuple(full((last, depth)) for last in lasts),
        tuple(jax.ShapeDtypeStruct((last, depth), bf16) for last in lasts),
        after=after,
        vmem=56,
    )(scalars, strip)


def image_kernel(strip, places, spot_ref, *refs):
    *parts, out_ref, sems = refs
    copies = []
    for at, (which, first) in enumerate(places):
        rows = pl.ds(pl.multiple_of(spot_ref[HALF + 1 + which] * strip + first, 16), parts[at].shape[0])
        copies.append(pltpu.make_async_copy(parts[at], out_ref.at[rows, :], sems.at[at]))
    for copy in copies:
        copy.start()
    for copy in copies:
        copy.wait()


def image_of(spots, strip, parts, after):
    depth = parts[0][0].shape[1]
    places = []
    for which, strip_parts in enumerate(parts):
        first = 0
        for part in strip_parts:
            places.append((which, first))
            first += part.shape[0]
    flat = [part for strip_parts in parts for part in strip_parts]
    anywhere = pl.BlockSpec(memory_space=pl.ANY)
    return call(
        functools.partial(image_kernel, strip, places),
        "image",
        (1,),
        1,
        [anywhere] * len(flat),
        full((4 * strip, depth)),
        jax.ShapeDtypeStruct((4 * strip, depth), bf16),
        [pltpu.SemaphoreType.DMA((len(flat),))],
        after=after,
        vmem=56,
    )(spots, *flat)


def head_grad_kernel(x_ref, back_ref, sum_ref, value_ref, out_ref):
    channels = back_ref.shape[0]
    rows = x_ref.shape[0] // 4
    act = jnp.zeros((EXTRA, channels), f32)
    for quad in range(4):
        first = quad * rows + rows - EXTRA
        act = act + x_ref[first : first + EXTRA, :channels].astype(f32)
    out_ref[:, :channels] = (sum_ref[:, 0:1] * act[0:1, :]).astype(bf16)
    strip = x_ref.shape[1]
    out_ref[:, channels : channels + strip] = value_ref[...]
    out_ref[:, channels + strip :] = lax.dot_general(
        back_ref[...], x_ref[...], (((1,), (1,)), ((), ())), preferred_element_type=f32
    ).astype(bf16)


def head_weight_grads(concat, unit_back, row_sums, values, after):
    channels = unit_back.shape[0]
    arrays = (concat, unit_back, row_sums, values)
    shape = (channels, channels + concat.shape[1] + concat.shape[0])
    return call(
        head_grad_kernel,
        "head_weight_grad",
        (1,),
        0,
        [full(array.shape) for array in arrays],
        full(shape),
        jax.ShapeDtypeStruct(shape, bf16),
        after=after,
        vmem=24,
    )(*arrays)


def strip_sum_kernel(columns, whole, masked, scalar_ref, *refs):
    block = refs[0].shape[0]
    step = pl.program_id(0)
    rows_all = refs[whole].shape[0] * (len(refs) - 1 - whole)
    pixel = step * block + lax.broadcasted_iota(jnp.int32, (block, LANES), 0)
    row = pixel // columns + scalar_ref[HALF + 1] * (rows_all // columns)
    height = scalar_ref[HEIGHT]
    inside = jnp.logical_and(row < height, pixel % columns < 2 * height)
    steps = refs[whole].shape[0] * (len(refs) - 1 - whole) // block
    count = steps // (len(refs) - 1 - whole)
    for at in range(steps):

        @pl.when(step == at)
        def _():
            part = refs[whole + at // count]
            rows = slice(at % count * block, (at % count + 1) * block)
            for first in range(0, refs[0].shape[1], LANES):
                lanes = slice(first, first + LANES)
                total = part[rows, lanes].astype(f32)
                for ref in refs[:whole]:
                    total = total + ref[:, lanes].astype(f32)
                if masked:
                    total = jnp.where(inside, total, 0.0)
                refs[-1][:, lanes] = total.astype(bf16)


def strip_sum(scalars, strips, parts, columns, masked, after):
    rows, depth = strips[0].shape
    spec = pl.BlockSpec((rows // 2, depth), lambda i, s: (i, 0))
    return call(
        functools.partial(strip_sum_kernel, columns, len(strips), masked),
        "strip_sum",
        (2,),
        1,
        [spec] * len(strips) + [full(part.shape) for part in parts],
        spec,
        jax.ShapeDtypeStruct((rows, depth), bf16),
        after=after,
        vmem=56,
    )(scalars, *strips, *parts)


def adam_kernel(start_ref, grad_ref, weight_ref, first_ref, second_ref, *rest):
    out_ref, mean_ref, square_ref, new_ref = rest[-4:]
    grad = grad_ref[...].astype(f32).reshape(out_ref.shape)
    mean, square, new = adamw_update(
        weight_ref[...], grad, first_ref[...], second_ref[...], conv_rate, weight_decay
    )
    out_ref[...] = grad
    mean_ref[...] = mean
    square_ref[...] = square
    new_ref[...] = new


def adam_taps(start, count, block, grads, weight, first, second, earlier, after):
    taps, chans, depth = weight.shape

    def piece(size, index):
        return pl.BlockSpec(tuple(pl.Element(n) for n in size), index)

    spec = piece((block, chans, depth), lambda i, s: (s[0] + i * block, 0, 0))
    anywhere = [pl.BlockSpec(memory_space=pl.ANY)] * len(earlier)
    return call(
        adam_kernel,
        "adamw",
        (count // block,),
        1,
        [piece((block * chans, depth), lambda i, s: ((s[1] + i * block) * chans, 0))]
        + [spec] * 3
        + anywhere,
        (spec,) * 4,
        (jax.ShapeDtypeStruct(weight.shape, f32),) * 4,
        aliases={5 + at: at for at in range(4)} if earlier else None,
        after=after,
        vmem=36,
    )(start, grads, weight, first, second, *earlier)


FIRST, SECOND, GAIN, SHIFT, AREA = 0, 8, 16, 24, 5
SUM_ROWS = 8
CENTRE, INVERSE, VARIANCE, COUNT, POOLED = 0, 8, 32, 40, 41
COEF_ROWS = 48
EXTRA = 16
TERMS = 64
HEIGHT, HALF = 8, 9


def lane_masks(columns):
    lane = lax.broadcasted_iota(jnp.int32, (1, LANES), 1) % columns
    masks = {}
    for dilation in dilations:
        for off in (-dilation, dilation):
            moved = lane + off
            masks[off] = jnp.logical_and(moved >= 0, moved < columns)
    return masks


def forward_kernel(columns, split, slot, scalar_ref, x_ref, wz_ref, wx_ref, mask_ref, *rest):
    pre_ref, stat_ref, taps = rest[-3:]
    step = pl.program_id(0)
    half = wz_ref.shape[0]
    block = x_ref.shape[0]
    sel = scalar_ref[slot]
    contract = (((1,), (1,)), ((), ()))
    pixels = x_ref[...]
    cols = pl.ds(pl.multiple_of(step * block, block), block)
    taps[pl.ds(pl.multiple_of(sel * half, 16), half), cols] = lax.dot_general(
        wz_ref[...], pixels, contract, preferred_element_type=f32
    )
    taps[pl.ds(pl.multiple_of((1 - sel) * half, 16), half), cols] = lax.dot_general(
        wx_ref[...], pixels, contract, preferred_element_type=f32
    )

    @pl.when(step == pl.num_programs(0) - 1)
    def _():
        total = taps.shape[1]
        tiles = total // LANES
        chans = pre_ref.shape[2]
        masks = lane_masks(columns)

        def rows_of(tap):
            first = tap * chans if tap <= split else (tap + 1) * chans
            return slice(first, first + chans)

        def tile(tap, at):
            return taps[rows_of(tap), at * LANES : (at + 1) * LANES]

        sums = [jnp.zeros((chans, LANES), f32) for _ in range(4)]
        squares = [jnp.zeros((chans, LANES), f32) for _ in range(4)]
        pooled = jnp.zeros((chans, LANES), f32)
        for at in range(tiles):
            lanes = slice(at * LANES, (at + 1) * LANES)
            weight = mask_ref[0:1, lanes]
            for branch in range(4):
                if branch == 0:
                    value = tile(0, at)
                else:
                    dilation = dilations[branch - 1]
                    jump = dilation * columns // LANES
                    value = None
                    for b in range(3):
                        part = None
                        for a in range(3):
                            source = at + (a - 1) * jump
                            if 0 <= source < tiles:
                                term = tile(1 + 9 * (branch - 1) + 3 * a + b, source)
                                part = term if part is None else part + term
                        off = (b - 1) * dilation
                        if off != 0:
                            part = pltpu.roll(part, (-off) % LANES, 1)
                            part = jnp.where(masks[off], part, 0.0)
                        value = part if value is None else value + part
                pre_ref[0, branch, :, lanes] = value
                weighted = value * weight
                sums[branch] = sums[branch] + weighted
                squares[branch] = squares[branch] + weighted * value
            pooled = pooled + tile(28, at)
        height = jnp.full((1, 1), scalar_ref[HEIGHT], jnp.int32).astype(f32)
        area = 2.0 * height * height
        pool = jnp.sum(pooled, axis=1, keepdims=True) / area
        columns_of = {FIRST + 4: pool, SECOND + 4: pool * pool, AREA: area}
        for branch in range(4):
            columns_of[FIRST + branch] = jnp.sum(sums[branch], axis=1, keepdims=True)
            columns_of[SECOND + branch] = jnp.sum(squares[branch], axis=1, keepdims=True)
        stat_ref[0] = put_lanes((chans, LANES), columns_of)


def forward_taps(slot, pixels, mask_rows, scalars, wz, wx, earlier, columns, chans, split, after):
    total, depth = pixels.shape
    block = total // 4
    half = wz.shape[0]
    keep = [pl.BlockSpec(memory_space=pl.ANY)] * len(earlier)
    return call(
        functools.partial(forward_kernel, columns, split, slot),
        "atrous_forward",
        (4,),
        1,
        [
            pl.BlockSpec((block, depth), lambda i, s: (i, 0)),
            full((half, depth)),
            full((half, depth)),
            full((8, total)),
        ]
        + keep,
        (
            pl.BlockSpec((1, 4, chans, total), lambda i, s: (s[4 + slot], 0, 0, 0)),
            pl.BlockSpec((1, chans, LANES), lambda i, s: (s[4 + slot], 0, 0)),
        ),
        (
            jax.ShapeDtypeStruct((4, 4, chans, total), f32),
            jax.ShapeDtypeStruct((4, chans, LANES), f32),
        ),
        [pltpu.VMEM((2 * half, total), f32)],
        {5: 0, 6: 1} if earlier else None,
        4 * half * total * depth,
        after,
        56,
    )(scalars, pixels, wz, wx, mask_rows, *earlier)


def pack_kernel(stat_ref, out_ref, work):
    chans = stat_ref.shape[1]
    work[...] = jnp.zeros_like(work)
    for z in range(4):
        work[z * chans : (z + 1) * chans, :] = stat_ref[z]
    rows = work[...].T
    rows = beside(rows[:8], rows[8:16], 4 * chans)
    for at in range(out_ref.shape[0]):
        out_ref[at] = rows


def pack_sums(stats, count, after):
    return call(
        pack_kernel,
        "branch_sums",
        (1,),
        0,
        [full(stats.shape)],
        full((count, SUM_ROWS, LANES)),
        jax.ShapeDtypeStruct((count, SUM_ROWS, LANES), f32),
        [pltpu.VMEM((LANES, LANES), f32)],
        after=after,
        vmem=24,
    )(stats)


def term_sum(block, which, norm, start):
    first = start + 3 * (6 * which + norm)
    return block[:, first : first + 1] + block[:, first + 1 : first + 2] + block[:, first + 2 : first + 3]


def pool_rows_of(rows_ref, own_width):
    def row(at):
        return rows_ref[at : at + 1, :]

    moved = row(POOLED) - row(CENTRE + 4)
    normed = row(GAIN + 4) * moved * row(INVERSE + 4) + row(SHIFT + 4)
    lane = lax.broadcasted_iota(jnp.int32, normed.shape, 1)
    return normed, moved * row(INVERSE + 4), lane < own_width


def act_kernel(image_total, quad_ref, parts_ref, own_ref, term_ref, pre_ref, out_ref, col_ref, row_ref):
    chans = pre_ref.shape[2]

    @pl.when(pl.program_id(0) == 0)
    def _():
        sums = jnp.sum(parts_ref[...], axis=0)
        second = pltpu.roll(sums, LANES - 4 * chans, 1)
        found = []
        for z in range(4):
            place = pl.multiple_of((4 * z + quad_ref[0]) * chans, chans)
            block = term_ref[pl.ds(place, chans), :].astype(f32)
            columns = {}
            for norm in range(5):
                columns[norm] = term_sum(block, 0, norm, LANES - TERMS)
                columns[8 + norm] = term_sum(block, 1, norm, LANES - TERMS)
            found.append(put_lanes((chans, LANES), columns))
        found.append(jnp.zeros((LANES - 4 * chans, LANES), f32))
        affine = jnp.concatenate(found, axis=0).T
        pixel_total = jnp.maximum(sums[AREA : AREA + 1], 1.0)
        index = lax.broadcasted_iota(jnp.int32, (8, LANES), 0)
        count = jnp.where(index == 4, image_total, pixel_total)
        centre = sums / count
        variance = second / count - centre * centre
        inverse = lax.rsqrt(variance + epsilon)
        other = jnp.where(index == 0, pixel_total, jnp.where(index == 1, own_ref[0, 4:5, :], 0.0))
        rows = jnp.concatenate(
            [centre, inverse, affine[:8], affine[8:16], variance, other],
            axis=0,
        )
        row_ref[...] = rows
        col_ref[...] = tall(rows)

    for z in range(4):
        span = slice(z * chans, (z + 1) * chans)
        for branch in range(4):
            moved = pre_ref[z, branch] - col_ref[span, CENTRE + branch : CENTRE + branch + 1]
            normed = (
                col_ref[span, GAIN + branch : GAIN + branch + 1]
                * moved
                * col_ref[span, INVERSE + branch : INVERSE + branch + 1]
                + col_ref[span, SHIFT + branch : SHIFT + branch + 1]
            )
            first = (4 * z + branch) * chans
            out_ref[0, first : first + chans, :] = gelu_both(normed)[0].astype(bf16)
    normed, _, valid = pool_rows_of(row_ref, 4 * chans)
    act = jnp.where(valid, gelu_both(normed)[0], 0.0)
    act = put_rows((EXTRA, LANES), {0: act + pltpu.roll(act, 4 * chans, 1)})
    lane = lax.broadcasted_iota(jnp.int32, act.shape, 1)
    for at in range(out_ref.shape[2] // LANES):
        owner = (lane + at * LANES) // (4 * chans)
        out_ref[0, 16 * chans :, at * LANES : (at + 1) * LANES] = jnp.where(
            owner == quad_ref[0], act, 0.0
        ).astype(bf16)


def activations(quad, parts, own, shared, pre, image_total):
    chans, total = pre.shape[2:]
    strip = total // 4
    rows = 16 * chans + EXTRA
    return call(
        functools.partial(act_kernel, image_total),
        "branch_act",
        (4,),
        1,
        [
            full(parts.shape),
            full((1, SUM_ROWS, LANES)),
            pl.BlockSpec((shared.shape[0], LANES), lambda i, s: (0, shared.shape[1] // LANES - 1)),
            pl.BlockSpec((4, 4, chans, strip), lambda i, s: (0, 0, 0, i)),
        ],
        (
            pl.BlockSpec((1, rows, strip), lambda i, s: (i, 0, 0)),
            full((LANES, LANES)),
            full((COEF_ROWS, LANES)),
        ),
        (
            jax.ShapeDtypeStruct((4, rows, strip), bf16),
            jax.ShapeDtypeStruct((LANES, LANES), f32),
            jax.ShapeDtypeStruct((COEF_ROWS, LANES), f32),
        ),
        vmem=24,
    )(quad, parts, own, shared, pre)


def unit_kernel(x_ref, shared_ref, mask_ref, unit_ref, out_ref):
    channels = shared_ref.shape[0]
    rows, strip = x_ref.shape[0] // 4, x_ref.shape[1]
    proj = shared_ref[:, channels + strip : shared_ref.shape[1] - TERMS]
    unit = jnp.dot(proj, x_ref[...], preferred_element_type=f32)
    act = jnp.zeros((EXTRA, channels), f32)
    for quad in range(4):
        first = quad * rows + rows - EXTRA
        act = act + x_ref[first : first + EXTRA, :channels].astype(f32)
    bias = shared_ref[:, :channels].astype(f32) * act[0:1, :]
    unit = unit + jnp.sum(bias, axis=1, keepdims=True)
    unit_ref[...] = unit
    weighted = unit * mask_ref[0:1, :]
    one = jnp.sum(weighted, axis=1, keepdims=True)
    two = jnp.sum(weighted * unit, axis=1, keepdims=True)
    sums = put_lanes((channels, LANES), {0: one, 1: two}).T[:8]
    sums = stacked(sums, 2)
    for at in range(out_ref.shape[0]):
        out_ref[at] = sums


def project(concat, shared, strip_mask, count):
    channels, strip = shared.shape[0], concat.shape[1]
    arrays = (concat, shared, strip_mask)
    return call(
        unit_kernel,
        "projection",
        (1,),
        0,
        [full(array.shape) for array in arrays],
        (full((channels, strip)), full((count, 4, LANES))),
        (
            jax.ShapeDtypeStruct((channels, strip), f32),
            jax.ShapeDtypeStruct((count, 4, LANES), f32),
        ),
        vmem=24,
    )(*arrays)


def head_kernel(parts_ref, unit_ref, shared_ref, mask_ref, row_ref, value_ref, delta_ref, col_ref, head_ref, out_ref):
    sums = unstacked(jnp.sum(parts_ref[...], axis=0))
    pixel_total = row_ref[COUNT : COUNT + 1, 0:1]
    centre = sums[0:1] / pixel_total
    variance = sums[1:2] / pixel_total - centre * centre
    inverse = lax.rsqrt(variance + epsilon)
    rows = put_rows(
        sums.shape, {0: centre, 1: inverse, 4: variance}
    )
    head_ref[...] = rows
    columns = tall(rows)
    width = shared_ref.shape[1]
    block = shared_ref[:, width - LANES :].astype(f32)
    lane = lax.broadcasted_iota(jnp.int32, columns.shape, 1)
    gain = term_sum(block, 0, 5, LANES - TERMS)
    shift = term_sum(block, 1, 5, LANES - TERMS)
    columns = jnp.where(lane == 2, gain, jnp.where(lane == 3, shift, columns))
    col_ref[...] = columns
    hat = (unit_ref[...] - columns[:, 0:1]) * columns[:, 1:2]
    normed = columns[:, 2:3] * hat + columns[:, 3:4]
    value, slope = gelu_both(normed)
    weight = mask_ref[0:1, :]
    value_ref[...] = (weight * value).astype(bf16)
    first = unit_ref.shape[0]
    cot = shared_ref[:, first : first + unit_ref.shape[1]].astype(f32)
    delta = slope * (weight * cot)
    delta_ref[...] = delta
    sums = put_lanes(
        columns.shape,
        {
            0: jnp.sum(delta, axis=1, keepdims=True),
            1: jnp.sum(delta * hat, axis=1, keepdims=True),
        },
    ).T[:8]
    sums = stacked(sums, 2)
    for at in range(out_ref.shape[0]):
        out_ref[at] = sums


def head_norm(parts, unit, shared, strip_mask, coef_rows):
    channels, strip = unit.shape
    count = parts.shape[0]
    return call(
        head_kernel,
        "head_norm",
        (1,),
        0,
        [full(parts.shape), full(unit.shape), full(shared.shape), full((8, strip)), full(coef_rows.shape)],
        (
            full((channels, strip)),
            full((channels, strip)),
            full((channels, LANES)),
            full((8, channels)),
            full((count, 4, LANES)),
        ),
        (
            jax.ShapeDtypeStruct((channels, strip), bf16),
            jax.ShapeDtypeStruct((channels, strip), f32),
            jax.ShapeDtypeStruct((channels, LANES), f32),
            jax.ShapeDtypeStruct((8, channels), f32),
            jax.ShapeDtypeStruct((count, 4, LANES), f32),
        ),
        vmem=24,
    )(parts, unit, shared, strip_mask, coef_rows)


def unit_back_kernel(
    parts_ref, unit_ref, delta_ref, col_ref, mask_ref, row_ref, shared_ref, back_ref, out_ref, sum_ref, moment_ref
):
    sums = unstacked(jnp.sum(parts_ref[...], axis=0))
    moment_ref[...] = sums
    moments = tall(sums)
    pixel_total = row_ref[COUNT : COUNT + 1, 0:1]
    inverse = col_ref[:, 1:2]
    hat = (unit_ref[...] - col_ref[:, 0:1]) * inverse
    back = mask_ref[0:1, :] * (
        (col_ref[:, 2:3] * inverse)
        * (delta_ref[...] - (moments[:, 0:1] + hat * moments[:, 1:2]) / pixel_total)
    )
    back = back.astype(bf16)
    back_ref[...] = back
    row_sums = jnp.sum(back.astype(f32), axis=1, keepdims=True)
    sum_ref[...] = jnp.broadcast_to(row_sums, sum_ref.shape)
    channels = shared_ref.shape[0]
    rows, width = out_ref.shape[1:]
    proj = shared_ref[:, channels + width : shared_ref.shape[1] - TERMS]
    terms = lax.dot_general(
        proj, back, (((0,), (0,)), ((), ())), preferred_element_type=f32
    )
    pool = jnp.sum(shared_ref[:, :channels].astype(f32) * row_sums, axis=0, keepdims=True)
    own = channels // 4
    for quad in range(4):
        first = quad * own // LANES * LANES
        part = pool[:, first : first + LANES]
        if quad * own != first:
            part = pltpu.roll(part, LANES - (quad * own - first), 1)
        lane = lax.broadcasted_iota(jnp.int32, part.shape, 1)
        part = jnp.where(lane < own, part, 0.0)
        high = part.astype(bf16).astype(f32)
        extra = put_rows((EXTRA, LANES), {0: high, 1: part - high})
        out_ref[quad, : rows - EXTRA, :] = terms[quad * rows : (quad + 1) * rows - EXTRA].astype(bf16)
        out_ref[quad, rows - EXTRA :, :LANES] = extra.astype(bf16)
        out_ref[quad, rows - EXTRA :, LANES:] = jnp.zeros((EXTRA, width - LANES), bf16)


def unit_backward(parts, unit, delta, cols, strip_mask, coef_rows, shared):
    channels, strip = unit.shape
    rows = (shared.shape[1] - channels - strip - TERMS) // 4
    arrays = (parts, unit, delta, cols, strip_mask, coef_rows, shared)
    return call(
        unit_back_kernel,
        "unit_back",
        (1,),
        0,
        [full(array.shape) for array in arrays],
        (
            full((channels, strip)),
            full((4, rows, strip)),
            full((channels, LANES)),
            full((8, channels)),
        ),
        (
            jax.ShapeDtypeStruct((channels, strip), bf16),
            jax.ShapeDtypeStruct((4, rows, strip), bf16),
            jax.ShapeDtypeStruct((channels, LANES), f32),
            jax.ShapeDtypeStruct((8, channels), f32),
        ),
        vmem=24,
    )(*arrays)


def branch_kernel(x_ref, pre_ref, col_ref, row_ref, mask_ref, delta_ref, pool_ref, out_ref, sums, pooled):
    step = pl.program_id(0)
    chans = pre_ref.shape[2]

    @pl.when(step == 0)
    def _():
        sums[...] = jnp.zeros_like(sums)
        pooled[...] = jnp.zeros_like(pooled)

    def fold(value):
        total = value[:, :LANES]
        for at in range(1, value.shape[1] // LANES):
            total = total + value[:, at * LANES : (at + 1) * LANES]
        return total

    weight = mask_ref[0:1, :]
    for z in range(4):
        span = slice(z * chans, (z + 1) * chans)
        for branch in range(4):
            first = (4 * z + branch) * chans
            hat = (
                pre_ref[z, branch] - col_ref[span, CENTRE + branch : CENTRE + branch + 1]
            ) * col_ref[span, INVERSE + branch : INVERSE + branch + 1]
            normed = (
                col_ref[span, GAIN + branch : GAIN + branch + 1] * hat
                + col_ref[span, SHIFT + branch : SHIFT + branch + 1]
            )
            delta = gelu_both(normed)[1] * (
                weight * x_ref[0, first : first + chans, :].astype(f32)
            )
            delta_ref[z, branch] = delta
            sums[8 * z + branch] = sums[8 * z + branch] + fold(delta)
            sums[8 * z + 4 + branch] = sums[8 * z + 4 + branch] + fold(delta * hat)
    extra = x_ref[0, 16 * chans :, :LANES].astype(f32)
    pooled[...] = pooled[...] + jnp.broadcast_to(extra[0:1] + extra[1:2], pooled.shape)

    @pl.when(step == pl.num_programs(0) - 1)
    def _():
        normed, hat, valid = pool_rows_of(row_ref, 4 * chans)
        delta = jnp.where(valid, gelu_both(normed)[1] * pooled[0:1, :], 0.0)
        hat = jnp.where(valid, hat, 0.0)
        pool_ref[...] = put_rows(pool_ref.shape, {0: delta, 1: hat})
        found = []
        for z in range(4):
            columns = {}
            for branch in range(4):
                columns[branch] = jnp.sum(sums[8 * z + branch], axis=1, keepdims=True)
                columns[8 + branch] = jnp.sum(sums[8 * z + 4 + branch], axis=1, keepdims=True)
            found.append(put_lanes((chans, LANES), columns))
        found.append(jnp.zeros((LANES - 4 * chans, LANES), f32))
        rows = jnp.concatenate(found, axis=0).T[:16]
        index = lax.broadcasted_iota(jnp.int32, rows.shape, 0)
        rows = jnp.where(index == 4, delta, jnp.where(index == 12, delta * hat, rows))
        rows = beside(rows[:8], rows[8:16], 4 * chans)
        for at in range(out_ref.shape[0]):
            out_ref[at] = rows


def branch_backward(concat_back, pre, coef_cols, coef_rows, mask_rows, count, after):
    chans, total = pre.shape[2:]
    rows, strip = concat_back.shape[1:]
    spread = pl.BlockSpec((4, 4, chans, strip), lambda i: (0, 0, 0, i))
    return call(
        branch_kernel,
        "branch_back",
        (4,),
        0,
        [
            pl.BlockSpec((1, rows, strip), lambda i: (i, 0, 0)),
            spread,
            full(coef_cols.shape),
            full(coef_rows.shape),
            pl.BlockSpec((8, strip), lambda i: (0, i)),
        ],
        (spread, full((8, LANES)), full((count, 8, LANES))),
        (
            jax.ShapeDtypeStruct(pre.shape, f32),
            jax.ShapeDtypeStruct((8, LANES), f32),
            jax.ShapeDtypeStruct((count, 8, LANES), f32),
        ),
        [pltpu.VMEM((32, chans, LANES), f32), pltpu.VMEM((8, LANES), f32)],
        after=after,
        vmem=24,
    )(concat_back, pre, coef_cols, coef_rows, mask_rows)


def weight_kernel(columns, image_total, slots, scalar_ref, parts_ref, pool_ref, mask_ref, x_ref, *refs):
    count = len(slots)
    col_refs, pre_refs, delta_refs = refs[:count], refs[count : 2 * count], refs[2 * count : 3 * count]
    outs = refs[3 * count : 6 * count]
    total_ref, moments = refs[6 * count :]
    half = outs[0].shape[0]
    chans = pre_refs[0].shape[2]
    start = 29 * chans - half
    sel = scalar_ref[HALF]

    @pl.when(pl.program_id(0) == 0)
    def _():
        sums = jnp.sum(parts_ref[...], axis=0)
        second = pltpu.roll(sums, LANES // 2, 1)
        moments[...] = tall(jnp.concatenate([sums, second, pool_ref[...]], axis=0))
        height = jnp.full((1, 1), scalar_ref[HEIGHT], jnp.int32).astype(f32)
        area = 2.0 * height * height
        masks = lane_masks(columns)
        for at, slot in enumerate(slots):
            own = moments[pl.ds(pl.multiple_of(scalar_ref[4 + slot] * chans, chans), chans), :]
            build_taps(
                own, col_refs[at][...], pre_refs[at], delta_refs[at], mask_ref, outs[3 * at + 2], masks, area, columns, image_total
            )

    for at in range(count):
        keep_ref, send_ref, taps_ref = outs[3 * at : 3 * at + 3]
        total_ref[...] = jnp.dot(taps_ref[...], x_ref[...], preferred_element_type=f32)
        keep_ref[...] = total_ref[pl.ds(pl.multiple_of(sel * start, 16), half), :].astype(bf16)
        send_ref[...] = total_ref[pl.ds(pl.multiple_of((1 - sel) * start, 16), half), :].astype(bf16)


def build_taps(own, coefs, pre_ref, delta_ref, mask_ref, taps_ref, masks, area, columns, image_total):
    chans = pre_ref.shape[2]

    def coef(at):
        return coefs[:, at : at + 1]

    def moment(at):
        return own[:, at : at + 1]

    pixel_total = coef(COUNT)
    pool_grad = (
        coef(GAIN + 4)
        * coef(INVERSE + 4)
        * (moment(16) - (moment(4) + moment(17) * moment(12)) / image_total)
    ) / area
    tiles = pre_ref.shape[3] // LANES
    for at in range(tiles):
        lanes = slice(at * LANES, (at + 1) * LANES)
        weight = mask_ref[0:1, lanes]
        taps_ref[28 * chans : 29 * chans, lanes] = (weight * pool_grad).astype(bf16)
        for branch in range(4):
            hat = (pre_ref[0, branch, :, lanes] - coef(CENTRE + branch)) * coef(INVERSE + branch)
            grad = weight * (
                (coef(GAIN + branch) * coef(INVERSE + branch))
                * (
                    delta_ref[0, branch, :, lanes]
                    - (moment(branch) + hat * moment(8 + branch)) / pixel_total
                )
            )
            if branch == 0:
                taps_ref[0:chans, lanes] = grad.astype(bf16)
                continue
            j, dilation = branch - 1, dilations[branch - 1]
            jump = dilation * columns // LANES
            for b in range(3):
                off = (b - 1) * dilation
                moved = grad
                if off != 0:
                    moved = pltpu.roll(grad, off % LANES, 1)
                    moved = jnp.where(masks[-off], moved, 0.0)
                moved = moved.astype(bf16)
                for a in range(3):
                    tap = 1 + 9 * j + 3 * a + b
                    span = slice(tap * chans, (tap + 1) * chans)
                    target = at + (a - 1) * jump
                    if 0 <= target < tiles:
                        taps_ref[span, target * LANES : (target + 1) * LANES] = moved
                    source = at - (a - 1) * jump
                    if not 0 <= source < tiles:
                        taps_ref[span, lanes] = jnp.zeros((chans, LANES), bf16)


def weight_grads(
    slots, scalars, parts, pool_rows, coef_cols, pre, delta, mask_rows, pixels, columns, half, image_total, after
):
    chans, total = pre.shape[2:]
    depth = pixels.shape[1]
    count = len(slots)
    steps = 2 if count == 1 else 4
    block = depth // steps

    def cols(slot):
        return pl.BlockSpec((chans, LANES), lambda i, s: (s[4 + slot], 0))

    def own(slot):
        return pl.BlockSpec((1, 4, chans, total), lambda i, s: (s[4 + slot], 0, 0, 0))

    outs = call(
        functools.partial(weight_kernel, columns, image_total, slots),
        "atrous_weight_grad",
        (steps,),
        1,
        [
            full(parts.shape),
            full(pool_rows.shape),
            full(mask_rows.shape),
            pl.BlockSpec((total, block), lambda i, s: (0, i)),
        ]
        + [cols(slot) for slot in slots]
        + [own(slot) for slot in slots] * 2,
        (
            pl.BlockSpec((half, block), lambda i, s: (0, i)),
            pl.BlockSpec((half, block), lambda i, s: (0, i)),
            full((29 * chans, total)),
        )
        * count,
        (
            jax.ShapeDtypeStruct((half, depth), bf16),
            jax.ShapeDtypeStruct((half, depth), bf16),
            jax.ShapeDtypeStruct((29 * chans, total), bf16),
        )
        * count,
        [pltpu.VMEM((29 * chans, block), f32), pltpu.VMEM((LANES, LANES), f32)],
        after=after,
        vmem=28 if slots[0] == 3 else 56,
    )(
        scalars,
        parts,
        pool_rows,
        mask_rows,
        pixels,
        *[coef_cols] * count,
        *[pre] * count,
        *[delta] * count,
    )
    return [outs[3 * at : 3 * at + 3] for at in range(count)]


def input_kernel(start, places, scalar_ref, *refs):
    taps, weights, outs = refs[0:4], refs[4:12], refs[12:15]
    all_weights, all_taps, result, weight_sems, tap_sems, out_sems = refs[15:]
    half, depth = weights[0].shape
    block = all_taps.shape[2]
    cut = depth // 2

    def tap_copies(strip):
        copies = []
        lanes = pl.ds(pl.multiple_of(scalar_ref[places[strip]] * block, LANES), block)
        for slot in range(4):
            sel = scalar_ref[slot]
            for which in range(2):
                first = sel * start if which == 0 else (1 - sel) * start
                at = 2 * slot + which
                copies.append(
                    pltpu.make_async_copy(
                        taps[slot].at[pl.ds(pl.multiple_of(first, 16), half), lanes],
                        all_taps.at[strip, pl.ds(at * half, half), :],
                        tap_sems.at[strip, at],
                    )
                )
        return copies

    def weight_copies(part):
        lanes = pl.ds(part * cut, cut)
        return [
            pltpu.make_async_copy(
                weights[at].at[:, lanes],
                all_weights.at[pl.ds(at * half, half), lanes],
                weight_sems.at[part, at],
            )
            for at in range(8)
        ]

    tap_lists = [tap_copies(0), tap_copies(1)]
    weight_lists = [weight_copies(0), weight_copies(1)]
    for copies in (tap_lists[0], weight_lists[0], weight_lists[1], tap_lists[1]):
        for copy in copies:
            copy.start()
    rows = outs[0].shape[0]
    out_lists = [
        [
            pltpu.make_async_copy(result.at[0, pl.ds(0, rows), :], outs[0], out_sems.at[0]),
            pltpu.make_async_copy(result.at[0, pl.ds(rows, rows), :], outs[1], out_sems.at[1]),
        ],
        [pltpu.make_async_copy(result.at[1], outs[2], out_sems.at[2])],
    ]
    for strip in range(2):
        for copy in tap_lists[strip]:
            copy.wait()
        for part in range(2):
            if strip == 0:
                for copy in weight_lists[part]:
                    copy.wait()
            lanes = slice(part * cut, (part + 1) * cut)
            result[strip, :, lanes] = lax.dot_general(
                all_taps[strip],
                all_weights[:, lanes],
                (((0,), (0,)), ((), ())),
                preferred_element_type=f32,
            ).astype(bf16)
        for copy in out_lists[strip]:
            copy.start()
    for copies in out_lists:
        for copy in copies:
            copy.wait()


def input_grads(flip, taps, weights, scalars, block, after):
    rows = taps[0].shape[0]
    half, depth = weights[0].shape
    shapes = ((block // 2, depth), (block // 2, depth), (block, depth))
    anywhere = pl.BlockSpec(memory_space=pl.ANY)
    low, high, own = call(
        functools.partial(input_kernel, rows - half, (HALF + 2 + flip, HALF + 1 + flip)),
        "atrous_input_grad",
        (1,),
        1,
        [anywhere] * 12,
        (anywhere,) * 3,
        tuple(jax.ShapeDtypeStruct(shape, bf16) for shape in shapes),
        [
            pltpu.VMEM((8 * half, depth), bf16),
            pltpu.VMEM((2, 8 * half, block), bf16),
            pltpu.VMEM((2, block, depth), bf16),
            pltpu.SemaphoreType.DMA((2, 8)),
            pltpu.SemaphoreType.DMA((2, 8)),
            pltpu.SemaphoreType.DMA((3,)),
        ],
        after=after,
        vmem=58,
    )(scalars, *taps, *weights)
    return [low, high], own


def local(
    features,
    scale_sizes,
    cotangent,
    branch_weight,
    branch_first,
    branch_second,
    head_weight,
    head_first,
    head_second,
    norm_params,
    norm_first,
    norm_second,
    running_stats,
):
    groups = lax.axis_size("dp")
    halves = groups == 2
    images = scale_sizes.shape[1]
    image_total = float(groups * images)
    x_id, z_id = lax.axis_index("dp"), lax.axis_index("z")
    quad_id = lax.axis_index("y") * 2 + lax.axis_index("c")
    wide_id = z_id * 4 + quad_id
    strip_rows, columns, depth = features.shape[1:]
    strip = strip_rows * columns
    total = 4 * strip
    tap_count, chans = branch_weight.shape[:2]
    all_ch = chans * 16
    split = (tap_count - 1) // 2
    half = (split + 1) * chans
    cells, everyone = ("dp", "z"), ("dp",) + PLANE
    rows = 16 * chans + EXTRA

    def exchange(parts, axes):
        return lax.all_to_all(parts, axes, 0, 0, tiled=True)

    height = lax.dynamic_index_in_dim(scale_sizes[0], z_id, 0, keepdims=False)
    pixel = jnp.arange(total, dtype=jnp.int32)
    inside = jnp.logical_and(pixel // columns < height, pixel % columns < 2 * height).astype(f32)
    own_inside = lax.dynamic_slice_in_dim(inside, quad_id * strip, strip, 0)
    mask_rows = jnp.broadcast_to(inside[None], (8, total))
    strip_mask = jnp.broadcast_to(own_inside[None], (8, strip))

    mid = jnp.logical_and(z_id >= 1, z_id <= 2).astype(jnp.int32)[None]

    sel = x_id.astype(jnp.int32) if halves else jnp.zeros((), jnp.int32)
    outer = z_id >= 2
    scalars = jnp.stack(
        [sel, sel, sel, sel]
        + [z_id, jnp.bitwise_xor(z_id, 1), jnp.where(outer, 1, 2), jnp.where(outer, 0, 3)]
        + [height, sel]
        + [jnp.bitwise_xor(quad_id, flip) for flip in range(4)]
    ).astype(jnp.int32)
    def over_groups(block):
        return lax.ppermute(block, "dp", SWAP)

    def along(parts, pairs):
        return [lax.ppermute(part, "z", pairs) for part in parts]

    def hold(parts, after):
        return [held(part, after) for part in parts]

    def pair_of(parts):
        return (parts[0], over_groups(parts[0])) if halves else tuple(parts)

    def pick_all(ones, twos, after):
        return [pick(mid, one, two, after) for one, two in zip(ones, twos)]

    zero = jnp.zeros((), jnp.int32)
    mine_w = cast_half(sel[None], branch_weight, split, ())
    other_w = cast_half(1 - sel[None], branch_weight, split, (mine_w,))
    sending = [mine_w] if halves else [mine_w, other_w]
    near, mid_one = along(sending, PAIR), along(sending, MID)

    own_strip = features[0].reshape(strip, depth)
    cut = strip // 16 * 7
    (masked_low,) = mask_strip(scalars, own_strip, columns, cut, (cut,), sending)
    masked, masked_high = mask_strip(
        scalars, own_strip, columns, strip, (strip, strip - cut), (masked_low,)
    )
    masked_parts = masked_low, masked_high
    low_y, high_y = (lax.ppermute(part, "y", SWAP) for part in masked_parts)
    over_c = lax.ppermute(masked, "c", SWAP)

    own_proj = head_weight.astype(bf16).reshape(chans, 5, 4, 4, chans)
    own_proj = jnp.transpose(own_proj, (0, 3, 2, 1, 4))
    pixel_proj = jnp.pad(
        own_proj[:, :, :, :4].reshape(chans, 4, 16 * chans), ((0, 0), (0, 0), (0, EXTRA))
    ).reshape(chans, 4 * rows)
    value = jnp.transpose(norm_params.reshape(12, chans))
    terms = []
    for _ in range(3):
        terms.append(barrier(value.astype(bf16)))
        value = value - terms[-1].astype(f32)
    terms = jnp.pad(jnp.stack(terms, axis=2).reshape(chans, 36), ((0, 0), (0, TERMS - 36)))
    shared = jnp.concatenate(
        [
            jnp.broadcast_to(own_proj[:, :, :, 4].reshape(1, chans, all_ch), (16, chans, all_ch)),
            jnp.transpose(cotangent[0].reshape(chans, 16, strip), (1, 0, 2)),
            jnp.broadcast_to(pixel_proj[None], (16, chans, 4 * rows)),
            jnp.broadcast_to(terms[None], (16, chans, TERMS)),
        ],
        axis=2,
    )

    slots = [(mine_w, other_w)]
    near = hold(near, [masked, mask_rows, scalars])
    mid_two = along(near, MID)
    near = pair_of(near)
    mid_one = hold(mid_one, near[:1])
    out_one = along(mid_one, OUTWARD)
    low_y = held(low_y, mid_one)
    mid_two = hold(mid_two, [low_y, other_w, shared, strip_mask])
    out_two = along(mid_two, OUTWARD)
    second = pick_all(mid_one, out_one, mid_two)
    second_pair = pair_of(second)
    high_y = held(high_y, second)
    low_yc, high_yc = (lax.ppermute(part, "c", SWAP) for part in (low_y, high_y))
    near = (near[0], held(near[1], (high_y,)))
    slots.append(near)
    parts = ((masked,), (over_c,), (low_y, high_y), (low_yc, high_yc))
    pixels = image_of(scalars, strip, parts, near[1:])

    def branch(slot, state, after):
        return forward_taps(
            slot, pixels, mask_rows, scalars, *slots[slot], state, columns, chans, split, after
        )

    state = branch(0, (), ())
    slots.append((second_pair[0], held(second_pair[1], [state[1]])))
    third = pick_all(mid_two, out_two, slots[2][1:])
    slots.append(pair_of(third))
    shared = exchange(held(shared, third), PLANE)
    shared = shared.reshape(all_ch, all_ch + strip + 4 * rows + TERMS)
    state = branch(1, state, third)
    state = branch(2, state, ())
    state = branch(3, state, ())
    pre, stats = state
    own_sums = pack_sums(stats, axes_size(cells), (shared,))
    quad = quad_id.astype(jnp.int32)[None]
    concat, coef_cols, coef_rows = activations(
        quad, exchange(own_sums, cells), own_sums, shared, pre, image_total
    )
    concat = exchange(concat, QUAD).reshape(4 * rows, strip)

    unit, head_sums = project(concat, shared, strip_mask, axes_size(everyone))
    head_values, head_delta, head_coefs, head_rows, head_sums = head_norm(
        exchange(head_sums, everyone), unit, shared, strip_mask, coef_rows
    )
    unit_back, concat_back, row_sums, head_moments = unit_backward(
        exchange(head_sums, everyone),
        unit,
        head_delta,
        head_coefs,
        strip_mask,
        coef_rows,
        shared,
    )

    delta, pool_rows, moments = branch_backward(
        exchange(concat_back, QUAD), pre, coef_cols, coef_rows, mask_rows, axes_size(cells), ()
    )
    moments = exchange(moments, cells)

    def weights_of(slots, after):
        return weight_grads(
            slots,
            scalars,
            moments,
            pool_rows,
            coef_cols,
            pre,
            delta,
            mask_rows,
            pixels,
            columns,
            half,
            image_total,
            after,
        )

    def group_sums(slot, after, *lists):
        if halves:
            return [add(slot[0], over_groups(slot[1]), *(parts[0] for parts in lists), after=after)]
        return [add(*parts, after=after) for parts in zip(slot[:2], *lists)]

    def swap_all(parts, axis):
        return [lax.ppermute(part, axis, SWAP) for part in parts]

    def add_all(*lists, after=()):
        return [add(*parts, after=after) for parts in zip(*lists)]

    flat_w = [part for slot in slots for part in slot]

    def features_of(flip, after):
        return input_grads(flip, taps, flat_w, scalars, strip, after)

    ((keep_c, send_c, taps_c),) = weights_of((3,), ())
    head_parts = head_weight_grads(concat, unit_back, row_sums, head_values, (taps_c,))
    head_parts = exchange(head_parts.reshape(16, chans, all_ch + strip + 4 * rows), PLANE)
    slot_b, slot_a, slot_o = weights_of((2, 1, 0), (taps_c,))
    taps = [slot_o[2], slot_a[2], slot_b[2], taps_c]
    third = group_sums((keep_c, send_c), (slot_o[2], head_parts))
    far_cross, far = features_of(2, third)
    second = group_sums(slot_b, (far,))
    mid_two = add_all(third, along(third, INWARD), after=second)
    far = strip_sum(scalars, (far,), swap_all(far_cross, "c"), columns, False, mid_two)
    near = group_sums(slot_a, (far,), along(mid_two, MID))
    mid_one = add_all(second, along(second, INWARD), after=near)

    head_output = head_parts[:, :, all_ch : all_ch + strip]
    head_output = jnp.transpose(head_output, (1, 0, 2)).reshape(1, chans, 16 * strip)
    head_parts = jnp.sum(head_parts.astype(f32), axis=0)
    pool_part = head_parts[:, :all_ch].reshape(chans, 4, 4, 1, chans)
    pixel_part = head_parts[:, all_ch + strip :].reshape(chans, 4, rows)[:, :, : 16 * chans]
    pixel_part = pixel_part.reshape(chans, 4, 4, 4, chans)
    head_grads = jnp.concatenate([pixel_part, pool_part], axis=3)
    head_grads = jnp.transpose(head_grads, (0, 3, 2, 1, 4)).reshape(chans, 5 * all_ch)
    near_cross, own_part = features_of(0, (*mid_one, head_grads))
    if halves:
        head_grads = head_grads + lax.ppermute(head_grads, "dp", SWAP)
    else:
        head_grads = lax.psum(head_grads, "dp")
    mine = group_sums(slot_o, (own_part, head_grads), along(near, PAIR), along(mid_one, MID))
    state = (branch_weight, branch_first, branch_second)
    if halves:
        other = over_groups(mine[0])
    else:
        mine = [lax.psum(part, "dp") for part in mine]
    cross = swap_all(near_cross, "c")
    total = held(own_part, mine).astype(f32) + jnp.concatenate(cross, axis=0).astype(f32)
    total = total + lax.ppermute(far, "y", SWAP).astype(f32)
    input_grad = (total * own_inside[:, None]).astype(bf16)
    input_grad = input_grad.reshape(1, strip_rows, columns, depth)
    start = jnp.stack([sel * split, zero])
    done = adam_taps(start, split + 1, 5, mine[0], *state, (), (input_grad,))
    start = jnp.stack([(1 - sel) * (split + 1), 1 - sel])
    done = adam_taps(start, split, 7, other if halves else mine[1], *state, done, ())
    branch_grads, branch_means, branch_squares, branch_updated = done

    def own_lanes(by_row):
        return lax.dynamic_slice_in_dim(by_row, z_id * chans, chans, 1)

    def own_head(by_row):
        return lax.dynamic_slice_in_dim(by_row, wide_id * chans, chans, 1)

    moments = jnp.sum(moments, axis=0)
    own_firsts, own_seconds = own_lanes(moments), own_lanes(moments[:, 4 * chans :])
    head_own = own_head(head_moments)
    norm_grads = jnp.stack(
        [
            jnp.concatenate([own_seconds[0:5], head_own[1:2]]),
            jnp.concatenate([own_firsts[0:5], head_own[0:1]]),
        ]
    )
    own_coefs, head_stats = own_lanes(coef_rows), own_head(head_rows)
    pixel_total = coef_rows[COUNT, 0]
    all_centres = jnp.concatenate([own_coefs[CENTRE : CENTRE + 5], head_stats[0:1]])
    all_variances = jnp.concatenate([own_coefs[VARIANCE : VARIANCE + 5], head_stats[4:5]])
    factors = jnp.where(
        jnp.arange(6) == 4, image_total / (image_total - 1.0), pixel_total / (pixel_total - 1.0)
    )
    running_next = (1.0 - momentum) * running_stats + momentum * jnp.stack(
        [all_centres, all_variances * factors[:, None]]
    )
    head_means, head_squares, head_updated = adamw_update(
        head_weight, head_grads, head_first, head_second, conv_rate, weight_decay
    )
    norm_means, norm_squares, norm_updated = adamw_update(
        norm_params, norm_grads, norm_first, norm_second, norm_rate, 0.0
    )
    return (
        head_output,
        input_grad,
        branch_grads,
        branch_means,
        branch_squares,
        branch_updated,
        head_grads,
        head_means,
        head_squares,
        head_updated,
        norm_grads,
        norm_means,
        norm_squares,
        norm_updated,
        running_next,
    )


def solution(mesh):
    groups, wide = mesh.devices.shape
    fine = Mesh(mesh.devices.reshape(groups, 4, 2, wide // 8), ("dp",) + PLANE)
    placed = (
        P("dp", PLANE, None, None),
        P("dp", None),
        P("dp", PLANE, None),
        P(None, PLANE, None),
        P(None, PLANE, None),
        P(None, PLANE, None),
        P(PLANE, None),
        P(PLANE, None),
        P(PLANE, None),
        P(None, None, PLANE),
        P(None, None, PLANE),
        P(None, None, PLANE),
        P(None, None, PLANE),
    )
    return jax.shard_map(
        local,
        mesh=fine,
        in_specs=placed,
        out_specs=(
            P("dp", PLANE, None),
            P("dp", PLANE, None, None),
            P(None, PLANE, None),
            P(None, PLANE, None),
            P(None, PLANE, None),
            P(None, PLANE, None),
            P(PLANE, None),
            P(PLANE, None),
            P(PLANE, None),
            P(PLANE, None),
            P(None, None, PLANE),
            P(None, None, PLANE),
            P(None, None, PLANE),
            P(None, None, PLANE),
            P(None, None, PLANE),
        ),
        check_vma=False,
    )
```
